32 devices in a mesh: rows: 4 (over y, x), seq: 8 (over z, core).
Axes of the slice: x: 2, y: 2, z: 4, core: 2. Of those that a mesh axis runs over, the one named last changes fastest.
Arguments:
- tokens: bfloat16 [12, 1024, 1024], P('rows', 'seq'), may hold values from -6 to 6
- bounds: int32 [12, 8], P('rows'), may hold values from 1 to 1023, as said below
- norm1_gain: float32 [1024], replicated, may hold values from 0.5 to 1.5
- w_branch: bfloat16 [1024, 1536], P('seq'), may hold values from -0.1875 to 0.1875
- w_rec: bfloat16 [1024, 1536], P('seq'), may hold values from -0.1875 to 0.1875
- conv_weight: float32 [4, 1536], replicated, may hold values from -3 to 3
- conv_bias: float32 [1536], replicated, may hold values from -3 to 3
- w_rate: bfloat16 [1536, 1536], P('seq'), may hold values from -0.15625 to 0.15625
- rate_bias: float32 [1536], replicated, may hold values from -4 to 4
- w_input: bfloat16 [1536, 1536], P('seq'), may hold values from -0.15625 to 0.15625
- input_bias: float32 [1536], replicated, may hold values from -4 to 4
- decay_param: float32 [1536], replicated, may hold values from -14 to -3
- w_out: bfloat16 [1536, 1024], P('seq'), may hold values from -0.3125 to 0.3125
- norm2_gain: float32 [1024], replicated, may hold values from 0.5 to 1.5
- w_gate: bfloat16 [1024, 3072], P('seq'), may hold values from -0.1875 to 0.1875
- w_up: bfloat16 [1024, 3072], P('seq'), may hold values from -0.1875 to 0.1875
- w_down: bfloat16 [3072, 1024], P('seq'), may hold values from -0.15625 to 0.15625
- cotangent: bfloat16 [12, 1024, 1024], P('rows', 'seq'), may hold values from -6 to 6
Outputs:
- mixed: bfloat16 [12, 1024, 1024], P('rows', 'seq')
- token_grad: bfloat16 [12, 1024, 1024], P('rows', 'seq')
- grad_norm1: float32 [1024], replicated
- grad_w_branch: float32 [1024, 1536], P('seq')
- grad_w_rec: float32 [1024, 1536], P('seq')
- grad_conv_weight: float32 [4, 1536], replicated
- grad_conv_bias: float32 [1536], replicated
- grad_w_rate: float32 [1536, 1536], P('seq')
- grad_rate_bias: float32 [1536], replicated
- grad_w_input: float32 [1536, 1536], P('seq')
- grad_input_bias: float32 [1536], replicated
- grad_decay_param: float32 [1536], replicated
- grad_w_out: float32 [1536, 1024], P('seq')
- grad_norm2: float32 [1024], replicated
- grad_w_gate: float32 [1024, 3072], P('seq')
- grad_w_up: float32 [1024, 3072], P('seq')
- grad_w_down: float32 [3072, 1024], P('seq')
The draws below stay inside these ranges and needn't reach their ends.
Inputs may be any that keep to these rules, and one draw needn't show every extreme that they name: `bounds`: sorted in each row, values may repeat. Each is the first token of a document; position 0 always starts one.
All inputs are finite; a program needn't handle non-finite values.
Results may differ from the reference program's by a relative error of at most 0.009.
Values may be sent and summed in bfloat16 or wider, within the bound.
A program may use at most 256 MiB of HBM per device.

```python
import jax
import jax.numpy as jnp
from jax import lax

D = 1024
RW = 1536
FF = 3072
CONV_WIDTH = 4
BOUNDS = 8
ROWS_DEV = 3
TOK_DEV = 128
ROWS = 12
LENGTH = 1024


def draw_bounds(key, part):
    key = jax.random.fold_in(key, 11)
    early_key, late_key, block_key, offset_key, reach_key, spread_key, pick_key = jax.random.split(key, 7)
    half = BOUNDS // 2
    block_count = LENGTH // TOK_DEV
    early = jax.random.randint(early_key, (ROWS, half), 1, TOK_DEV, dtype=jnp.int32)
    late = LENGTH - jax.random.randint(late_key, (ROWS, BOUNDS - half), 1, TOK_DEV, dtype=jnp.int32)
    spanning = jnp.concatenate([early, late], axis=1)
    forced = BOUNDS // 2
    starts = jax.random.randint(block_key, (ROWS, forced), 1, block_count, dtype=jnp.int32) * TOK_DEV
    offsets = jax.random.randint(offset_key, (ROWS, forced), 0, 3, dtype=jnp.int32)
    reach = jax.random.randint(reach_key, (ROWS, BOUNDS - forced), 2, LENGTH, dtype=jnp.int32)
    heavy = jax.random.randint(spread_key, (ROWS, BOUNDS - forced), 1, reach, dtype=jnp.int32)
    packed = jnp.concatenate([starts + offsets, heavy], axis=1)
    chosen = jax.random.randint(pick_key, (ROWS // ROWS_DEV,), 0, ROWS_DEV, dtype=jnp.int32)
    row_ids = jnp.arange(ROWS, dtype=jnp.int32)
    is_spanning = row_ids % ROWS_DEV == jnp.repeat(chosen, ROWS_DEV)
    result = jnp.where(is_spanning[:, None], spanning, packed)
    return jnp.sort(result, axis=1).astype(jnp.int32)


def shard_levels(key, extent, cuts, low, largest):
    level, own = 1.0, jax.random.fold_in(key, 6)
    for dim, blocks in cuts:
        heights = jnp.exp(jax.random.uniform(jax.random.fold_in(own, dim), (blocks,), jnp.float32, low / len(cuts), largest / len(cuts)))
        level = level * jnp.repeat(heights, extent[dim] // blocks).reshape([-1 if axis == dim else 1 for axis in range(len(extent))])
    return level


def centred(key, extent, spread, bound, cuts=(), kind=jnp.bfloat16):
    factor_of = shard_levels(key, extent, cuts, -0.22, 0.18) if cuts else 1.0
    entries = jax.random.normal(key, extent, jnp.float32) * spread * factor_of
    return jnp.minimum(jnp.maximum(entries, -bound), bound).astype(kind)


def setup_inputs(seed: int = 0) -> dict:
    keys = jax.random.split(jax.random.key(seed), 19)
    tokens = centred(keys[0], (ROWS, LENGTH, D), 1.0, 6.0, ((0, 4), (1, 8)))
    bounds = draw_bounds(jax.random.fold_in(keys[18], 71), 0)
    norm1_gain = jnp.clip(1.0 + 0.1 * jax.random.normal(keys[2], (D,), jnp.float32), 0.5, 1.5)
    w_branch = centred(keys[3], (D, RW), D ** -0.5, 0.1875, ((0, 8),))
    w_rec = centred(keys[4], (D, RW), D ** -0.5, 0.1875, ((0, 8),))
    conv_weight = centred(keys[5], (CONV_WIDTH, RW), 0.5, 3.0, (), jnp.float32)
    conv_bias = centred(keys[6], (RW,), 0.5, 3.0, (), jnp.float32)
    w_rate = centred(keys[7], (RW, RW), RW ** -0.5, 0.15625, ((0, 8),))
    rate_bias = centred(keys[8], (RW,), 1.0, 4.0, (), jnp.float32)
    w_input = centred(keys[9], (RW, RW), RW ** -0.5, 0.15625, ((0, 8),))
    input_bias = centred(keys[10], (RW,), 1.0, 4.0, (), jnp.float32)
    decay_param = jnp.clip(jax.random.uniform(keys[11], (RW,), jnp.float32, -14.0, -3.0), -14.0, -3.0)
    w_out = centred(keys[12], (RW, D), (RW // 4) ** -0.5, 0.3125, ((0, 8),))
    norm2_gain = jnp.clip(1.0 + 0.1 * jax.random.normal(keys[13], (D,), jnp.float32), 0.5, 1.5)
    w_gate = centred(keys[14], (D, FF), D ** -0.5, 0.1875, ((0, 8),))
    w_up = centred(keys[15], (D, FF), D ** -0.5, 0.1875, ((0, 8),))
    w_down = centred(keys[16], (FF, D), (FF // 2) ** -0.5, 0.15625, ((0, 8),))
    cotangent = centred(keys[17], (ROWS, LENGTH, D), 1.0, 6.0, ((0, 4), (1, 8)))
    return dict(tokens=tokens, bounds=bounds, norm1_gain=norm1_gain, w_branch=w_branch, w_rec=w_rec, conv_weight=conv_weight, conv_bias=conv_bias, w_rate=w_rate, rate_bias=rate_bias, w_input=w_input, input_bias=input_bias, decay_param=decay_param, w_out=w_out, norm2_gain=norm2_gain, w_gate=w_gate, w_up=w_up, w_down=w_down, cotangent=cotangent)


epsilon = 1e-06
highest = lax.Precision.HIGHEST

@jax.custom_vjp
def low(v):
    return lax.optimization_barrier(v.astype(jnp.bfloat16)).astype(jnp.float32)

@jax.custom_vjp
def low_back(v):
    return v

def low_keep(v):
    return (low(v), None)

def low_pass(kept, grad):
    return (grad,)

def back_keep(v):
    return (v, None)

def back_low(kept, grad):
    return (low(grad),)
low.defvjp(low_keep, low_pass)
low_back.defvjp(back_keep, back_low)

def product(left, right):
    return jnp.dot(left, right, precision=highest)

def rms_norm(values, gain):
    return values * lax.rsqrt(lax.optimization_barrier(jnp.mean(values * values, axis=-1, keepdims=True)) + epsilon) * gain

def combine(earlier, latter):
    return (earlier[0] * latter[0], latter[0] * earlier[1] + latter[1])

def conv_masks(padded_resets):
    keep_mask = 1.0 - padded_resets
    first = keep_mask[..., 3:]
    second = first * keep_mask[..., 2:-1]
    third = second * keep_mask[..., 1:-2]
    return (first, second, third)

def convolve(padded, masks, conv_weight, conv_bias):
    result = conv_bias + conv_weight[0] * padded[..., 3:, :]
    result = result + conv_weight[1] * masks[0][..., None] * padded[..., 2:-1, :]
    result = result + conv_weight[2] * masks[1][..., None] * padded[..., 1:-2, :]
    return result + conv_weight[3] * masks[2][..., None] * padded[..., :-3, :]

def gate_terms(rate_pre, input_pre, conv_out, decay_param, rate_bias, input_bias, resets):
    rate_gate = jax.nn.sigmoid(rate_pre + rate_bias)
    input_gate = jax.nn.sigmoid(input_pre + input_bias)
    log_rate = -8.0 * jax.nn.softplus(decay_param) * rate_gate
    keep_mask = 1.0 - resets[..., None]
    decays = jnp.exp(log_rate) * keep_mask
    scales = resets[..., None] + keep_mask * jnp.sqrt(-jnp.expm1(2.0 * log_rate))
    return (decays, scales * input_gate * conv_out)

def row_forward(inputs, resets, norm1_gain, w_branch, w_rec, conv_weight, conv_bias, w_rate, rate_bias, w_input, input_bias, decay_param, w_out, norm2_gain, w_gate, w_up, w_down):
    normed = low(rms_norm(inputs, norm1_gain))
    branch_pre = low_back(product(normed, w_branch))
    rec_in = low_back(product(normed, w_rec))
    padded = jnp.concatenate([jnp.zeros((3, rec_in.shape[1]), jnp.float32), rec_in], axis=0)
    padded_resets = jnp.concatenate([jnp.zeros((3,), jnp.float32), resets])
    conv_out = convolve(padded, conv_masks(padded_resets), conv_weight, conv_bias)
    conv_low = low(conv_out)
    rate_pre = low_back(product(conv_low, w_rate))
    input_pre = low_back(product(conv_low, w_input))
    decays, drives = gate_terms(rate_pre, input_pre, conv_out, decay_param, rate_bias, input_bias, resets)
    states = lax.associative_scan(combine, (decays, drives), axis=0)[1]
    mixed_in = low(states * jax.nn.gelu(branch_pre, approximate=True))
    resid = inputs + low_back(product(mixed_in, w_out))
    normed2 = low(rms_norm(resid, norm2_gain))
    gate_pre = low_back(product(normed2, w_gate))
    up_pre = low_back(product(normed2, w_up))
    hidden = low(jax.nn.gelu(gate_pre, approximate=True) * up_pre)
    return resid + low_back(product(hidden, w_down))

def reference(tokens, bounds, norm1_gain, w_branch, w_rec, conv_weight, conv_bias, w_rate, rate_bias, w_input, input_bias, decay_param, w_out, norm2_gain, w_gate, w_up, w_down, cotangent):
    positions = jnp.arange(LENGTH, dtype=jnp.int32)
    marked = jnp.any(positions[None, :, None] == bounds[:, None, :], axis=2) | (positions == 0)[None, :]
    resets = marked.astype(jnp.float32)
    params = (norm1_gain, w_branch.astype(jnp.float32), w_rec.astype(jnp.float32), conv_weight, conv_bias, w_rate.astype(jnp.float32), rate_bias, w_input.astype(jnp.float32), input_bias, decay_param, w_out.astype(jnp.float32), norm2_gain, w_gate.astype(jnp.float32), w_up.astype(jnp.float32), w_down.astype(jnp.float32))

    def forward(inputs, *weights):

        def one_row(pair):
            return row_forward(pair[0], pair[1], *weights)
        return lax.map(jax.checkpoint(one_row), (inputs, resets))
    outputs, pull = jax.vjp(forward, tokens.astype(jnp.float32), *params)
    grads = pull(cotangent.astype(jnp.float32))
    return (outputs.astype(jnp.bfloat16), grads[0].astype(jnp.bfloat16), grads[1], grads[2], grads[3], grads[4], grads[5], grads[6], grads[7], grads[8], grads[9], grads[10], grads[11], grads[12], grads[13], grads[14], grads[15])
```

```python
import functools

import jax
import jax.numpy as jnp
from jax import lax
from jax.experimental import pallas as pl
from jax.experimental.pallas import tpu as pltpu
from jax.sharding import PartitionSpec as P

epsilon = 1e-06
MESH = pl.DeviceIdType.MESH
ANY = pl.BlockSpec(memory_space=pl.ANY)
VMEM = pl.BlockSpec(memory_space=pltpu.VMEM)


def place():
    r = lax.axis_index("rows")
    s = lax.axis_index("seq")
    return r, s, lax.div(s, 2), lax.rem(s, 2)


def greet(peers):
    barrier = pltpu.get_barrier_semaphore()
    for peer in peers:
        pl.semaphore_signal(barrier, inc=1, device_id=peer, device_id_type=MESH)
    pl.semaphore_wait(barrier, len(peers))


def peers_of(r, s, z, c):
    mate = (r, s + 1 - 2 * c)
    along_x = (r + 1 - 2 * lax.rem(r, 2), s)
    along_y = (lax.rem(r + 2, 4), s)
    along_z = [(r, lax.rem(z + k, 4) * 2 + c) for k in (1, 2, 3)]
    return mate, along_x, along_y, along_z


def gather_kernel(count, *refs):
    shards, fulls = refs[:count], refs[count : 2 * count]
    send, recv, local = refs[2 * count :]
    r, s, z, c = place()
    mate, along_x, along_y, along_z = peers_of(r, s, z, c)
    across_x, across_y = along_x[0], along_y[0]
    greet([mate, along_x, along_y] + along_z)

    def remote(m, slot, src, dst, device):
        return pltpu.make_async_remote_copy(
            src_ref=src,
            dst_ref=dst,
            send_sem=send.at[m, slot],
            recv_sem=recv.at[m, slot],
            device_id=device,
            device_id_type=MESH,
        )

    def region(m, source, quarter, begin, length):
        depth, width = shards[m].shape
        part = width // 4
        row = pl.multiple_of((source * 2 + c) * depth + begin, 16)
        column = pl.multiple_of(quarter * part, 128)
        return fulls[m].at[pl.ds(row, length), pl.ds(column, part)]

    live = []

    def start(copy):
        copy.start()
        live.append(copy)
        return copy

    stage_own, stage_z, stage_x, stage_y, stage_d, stage_c = {}, {}, {}, {}, {}, {}

    def begin(m):
        depth, width = shards[m].shape
        part = width // 4
        rows = pl.ds(pl.multiple_of(s * depth, 16), depth)
        own = pltpu.make_async_copy(shards[m], fulls[m].at[rows], local.at[m])
        own.start()
        column = pl.multiple_of(r * part, 128)
        stage_z[m] = [
            start(
                remote(
                    m,
                    k,
                    shards[m].at[:, pl.ds(column, part)],
                    region(m, z, r, 0, depth),
                    along_z[k - 1],
                )
            )
            for k in (1, 2, 3)
        ]
        stage_own[m] = (own, start(remote(m, 0, shards[m], fulls[m].at[rows], mate)))

    def sources(k):
        return lax.rem(z + 4 - k, 4)

    begin(0)
    begin(1)
    for tick in range(count + 2):
        m = tick
        if m < count:
            depth = shards[m].shape[0]
            stage_x[m], stage_y[m] = [], []
            for k in (1, 2, 3):
                stage_z[m][k - 1].wait_recv()
                piece = region(m, sources(k), r, 0, depth)
                stage_x[m].append(start(remote(m, 3 + k, piece, piece, along_x)))
                stage_y[m].append(start(remote(m, 6 + k, piece, piece, along_y)))
        if tick + 2 < count:
            begin(tick + 2)
        m = tick - 1
        if 0 <= m < count:
            depth = shards[m].shape[0]
            half = depth // 2
            stage_d[m] = []
            for k in (1, 2, 3):
                stage_x[m][k - 1].wait_recv()
                piece = region(m, sources(k), across_x, 0, half)
                stage_d[m].append(start(remote(m, 9 + k, piece, piece, along_y)))
                stage_y[m][k - 1].wait_recv()
                piece = region(m, sources(k), across_y, half, half)
                stage_d[m].append(start(remote(m, 12 + k, piece, piece, along_x)))
        m = tick - 2
        if 0 <= m < count:
            depth = shards[m].shape[0]
            stage_c[m] = []
            for k in (1, 2, 3):
                stage_d[m][2 * k - 2].wait_recv()
                stage_d[m][2 * k - 1].wait_recv()
                rows = pl.ds(pl.multiple_of((sources(k) * 2 + c) * depth, 16), depth)
                piece = fulls[m].at[rows]
                stage_c[m].append(start(remote(m, 15 + k, piece, piece, mate)))
    for m in range(count):
        own, twin = stage_own[m]
        own.wait()
        twin.wait_recv()
        for copy in stage_c[m]:
            copy.wait_recv()
    for copy in live:
        copy.wait_send()


def gather_all(shards, axis_size):
    if axis_size != 8 or lax.axis_size("rows") != 4:
        return tuple(lax.all_gather(a, "seq", axis=0, tiled=True) for a in shards)
    count = len(shards)
    return pl.pallas_call(
        functools.partial(gather_kernel, count),
        out_shape=tuple(
            jax.ShapeDtypeStruct((a.shape[0] * axis_size, a.shape[1]), a.dtype) for a in shards
        ),
        in_specs=[ANY] * count,
        out_specs=(ANY,) * count,
        scratch_shapes=[
            pltpu.SemaphoreType.DMA((count, 19)),
            pltpu.SemaphoreType.DMA((count, 19)),
            pltpu.SemaphoreType.DMA((count,)),
        ],
        compiler_params=pltpu.CompilerParams(collective_id=0, has_side_effects=True),
        name="gather_weights",
    )(*shards)


def blocks_add(total, term, lead, rows):
    def one(i, carry):
        total_at = total(i)
        total_at[...] = total_at[...] + term(i)[...]
        return carry

    lax.fori_loop(0, lead, one, 0)


def reduce_kernel(count, has_small, *refs):
    refs = list(refs)
    grads = [refs.pop(0) for _ in range(count)]
    small_in = refs.pop(0) if has_small else None
    outs = [refs.pop(0) for _ in range(count)]
    small_out = refs.pop(0) if has_small else None
    held, own, first, second, third, final = (
        [refs.pop(0) for _ in range(count)] for _ in range(6)
    )
    send, recv, local = refs.pop(0), refs.pop(0), refs.pop(0)
    if has_small:
        small_held, small_got, small_send, small_recv = refs
    r, s, z, c = place()
    mate, along_x, along_y, along_z = peers_of(r, s, z, c)
    across_x, across_y = along_x[0], along_y[0]
    diagonal = (3 - r, s)
    rx, ry = lax.rem(r, 2), lax.div(r, 2)
    greet([mate, along_x, along_y, diagonal] + along_z)
    live = []

    def remote(m, slot, src, dst, device):
        copy = pltpu.make_async_remote_copy(
            src_ref=src,
            dst_ref=dst,
            send_sem=send.at[m, slot],
            recv_sem=recv.at[m, slot],
            device_id=device,
            device_id_type=MESH,
        )
        copy.start()
        live.append(copy)
        return copy

    at_c, at_one, at_two, at_z, at_end, at_out = {}, {}, {}, {}, {}, {}

    def begin(m):
        part = held[m].shape[3]
        at_c[m] = []
        for q in range(4):
            columns = pl.ds(q * part, part)
            far = remote(m, q, grads[m].at[:, 1 - c, :, columns], held[m].at[q], mate)
            near = pltpu.make_async_copy(
                grads[m].at[:, c, :, columns], own[m].at[q], local.at[m, q]
            )
            near.start()
            at_c[m].append((far, near))

    small_copies = []

    def small_exchange(slot, device):
        copy = pltpu.make_async_remote_copy(
            src_ref=small_held.at[slot],
            dst_ref=small_got.at[slot],
            send_sem=small_send.at[slot],
            recv_sem=small_recv.at[slot],
            device_id=device,
            device_id_type=MESH,
        )
        copy.start()
        small_copies.append(copy)
        return copy

    if has_small:
        small_held[0] = small_in[...]
        swap = small_exchange(0, mate)
    begin(0)
    if count > 1:
        begin(1)
    for tick in range(count + 4):
        m = tick
        if m < count:
            _, _, depth, part = held[m].shape
            half = depth // 2
            for far, near in at_c[m]:
                far.wait_recv()
                near.wait()

            def add_all(i, carry, m=m):
                q, b = lax.div(i, 4), lax.rem(i, 4)
                held[m][q, b] = held[m][q, b] + own[m][q, b]
                return carry

            lax.fori_loop(0, 16, add_all, 0)
            at_one[m] = []
            for other in range(2):
                quarter = other * 2 + (1 - rx)
                at_one[m].append(
                    remote(
                        m,
                        4 + other,
                        held[m].at[quarter, :, pl.ds(0, half)],
                        first[m].at[0, other],
                        along_x,
                    )
                )
                quarter = (1 - ry) * 2 + other
                at_one[m].append(
                    remote(
                        m,
                        6 + other,
                        held[m].at[quarter, :, pl.ds(half, half)],
                        first[m].at[1, other],
                        along_y,
                    )
                )
        if tick + 2 < count:
            begin(tick + 2)
        m = tick - 1
        if 0 <= m < count:
            _, _, depth, part = held[m].shape
            half = depth // 2
            for copy in at_one[m]:
                copy.wait_recv()

            def add_one(i, carry, m=m, half=half):
                other, b = lax.div(i, 4), lax.rem(i, 4)
                qx = other * 2 + rx
                held[m][qx, b, :half] = held[m][qx, b, :half] + first[m][0, other, b]
                qy = ry * 2 + other
                held[m][qy, b, half:] = held[m][qy, b, half:] + first[m][1, other, b]
                return carry

            lax.fori_loop(0, 8, add_one, 0)
            at_two[m] = [
                remote(
                    m,
                    8,
                    held[m].at[(1 - ry) * 2 + rx, :, pl.ds(0, half)],
                    second[m].at[0],
                    along_y,
                ),
                remote(
                    m,
                    9,
                    held[m].at[ry * 2 + (1 - rx), :, pl.ds(half, half)],
                    second[m].at[1],
                    along_x,
                ),
            ]
        if has_small and tick == 1:
            swap.wait_recv()
            small_held[1] = small_held[0] + small_got[0]
            swap = small_exchange(1, along_x)
        m = tick - 2
        if 0 <= m < count:
            _, _, depth, part = held[m].shape
            half = depth // 2
            for copy in at_two[m]:
                copy.wait_recv()

            def add_two(b, carry, m=m, half=half):
                held[m][r, b, :half] = held[m][r, b, :half] + second[m][0, b]
                held[m][r, b, half:] = held[m][r, b, half:] + second[m][1, b]
                return carry

            lax.fori_loop(0, 4, add_two, 0)
            at_z[m] = [
                remote(
                    m,
                    9 + k,
                    held[m].at[r, lax.rem(z + k, 4)],
                    third[m].at[k - 1],
                    along_z[k - 1],
                )
                for k in (1, 2, 3)
            ]
        if has_small and tick == 2:
            swap.wait_recv()
            small_held[2] = small_held[1] + small_got[1]
            swap = small_exchange(2, along_y)
        m = tick - 3
        if 0 <= m < count:
            for copy in at_z[m]:
                copy.wait_recv()
            mine = held[m][r, z].astype(jnp.float32)
            for k in range(3):
                mine = mine + third[m][k].astype(jnp.float32)
            final[m][r] = mine.astype(jnp.bfloat16)
            at_end[m] = [
                remote(m, 13 + i, final[m].at[r], final[m].at[r], device)
                for i, device in enumerate((along_x, along_y, diagonal))
            ]
        if has_small and tick == 3:
            swap.wait_recv()
            small_held[3] = small_held[2] + small_got[2]
            spread = []
            for k in (1, 2, 3):
                copy = pltpu.make_async_remote_copy(
                    src_ref=small_held.at[3],
                    dst_ref=small_got.at[2 + k],
                    send_sem=small_send.at[2 + k],
                    recv_sem=small_recv.at[2 + k],
                    device_id=along_z[k - 1],
                    device_id_type=MESH,
                )
                copy.start()
                small_copies.append(copy)
                spread.append(copy)
        m = tick - 4
        if 0 <= m < count:
            for copy in at_end[m]:
                copy.wait_recv()
            out = pltpu.make_async_copy(final[m], outs[m], local.at[m, 4])
            out.start()
            at_out[m] = out
    if has_small:
        for copy in spread:
            copy.wait_recv()
        small_got[6] = small_held[3]
        total = None
        for source in range(4):
            k = lax.rem(z + 4 - source, 4)
            slot = jnp.where(k == 0, 6, 2 + k)
            term = small_got[slot]
            total = term if total is None else total + term
        small_out[...] = total
        for copy in small_copies:
            copy.wait_send()
    for m in range(count):
        at_out[m].wait()
    for copy in live:
        copy.wait_send()


def reduce_all(grads, small, axis_size, tag):
    if axis_size != 8 or lax.axis_size("rows") != 4:
        blocks = [
            lax.psum(lax.psum_scatter(g, "seq", scatter_dimension=0, tiled=True), "rows")
            for g in grads
        ]
        if small is not None:
            small = lax.psum(small, ("rows", "seq"))
        return [b.astype(jnp.float32) for b in blocks], small
    count = len(grads)
    shapes = [(g.shape[0] // axis_size, g.shape[1] // 4) for g in grads]
    views = [g.reshape(4, 2, k, 4 * n) for g, (k, n) in zip(grads, shapes)]
    low = jnp.bfloat16
    out_shape = [jax.ShapeDtypeStruct((4, k, n), low) for k, n in shapes]
    out_specs = [ANY] * count
    in_specs = [ANY] * count
    scratch = [pltpu.VMEM((4, 4, k, n), low) for k, n in shapes]
    scratch += [pltpu.VMEM((4, 4, k, n), low) for k, n in shapes]
    scratch += [pltpu.VMEM((2, 2, 4, k // 2, n), low) for k, n in shapes]
    scratch += [pltpu.VMEM((2, 4, k // 2, n), low) for k, n in shapes]
    scratch += [pltpu.VMEM((3, k, n), low) for k, n in shapes]
    scratch += [pltpu.VMEM((4, k, n), low) for k, n in shapes]
    scratch += [
        pltpu.SemaphoreType.DMA((count, 16)),
        pltpu.SemaphoreType.DMA((count, 16)),
        pltpu.SemaphoreType.DMA((count, 5)),
    ]
    args = list(views)
    if small is not None:
        args.append(small)
        in_specs.append(VMEM)
        out_shape.append(jax.ShapeDtypeStruct(small.shape, small.dtype))
        out_specs.append(VMEM)
        scratch += [
            pltpu.VMEM((4,) + small.shape, small.dtype),
            pltpu.VMEM((7,) + small.shape, small.dtype),
            pltpu.SemaphoreType.DMA((6,)),
            pltpu.SemaphoreType.DMA((6,)),
        ]
    results = pl.pallas_call(
        functools.partial(reduce_kernel, count, small is not None),
        out_shape=tuple(out_shape),
        in_specs=in_specs,
        out_specs=tuple(out_specs),
        scratch_shapes=scratch,
        compiler_params=pltpu.CompilerParams(
            collective_id=tag, has_side_effects=True, vmem_limit_bytes=60 * 1024 * 1024
        ),
        name="reduce_grads",
    )(*args)
    blocks = [
        b.transpose(1, 0, 2).reshape(k, 4 * n).astype(jnp.float32)
        for b, (k, n) in zip(results[:count], shapes)
    ]
    return blocks, (results[count] if small is not None else None)


def scan_kernel(reverse, a_ref, b_ref, p_ref, h_ref):
    steps, width = a_ref.shape[1:]
    tiles = steps // 8
    spot = lax.broadcasted_iota(jnp.int32, (8, width), 0)

    def shift(values, distance, fill):
        if reverse:
            moved = pltpu.roll(values, 8 - distance, 0)
            return jnp.where(spot >= 8 - distance, fill, moved)
        moved = pltpu.roll(values, distance, 0)
        return jnp.where(spot < distance, fill, moved)

    def tile(i, carry):
        carry_a, carry_b = carry
        t = tiles - 1 - i if reverse else i
        rows = pl.ds(pl.multiple_of(t * 8, 8), 8)
        a, b = a_ref[0, rows, :], b_ref[0, rows, :]
        for distance in (1, 2, 4):
            b = b + a * shift(b, distance, 0.0)
            a = a * shift(a, distance, 1.0)
        b = b + a * carry_b
        a = a * carry_a
        p_ref[0, rows, :] = a
        h_ref[0, rows, :] = b
        edge = slice(0, 1) if reverse else slice(7, 8)
        return a[edge], b[edge]

    ones, zeros = jnp.ones((1, width), jnp.float32), jnp.zeros((1, width), jnp.float32)
    lax.fori_loop(0, tiles, tile, (ones, zeros))


def scan(a, b, reverse):
    count, steps, width = a.shape
    block = pl.BlockSpec((1, steps, 512), lambda i, j: (i, 0, j))
    return pl.pallas_call(
        functools.partial(scan_kernel, reverse),
        grid=(count, width // 512),
        in_specs=[block, block],
        out_specs=(block, block),
        out_shape=(jax.ShapeDtypeStruct(a.shape, a.dtype),) * 2,
        name="scan_back" if reverse else "scan_ahead",
    )(a, b)


def from_behind(block, axis, distance):
    devices = range(lax.axis_size(axis))
    route = [(i - distance, i) for i in devices if i - distance in devices]
    return lax.ppermute(block, axis, route)


def prefix(part, axis, combine, identity, reverse):
    count = lax.axis_size(axis)
    place = lax.axis_index(axis)
    ahead = count - 1 - place if reverse else place
    gathered = jax.tree.map(lambda a: lax.all_gather(a, axis), part)
    state = jax.tree.map(lambda a, e: jnp.zeros_like(a) + jnp.asarray(e, a.dtype), part, identity)

    def one(turn, state):
        source = count - 1 - turn if reverse else turn
        return combine(
            state, jax.tree.map(lambda a: lax.dynamic_index_in_dim(a, source, 0, False), gathered)
        )

    return lax.fori_loop(0, ahead, one, state)


def rms_norm(values, gain):
    return values * lax.rsqrt(jnp.mean(values * values, axis=-1, keepdims=True) + epsilon) * gain


def combine(earlier, latter):
    return (earlier[0] * latter[0], latter[0] * earlier[1] + latter[1])


def conv_masks(padded_resets):
    keep_mask = 1.0 - padded_resets
    first = keep_mask[..., 3:]
    second = first * keep_mask[..., 2:-1]
    third = second * keep_mask[..., 1:-2]
    return (first, second, third)


def convolve(padded, masks, conv_weight, conv_bias):
    result = conv_bias + conv_weight[0] * padded[..., 3:, :]
    result = result + conv_weight[1] * masks[0][..., None] * padded[..., 2:-1, :]
    result = result + conv_weight[2] * masks[1][..., None] * padded[..., 1:-2, :]
    return result + conv_weight[3] * masks[2][..., None] * padded[..., :-3, :]


def gate_terms(rate_pre, input_pre, conv_out, decay_param, rate_bias, input_bias, resets):
    rate_gate = jax.nn.sigmoid(rate_pre + rate_bias)
    input_gate = jax.nn.sigmoid(input_pre + input_bias)
    log_rate = -8.0 * jax.nn.softplus(decay_param) * rate_gate
    keep_mask = 1.0 - resets[..., None]
    decays = jnp.exp(log_rate) * keep_mask
    scales = resets[..., None] + keep_mask * jnp.sqrt(-jnp.expm1(2.0 * log_rate))
    return (decays, scales * input_gate * conv_out)


def forward_product(values, weight):
    return jnp.dot(values, weight, preferred_element_type=jnp.float32)


def outer(left, right):
    return lax.dot_general(
        left, right, (((0,), (0,)), ((), ())), preferred_element_type=jnp.float32
    )


def back_product(grads, weight):
    return lax.dot_general(
        grads, weight, (((1,), (1,)), ((), ())), preferred_element_type=jnp.float32
    )


def body(
    tokens,
    bounds,
    norm1_gain,
    w_branch,
    w_rec,
    conv_weight,
    conv_bias,
    w_rate,
    rate_bias,
    w_input,
    input_bias,
    decay_param,
    w_out,
    norm2_gain,
    w_gate,
    w_up,
    w_down,
    cotangent,
):
    axis_size = lax.axis_size("seq")
    full_rec, full_rate, full_input, full_branch, full_out, full_gate, full_up, full_down = gather_all(
        (w_rec, w_rate, w_input, w_branch, w_out, w_gate, w_up, w_down), axis_size
    )
    row_count, tok_count, model_width = tokens.shape
    rec_width = full_rec.shape[1]
    offset = lax.axis_index("seq") * tok_count
    positions = offset - 3 + jnp.arange(tok_count + 3, dtype=jnp.int32)
    marked = (
        jnp.any(positions[None, :, None] == bounds[:, None, :], axis=2) | (positions == 0)[None, :]
    )
    padded_resets = marked.astype(jnp.float32)
    resets = padded_resets[:, 3:]
    masks = conv_masks(padded_resets)
    inputs = tokens.astype(jnp.float32).reshape(-1, model_width)
    normed = rms_norm(inputs, norm1_gain).astype(jnp.bfloat16)
    branch_pre = forward_product(normed, full_branch)
    rec_in = forward_product(normed, full_rec).reshape(row_count, tok_count, rec_width)
    rim = from_behind(rec_in[:, tok_count - 3 :, :], "seq", 1)
    padded = jnp.concatenate([rim, rec_in], axis=1)
    conv_out = convolve(padded, masks, conv_weight, conv_bias)
    conv_low = conv_out.astype(jnp.bfloat16).reshape(-1, rec_width)
    rate_pre = forward_product(conv_low, full_rate).reshape(conv_out.shape)
    input_pre = forward_product(conv_low, full_input).reshape(conv_out.shape)

    def gates_of(rate_arg, input_arg, conv_arg, decay_arg, rate_arg_bias, input_arg_bias):
        return gate_terms(
            rate_arg, input_arg, conv_arg, decay_arg, rate_arg_bias, input_arg_bias, resets
        )

    decays, drives = gates_of(rate_pre, input_pre, conv_out, decay_param, rate_bias, input_bias)
    prefix_decay, local_states = scan(decays, drives, False)
    ones_pair = jnp.ones((row_count, rec_width), jnp.float32)
    zeros_pair = jnp.zeros((row_count, rec_width), jnp.float32)
    carry_in = prefix(
        (prefix_decay[:, -1], local_states[:, -1]), "seq", combine, (ones_pair, zeros_pair), False
    )[1]
    states = local_states + prefix_decay * carry_in[:, None, :]
    earlier_states = jnp.concatenate([carry_in[:, None, :], states[:, :-1, :]], axis=1)
    branch_act = jax.nn.gelu(branch_pre, approximate=True).reshape(states.shape)
    mixed_in = (states * branch_act).astype(jnp.bfloat16).reshape(-1, rec_width)
    resid = inputs + forward_product(mixed_in, full_out)
    normed2 = rms_norm(resid, norm2_gain).astype(jnp.bfloat16)
    gate_pre = forward_product(normed2, full_gate)
    up_pre = forward_product(normed2, full_up)
    hidden = (jax.nn.gelu(gate_pre, approximate=True) * up_pre).astype(jnp.bfloat16)
    mixed = (resid + forward_product(hidden, full_down)).astype(jnp.bfloat16).reshape(tokens.shape)
    cot_low = cotangent.reshape(-1, model_width)
    grad_down = outer(hidden, cot_low)
    grad_hidden = back_product(cot_low, full_down)
    _, pull_mlp = jax.vjp(
        lambda gate_arg, up_arg: jax.nn.gelu(gate_arg, approximate=True) * up_arg, gate_pre, up_pre
    )
    grad_gate_pre, grad_up_pre = pull_mlp(grad_hidden)
    gate_low = grad_gate_pre.astype(jnp.bfloat16)
    up_low = grad_up_pre.astype(jnp.bfloat16)
    grad_gate = outer(normed2, gate_low)
    grad_up = outer(normed2, up_low)
    grad_normed2 = back_product(gate_low, full_gate) + back_product(up_low, full_up)
    _, pull_norm2 = jax.vjp(rms_norm, resid, norm2_gain)
    grad_resid_norm, grad_norm2 = pull_norm2(grad_normed2)
    grad_resid = cot_low.astype(jnp.float32) + grad_resid_norm
    resid_low = grad_resid.astype(jnp.bfloat16)
    grad_out = outer(mixed_in, resid_low)
    grad_mixed = back_product(resid_low, full_out).reshape(states.shape)
    grad_states = grad_mixed * branch_act
    _, pull_branch = jax.vjp(lambda pre_arg: jax.nn.gelu(pre_arg, approximate=True), branch_pre)
    branch_low = pull_branch((grad_mixed * states).reshape(-1, rec_width))[0].astype(jnp.bfloat16)
    next_decays = jnp.concatenate([decays[:, 1:, :], ones_pair[:, None, :]], axis=1)
    suffix_decay, local_grads = scan(next_decays, grad_states, True)
    element = (prefix_decay[:, -1], decays[:, 0] * local_grads[:, 0])
    carry_back = prefix(element, "seq", combine, (ones_pair, zeros_pair), True)[1]
    state_grads = local_grads + suffix_decay * carry_back[:, None, :]
    _, pull_gates = jax.vjp(
        gates_of, rate_pre, input_pre, conv_out, decay_param, rate_bias, input_bias
    )
    grad_rate_pre, grad_input_pre, grad_conv_direct, grad_decay, grad_rate_bias, grad_input_bias = (
        pull_gates((state_grads * earlier_states, state_grads))
    )
    rate_low = grad_rate_pre.astype(jnp.bfloat16).reshape(-1, rec_width)
    input_low = grad_input_pre.astype(jnp.bfloat16).reshape(-1, rec_width)
    grad_rate = outer(conv_low, rate_low)
    grad_input = outer(conv_low, input_low)
    grad_conv = grad_conv_direct + (
        back_product(rate_low, full_rate) + back_product(input_low, full_input)
    ).reshape(conv_out.shape)
    _, pull_conv = jax.vjp(
        lambda pad_arg, weight_arg, bias_arg: convolve(pad_arg, masks, weight_arg, bias_arg),
        padded,
        conv_weight,
        conv_bias,
    )
    grad_padded, grad_conv_weight, grad_conv_bias = pull_conv(grad_conv)
    rim_back = from_behind(grad_padded[:, :3, :], "seq", -1)
    grad_rec = grad_padded[:, 3:, :] + jnp.concatenate(
        [jnp.zeros((row_count, tok_count - 3, rec_width), jnp.float32), rim_back], axis=1
    )
    rec_low = grad_rec.astype(jnp.bfloat16).reshape(-1, rec_width)
    grad_rec_w = outer(normed, rec_low)
    grad_branch_w = outer(normed, branch_low)
    grad_normed = back_product(branch_low, full_branch) + back_product(rec_low, full_rec)
    _, pull_norm1 = jax.vjp(rms_norm, inputs, norm1_gain)
    grad_inputs, grad_norm1 = pull_norm1(grad_normed)
    token_grad = (grad_resid + grad_inputs).astype(jnp.bfloat16).reshape(tokens.shape)
    low = jnp.bfloat16
    ff, _ = reduce_all(
        [g.astype(low) for g in (grad_down, grad_gate, grad_up)], None, axis_size, 1
    )
    flat = jnp.concatenate(
        [
            g.reshape(-1)
            for g in (
                grad_norm1,
                grad_conv_weight,
                grad_conv_bias,
                grad_rate_bias,
                grad_input_bias,
                grad_decay,
                grad_norm2,
            )
        ]
    )
    size = flat.shape[0]
    flat = jnp.pad(flat, (0, -size % 8192)).reshape(-1, 1024)
    rec, flat = reduce_all(
        [g.astype(low) for g in (grad_out, grad_rate, grad_input, grad_branch_w, grad_rec_w)],
        flat,
        axis_size,
        2,
    )
    flat = flat.reshape(-1)
    small, begin = [], 0
    for like in (
        grad_norm1,
        grad_conv_weight,
        grad_conv_bias,
        grad_rate_bias,
        grad_input_bias,
        grad_decay,
        grad_norm2,
    ):
        small.append(flat[begin : begin + like.size].reshape(like.shape))
        begin += like.size
    summed = (rec[3], rec[4], rec[1], rec[2], rec[0], ff[1], ff[2], ff[0])
    return (
        mixed,
        token_grad,
        small[0],
        summed[0],
        summed[1],
        small[1],
        small[2],
        summed[2],
        small[3],
        summed[3],
        small[4],
        small[5],
        summed[4],
        small[6],
        summed[5],
        summed[6],
        summed[7],
    )


def solution(mesh):
    in_specs = (
        P("rows", "seq", None),
        P("rows", None),
        P(),
        P("seq", None),
        P("seq", None),
        P(),
        P(),
        P("seq", None),
        P(),
        P("seq", None),
        P(),
        P(),
        P("seq", None),
        P(),
        P("seq", None),
        P("seq", None),
        P("seq", None),
        P("rows", "seq", None),
    )
    out_specs = (
        P("rows", "seq", None),
        P("rows", "seq", None),
        P(),
        P("seq", None),
        P("seq", None),
        P(),
        P(),
        P("seq", None),
        P(),
        P("seq", None),
        P(),
        P(),
        P("seq", None),
        P(),
        P("seq", None),
        P("seq", None),
        P("seq", None),
    )
    return jax.shard_map(body, mesh=mesh, in_specs=in_specs, out_specs=out_specs, check_vma=False)
```

```python
import functools

import jax
import jax.numpy as jnp
from jax import lax
from jax.experimental import pallas as pl
from jax.experimental.pallas import tpu as pltpu
from jax.sharding import PartitionSpec as P

epsilon = 1e-06
MESH = pl.DeviceIdType.MESH
ANY = pl.BlockSpec(memory_space=pl.ANY)
VMEM = pl.BlockSpec(memory_space=pltpu.VMEM)


def place():
    r = lax.axis_index("rows")
    s = lax.axis_index("seq")
    return r, s, lax.div(s, 2), lax.rem(s, 2)


def greet(peers):
    barrier = pltpu.get_barrier_semaphore()
    for peer in peers:
        pl.semaphore_signal(barrier, inc=1, device_id=peer, device_id_type=MESH)
    pl.semaphore_wait(barrier, len(peers))


def peers_of(r, s, z, c):
    mate = (r, s + 1 - 2 * c)
    along_x = (r + 1 - 2 * lax.rem(r, 2), s)
    along_y = (lax.rem(r + 2, 4), s)
    along_z = [(r, lax.rem(z + k, 4) * 2 + c) for k in (1, 2, 3)]
    return mate, along_x, along_y, along_z


def reduce_kernel(count, has_small, *refs):
    refs = list(refs)
    grads = [refs.pop(0) for _ in range(count)]
    small_in = refs.pop(0) if has_small else None
    outs = [refs.pop(0) for _ in range(count)]
    small_out = refs.pop(0) if has_small else None
    held, own, first, second, third, final = (
        [refs.pop(0) for _ in range(count)] for _ in range(6)
    )
    send, recv, local = refs.pop(0), refs.pop(0), refs.pop(0)
    if has_small:
        small_held, small_got, small_send, small_recv = refs
    r, s, z, c = place()
    mate, along_x, along_y, along_z = peers_of(r, s, z, c)
    across_x, across_y = along_x[0], along_y[0]
    diagonal = (3 - r, s)
    rx, ry = lax.rem(r, 2), lax.div(r, 2)
    greet([mate, along_x, along_y, diagonal] + along_z)
    live = []

    def remote(m, slot, src, dst, device):
        copy = pltpu.make_async_remote_copy(
            src_ref=src,
            dst_ref=dst,
            send_sem=send.at[m, slot],
            recv_sem=recv.at[m, slot],
            device_id=device,
            device_id_type=MESH,
        )
        copy.start()
        live.append(copy)
        return copy

    at_c, at_one, at_two, at_z, at_end, at_out = {}, {}, {}, {}, {}, {}

    def begin(m):
        part = held[m].shape[3]
        at_c[m] = []
        for q in range(4):
            columns = pl.ds(q * part, part)
            far = remote(m, q, grads[m].at[:, 1 - c, :, columns], held[m].at[q], mate)
            near = pltpu.make_async_copy(
                grads[m].at[:, c, :, columns], own[m].at[q], local.at[m, q]
            )
            near.start()
            at_c[m].append((far, near))

    small_copies = []

    def small_exchange(slot, device):
        copy = pltpu.make_async_remote_copy(
            src_ref=small_held.at[slot],
            dst_ref=small_got.at[slot],
            send_sem=small_send.at[slot],
            recv_sem=small_recv.at[slot],
            device_id=device,
            device_id_type=MESH,
        )
        copy.start()
        small_copies.append(copy)
        return copy

    if has_small:
        small_held[0] = small_in[...]
        swap = small_exchange(0, mate)
    begin(0)
    if count > 1:
        begin(1)
    for tick in range(count + 4):
        m = tick
        if m < count:
            _, _, depth, part = held[m].shape
            half = depth // 2
            for far, near in at_c[m]:
                far.wait_recv()
                near.wait()

            def add_all(i, carry, m=m):
                q, b = lax.div(i, 4), lax.rem(i, 4)
                held[m][q, b] = held[m][q, b] + own[m][q, b]
                return carry

            lax.fori_loop(0, 16, add_all, 0)
            at_one[m] = []
            for other in range(2):
                quarter = other * 2 + (1 - rx)
                at_one[m].append(
                    remote(
                        m,
                        4 + other,
                        held[m].at[quarter, :, pl.ds(0, half)],
                        first[m].at[0, other],
                        along_x,
                    )
                )
                quarter = (1 - ry) * 2 + other
                at_one[m].append(
                    remote(
                        m,
                        6 + other,
                        held[m].at[quarter, :, pl.ds(half, half)],
                        first[m].at[1, other],
                        along_y,
                    )
                )
        if tick + 2 < count:
            begin(tick + 2)
        m = tick - 1
        if 0 <= m < count:
            _, _, depth, part = held[m].shape
            half = depth // 2
            for copy in at_one[m]:
                copy.wait_recv()

            def add_one(i, carry, m=m, half=half):
                other, b = lax.div(i, 4), lax.rem(i, 4)
                qx = other * 2 + rx
                held[m][qx, b, :half] = held[m][qx, b, :half] + first[m][0, other, b]
                qy = ry * 2 + other
                held[m][qy, b, half:] = held[m][qy, b, half:] + first[m][1, other, b]
                return carry

            lax.fori_loop(0, 8, add_one, 0)
            at_two[m] = [
                remote(
                    m,
                    8,
                    held[m].at[(1 - ry) * 2 + rx, :, pl.ds(0, half)],
                    second[m].at[0],
                    along_y,
                ),
                remote(
                    m,
                    9,
                    held[m].at[ry * 2 + (1 - rx), :, pl.ds(half, half)],
                    second[m].at[1],
                    along_x,
                ),
            ]
        if has_small and tick == 1:
            swap.wait_recv()
            small_held[1] = small_held[0] + small_got[0]
            swap = small_exchange(1, along_x)
        m = tick - 2
        if 0 <= m < count:
            _, _, depth, part = held[m].shape
            half = depth // 2
            for copy in at_two[m]:
                copy.wait_recv()

            def add_two(b, carry, m=m, half=half):
                held[m][r, b, :half] = held[m][r, b, :half] + second[m][0, b]
                held[m][r, b, half:] = held[m][r, b, half:] + second[m][1, b]
                return carry

            lax.fori_loop(0, 4, add_two, 0)
            at_z[m] = [
                remote(
                    m,
                    9 + k,
                    held[m].at[r, lax.rem(z + k, 4)],
                    third[m].at[k - 1],
                    along_z[k - 1],
                )
                for k in (1, 2, 3)
            ]
        if has_small and tick == 2:
            swap.wait_recv()
            small_held[2] = small_held[1] + small_got[1]
            swap = small_exchange(2, along_y)
        m = tick - 3
        if 0 <= m < count:
            for copy in at_z[m]:
                copy.wait_recv()
            mine = held[m][r, z].astype(jnp.float32)
            for k in range(3):
                mine = mine + third[m][k].astype(jnp.float32)
            final[m][r] = mine.astype(jnp.bfloat16)
            at_end[m] = [
                remote(m, 13 + i, final[m].at[r], final[m].at[r], device)
                for i, device in enumerate((along_x, along_y, diagonal))
            ]
        if has_small and tick == 3:
            swap.wait_recv()
            small_held[3] = small_held[2] + small_got[2]
            spread = []
            for k in (1, 2, 3):
                copy = pltpu.make_async_remote_copy(
                    src_ref=small_held.at[3],
                    dst_ref=small_got.at[2 + k],
                    send_sem=small_send.at[2 + k],
                    recv_sem=small_recv.at[2 + k],
                    device_id=along_z[k - 1],
                    device_id_type=MESH,
                )
                copy.start()
                small_copies.append(copy)
                spread.append(copy)
        m = tick - 4
        if 0 <= m < count:
            for copy in at_end[m]:
                copy.wait_recv()
            out = pltpu.make_async_copy(final[m], outs[m], local.at[m, 4])
            out.start()
            at_out[m] = out
    if has_small:
        for copy in spread:
            copy.wait_recv()
        small_got[6] = small_held[3]
        total = None
        for source in range(4):
            k = lax.rem(z + 4 - source, 4)
            slot = jnp.where(k == 0, 6, 2 + k)
            term = small_got[slot]
            total = term if total is None else total + term
        small_out[...] = total
        for copy in small_copies:
            copy.wait_send()
    for m in range(count):
        at_out[m].wait()
    for copy in live:
        copy.wait_send()


def reduce_all(grads, small, axis_size, tag):
    if axis_size != 8 or lax.axis_size("rows") != 4:
        blocks = [
            lax.psum(lax.psum_scatter(g, "seq", scatter_dimension=0, tiled=True), "rows")
            for g in grads
        ]
        if small is not None:
            small = lax.psum(small, ("rows", "seq"))
        return [b.astype(jnp.float32) for b in blocks], small
    count = len(grads)
    shapes = [(g.shape[0] // axis_size, g.shape[1] // 4) for g in grads]
    views = [g.reshape(4, 2, k, 4 * n) for g, (k, n) in zip(grads, shapes)]
    low = jnp.bfloat16
    out_shape = [jax.ShapeDtypeStruct((4, k, n), low) for k, n in shapes]
    out_specs = [ANY] * count
    in_specs = [ANY] * count
    scratch = [pltpu.VMEM((4, 4, k, n), low) for k, n in shapes]
    scratch += [pltpu.VMEM((4, 4, k, n), low) for k, n in shapes]
    scratch += [pltpu.VMEM((2, 2, 4, k // 2, n), low) for k, n in shapes]
    scratch += [pltpu.VMEM((2, 4, k // 2, n), low) for k, n in shapes]
    scratch += [pltpu.VMEM((3, k, n), low) for k, n in shapes]
    scratch += [pltpu.VMEM((4, k, n), low) for k, n in shapes]
    scratch += [
        pltpu.SemaphoreType.DMA((count, 16)),
        pltpu.SemaphoreType.DMA((count, 16)),
        pltpu.SemaphoreType.DMA((count, 5)),
    ]
    args = list(views)
    if small is not None:
        args.append(small)
        in_specs.append(VMEM)
        out_shape.append(jax.ShapeDtypeStruct(small.shape, small.dtype))
        out_specs.append(VMEM)
        scratch += [
            pltpu.VMEM((4,) + small.shape, small.dtype),
            pltpu.VMEM((7,) + small.shape, small.dtype),
            pltpu.SemaphoreType.DMA((6,)),
            pltpu.SemaphoreType.DMA((6,)),
        ]
    results = pl.pallas_call(
        functools.partial(reduce_kernel, count, small is not None),
        out_shape=tuple(out_shape),
        in_specs=in_specs,
        out_specs=tuple(out_specs),
        scratch_shapes=scratch,
        compiler_params=pltpu.CompilerParams(
            collective_id=tag, has_side_effects=True, vmem_limit_bytes=60 * 1024 * 1024
        ),
        name="reduce_grads",
    )(*args)
    blocks = [
        b.transpose(1, 0, 2).reshape(k, 4 * n).astype(jnp.float32)
        for b, (k, n) in zip(results[:count], shapes)
    ]
    return blocks, (results[count] if small is not None else None)


def scan_kernel(reverse, a_ref, b_ref, p_ref, h_ref):
    steps, width = a_ref.shape[1:]
    tiles = steps // 8
    spot = lax.broadcasted_iota(jnp.int32, (8, width), 0)

    def shift(values, distance, fill):
        if reverse:
            moved = pltpu.roll(values, 8 - distance, 0)
            return jnp.where(spot >= 8 - distance, fill, moved)
        moved = pltpu.roll(values, distance, 0)
        return jnp.where(spot < distance, fill, moved)

    def tile(i, carry):
        carry_a, carry_b = carry
        t = tiles - 1 - i if reverse else i
        rows = pl.ds(pl.multiple_of(t * 8, 8), 8)
        a, b = a_ref[0, rows, :], b_ref[0, rows, :]
        for distance in (1, 2, 4):
            b = b + a * shift(b, distance, 0.0)
            a = a * shift(a, distance, 1.0)
        b = b + a * carry_b
        a = a * carry_a
        p_ref[0, rows, :] = a
        h_ref[0, rows, :] = b
        edge = slice(0, 1) if reverse else slice(7, 8)
        return a[edge], b[edge]

    ones, zeros = jnp.ones((1, width), jnp.float32), jnp.zeros((1, width), jnp.float32)
    lax.fori_loop(0, tiles, tile, (ones, zeros))


def scan(a, b, reverse):
    count, steps, width = a.shape
    block = pl.BlockSpec((1, steps, 512), lambda i, j: (i, 0, j))
    return pl.pallas_call(
        functools.partial(scan_kernel, reverse),
        grid=(count, width // 512),
        in_specs=[block, block],
        out_specs=(block, block),
        out_shape=(jax.ShapeDtypeStruct(a.shape, a.dtype),) * 2,
        name="scan_back" if reverse else "scan_ahead",
    )(a, b)

def gelu_parts(v):
    inner = 0.7978845608028654 * (v + 0.044715 * v * v * v)
    t = jnp.tanh(inner)
    slope = 0.7978845608028654 * (1.0 + 0.134145 * v * v)
    return 0.5 * v * (1.0 + t), 0.5 * (1.0 + t) + 0.5 * v * (1.0 - t * t) * slope


def gelu_of(v):
    return 0.5 * v * (1.0 + jnp.tanh(0.7978845608028654 * (v + 0.044715 * v * v * v)))


def minus_expm1(v, power):
    total = 1.0 / 40320.0
    for term in (5040.0, 720.0, 120.0, 24.0, 6.0, 2.0, 1.0):
        total = total * v + 1.0 / term
    return jnp.where(v > -0.5, -v * total, 1.0 - power)


def tile_scan(a, b, reverse):
    spot = lax.broadcasted_iota(jnp.int32, a.shape, 0)
    for distance in (1, 2, 4):
        if reverse:
            inside = spot < 8 - distance
            back_a, back_b = pltpu.roll(a, 8 - distance, 0), pltpu.roll(b, 8 - distance, 0)
        else:
            inside = spot >= distance
            back_a, back_b = pltpu.roll(a, distance, 0), pltpu.roll(b, distance, 0)
        b = b + a * jnp.where(inside, back_b, 0.0)
        a = a * jnp.where(inside, back_a, 1.0)
    return a, b


def loop(count, body):
    def one(i, carry):
        body(i)
        return carry

    lax.fori_loop(0, count, one, 0)


def at(i, size):
    return pl.ds(pl.multiple_of(i * size, size), size)


def forward_kernel(*refs):
    refs = list(refs)

    def take(n):
        taken, refs[:n] = refs[:n], []
        return taken

    shards = take(8)
    tokens, marks, gain1, conv_w, conv_b, rate_b, input_b, decay_scale, gain2 = take(9)
    fulls = take(8)
    outs = take(12)
    (w_rec, w_rate, w_input, w_branch, w_out) = weights = take(5)
    normed, padded, conv_out, conv_low, rate_pre, input_pre = take(6)
    products, states, branch_pre, mixed_in, resid, normed2 = take(6)
    rim, ends, got, carry_in = take(4)
    send, recv, local, near_send, near_recv, load_sem, save_sem = refs
    count = 8
    r, s, z, c = place()
    mate, along_x, along_y, along_z = peers_of(r, s, z, c)
    across_x, across_y = along_x[0], along_y[0]
    others = [(r, lax.rem(s + k, 8)) for k in range(1, 8)]
    greet(others + [along_x, along_y])
    live, pending = [], []

    def start(copy):
        copy.start()
        live.append(copy)
        return copy

    def remote(m, slot, src, dst, device):
        return start(
            pltpu.make_async_remote_copy(
                src_ref=src,
                dst_ref=dst,
                send_sem=send.at[m, slot],
                recv_sem=recv.at[m, slot],
                device_id=device,
                device_id_type=MESH,
            )
        )

    def near(slot, src, dst, device):
        return start(
            pltpu.make_async_remote_copy(
                src_ref=src,
                dst_ref=dst,
                send_sem=near_send.at[slot],
                recv_sem=near_recv.at[slot],
                device_id=device,
                device_id_type=MESH,
            )
        )

    def save(slot, src, dst):
        copy = pltpu.make_async_copy(src, dst, save_sem.at[slot])
        copy.start()
        pending.append(copy)

    def region(m, source, quarter, begin, length):
        depth, width = shards[m].shape
        part = width // 4
        row = pl.multiple_of((source * 2 + c) * depth + begin, 16)
        column = pl.multiple_of(quarter * part, 128)
        return fulls[m].at[pl.ds(row, length), pl.ds(column, part)]

    stage_own, stage_z, stage_x, stage_y, stage_d, stage_c = {}, {}, {}, {}, {}, {}

    def begin(m):
        depth, width = shards[m].shape
        part = width // 4
        rows = pl.ds(pl.multiple_of(s * depth, 16), depth)
        own = pltpu.make_async_copy(shards[m], fulls[m].at[rows], local.at[m])
        own.start()
        column = pl.multiple_of(r * part, 128)
        stage_z[m] = [
            remote(
                m,
                k,
                shards[m].at[:, pl.ds(column, part)],
                region(m, z, r, 0, depth),
                along_z[k - 1],
            )
            for k in (1, 2, 3)
        ]
        stage_own[m] = (own, remote(m, 0, shards[m], fulls[m].at[rows], mate))

    def sources(k):
        return lax.rem(z + 4 - k, 4)

    def tick(now):
        m = now
        if m < count:
            depth = shards[m].shape[0]
            stage_x[m], stage_y[m] = [], []
            for k in (1, 2, 3):
                stage_z[m][k - 1].wait_recv()
                piece = region(m, sources(k), r, 0, depth)
                stage_x[m].append(remote(m, 3 + k, piece, piece, along_x))
                stage_y[m].append(remote(m, 6 + k, piece, piece, along_y))
        if now + 2 < count:
            begin(now + 2)
        m = now - 1
        if 0 <= m < count:
            depth = shards[m].shape[0]
            half = depth // 2
            stage_d[m] = []
            for k in (1, 2, 3):
                stage_x[m][k - 1].wait_recv()
                piece = region(m, sources(k), across_x, 0, half)
                stage_d[m].append(remote(m, 9 + k, piece, piece, along_y))
                stage_y[m][k - 1].wait_recv()
                piece = region(m, sources(k), across_y, half, half)
                stage_d[m].append(remote(m, 12 + k, piece, piece, along_x))
        m = now - 2
        if 0 <= m < count:
            depth = shards[m].shape[0]
            stage_c[m] = []
            for k in (1, 2, 3):
                stage_d[m][2 * k - 2].wait_recv()
                stage_d[m][2 * k - 1].wait_recv()
                rows = pl.ds(pl.multiple_of((sources(k) * 2 + c) * depth, 16), depth)
                piece = fulls[m].at[rows]
                stage_c[m].append(remote(m, 15 + k, piece, piece, mate))

    loads = {}

    def arrive(m):
        own, twin = stage_own[m]
        own.wait()
        twin.wait_recv()
        for copy in stage_c[m]:
            copy.wait_recv()
        if m < 5:
            loads[m] = pltpu.make_async_copy(fulls[m], weights[m], load_sem.at[m])
            loads[m].start()

    def product(left, right, store):
        width = right.shape[1]

        def one(j):
            columns = at(j, 512)
            store(
                columns,
                jnp.dot(left[...], right[:, columns], preferred_element_type=jnp.float32),
            )

        loop(width // 512, one)

    def first_norm():
        def one(i):
            rows = at(i, 32)
            values = tokens[rows, :].astype(jnp.float32)
            scale = lax.rsqrt(jnp.mean(values * values, axis=-1, keepdims=True) + epsilon)
            normed[rows, :] = (values * scale * gain1[...]).astype(jnp.bfloat16)

        loop(12, one)
        save(0, normed, outs[0])

    def rec_product():
        loads[0].wait()

        def store(columns, values):
            for row in range(3):
                padded[row, 8:136, columns] = values[row * 128 : (row + 1) * 128]

        product(normed, w_rec, store)
        return near(0, padded.at[:, pl.ds(128, 8), :], rim, others[0])

    def convolution(copy):
        copy.wait_recv()
        for row in range(3):
            padded[row, 0:8, :] = jnp.where(s > 0, rim[row], 0.0)
        save(1, padded, outs[1])

        def one(i):
            row, rest = lax.div(i, 12), lax.rem(i, 12)
            block, column = lax.div(rest, 3), lax.rem(rest, 3)
            columns = at(column, 512)
            window = padded[row, pl.ds(pl.multiple_of(block * 32, 8), 40), columns]
            rows = pl.ds(pl.multiple_of(row * 128 + block * 32, 32), 32)
            total = conv_b[:, columns] + conv_w[0:1, columns] * window[8:]
            for k in (1, 2, 3):
                shifted = pltpu.roll(window, k, 0)[8:]
                total = total + conv_w[k : k + 1, columns] * (marks[rows, k : k + 1] * shifted)
            conv_out[rows, columns] = total
            conv_low[rows, columns] = total.astype(jnp.bfloat16)

        loop(36, one)
        save(2, conv_out, outs[2])
        save(3, conv_low, outs[3])

    def gate_product(which):
        target, weight = ((rate_pre, w_rate), (input_pre, w_input))[which]
        loads[1 + which].wait()

        def store(columns, values):
            target[:, columns] = values

        product(conv_low, weight, store)
        save(4 + which, target, outs[4 + which])

    def branch_product():
        loads[3].wait()

        def store(columns, values):
            branch_pre[:, columns] = values

        product(normed, w_branch, store)
        save(7, branch_pre, outs[7])

    def local_scan():
        def one(column):
            columns = at(column, 512)

            def tile(t, carry):
                results = []
                for row in range(3):
                    rows = pl.ds(pl.multiple_of(row * 128 + t * 8, 8), 8)
                    reset = marks[rows, 0:1]
                    rate_gate = jax.nn.sigmoid(rate_pre[rows, columns] + rate_b[:, columns])
                    input_gate = jax.nn.sigmoid(input_pre[rows, columns] + input_b[:, columns])
                    log_rate = decay_scale[:, columns] * rate_gate
                    keep = 1.0 - reset
                    pace = jnp.exp(log_rate)
                    left = minus_expm1(2.0 * log_rate, pace * pace)
                    scale = reset + keep * jnp.sqrt(left)
                    a, b = tile_scan(
                        pace * keep, scale * input_gate * conv_out[rows, columns], False
                    )
                    b = b + a * carry[2 * row + 1]
                    a = a * carry[2 * row]
                    products[rows, columns] = a
                    states[rows, columns] = b
                    results += [a[7:8], b[7:8]]
                return tuple(results)

            ones, zeros = jnp.ones((1, 512), jnp.float32), jnp.zeros((1, 512), jnp.float32)
            last = lax.fori_loop(0, 16, tile, (ones, zeros) * 3)
            for row in range(3):
                ends[row : row + 1, columns] = last[2 * row]
                ends[3 + row : 4 + row, columns] = last[2 * row + 1]

        loop(3, one)
        return [near(k, ends, got.at[k], others[k - 1]) for k in range(1, 8)]

    def carry_states(copies):
        for copy in copies:
            copy.wait_recv()

        def one(column):
            columns = at(column, 512)
            state = jnp.zeros((3, 512), jnp.float32)
            for k in range(7, 0, -1):
                after = got[k, 3:6, columns] + got[k, 0:3, columns] * state
                state = jnp.where(k <= s, after, state)
            carry_in[0:3, columns] = state

        loop(3, one)
        save(10, carry_in, outs[10])

    def mix():
        def one(i):
            row, rest = lax.div(i, 12), lax.rem(i, 12)
            block, column = lax.div(rest, 3), lax.rem(rest, 3)
            columns = at(column, 512)
            rows = pl.ds(pl.multiple_of(row * 128 + block * 32, 32), 32)
            carried = carry_in[pl.ds(row, 1), columns]
            state = states[rows, columns] + products[rows, columns] * carried
            states[rows, columns] = state
            mixed_in[rows, columns] = (state * gelu_of(branch_pre[rows, columns])).astype(
                jnp.bfloat16
            )

        loop(36, one)
        save(6, states, outs[6])
        save(8, mixed_in, outs[8])

    def out_product():
        loads[4].wait()

        def store(columns, values):
            resid[:, columns] = tokens[:, columns].astype(jnp.float32) + values

        product(mixed_in, w_out, store)
        save(9, resid, outs[9])

        def one(i):
            rows = at(i, 32)
            values = resid[rows, :]
            scale = lax.rsqrt(jnp.mean(values * values, axis=-1, keepdims=True) + epsilon)
            normed2[rows, :] = (values * scale * gain2[...]).astype(jnp.bfloat16)

        loop(12, one)
        save(11, normed2, outs[11])

    carry_in[...] = jnp.zeros_like(carry_in)
    ends[...] = jnp.zeros_like(ends)
    begin(0)
    begin(1)
    first_norm()
    tick(0)
    tick(1)
    tick(2)
    arrive(0)
    rim_copy = rec_product()
    tick(3)
    arrive(1)
    convolution(rim_copy)
    gate_product(0)
    tick(4)
    arrive(2)
    gate_product(1)
    tick(5)
    ends_copies = local_scan()
    arrive(3)
    branch_product()
    tick(6)
    carry_states(ends_copies)
    mix()
    arrive(4)
    tick(7)
    out_product()
    tick(8)
    tick(9)
    for m in (5, 6, 7):
        arrive(m)
    for copy in live:
        copy.wait_send()
    for copy in pending:
        copy.wait()


def forward_all(shards, tokens, marks, vectors):
    low, full = jnp.bfloat16, jnp.float32
    tok, model = tokens.shape
    rec = shards[0].shape[1]
    shape = jax.ShapeDtypeStruct
    saved = (
        shape((tok, model), low),
        shape((3, 136, rec), full),
        shape((tok, rec), full),
        shape((tok, rec), low),
        shape((tok, rec), full),
        shape((tok, rec), full),
        shape((tok, rec), full),
        shape((tok, rec), full),
        shape((tok, rec), low),
        shape((tok, model), full),
        shape((8, rec), full),
        shape((tok, model), low),
    )
    fulls = tuple(shape((a.shape[0] * 8, a.shape[1]), low) for a in shards)
    results = pl.pallas_call(
        forward_kernel,
        out_shape=fulls + saved,
        in_specs=[ANY] * 8 + [VMEM] * 9,
        out_specs=(ANY,) * 20,
        scratch_shapes=[pltpu.VMEM(a.shape, low) for a in fulls[:5]]
        + [
            pltpu.VMEM((tok, model), low),
            pltpu.VMEM((3, 136, rec), full),
            pltpu.VMEM((tok, rec), full),
            pltpu.VMEM((tok, rec), low),
            pltpu.VMEM((tok, rec), full),
            pltpu.VMEM((tok, rec), full),
            pltpu.VMEM((tok, rec), full),
            pltpu.VMEM((tok, rec), full),
            pltpu.VMEM((tok, rec), full),
            pltpu.VMEM((tok, rec), low),
            pltpu.VMEM((tok, model), full),
            pltpu.VMEM((tok, model), low),
            pltpu.VMEM((3, 8, rec), full),
            pltpu.VMEM((8, rec), full),
            pltpu.VMEM((8, 8, rec), full),
            pltpu.VMEM((8, rec), full),
            pltpu.SemaphoreType.DMA((8, 19)),
            pltpu.SemaphoreType.DMA((8, 19)),
            pltpu.SemaphoreType.DMA((8,)),
            pltpu.SemaphoreType.DMA((8,)),
            pltpu.SemaphoreType.DMA((8,)),
            pltpu.SemaphoreType.DMA((5,)),
            pltpu.SemaphoreType.DMA((12,)),
        ],
        compiler_params=pltpu.CompilerParams(
            collective_id=0, has_side_effects=True, vmem_limit_bytes=60 * 1024 * 1024
        ),
        name="recurrent_forward",
    )(*shards, tokens, marks, *vectors)
    return results[:8], results[8:]

def from_behind(block, axis, distance):
    devices = range(lax.axis_size(axis))
    route = [(i - distance, i) for i in devices if i - distance in devices]
    return lax.ppermute(block, axis, route)


def prefix(part, axis, combine, identity, reverse):
    count = lax.axis_size(axis)
    place = lax.axis_index(axis)
    ahead = count - 1 - place if reverse else place
    gathered = jax.tree.map(lambda a: lax.all_gather(a, axis), part)
    state = jax.tree.map(lambda a, e: jnp.zeros_like(a) + jnp.asarray(e, a.dtype), part, identity)

    def one(turn, state):
        source = count - 1 - turn if reverse else turn
        return combine(
            state, jax.tree.map(lambda a: lax.dynamic_index_in_dim(a, source, 0, False), gathered)
        )

    return lax.fori_loop(0, ahead, one, state)


def rms_norm(values, gain):
    return values * lax.rsqrt(jnp.mean(values * values, axis=-1, keepdims=True) + epsilon) * gain


def combine(earlier, latter):
    return (earlier[0] * latter[0], latter[0] * earlier[1] + latter[1])


def conv_masks(padded_resets):
    keep_mask = 1.0 - padded_resets
    first = keep_mask[..., 3:]
    second = first * keep_mask[..., 2:-1]
    third = second * keep_mask[..., 1:-2]
    return (first, second, third)


def convolve(padded, masks, conv_weight, conv_bias):
    result = conv_bias + conv_weight[0] * padded[..., 3:, :]
    result = result + conv_weight[1] * masks[0][..., None] * padded[..., 2:-1, :]
    result = result + conv_weight[2] * masks[1][..., None] * padded[..., 1:-2, :]
    return result + conv_weight[3] * masks[2][..., None] * padded[..., :-3, :]


def gate_terms(rate_pre, input_pre, conv_out, decay_param, rate_bias, input_bias, resets):
    rate_gate = jax.nn.sigmoid(rate_pre + rate_bias)
    input_gate = jax.nn.sigmoid(input_pre + input_bias)
    log_rate = -8.0 * jax.nn.softplus(decay_param) * rate_gate
    keep_mask = 1.0 - resets[..., None]
    decays = jnp.exp(log_rate) * keep_mask
    scales = resets[..., None] + keep_mask * jnp.sqrt(-jnp.expm1(2.0 * log_rate))
    return (decays, scales * input_gate * conv_out)


def forward_product(values, weight):
    return jnp.dot(values, weight, preferred_element_type=jnp.float32)


def outer(left, right):
    return lax.dot_general(
        left, right, (((0,), (0,)), ((), ())), preferred_element_type=jnp.float32
    )


def back_product(grads, weight):
    return lax.dot_general(
        grads, weight, (((1,), (1,)), ((), ())), preferred_element_type=jnp.float32
    )


def plain_body(
    tokens,
    bounds,
    norm1_gain,
    w_branch,
    w_rec,
    conv_weight,
    conv_bias,
    w_rate,
    rate_bias,
    w_input,
    input_bias,
    decay_param,
    w_out,
    norm2_gain,
    w_gate,
    w_up,
    w_down,
    cotangent,
):
    gathered = (
        lax.all_gather(w_branch, "seq", axis=0, tiled=True),
        lax.all_gather(w_rec, "seq", axis=0, tiled=True),
        lax.all_gather(w_rate, "seq", axis=0, tiled=True),
        lax.all_gather(w_input, "seq", axis=0, tiled=True),
        lax.all_gather(w_out, "seq", axis=0, tiled=True),
        lax.all_gather(w_gate, "seq", axis=0, tiled=True),
        lax.all_gather(w_up, "seq", axis=0, tiled=True),
        lax.all_gather(w_down, "seq", axis=0, tiled=True),
    )
    full_branch, full_rec, full_rate, full_input, full_out, full_gate, full_up, full_down = gathered
    row_count, tok_count, model_width = tokens.shape
    rec_width = full_rec.shape[1]
    offset = lax.axis_index("seq") * tok_count
    positions = offset - 3 + jnp.arange(tok_count + 3, dtype=jnp.int32)
    marked = (
        jnp.any(positions[None, :, None] == bounds[:, None, :], axis=2) | (positions == 0)[None, :]
    )
    padded_resets = marked.astype(jnp.float32)
    resets = padded_resets[:, 3:]
    masks = conv_masks(padded_resets)
    inputs = tokens.astype(jnp.float32).reshape(-1, model_width)
    normed = rms_norm(inputs, norm1_gain).astype(jnp.bfloat16)
    branch_pre = forward_product(normed, full_branch)
    rec_in = forward_product(normed, full_rec).reshape(row_count, tok_count, rec_width)
    rim = from_behind(rec_in[:, tok_count - 3 :, :], "seq", 1)
    padded = jnp.concatenate([rim, rec_in], axis=1)
    conv_out = convolve(padded, masks, conv_weight, conv_bias)
    conv_low = conv_out.astype(jnp.bfloat16).reshape(-1, rec_width)
    rate_pre = forward_product(conv_low, full_rate).reshape(conv_out.shape)
    input_pre = forward_product(conv_low, full_input).reshape(conv_out.shape)

    def gates_of(rate_arg, input_arg, conv_arg, decay_arg, rate_arg_bias, input_arg_bias):
        return gate_terms(
            rate_arg, input_arg, conv_arg, decay_arg, rate_arg_bias, input_arg_bias, resets
        )

    decays, drives = gates_of(rate_pre, input_pre, conv_out, decay_param, rate_bias, input_bias)
    prefix_decay, local_states = lax.associative_scan(combine, (decays, drives), axis=1)
    ones_pair = jnp.ones((row_count, rec_width), jnp.float32)
    zeros_pair = jnp.zeros((row_count, rec_width), jnp.float32)
    carry_in = prefix(
        (prefix_decay[:, -1], local_states[:, -1]), "seq", combine, (ones_pair, zeros_pair), False
    )[1]
    states = local_states + prefix_decay * carry_in[:, None, :]
    earlier_states = jnp.concatenate([carry_in[:, None, :], states[:, :-1, :]], axis=1)
    branch_act = jax.nn.gelu(branch_pre, approximate=True).reshape(states.shape)
    mixed_in = (states * branch_act).astype(jnp.bfloat16).reshape(-1, rec_width)
    resid = inputs + forward_product(mixed_in, full_out)
    normed2 = rms_norm(resid, norm2_gain).astype(jnp.bfloat16)
    gate_pre = forward_product(normed2, full_gate)
    up_pre = forward_product(normed2, full_up)
    hidden = (jax.nn.gelu(gate_pre, approximate=True) * up_pre).astype(jnp.bfloat16)
    mixed = (resid + forward_product(hidden, full_down)).astype(jnp.bfloat16).reshape(tokens.shape)
    cot_low = cotangent.reshape(-1, model_width)
    grad_down = outer(hidden, cot_low)
    grad_hidden = back_product(cot_low, full_down)
    _, pull_mlp = jax.vjp(
        lambda gate_arg, up_arg: jax.nn.gelu(gate_arg, approximate=True) * up_arg, gate_pre, up_pre
    )
    grad_gate_pre, grad_up_pre = pull_mlp(grad_hidden)
    gate_low = grad_gate_pre.astype(jnp.bfloat16)
    up_low = grad_up_pre.astype(jnp.bfloat16)
    grad_gate = outer(normed2, gate_low)
    grad_up = outer(normed2, up_low)
    grad_normed2 = back_product(gate_low, full_gate) + back_product(up_low, full_up)
    _, pull_norm2 = jax.vjp(rms_norm, resid, norm2_gain)
    grad_resid_norm, grad_norm2 = pull_norm2(grad_normed2)
    grad_resid = cot_low.astype(jnp.float32) + grad_resid_norm
    resid_low = grad_resid.astype(jnp.bfloat16)
    grad_out = outer(mixed_in, resid_low)
    grad_mixed = back_product(resid_low, full_out).reshape(states.shape)
    grad_states = grad_mixed * branch_act
    _, pull_branch = jax.vjp(lambda pre_arg: jax.nn.gelu(pre_arg, approximate=True), branch_pre)
    branch_low = pull_branch((grad_mixed * states).reshape(-1, rec_width))[0].astype(jnp.bfloat16)
    next_decays = jnp.concatenate([decays[:, 1:, :], ones_pair[:, None, :]], axis=1)
    suffix_decay, local_grads = lax.associative_scan(
        combine, (next_decays, grad_states), axis=1, reverse=True
    )
    element = (prefix_decay[:, -1], decays[:, 0] * local_grads[:, 0])
    carry_back = prefix(element, "seq", combine, (ones_pair, zeros_pair), True)[1]
    state_grads = local_grads + suffix_decay * carry_back[:, None, :]
    _, pull_gates = jax.vjp(
        gates_of, rate_pre, input_pre, conv_out, decay_param, rate_bias, input_bias
    )
    grad_rate_pre, grad_input_pre, grad_conv_direct, grad_decay, grad_rate_bias, grad_input_bias = (
        pull_gates((state_grads * earlier_states, state_grads))
    )
    rate_low = grad_rate_pre.astype(jnp.bfloat16).reshape(-1, rec_width)
    input_low = grad_input_pre.astype(jnp.bfloat16).reshape(-1, rec_width)
    grad_rate = outer(conv_low, rate_low)
    grad_input = outer(conv_low, input_low)
    grad_conv = grad_conv_direct + (
        back_product(rate_low, full_rate) + back_product(input_low, full_input)
    ).reshape(conv_out.shape)
    _, pull_conv = jax.vjp(
        lambda pad_arg, weight_arg, bias_arg: convolve(pad_arg, masks, weight_arg, bias_arg),
        padded,
        conv_weight,
        conv_bias,
    )
    grad_padded, grad_conv_weight, grad_conv_bias = pull_conv(grad_conv)
    rim_back = from_behind(grad_padded[:, :3, :], "seq", -1)
    grad_rec = grad_padded[:, 3:, :] + jnp.concatenate(
        [jnp.zeros((row_count, tok_count - 3, rec_width), jnp.float32), rim_back], axis=1
    )
    rec_low = grad_rec.astype(jnp.bfloat16).reshape(-1, rec_width)
    grad_rec_w = outer(normed, rec_low)
    grad_branch_w = outer(normed, branch_low)
    grad_normed = back_product(branch_low, full_branch) + back_product(rec_low, full_rec)
    _, pull_norm1 = jax.vjp(rms_norm, inputs, norm1_gain)
    grad_inputs, grad_norm1 = pull_norm1(grad_normed)
    token_grad = (grad_resid + grad_inputs).astype(jnp.bfloat16).reshape(tokens.shape)
    grad_mats = (
        grad_branch_w,
        grad_rec_w,
        grad_rate,
        grad_input,
        grad_out,
        grad_gate,
        grad_up,
        grad_down,
    )
    blocks = (
        lax.psum_scatter(grad_mats[0], "seq", scatter_dimension=0, tiled=True),
        lax.psum_scatter(grad_mats[1], "seq", scatter_dimension=0, tiled=True),
        lax.psum_scatter(grad_mats[2], "seq", scatter_dimension=0, tiled=True),
        lax.psum_scatter(grad_mats[3], "seq", scatter_dimension=0, tiled=True),
        lax.psum_scatter(grad_mats[4], "seq", scatter_dimension=0, tiled=True),
        lax.psum_scatter(grad_mats[5], "seq", scatter_dimension=0, tiled=True),
        lax.psum_scatter(grad_mats[6], "seq", scatter_dimension=0, tiled=True),
        lax.psum_scatter(grad_mats[7], "seq", scatter_dimension=0, tiled=True),
    )
    summed = lax.psum(
        (blocks[0], blocks[1], blocks[2], blocks[3], blocks[4], blocks[5], blocks[6], blocks[7]),
        "rows",
    )
    small = lax.psum(
        (
            grad_norm1,
            grad_conv_weight,
            grad_conv_bias,
            grad_rate_bias,
            grad_input_bias,
            grad_decay,
            grad_norm2,
        ),
        ("rows", "seq"),
    )
    return (
        mixed,
        token_grad,
        small[0],
        summed[0],
        summed[1],
        small[1],
        small[2],
        summed[2],
        small[3],
        summed[3],
        small[4],
        small[5],
        summed[4],
        small[6],
        summed[5],
        summed[6],
        summed[7],
    )


def body(*args):
    if lax.axis_size("rows") == 4 and lax.axis_size("seq") == 8:
        return staged_body(*args)
    return plain_body(*args)


def staged_body(
    tokens,
    bounds,
    norm1_gain,
    w_branch,
    w_rec,
    conv_weight,
    conv_bias,
    w_rate,
    rate_bias,
    w_input,
    input_bias,
    decay_param,
    w_out,
    norm2_gain,
    w_gate,
    w_up,
    w_down,
    cotangent,
):
    row_count, tok_count, model_width = tokens.shape
    rec_width = w_rec.shape[1]
    offset = lax.axis_index("seq") * tok_count
    positions = offset - 3 + jnp.arange(tok_count + 3, dtype=jnp.int32)
    marked = (
        jnp.any(positions[None, :, None] == bounds[:, None, :], axis=2) | (positions == 0)[None, :]
    )
    padded_resets = marked.astype(jnp.float32)
    resets = padded_resets[:, 3:]
    masks = conv_masks(padded_resets)
    marks = jnp.stack((resets,) + masks + (resets,) * 4, axis=2).reshape(-1, 8)
    flat_tokens = tokens.reshape(-1, model_width)
    decay_scale = (-8.0 * jax.nn.softplus(decay_param))[None]
    fulls, saved = forward_all(
        (w_rec, w_rate, w_input, w_branch, w_out, w_gate, w_up, w_down),
        flat_tokens,
        marks,
        (
            norm1_gain[None],
            conv_weight,
            conv_bias[None],
            rate_bias[None],
            input_bias[None],
            decay_scale,
            norm2_gain[None],
        ),
    )
    full_rec, full_rate, full_input, full_branch, full_out, full_gate, full_up, full_down = fulls
    normed, padded_all, conv_out, conv_low, rate_pre, input_pre = saved[:6]
    states, branch_pre, mixed_in, resid, carried, normed2 = saved[6:]
    shape = (row_count, tok_count, rec_width)
    conv_out, rate_pre, input_pre = (a.reshape(shape) for a in (conv_out, rate_pre, input_pre))
    states = states.reshape(shape)
    carry_in = carried[:3]
    padded = padded_all[:, 5:, :]
    inputs = flat_tokens.astype(jnp.float32)

    def gates_of(rate_arg, input_arg, conv_arg, decay_arg, rate_arg_bias, input_arg_bias):
        return gate_terms(
            rate_arg, input_arg, conv_arg, decay_arg, rate_arg_bias, input_arg_bias, resets
        )

    decays, drives = gates_of(rate_pre, input_pre, conv_out, decay_param, rate_bias, input_bias)
    ones_pair = jnp.ones((row_count, rec_width), jnp.float32)
    zeros_pair = jnp.zeros((row_count, rec_width), jnp.float32)
    earlier_states = jnp.concatenate([carry_in[:, None, :], states[:, :-1, :]], axis=1)
    branch_act = jax.nn.gelu(branch_pre, approximate=True).reshape(states.shape)
    gate_pre = forward_product(normed2, full_gate)
    up_pre = forward_product(normed2, full_up)
    hidden = (jax.nn.gelu(gate_pre, approximate=True) * up_pre).astype(jnp.bfloat16)
    mixed = (resid + forward_product(hidden, full_down)).astype(jnp.bfloat16).reshape(tokens.shape)
    cot_low = cotangent.reshape(-1, model_width)
    grad_down = outer(hidden, cot_low)
    grad_hidden = back_product(cot_low, full_down)
    _, pull_mlp = jax.vjp(
        lambda gate_arg, up_arg: jax.nn.gelu(gate_arg, approximate=True) * up_arg, gate_pre, up_pre
    )
    grad_gate_pre, grad_up_pre = pull_mlp(grad_hidden)
    gate_low = grad_gate_pre.astype(jnp.bfloat16)
    up_low = grad_up_pre.astype(jnp.bfloat16)
    grad_gate = outer(normed2, gate_low)
    grad_up = outer(normed2, up_low)
    grad_normed2 = back_product(gate_low, full_gate) + back_product(up_low, full_up)
    _, pull_norm2 = jax.vjp(rms_norm, resid, norm2_gain)
    grad_resid_norm, grad_norm2 = pull_norm2(grad_normed2)
    grad_resid = cot_low.astype(jnp.float32) + grad_resid_norm
    resid_low = grad_resid.astype(jnp.bfloat16)
    grad_out = outer(mixed_in, resid_low)
    grad_mixed = back_product(resid_low, full_out).reshape(states.shape)
    grad_states = grad_mixed * branch_act
    _, pull_branch = jax.vjp(lambda pre_arg: jax.nn.gelu(pre_arg, approximate=True), branch_pre)
    branch_low = pull_branch((grad_mixed * states).reshape(-1, rec_width))[0].astype(jnp.bfloat16)
    next_decays = jnp.concatenate([decays[:, 1:, :], ones_pair[:, None, :]], axis=1)
    suffix_decay, local_grads = scan(next_decays, grad_states, True)
    element = (decays[:, 0] * suffix_decay[:, 0], decays[:, 0] * local_grads[:, 0])
    carry_back = prefix(element, "seq", combine, (ones_pair, zeros_pair), True)[1]
    state_grads = local_grads + suffix_decay * carry_back[:, None, :]
    _, pull_gates = jax.vjp(
        gates_of, rate_pre, input_pre, conv_out, decay_param, rate_bias, input_bias
    )
    grad_rate_pre, grad_input_pre, grad_conv_direct, grad_decay, grad_rate_bias, grad_input_bias = (
        pull_gates((state_grads * earlier_states, state_grads))
    )
    rate_low = grad_rate_pre.astype(jnp.bfloat16).reshape(-1, rec_width)
    input_low = grad_input_pre.astype(jnp.bfloat16).reshape(-1, rec_width)
    grad_rate = outer(conv_low, rate_low)
    grad_input = outer(conv_low, input_low)
    grad_conv = grad_conv_direct + (
        back_product(rate_low, full_rate) + back_product(input_low, full_input)
    ).reshape(conv_out.shape)
    _, pull_conv = jax.vjp(
        lambda pad_arg, weight_arg, bias_arg: convolve(pad_arg, masks, weight_arg, bias_arg),
        padded,
        conv_weight,
        conv_bias,
    )
    grad_padded, grad_conv_weight, grad_conv_bias = pull_conv(grad_conv)
    rim_back = from_behind(grad_padded[:, :3, :], "seq", -1)
    grad_rec = grad_padded[:, 3:, :] + jnp.concatenate(
        [jnp.zeros((row_count, tok_count - 3, rec_width), jnp.float32), rim_back], axis=1
    )
    rec_low = grad_rec.astype(jnp.bfloat16).reshape(-1, rec_width)
    grad_rec_w = outer(normed, rec_low)
    grad_branch_w = outer(normed, branch_low)
    grad_normed = back_product(branch_low, full_branch) + back_product(rec_low, full_rec)
    _, pull_norm1 = jax.vjp(rms_norm, inputs, norm1_gain)
    grad_inputs, grad_norm1 = pull_norm1(grad_normed)
    token_grad = (grad_resid + grad_inputs).astype(jnp.bfloat16).reshape(tokens.shape)
    low = jnp.bfloat16
    axis_size = 8
    ff, _ = reduce_all(
        [g.astype(low) for g in (grad_down, grad_gate, grad_up)], None, axis_size, 1
    )
    flat = jnp.concatenate(
        [
            g.reshape(-1)
            for g in (
                grad_norm1,
                grad_conv_weight,
                grad_conv_bias,
                grad_rate_bias,
                grad_input_bias,
                grad_decay,
                grad_norm2,
            )
        ]
    )
    size = flat.shape[0]
    flat = jnp.pad(flat, (0, -size % 8192)).reshape(-1, 1024)
    rec, flat = reduce_all(
        [g.astype(low) for g in (grad_out, grad_rate, grad_input, grad_branch_w, grad_rec_w)],
        flat,
        axis_size,
        2,
    )
    flat = flat.reshape(-1)
    small, begin = [], 0
    for like in (
        grad_norm1,
        grad_conv_weight,
        grad_conv_bias,
        grad_rate_bias,
        grad_input_bias,
        grad_decay,
        grad_norm2,
    ):
        small.append(flat[begin : begin + like.size].reshape(like.shape))
        begin += like.size
    summed = (rec[3], rec[4], rec[1], rec[2], rec[0], ff[1], ff[2], ff[0])
    return (
        mixed,
        token_grad,
        small[0],
        summed[0],
        summed[1],
        small[1],
        small[2],
        summed[2],
        small[3],
        summed[3],
        small[4],
        small[5],
        summed[4],
        small[6],
        summed[5],
        summed[6],
        summed[7],
    )


def solution(mesh):
    in_specs = (
        P("rows", "seq", None),
        P("rows", None),
        P(),
        P("seq", None),
        P("seq", None),
        P(),
        P(),
        P("seq", None),
        P(),
        P("seq", None),
        P(),
        P(),
        P("seq", None),
        P(),
        P("seq", None),
        P("seq", None),
        P("seq", None),
        P("rows", "seq", None),
    )
    out_specs = (
        P("rows", "seq", None),
        P("rows", "seq", None),
        P(),
        P("seq", None),
        P("seq", None),
        P(),
        P(),
        P("seq", None),
        P(),
        P("seq", None),
        P(),
        P(),
        P("seq", None),
        P(),
        P("seq", None),
        P("seq", None),
        P("seq", None),
    )
    return jax.shard_map(
        body, mesh=mesh, in_specs=in_specs, out_specs=out_specs, check_vma=False)
```

```python
import functools

import jax
import jax.numpy as jnp
from jax import lax
from jax.experimental import pallas as pl
from jax.experimental.pallas import tpu as pltpu
from jax.sharding import PartitionSpec as P

epsilon = 1e-06
MESH = pl.DeviceIdType.MESH
ANY = pl.BlockSpec(memory_space=pl.ANY)
VMEM = pl.BlockSpec(memory_space=pltpu.VMEM)


def place():
    r = lax.axis_index("rows")
    s = lax.axis_index("seq")
    return r, s, lax.div(s, 2), lax.rem(s, 2)


def greet(peers):
    barrier = pltpu.get_barrier_semaphore()
    for peer in peers:
        pl.semaphore_signal(barrier, inc=1, device_id=peer, device_id_type=MESH)
    pl.semaphore_wait(barrier, len(peers))


def peers_of(r, s, z, c):
    mate = (r, s + 1 - 2 * c)
    along_x = (r + 1 - 2 * lax.rem(r, 2), s)
    along_y = (lax.rem(r + 2, 4), s)
    along_z = [(r, lax.rem(z + k, 4) * 2 + c) for k in (1, 2, 3)]
    return mate, along_x, along_y, along_z


def gelu_parts(v):
    inner = 0.7978845608028654 * (v + 0.044715 * v * v * v)
    t = jnp.tanh(inner)
    slope = 0.7978845608028654 * (1.0 + 0.134145 * v * v)
    return 0.5 * v * (1.0 + t), 0.5 * (1.0 + t) + 0.5 * v * (1.0 - t * t) * slope


def gelu_of(v):
    return 0.5 * v * (1.0 + jnp.tanh(0.7978845608028654 * (v + 0.044715 * v * v * v)))


def minus_expm1(v, power):
    total = 1.0 / 40320.0
    for term in (5040.0, 720.0, 120.0, 24.0, 6.0, 2.0, 1.0):
        total = total * v + 1.0 / term
    return jnp.where(v > -0.5, -v * total, 1.0 - power)


def tile_scan(a, b, reverse):
    spot = lax.broadcasted_iota(jnp.int32, a.shape, 0)
    for distance in (1, 2, 4):
        if reverse:
            inside = spot < 8 - distance
            back_a, back_b = pltpu.roll(a, 8 - distance, 0), pltpu.roll(b, 8 - distance, 0)
        else:
            inside = spot >= distance
            back_a, back_b = pltpu.roll(a, distance, 0), pltpu.roll(b, distance, 0)
        b = b + a * jnp.where(inside, back_b, 0.0)
        a = a * jnp.where(inside, back_a, 1.0)
    return a, b


def loop(count, body):
    def one(i, carry):
        body(i)
        return carry

    lax.fori_loop(0, count, one, 0)


def at(i, size):
    return pl.ds(pl.multiple_of(i * size, size), size)


def forward_kernel(*refs):
    refs = list(refs)

    def take(n):
        taken, refs[:n] = refs[:n], []
        return taken

    shards = take(8)
    tokens, marks, gain1, conv_w, conv_b, rate_b, input_b, decay_scale, gain2 = take(9)
    fulls = take(8)
    outs = take(12)
    (w_rec, w_rate, w_input, w_branch, w_out) = weights = take(5)
    normed, padded, conv_out, conv_low, rate_pre, input_pre = take(6)
    products, states, branch_pre, mixed_in, resid, normed2 = take(6)
    rim, ends, got, carry_in = take(4)
    send, recv, local, near_send, near_recv, load_sem, save_sem = refs
    count = 8
    r, s, z, c = place()
    mate, along_x, along_y, along_z = peers_of(r, s, z, c)
    across_x, across_y = along_x[0], along_y[0]
    others = [(r, lax.rem(s + k, 8)) for k in range(1, 8)]
    greet(others + [along_x, along_y])
    live, pending = [], []

    def start(copy):
        copy.start()
        live.append(copy)
        return copy

    def remote(m, slot, src, dst, device):
        return start(
            pltpu.make_async_remote_copy(
                src_ref=src,
                dst_ref=dst,
                send_sem=send.at[m, slot],
                recv_sem=recv.at[m, slot],
                device_id=device,
                device_id_type=MESH,
            )
        )

    def near(slot, src, dst, device):
        return start(
            pltpu.make_async_remote_copy(
                src_ref=src,
                dst_ref=dst,
                send_sem=near_send.at[slot],
                recv_sem=near_recv.at[slot],
                device_id=device,
                device_id_type=MESH,
            )
        )

    def save(slot, src, dst):
        copy = pltpu.make_async_copy(src, dst, save_sem.at[slot])
        copy.start()
        pending.append(copy)

    def region(m, source, quarter, begin, length):
        depth, width = shards[m].shape
        part = width // 4
        row = pl.multiple_of((source * 2 + c) * depth + begin, 16)
        column = pl.multiple_of(quarter * part, 128)
        return fulls[m].at[pl.ds(row, length), pl.ds(column, part)]

    stage_own, stage_z, stage_x, stage_y, stage_d, stage_c = {}, {}, {}, {}, {}, {}

    def begin(m):
        depth, width = shards[m].shape
        part = width // 4
        rows = pl.ds(pl.multiple_of(s * depth, 16), depth)
        own = pltpu.make_async_copy(shards[m], fulls[m].at[rows], local.at[m])
        own.start()
        column = pl.multiple_of(r * part, 128)
        stage_z[m] = [
            remote(
                m,
                k,
                shards[m].at[:, pl.ds(column, part)],
                region(m, z, r, 0, depth),
                along_z[k - 1],
            )
            for k in (1, 2, 3)
        ]
        stage_own[m] = (own, remote(m, 0, shards[m], fulls[m].at[rows], mate))

    def sources(k):
        return lax.rem(z + 4 - k, 4)

    def tick(now):
        m = now
        if m < count:
            depth = shards[m].shape[0]
            stage_x[m], stage_y[m] = [], []
            for k in (1, 2, 3):
                stage_z[m][k - 1].wait_recv()
                piece = region(m, sources(k), r, 0, depth)
                stage_x[m].append(remote(m, 3 + k, piece, piece, along_x))
                stage_y[m].append(remote(m, 6 + k, piece, piece, along_y))
        if now + 2 < count:
            begin(now + 2)
        m = now - 1
        if 0 <= m < count:
            depth = shards[m].shape[0]
            half = depth // 2
            stage_d[m] = []
            for k in (1, 2, 3):
                stage_x[m][k - 1].wait_recv()
                piece = region(m, sources(k), across_x, 0, half)
                stage_d[m].append(remote(m, 9 + k, piece, piece, along_y))
                stage_y[m][k - 1].wait_recv()
                piece = region(m, sources(k), across_y, half, half)
                stage_d[m].append(remote(m, 12 + k, piece, piece, along_x))
        m = now - 2
        if 0 <= m < count:
            depth = shards[m].shape[0]
            stage_c[m] = []
            for k in (1, 2, 3):
                stage_d[m][2 * k - 2].wait_recv()
                stage_d[m][2 * k - 1].wait_recv()
                rows = pl.ds(pl.multiple_of((sources(k) * 2 + c) * depth, 16), depth)
                piece = fulls[m].at[rows]
                stage_c[m].append(remote(m, 15 + k, piece, piece, mate))

    loads = {}

    def arrive(m):
        own, twin = stage_own[m]
        own.wait()
        twin.wait_recv()
        for copy in stage_c[m]:
            copy.wait_recv()
        if m < 5:
            loads[m] = pltpu.make_async_copy(fulls[m], weights[m], load_sem.at[m])
            loads[m].start()

    def product(left, right, store):
        width = right.shape[1]

        def one(j):
            columns = at(j, 512)
            store(
                columns,
                jnp.dot(left[...], right[:, columns], preferred_element_type=jnp.float32),
            )

        loop(width // 512, one)

    def first_norm():
        def one(i):
            rows = at(i, 32)
            values = tokens[rows, :].astype(jnp.float32)
            scale = lax.rsqrt(jnp.mean(values * values, axis=-1, keepdims=True) + epsilon)
            normed[rows, :] = (values * scale * gain1[...]).astype(jnp.bfloat16)

        loop(12, one)
        save(0, normed, outs[0])

    def rec_product():
        loads[0].wait()

        def store(columns, values):
            for row in range(3):
                padded[row, 8:136, columns] = values[row * 128 : (row + 1) * 128]

        product(normed, w_rec, store)
        return near(0, padded.at[:, pl.ds(128, 8), :], rim, others[0])

    def convolution(copy):
        copy.wait_recv()
        for row in range(3):
            padded[row, 0:8, :] = jnp.where(s > 0, rim[row], 0.0)
        save(1, padded, outs[1])

        def one(i):
            row, rest = lax.div(i, 12), lax.rem(i, 12)
            block, column = lax.div(rest, 3), lax.rem(rest, 3)
            columns = at(column, 512)
            window = padded[row, pl.ds(pl.multiple_of(block * 32, 8), 40), columns]
            rows = pl.ds(pl.multiple_of(row * 128 + block * 32, 32), 32)
            spot = pl.ds(pl.multiple_of(block * 32, 32), 32)
            total = conv_b[:, columns] + conv_w[0:1, columns] * window[8:]
            for k in (1, 2, 3):
                shifted = pltpu.roll(window, k, 0)[8:]
                total = total + conv_w[k : k + 1, columns] * (marks[row, spot, k : k + 1] * shifted)
            conv_out[rows, columns] = total
            conv_low[rows, columns] = total.astype(jnp.bfloat16)

        loop(36, one)
        save(2, conv_out, outs[2])
        save(3, conv_low, outs[3])

    def gate_product(which):
        target, weight = ((rate_pre, w_rate), (input_pre, w_input))[which]
        loads[1 + which].wait()

        def store(columns, values):
            target[:, columns] = values

        product(conv_low, weight, store)
        save(4 + which, target, outs[4 + which])

    def branch_product():
        loads[3].wait()

        def store(columns, values):
            branch_pre[:, columns] = values

        product(normed, w_branch, store)
        save(7, branch_pre, outs[7])

    def local_scan():
        def one(column):
            columns = at(column, 512)

            def tile(t, carry):
                results = []
                for row in range(3):
                    rows = pl.ds(pl.multiple_of(row * 128 + t * 8, 8), 8)
                    reset = marks[row, pl.ds(pl.multiple_of(t * 8, 8), 8), 0:1]
                    rate_gate = jax.nn.sigmoid(rate_pre[rows, columns] + rate_b[:, columns])
                    input_gate = jax.nn.sigmoid(input_pre[rows, columns] + input_b[:, columns])
                    log_rate = decay_scale[:, columns] * rate_gate
                    keep = 1.0 - reset
                    pace = jnp.exp(log_rate)
                    left = minus_expm1(2.0 * log_rate, pace * pace)
                    scale = reset + keep * jnp.sqrt(left)
                    a, b = tile_scan(
                        pace * keep, scale * input_gate * conv_out[rows, columns], False
                    )
                    b = b + a * carry[2 * row + 1]
                    a = a * carry[2 * row]
                    products[rows, columns] = a
                    states[rows, columns] = b
                    results += [a[7:8], b[7:8]]
                return tuple(results)

            ones, zeros = jnp.ones((1, 512), jnp.float32), jnp.zeros((1, 512), jnp.float32)
            last = lax.fori_loop(0, 16, tile, (ones, zeros) * 3)
            for row in range(3):
                ends[row : row + 1, columns] = last[2 * row]
                ends[3 + row : 4 + row, columns] = last[2 * row + 1]

        loop(3, one)
        return [near(k, ends, got.at[k], others[k - 1]) for k in range(1, 8)]

    def carry_states(copies):
        for copy in copies:
            copy.wait_recv()

        def one(column):
            columns = at(column, 512)
            state = jnp.zeros((3, 512), jnp.float32)
            for k in range(7, 0, -1):
                after = got[k, 3:6, columns] + got[k, 0:3, columns] * state
                state = jnp.where(k <= s, after, state)
            carry_in[0:3, columns] = state

        loop(3, one)
        save(10, carry_in, outs[10])

    def mix():
        def one(i):
            row, rest = lax.div(i, 12), lax.rem(i, 12)
            block, column = lax.div(rest, 3), lax.rem(rest, 3)
            columns = at(column, 512)
            rows = pl.ds(pl.multiple_of(row * 128 + block * 32, 32), 32)
            carried = carry_in[pl.ds(row, 1), columns]
            state = states[rows, columns] + products[rows, columns] * carried
            states[rows, columns] = state
            mixed_in[rows, columns] = (state * gelu_of(branch_pre[rows, columns])).astype(
                jnp.bfloat16
            )

        loop(36, one)
        save(6, states, outs[6])
        save(8, mixed_in, outs[8])

    def out_product():
        loads[4].wait()

        def store(columns, values):
            resid[:, columns] = tokens[:, columns].astype(jnp.float32) + values

        product(mixed_in, w_out, store)
        save(9, resid, outs[9])

        def one(i):
            rows = at(i, 32)
            values = resid[rows, :]
            scale = lax.rsqrt(jnp.mean(values * values, axis=-1, keepdims=True) + epsilon)
            normed2[rows, :] = (values * scale * gain2[...]).astype(jnp.bfloat16)

        loop(12, one)
        save(11, normed2, outs[11])

    carry_in[...] = jnp.zeros_like(carry_in)
    ends[...] = jnp.zeros_like(ends)
    begin(0)
    begin(1)
    first_norm()
    tick(0)
    tick(1)
    tick(2)
    arrive(0)
    rim_copy = rec_product()
    tick(3)
    arrive(1)
    convolution(rim_copy)
    gate_product(0)
    tick(4)
    arrive(2)
    gate_product(1)
    tick(5)
    ends_copies = local_scan()
    arrive(3)
    branch_product()
    tick(6)
    carry_states(ends_copies)
    mix()
    arrive(4)
    tick(7)
    out_product()
    tick(8)
    tick(9)
    for m in (5, 6, 7):
        arrive(m)
    for copy in live:
        copy.wait_send()
    for copy in pending:
        copy.wait()


def forward_all(shards, tokens, marks, vectors):
    low, full = jnp.bfloat16, jnp.float32
    tok, model = tokens.shape
    rec = shards[0].shape[1]
    shape = jax.ShapeDtypeStruct
    saved = (
        shape((tok, model), low),
        shape((3, 136, rec), full),
        shape((tok, rec), full),
        shape((tok, rec), low),
        shape((tok, rec), full),
        shape((tok, rec), full),
        shape((tok, rec), full),
        shape((tok, rec), full),
        shape((tok, rec), low),
        shape((tok, model), full),
        shape((8, rec), full),
        shape((tok, model), low),
    )
    fulls = tuple(shape((a.shape[0] * 8, a.shape[1]), low) for a in shards)
    results = pl.pallas_call(
        forward_kernel,
        out_shape=fulls + saved,
        in_specs=[ANY] * 8 + [VMEM] * 9,
        out_specs=(ANY,) * 20,
        scratch_shapes=[pltpu.VMEM(a.shape, low) for a in fulls[:5]]
        + [
            pltpu.VMEM((tok, model), low),
            pltpu.VMEM((3, 136, rec), full),
            pltpu.VMEM((tok, rec), full),
            pltpu.VMEM((tok, rec), low),
            pltpu.VMEM((tok, rec), full),
            pltpu.VMEM((tok, rec), full),
            pltpu.VMEM((tok, rec), full),
            pltpu.VMEM((tok, rec), full),
            pltpu.VMEM((tok, rec), full),
            pltpu.VMEM((tok, rec), low),
            pltpu.VMEM((tok, model), full),
            pltpu.VMEM((tok, model), low),
            pltpu.VMEM((3, 8, rec), full),
            pltpu.VMEM((8, rec), full),
            pltpu.VMEM((8, 8, rec), full),
            pltpu.VMEM((8, rec), full),
            pltpu.SemaphoreType.DMA((8, 19)),
            pltpu.SemaphoreType.DMA((8, 19)),
            pltpu.SemaphoreType.DMA((8,)),
            pltpu.SemaphoreType.DMA((8,)),
            pltpu.SemaphoreType.DMA((8,)),
            pltpu.SemaphoreType.DMA((5,)),
            pltpu.SemaphoreType.DMA((12,)),
        ],
        compiler_params=pltpu.CompilerParams(
            collective_id=0, has_side_effects=True, vmem_limit_bytes=60 * 1024 * 1024
        ),
        name="recurrent_forward",
    )(*shards, tokens, marks, *vectors)
    return results[:8], results[8:]

class Reduction:
    def __init__(self, grads, outs, scratch, sems):
        self.grads, self.outs = grads, outs
        self.count = len(grads)
        self.held, self.own, self.first, self.second, self.third, self.final = scratch
        self.send, self.recv, self.local = sems
        self.live = []
        self.at_c, self.at_one, self.at_two, self.at_z, self.at_end, self.at_out = (
            {} for _ in range(6)
        )
        r, s, z, c = place()
        self.r, self.z, self.c = r, z, c
        self.mate, self.along_x, self.along_y, self.along_z = peers_of(r, s, z, c)
        self.diagonal = (3 - r, s)
        self.rx, self.ry = lax.rem(r, 2), lax.div(r, 2)

    def peers(self):
        return [self.mate, self.along_x, self.along_y, self.diagonal] + self.along_z

    def remote(self, m, slot, src, dst, device):
        copy = pltpu.make_async_remote_copy(
            src_ref=src,
            dst_ref=dst,
            send_sem=self.send.at[m, slot],
            recv_sem=self.recv.at[m, slot],
            device_id=device,
            device_id_type=MESH,
        )
        copy.start()
        self.live.append(copy)
        return copy

    def load(self, m, q):
        part = self.held[m].shape[3]
        near = pltpu.make_async_copy(
            self.grads[m].at[:, self.c, :, pl.ds(q * part, part)],
            self.own[m].at[q % 2],
            self.local.at[m, q],
        )
        near.start()
        return near

    def begin(self, m):
        part = self.held[m].shape[3]
        far = [
            self.remote(
                m,
                q,
                self.grads[m].at[:, 1 - self.c, :, pl.ds(q * part, part)],
                self.held[m].at[q],
                self.mate,
            )
            for q in range(4)
        ]
        self.at_c[m] = (far, [self.load(m, 0), self.load(m, 1)])

    def stage_core(self, m):
        held, own = self.held[m], self.own[m]
        half = held.shape[2] // 2
        far, near = self.at_c[m]
        for q in range(4):
            far[q].wait_recv()
            near[q].wait()

            def add(b):
                held[q, b] = held[q, b] + own[q % 2, b]

            loop(4, add)
            if q < 2:
                near.append(self.load(m, q + 2))
        self.at_one[m] = []
        for other in range(2):
            quarter = other * 2 + (1 - self.rx)
            self.at_one[m].append(
                self.remote(
                    m,
                    4 + other,
                    held.at[quarter, :, pl.ds(0, half)],
                    self.first[m].at[0, other],
                    self.along_x,
                )
            )
            quarter = (1 - self.ry) * 2 + other
            self.at_one[m].append(
                self.remote(
                    m,
                    6 + other,
                    held.at[quarter, :, pl.ds(half, half)],
                    self.first[m].at[1, other],
                    self.along_y,
                )
            )

    def stage_one(self, m):
        held, first = self.held[m], self.first[m]
        half = held.shape[2] // 2
        for copy in self.at_one[m]:
            copy.wait_recv()

        def add(i):
            other, b = lax.div(i, 4), lax.rem(i, 4)
            qx = other * 2 + self.rx
            held[qx, b, :half] = held[qx, b, :half] + first[0, other, b]
            qy = self.ry * 2 + other
            held[qy, b, half:] = held[qy, b, half:] + first[1, other, b]

        loop(8, add)
        self.at_two[m] = [
            self.remote(
                m,
                8,
                held.at[(1 - self.ry) * 2 + self.rx, :, pl.ds(0, half)],
                self.second[m].at[0],
                self.along_y,
            ),
            self.remote(
                m,
                9,
                held.at[self.ry * 2 + (1 - self.rx), :, pl.ds(half, half)],
                self.second[m].at[1],
                self.along_x,
            ),
        ]

    def stage_two(self, m):
        held, second, r = self.held[m], self.second[m], self.r
        half = held.shape[2] // 2
        for copy in self.at_two[m]:
            copy.wait_recv()

        def add(b):
            held[r, b, :half] = held[r, b, :half] + second[0, b]
            held[r, b, half:] = held[r, b, half:] + second[1, b]

        loop(4, add)
        self.at_z[m] = [
            self.remote(
                m,
                9 + k,
                held.at[r, lax.rem(self.z + k, 4)],
                self.third[m].at[k - 1],
                self.along_z[k - 1],
            )
            for k in (1, 2, 3)
        ]

    def stage_z(self, m):
        held, third, final, r = self.held[m], self.third[m], self.final[m], self.r
        for copy in self.at_z[m]:
            copy.wait_recv()
        depth = held.shape[2]

        def add(i):
            rows = at(i, 32)
            mine = held[r, self.z, rows, :].astype(jnp.float32)
            for k in range(3):
                mine = mine + third[k, rows, :].astype(jnp.float32)
            final[r, rows, :] = mine.astype(jnp.bfloat16)

        loop(depth // 32, add)
        self.at_end[m] = [
            self.remote(m, 13 + i, final.at[r], final.at[r], device)
            for i, device in enumerate((self.along_x, self.along_y, self.diagonal))
        ]

    def stage_end(self, m):
        for copy in self.at_end[m]:
            copy.wait_recv()
        out = pltpu.make_async_copy(self.final[m], self.outs[m], self.local.at[m, 4])
        out.start()
        self.at_out[m] = out

    def tick(self, now):
        stages = (self.stage_core, self.stage_one, self.stage_two, self.stage_z, self.stage_end)
        for late, stage in enumerate(stages):
            if 0 <= now - late < self.count:
                stage(now - late)
            if late == 0 and now + 2 < self.count:
                self.begin(now + 2)

    def ticks(self):
        return self.count + 4

    def close(self):
        for m in range(self.count):
            self.at_out[m].wait()
        for copy in self.live:
            copy.wait_send()


REDUCTION_SEMS = 16


def reduction_memory(shapes):
    low = jnp.bfloat16
    count = len(shapes)
    scratch = [pltpu.VMEM((4, 4, k, n), low) for k, n in shapes]
    scratch += [pltpu.VMEM((2, 4, k, n), low) for k, n in shapes]
    scratch += [pltpu.VMEM((2, 2, 4, k // 2, n), low) for k, n in shapes]
    scratch += [pltpu.VMEM((2, 4, k // 2, n), low) for k, n in shapes]
    scratch += [pltpu.VMEM((3, k, n), low) for k, n in shapes]
    scratch += [pltpu.VMEM((4, k, n), low) for k, n in shapes]
    return scratch + [
        pltpu.SemaphoreType.DMA((count, REDUCTION_SEMS)),
        pltpu.SemaphoreType.DMA((count, REDUCTION_SEMS)),
        pltpu.SemaphoreType.DMA((count, 5)),
    ]


def take_reduction(take, count):
    scratch = [take(count) for _ in range(6)]
    return scratch, take(3)


def taker(refs):
    refs = list(refs)

    def take(n):
        taken, refs[:n] = refs[:n], []
        return taken

    return take


def split_rows(grad):
    return grad.reshape(4, 2, grad.shape[0] // 8, grad.shape[1])


def quarter_shape(grad):
    return grad.shape[0] // 8, grad.shape[1] // 4


def joined(block):
    quarters, depth, part = block.shape
    return block.transpose(1, 0, 2).reshape(depth, quarters * part).astype(jnp.float32)


def reduce_kernel(count, *refs):
    take = taker(refs)
    grads = take(count)
    (small_in,) = take(1)
    outs = take(count)
    (small_out,) = take(1)
    reduction = Reduction(grads, outs, *take_reduction(take, count))
    small_held, small_got, small_send, small_recv = take(4)
    z = reduction.z
    greet(reduction.peers())
    small_copies = []

    def swap_small(slot, source, device):
        copy = pltpu.make_async_remote_copy(
            src_ref=small_held.at[source],
            dst_ref=small_got.at[slot],
            send_sem=small_send.at[slot],
            recv_sem=small_recv.at[slot],
            device_id=device,
            device_id_type=MESH,
        )
        copy.start()
        small_copies.append(copy)
        return copy

    small_held[0] = small_in[...]
    swap = swap_small(0, 0, reduction.mate)
    reduction.begin(0)
    if count > 1:
        reduction.begin(1)
    for now in range(reduction.ticks()):
        reduction.tick(now)
        if now < 2:
            swap.wait_recv()
            small_held[now + 1] = small_held[now] + small_got[now]
            swap = swap_small(now + 1, now + 1, (reduction.along_x, reduction.along_y)[now])
        if now == 2:
            swap.wait_recv()
            small_held[3] = small_held[2] + small_got[2]
            spread = [swap_small(2 + k, 3, reduction.along_z[k - 1]) for k in (1, 2, 3)]
    for copy in spread:
        copy.wait_recv()
    small_got[6] = small_held[3]
    total = None
    for source in range(4):
        k = lax.rem(z + 4 - source, 4)
        slot = jnp.where(k == 0, 6, 2 + k)
        term = small_got[slot]
        total = term if total is None else total + term
    small_out[...] = total
    for copy in small_copies:
        copy.wait_send()
    reduction.close()


def reduce_all(grads, small, tag):
    count = len(grads)
    shapes = [quarter_shape(g) for g in grads]
    results = pl.pallas_call(
        functools.partial(reduce_kernel, count),
        out_shape=tuple(jax.ShapeDtypeStruct((4, k, n), jnp.bfloat16) for k, n in shapes)
        + (jax.ShapeDtypeStruct(small.shape, small.dtype),),
        in_specs=[ANY] * count + [VMEM],
        out_specs=(ANY,) * count + (VMEM,),
        scratch_shapes=reduction_memory(shapes)
        + [
            pltpu.VMEM((4,) + small.shape, small.dtype),
            pltpu.VMEM((7,) + small.shape, small.dtype),
            pltpu.SemaphoreType.DMA((6,)),
            pltpu.SemaphoreType.DMA((6,)),
        ],
        compiler_params=pltpu.CompilerParams(
            collective_id=tag, has_side_effects=True, vmem_limit_bytes=60 * 1024 * 1024
        ),
        name="reduce_grads",
    )(*[split_rows(g) for g in grads], small)
    return [joined(b) for b in results[:count]], results[count]


def backward_kernel(count, *refs):
    take = taker(refs)
    grads = take(count)
    full_out, full_rate, full_input, full_branch, full_rec = take(5)
    saved_states, saved_branch, saved_rate, saved_input, saved_conv, saved_rec = take(6)
    resid_low, marks, tokens, grad_resid, normed, conv_low, mixed_in, carried = take(8)
    conv_w, rate_b, input_b, decay_scale, gain1 = take(5)
    outs = take(count)
    d_out, d_rate, d_input, d_branch, d_rec, token_grad = take(6)
    small, small_norm = take(2)
    reduction = Reduction(grads, outs, *take_reduction(take, count))
    ring, past, branch_pre, rate_pre, input_pre, conv_out = take(6)
    flow, grads_conv, branch_low, rate_low, input_low, stage = take(6)
    rim, ends, got, carry = take(4)
    near_send, near_recv, load_sem, ring_sem, stage_sem = take(5)
    r, s, z, c = place()
    others = [(r, lax.rem(s + k, 8)) for k in range(1, 8)]
    greet(others + [reduction.along_x, reduction.along_y, reduction.diagonal])
    live = []

    def near(slot, src, dst, device):
        copy = pltpu.make_async_remote_copy(
            src_ref=src,
            dst_ref=dst,
            send_sem=near_send.at[slot],
            recv_sem=near_recv.at[slot],
            device_id=device,
            device_id_type=MESH,
        )
        copy.start()
        live.append(copy)
        return copy

    def bring(slot, src, dst):
        copy = pltpu.make_async_copy(src, dst, load_sem.at[slot])
        copy.start()
        return copy

    tiles = []
    for weight in (full_out, full_rate, full_input, full_branch, full_rec):
        tiles.append([(weight, j) for j in range(weight.shape[0] // 512)])
    out_tiles, rate_tiles, input_tiles, branch_tiles, rec_tiles = tiles
    order = list(out_tiles)
    for pair in zip(rate_tiles, input_tiles):
        order += pair
    for pair in zip(branch_tiles, rec_tiles):
        order += pair
    fetches = {}

    def fetch(i):
        if i < len(order):
            weight, j = order[i]
            copy = pltpu.make_async_copy(
                weight.at[pl.ds(j * 512, 512)],
                ring.at[i % 3, :, pl.ds(0, weight.shape[1])],
                ring_sem.at[i % 3],
            )
            copy.start()
            fetches[i] = copy

    def back_tile(i, left, depth):
        fetches[i].wait()
        return lax.dot_general(
            left[...],
            ring[i % 3, :, pl.ds(0, depth)],
            (((1,), (1,)), ((), ())),
            preferred_element_type=jnp.float32,
        )

    staged = [None, None]
    turn = [0]

    def outer_product(left, right, target):
        for strip in range(left.shape[1] // 512):
            slot = turn[0] % 2
            turn[0] += 1
            if staged[slot] is not None:
                staged[slot].wait()
            rows = pl.ds(strip * 512, 512)
            width = right.shape[1]

            def one(j):
                columns = at(j, 512)
                stage[slot, :, columns] = lax.dot_general(
                    left[:, rows],
                    right[:, columns],
                    (((0,), (0,)), ((), ())),
                    preferred_element_type=jnp.float32,
                ).astype(jnp.bfloat16)

            loop(width // 512, one)
            copy = pltpu.make_async_copy(
                stage.at[slot, :, pl.ds(0, width)], target.at[rows], stage_sem.at[slot]
            )
            copy.start()
            staged[slot] = copy

    def block_of(i):
        row, block = lax.div(i, 4), lax.rem(i, 4)
        return row, block, pl.ds(pl.multiple_of(row * 128 + block * 32, 32), 32)

    def folded(values):
        return values[0:8] + values[8:16] + values[16:24] + values[24:32]

    def gates(rows, columns, mark_rows):
        rate_gate = jax.nn.sigmoid(rate_pre[rows, columns] + rate_b[:, columns])
        log_rate = decay_scale[:, columns] * rate_gate
        return rate_gate, log_rate, jnp.exp(log_rate)

    def branch_back():
        def one(i):
            column, rest = lax.div(i, 12), lax.rem(i, 12)
            row, block, rows = block_of(rest)
            columns = at(column, 512)
            act, slope = gelu_parts(branch_pre[rows, columns])
            grad = flow[rows, columns]
            state = past[row, pl.ds(pl.multiple_of(block * 32 + 8, 8), 32), columns]
            flow[rows, columns] = grad * act
            branch_low[rows, columns] = (grad * state * slope).astype(jnp.bfloat16)

        loop(36, one)

    def scan_back():
        def one(column):
            columns = at(column, 512)
            spot = lax.broadcasted_iota(jnp.int32, (8, 512), 0)

            def tile(i, state):
                t = 15 - i
                results = []
                for row in range(3):
                    rows = pl.ds(pl.multiple_of(row * 128 + t * 8, 8), 8)
                    keep = 1.0 - marks[row, pl.ds(pl.multiple_of(t * 8, 8), 8), 0:1]
                    _, _, pace = gates(rows, columns, None)
                    decay = pace * keep
                    follow, carry_a, carry_b = state[3 * row : 3 * row + 3]
                    later = jnp.where(spot == 7, follow, pltpu.roll(decay, 7, 0))
                    a, b = tile_scan(later, flow[rows, columns], True)
                    b = b + a * carry_b
                    a = a * carry_a
                    branch_pre[rows, columns] = a
                    flow[rows, columns] = b
                    results += [decay[0:1], a[0:1], b[0:1]]
                return tuple(results)

            ones, zeros = jnp.ones((1, 512), jnp.float32), jnp.zeros((1, 512), jnp.float32)
            last = lax.fori_loop(0, 16, tile, (ones, ones, zeros) * 3)
            for row in range(3):
                decay, a, b = last[3 * row : 3 * row + 3]
                ends[row : row + 1, columns] = decay * a
                ends[3 + row : 4 + row, columns] = decay * b

        loop(3, one)
        return [near(k, ends, got.at[k], others[k - 1]) for k in range(1, 8)]

    def carry_back(copies):
        for copy in copies:
            copy.wait_recv()

        def one(column):
            columns = at(column, 512)
            state = jnp.zeros((3, 512), jnp.float32)
            for ahead in range(7, 0, -1):
                k = 8 - ahead
                after = got[k, 3:6, columns] + got[k, 0:3, columns] * state
                state = jnp.where(s + ahead <= 7, after, state)
            carry[0:3, columns] = state

        loop(3, one)

    def gates_back():
        def one(column):
            columns = at(column, 512)

            def block_step(i, sums):
                row, block, rows = block_of(i)
                mark = pl.ds(pl.multiple_of(block * 32, 32), 32)
                reset = marks[row, mark, 0:1]
                keep = 1.0 - reset
                rate_gate, log_rate, pace = gates(rows, columns, mark)
                input_gate = jax.nn.sigmoid(input_pre[rows, columns] + input_b[:, columns])
                power = pace * pace
                root = jnp.sqrt(minus_expm1(2.0 * log_rate, power))
                scale = reset + keep * root
                conv = conv_out[rows, columns]
                grad = flow[rows, columns] + branch_pre[rows, columns] * carry[
                    pl.ds(row, 1), columns
                ]
                window = past[row, pl.ds(pl.multiple_of(block * 32, 8), 40), columns]
                before = pltpu.roll(window, 1, 0)[8:]
                grad_log = keep * grad * (before * pace - input_gate * conv * power / root)
                decay_sum = rate_gate * grad_log
                rate_grad = decay_scale[:, columns] * decay_sum * (1.0 - rate_gate)
                direct = grad * scale * input_gate
                input_grad = direct * conv * (1.0 - input_gate)
                rate_low[rows, columns] = rate_grad.astype(jnp.bfloat16)
                input_low[rows, columns] = input_grad.astype(jnp.bfloat16)
                rate_pre[rows, columns] = direct
                return (
                    sums[0] + folded(decay_sum),
                    sums[1] + folded(rate_grad),
                    sums[2] + folded(input_grad),
                )

            zeros = jnp.zeros((8, 512), jnp.float32)
            sums = lax.fori_loop(0, 12, block_step, (zeros,) * 3)
            for spot, values in enumerate(sums):
                small[5 + spot : 6 + spot, columns] = jnp.sum(values, axis=0, keepdims=True)

        loop(3, one)

    def conv_back(copy):
        copy.wait_recv()
        for row in range(3):
            grads_conv[row, 128:136, :] = jnp.where(s < 7, rim[row], 0.0)

        def one(column):
            columns = at(column, 512)

            def block_step(i, sums):
                row, block, rows = block_of(i)
                span = pl.ds(pl.multiple_of(block * 32, 8), 40)
                ahead = grads_conv[row, span, columns]
                behind = past[row, span, columns]
                grad = ahead[:32]
                total = conv_w[0:1, columns] * grad
                new = [sums[0] + folded(grad * behind[8:])]
                for k in (1, 2, 3):
                    kept = ahead * marks[row, span, k : k + 1]
                    total = total + conv_w[k : k + 1, columns] * pltpu.roll(kept, 40 - k, 0)[:32]
                    new.append(
                        sums[k] + folded(kept[:32] * pltpu.roll(behind, k, 0)[8:])
                    )
                new.append(sums[4] + folded(grad))
                rate_low[rows, columns] = total.astype(jnp.bfloat16)
                return tuple(new)

            zeros = jnp.zeros((8, 512), jnp.float32)
            sums = lax.fori_loop(0, 12, block_step, (zeros,) * 5)
            for spot, values in enumerate(sums):
                small[spot : spot + 1, columns] = jnp.sum(values, axis=0, keepdims=True)

        loop(3, one)

    def norm_back():
        def one(i, total):
            rows = at(i, 16)
            values = tokens[rows, :].astype(jnp.float32)
            scale = lax.rsqrt(jnp.mean(values * values, axis=-1, keepdims=True) + epsilon)
            grad = input_pre[rows, pl.ds(0, 1024)]
            back = grad * gain1[...]
            mean = jnp.mean(values * back, axis=-1, keepdims=True)
            result = grad_resid[rows, :] + scale * back - values * (scale * scale * scale * mean)
            stage[0, rows, pl.ds(0, 1024)] = result.astype(jnp.bfloat16)
            part = grad * values * scale
            return total + part[0:8] + part[8:16]

        if staged[0] is not None:
            staged[0].wait()
        total = lax.fori_loop(0, 24, one, jnp.zeros((8, 1024), jnp.float32))
        small_norm[...] = jnp.sum(total, axis=0, keepdims=True)
        copy = pltpu.make_async_copy(
            stage.at[0, pl.ds(0, 384), pl.ds(0, 1024)], token_grad, stage_sem.at[0]
        )
        copy.start()
        staged[0] = copy

    reduction.begin(0)
    reduction.begin(1)
    loads = [
        bring(0, saved_branch, branch_pre),
        bring(1, saved_states, past.at[:, pl.ds(8, 128), :]),
        bring(2, saved_rate, rate_pre),
        bring(3, saved_input, input_pre),
        bring(4, saved_conv, conv_out),
    ]
    for i in range(3):
        fetch(i)
    ends[...] = jnp.zeros_like(ends)
    for row in range(3):
        past[row, 0:8, :] = jnp.broadcast_to(carried[row : row + 1, :], (8, past.shape[2]))
    for i in range(3):
        flow[:, pl.ds(i * 512, 512)] = back_tile(i, resid_low, 1024)
        fetch(i + 3)
    reduction.tick(0)
    loads[0].wait()
    loads[1].wait()
    branch_back()
    loads[2].wait()
    copies = scan_back()
    outer_product(mixed_in, resid_low, d_out)
    reduction.tick(1)
    carry_back(copies)
    loads[3].wait()
    loads[4].wait()
    gates_back()
    loads.append(bring(5, saved_rec, past))
    at_tile = 3
    for j in range(3):
        columns = pl.ds(j * 512, 512)
        total = rate_pre[:, columns]
        total = total + back_tile(at_tile, rate_low, 1536)
        fetch(at_tile + 3)
        total = total + back_tile(at_tile + 1, input_low, 1536)
        fetch(at_tile + 4)
        at_tile += 2
        for row in range(3):
            grads_conv[row, 0:128, columns] = total[row * 128 : (row + 1) * 128]
    rim_copy = near(0, grads_conv.at[:, pl.ds(0, 8), :], rim, others[6])
    reduction.tick(2)
    outer_product(conv_low, rate_low, d_rate)
    loads[5].wait()
    conv_back(rim_copy)
    for j in range(2):
        columns = pl.ds(j * 512, 512)
        total = back_tile(at_tile, branch_low, 1536)
        fetch(at_tile + 3)
        total = total + back_tile(at_tile + 1, rate_low, 1536)
        fetch(at_tile + 4)
        at_tile += 2
        input_pre[:, columns] = total
    reduction.tick(3)
    outer_product(normed, rate_low, d_rec)
    outer_product(conv_low, input_low, d_input)
    reduction.tick(4)
    outer_product(normed, branch_low, d_branch)
    norm_back()
    for now in range(5, reduction.ticks()):
        reduction.tick(now)
    for copy in staged:
        copy.wait()
    for copy in live:
        copy.wait_send()
    reduction.close()


def backward_all(grads, fulls, saved, local, vectors):
    low, full = jnp.bfloat16, jnp.float32
    shape, memory = jax.ShapeDtypeStruct, pltpu.VMEM
    shapes = [quarter_shape(g) for g in grads]
    count = len(grads)
    tok, model = local[0].shape
    rec = fulls[0].shape[0]
    out_shape = tuple(shape((4, k, n), low) for k, n in shapes) + (
        shape((rec, model), low),
        shape((rec, rec), low),
        shape((rec, rec), low),
        shape((model, rec), low),
        shape((model, rec), low),
        shape((tok, model), low),
        shape((8, rec), full),
        shape((1, model), full),
    )
    results = pl.pallas_call(
        functools.partial(backward_kernel, count),
        out_shape=out_shape,
        in_specs=[ANY] * (count + 11) + [VMEM] * 13,
        out_specs=(ANY,) * (count + 6) + (VMEM,) * 2,
        scratch_shapes=reduction_memory(shapes)
        + [
            memory((3, 512, rec), low),
            memory((3, 136, rec), full),
            memory((tok, rec), full),
            memory((tok, rec), full),
            memory((tok, rec), full),
            memory((tok, rec), full),
            memory((tok, rec), full),
            memory((3, 136, rec), full),
            memory((tok, rec), low),
            memory((tok, rec), low),
            memory((tok, rec), low),
            memory((2, 512, rec), low),
            memory((3, 8, rec), full),
            memory((8, rec), full),
            memory((8, 8, rec), full),
            memory((8, rec), full),
            pltpu.SemaphoreType.DMA((8,)),
            pltpu.SemaphoreType.DMA((8,)),
            pltpu.SemaphoreType.DMA((6,)),
            pltpu.SemaphoreType.DMA((3,)),
            pltpu.SemaphoreType.DMA((2,)),
        ],
        compiler_params=pltpu.CompilerParams(
            collective_id=1, has_side_effects=True, vmem_limit_bytes=62 * 1024 * 1024
        ),
        name="recurrent_backward",
    )(*[split_rows(g) for g in grads], *fulls, *saved, *local, *vectors)
    return [joined(b) for b in results[:count]], results[count:]


def from_behind(block, axis, distance):
    devices = range(lax.axis_size(axis))
    route = [(i - distance, i) for i in devices if i - distance in devices]
    return lax.ppermute(block, axis, route)


def prefix(part, axis, combine, identity, reverse):
    count = lax.axis_size(axis)
    place = lax.axis_index(axis)
    ahead = count - 1 - place if reverse else place
    gathered = jax.tree.map(lambda a: lax.all_gather(a, axis), part)
    state = jax.tree.map(lambda a, e: jnp.zeros_like(a) + jnp.asarray(e, a.dtype), part, identity)

    def one(turn, state):
        source = count - 1 - turn if reverse else turn
        return combine(
            state, jax.tree.map(lambda a: lax.dynamic_index_in_dim(a, source, 0, False), gathered)
        )

    return lax.fori_loop(0, ahead, one, state)


def rms_norm(values, gain):
    return values * lax.rsqrt(jnp.mean(values * values, axis=-1, keepdims=True) + epsilon) * gain


def combine(earlier, latter):
    return (earlier[0] * latter[0], latter[0] * earlier[1] + latter[1])


def conv_masks(padded_resets):
    keep_mask = 1.0 - padded_resets
    first = keep_mask[..., 3:]
    second = first * keep_mask[..., 2:-1]
    third = second * keep_mask[..., 1:-2]
    return (first, second, third)


def convolve(padded, masks, conv_weight, conv_bias):
    result = conv_bias + conv_weight[0] * padded[..., 3:, :]
    result = result + conv_weight[1] * masks[0][..., None] * padded[..., 2:-1, :]
    result = result + conv_weight[2] * masks[1][..., None] * padded[..., 1:-2, :]
    return result + conv_weight[3] * masks[2][..., None] * padded[..., :-3, :]


def gate_terms(rate_pre, input_pre, conv_out, decay_param, rate_bias, input_bias, resets):
    rate_gate = jax.nn.sigmoid(rate_pre + rate_bias)
    input_gate = jax.nn.sigmoid(input_pre + input_bias)
    log_rate = -8.0 * jax.nn.softplus(decay_param) * rate_gate
    keep_mask = 1.0 - resets[..., None]
    decays = jnp.exp(log_rate) * keep_mask
    scales = resets[..., None] + keep_mask * jnp.sqrt(-jnp.expm1(2.0 * log_rate))
    return (decays, scales * input_gate * conv_out)


def forward_product(values, weight):
    return jnp.dot(values, weight, preferred_element_type=jnp.float32)


def outer(left, right):
    return lax.dot_general(
        left, right, (((0,), (0,)), ((), ())), preferred_element_type=jnp.float32
    )


def back_product(grads, weight):
    return lax.dot_general(
        grads, weight, (((1,), (1,)), ((), ())), preferred_element_type=jnp.float32
    )


def plain_body(
    tokens,
    bounds,
    norm1_gain,
    w_branch,
    w_rec,
    conv_weight,
    conv_bias,
    w_rate,
    rate_bias,
    w_input,
    input_bias,
    decay_param,
    w_out,
    norm2_gain,
    w_gate,
    w_up,
    w_down,
    cotangent,
):
    gathered = (
        lax.all_gather(w_branch, "seq", axis=0, tiled=True),
        lax.all_gather(w_rec, "seq", axis=0, tiled=True),
        lax.all_gather(w_rate, "seq", axis=0, tiled=True),
        lax.all_gather(w_input, "seq", axis=0, tiled=True),
        lax.all_gather(w_out, "seq", axis=0, tiled=True),
        lax.all_gather(w_gate, "seq", axis=0, tiled=True),
        lax.all_gather(w_up, "seq", axis=0, tiled=True),
        lax.all_gather(w_down, "seq", axis=0, tiled=True),
    )
    full_branch, full_rec, full_rate, full_input, full_out, full_gate, full_up, full_down = gathered
    row_count, tok_count, model_width = tokens.shape
    rec_width = full_rec.shape[1]
    offset = lax.axis_index("seq") * tok_count
    positions = offset - 3 + jnp.arange(tok_count + 3, dtype=jnp.int32)
    marked = (
        jnp.any(positions[None, :, None] == bounds[:, None, :], axis=2) | (positions == 0)[None, :]
    )
    padded_resets = marked.astype(jnp.float32)
    resets = padded_resets[:, 3:]
    masks = conv_masks(padded_resets)
    inputs = tokens.astype(jnp.float32).reshape(-1, model_width)
    normed = rms_norm(inputs, norm1_gain).astype(jnp.bfloat16)
    branch_pre = forward_product(normed, full_branch)
    rec_in = forward_product(normed, full_rec).reshape(row_count, tok_count, rec_width)
    rim = from_behind(rec_in[:, tok_count - 3 :, :], "seq", 1)
    padded = jnp.concatenate([rim, rec_in], axis=1)
    conv_out = convolve(padded, masks, conv_weight, conv_bias)
    conv_low = conv_out.astype(jnp.bfloat16).reshape(-1, rec_width)
    rate_pre = forward_product(conv_low, full_rate).reshape(conv_out.shape)
    input_pre = forward_product(conv_low, full_input).reshape(conv_out.shape)

    def gates_of(rate_arg, input_arg, conv_arg, decay_arg, rate_arg_bias, input_arg_bias):
        return gate_terms(
            rate_arg, input_arg, conv_arg, decay_arg, rate_arg_bias, input_arg_bias, resets
        )

    decays, drives = gates_of(rate_pre, input_pre, conv_out, decay_param, rate_bias, input_bias)
    prefix_decay, local_states = lax.associative_scan(combine, (decays, drives), axis=1)
    ones_pair = jnp.ones((row_count, rec_width), jnp.float32)
    zeros_pair = jnp.zeros((row_count, rec_width), jnp.float32)
    carry_in = prefix(
        (prefix_decay[:, -1], local_states[:, -1]), "seq", combine, (ones_pair, zeros_pair), False
    )[1]
    states = local_states + prefix_decay * carry_in[:, None, :]
    earlier_states = jnp.concatenate([carry_in[:, None, :], states[:, :-1, :]], axis=1)
    branch_act = jax.nn.gelu(branch_pre, approximate=True).reshape(states.shape)
    mixed_in = (states * branch_act).astype(jnp.bfloat16).reshape(-1, rec_width)
    resid = inputs + forward_product(mixed_in, full_out)
    normed2 = rms_norm(resid, norm2_gain).astype(jnp.bfloat16)
    gate_pre = forward_product(normed2, full_gate)
    up_pre = forward_product(normed2, full_up)
    hidden = (jax.nn.gelu(gate_pre, approximate=True) * up_pre).astype(jnp.bfloat16)
    mixed = (resid + forward_product(hidden, full_down)).astype(jnp.bfloat16).reshape(tokens.shape)
    cot_low = cotangent.reshape(-1, model_width)
    grad_down = outer(hidden, cot_low)
    grad_hidden = back_product(cot_low, full_down)
    _, pull_mlp = jax.vjp(
        lambda gate_arg, up_arg: jax.nn.gelu(gate_arg, approximate=True) * up_arg, gate_pre, up_pre
    )
    grad_gate_pre, grad_up_pre = pull_mlp(grad_hidden)
    gate_low = grad_gate_pre.astype(jnp.bfloat16)
    up_low = grad_up_pre.astype(jnp.bfloat16)
    grad_gate = outer(normed2, gate_low)
    grad_up = outer(normed2, up_low)
    grad_normed2 = back_product(gate_low, full_gate) + back_product(up_low, full_up)
    _, pull_norm2 = jax.vjp(rms_norm, resid, norm2_gain)
    grad_resid_norm, grad_norm2 = pull_norm2(grad_normed2)
    grad_resid = cot_low.astype(jnp.float32) + grad_resid_norm
    resid_low = grad_resid.astype(jnp.bfloat16)
    grad_out = outer(mixed_in, resid_low)
    grad_mixed = back_product(resid_low, full_out).reshape(states.shape)
    grad_states = grad_mixed * branch_act
    _, pull_branch = jax.vjp(lambda pre_arg: jax.nn.gelu(pre_arg, approximate=True), branch_pre)
    branch_low = pull_branch((grad_mixed * states).reshape(-1, rec_width))[0].astype(jnp.bfloat16)
    next_decays = jnp.concatenate([decays[:, 1:, :], ones_pair[:, None, :]], axis=1)
    suffix_decay, local_grads = lax.associative_scan(
        combine, (next_decays, grad_states), axis=1, reverse=True
    )
    element = (prefix_decay[:, -1], decays[:, 0] * local_grads[:, 0])
    carry_back = prefix(element, "seq", combine, (ones_pair, zeros_pair), True)[1]
    state_grads = local_grads + suffix_decay * carry_back[:, None, :]
    _, pull_gates = jax.vjp(
        gates_of, rate_pre, input_pre, conv_out, decay_param, rate_bias, input_bias
    )
    grad_rate_pre, grad_input_pre, grad_conv_direct, grad_decay, grad_rate_bias, grad_input_bias = (
        pull_gates((state_grads * earlier_states, state_grads))
    )
    rate_low = grad_rate_pre.astype(jnp.bfloat16).reshape(-1, rec_width)
    input_low = grad_input_pre.astype(jnp.bfloat16).reshape(-1, rec_width)
    grad_rate = outer(conv_low, rate_low)
    grad_input = outer(conv_low, input_low)
    grad_conv = grad_conv_direct + (
        back_product(rate_low, full_rate) + back_product(input_low, full_input)
    ).reshape(conv_out.shape)
    _, pull_conv = jax.vjp(
        lambda pad_arg, weight_arg, bias_arg: convolve(pad_arg, masks, weight_arg, bias_arg),
        padded,
        conv_weight,
        conv_bias,
    )
    grad_padded, grad_conv_weight, grad_conv_bias = pull_conv(grad_conv)
    rim_back = from_behind(grad_padded[:, :3, :], "seq", -1)
    grad_rec = grad_padded[:, 3:, :] + jnp.concatenate(
        [jnp.zeros((row_count, tok_count - 3, rec_width), jnp.float32), rim_back], axis=1
    )
    rec_low = grad_rec.astype(jnp.bfloat16).reshape(-1, rec_width)
    grad_rec_w = outer(normed, rec_low)
    grad_branch_w = outer(normed, branch_low)
    grad_normed = back_product(branch_low, full_branch) + back_product(rec_low, full_rec)
    _, pull_norm1 = jax.vjp(rms_norm, inputs, norm1_gain)
    grad_inputs, grad_norm1 = pull_norm1(grad_normed)
    token_grad = (grad_resid + grad_inputs).astype(jnp.bfloat16).reshape(tokens.shape)
    grad_mats = (
        grad_branch_w,
        grad_rec_w,
        grad_rate,
        grad_input,
        grad_out,
        grad_gate,
        grad_up,
        grad_down,
    )
    blocks = (
        lax.psum_scatter(grad_mats[0], "seq", scatter_dimension=0, tiled=True),
        lax.psum_scatter(grad_mats[1], "seq", scatter_dimension=0, tiled=True),
        lax.psum_scatter(grad_mats[2], "seq", scatter_dimension=0, tiled=True),
        lax.psum_scatter(grad_mats[3], "seq", scatter_dimension=0, tiled=True),
        lax.psum_scatter(grad_mats[4], "seq", scatter_dimension=0, tiled=True),
        lax.psum_scatter(grad_mats[5], "seq", scatter_dimension=0, tiled=True),
        lax.psum_scatter(grad_mats[6], "seq", scatter_dimension=0, tiled=True),
        lax.psum_scatter(grad_mats[7], "seq", scatter_dimension=0, tiled=True),
    )
    summed = lax.psum(
        (blocks[0], blocks[1], blocks[2], blocks[3], blocks[4], blocks[5], blocks[6], blocks[7]),
        "rows",
    )
    small = lax.psum(
        (
            grad_norm1,
            grad_conv_weight,
            grad_conv_bias,
            grad_rate_bias,
            grad_input_bias,
            grad_decay,
            grad_norm2,
        ),
        ("rows", "seq"),
    )
    return (
        mixed,
        token_grad,
        small[0],
        summed[0],
        summed[1],
        small[1],
        small[2],
        summed[2],
        small[3],
        summed[3],
        small[4],
        small[5],
        summed[4],
        small[6],
        summed[5],
        summed[6],
        summed[7],
    )


def body(*args):
    if lax.axis_size("rows") == 4 and lax.axis_size("seq") == 8:
        return staged_body(*args)
    return plain_body(*args)


def staged_body(
    tokens,
    bounds,
    norm1_gain,
    w_branch,
    w_rec,
    conv_weight,
    conv_bias,
    w_rate,
    rate_bias,
    w_input,
    input_bias,
    decay_param,
    w_out,
    norm2_gain,
    w_gate,
    w_up,
    w_down,
    cotangent,
):
    row_count, tok_count, model_width = tokens.shape
    rec_width = w_rec.shape[1]
    offset = lax.axis_index("seq") * tok_count
    positions = offset - 3 + jnp.arange(tok_count + 11, dtype=jnp.int32)
    marked = (
        jnp.any(positions[None, :, None] == bounds[:, None, :], axis=2) | (positions == 0)[None, :]
    )
    padded_resets = marked.astype(jnp.float32)
    resets = padded_resets[:, 3:]
    masks = conv_masks(padded_resets)
    marks = jnp.stack((resets,) + masks + (resets,) * 4, axis=2)
    flat_tokens = tokens.reshape(-1, model_width)
    decay_scale = (-8.0 * jax.nn.softplus(decay_param))[None]
    fulls, saved = forward_all(
        (w_rec, w_rate, w_input, w_branch, w_out, w_gate, w_up, w_down),
        flat_tokens,
        marks,
        (
            norm1_gain[None],
            conv_weight,
            conv_bias[None],
            rate_bias[None],
            input_bias[None],
            decay_scale,
            norm2_gain[None],
        ),
    )
    full_rec, full_rate, full_input, full_branch, full_out, full_gate, full_up, full_down = fulls
    normed, padded, conv_out, conv_low, rate_pre, input_pre = saved[:6]
    states, branch_pre, mixed_in, resid, carried, normed2 = saved[6:]
    gate_pre = forward_product(normed2, full_gate)
    up_pre = forward_product(normed2, full_up)
    hidden = (jax.nn.gelu(gate_pre, approximate=True) * up_pre).astype(jnp.bfloat16)
    mixed = (resid + forward_product(hidden, full_down)).astype(jnp.bfloat16).reshape(tokens.shape)
    cot_low = cotangent.reshape(-1, model_width)
    grad_down = outer(hidden, cot_low)
    grad_hidden = back_product(cot_low, full_down)
    _, pull_mlp = jax.vjp(
        lambda gate_arg, up_arg: jax.nn.gelu(gate_arg, approximate=True) * up_arg, gate_pre, up_pre
    )
    grad_gate_pre, grad_up_pre = pull_mlp(grad_hidden)
    gate_low = grad_gate_pre.astype(jnp.bfloat16)
    up_low = grad_up_pre.astype(jnp.bfloat16)
    grad_gate = outer(normed2, gate_low)
    grad_up = outer(normed2, up_low)
    grad_normed2 = back_product(gate_low, full_gate) + back_product(up_low, full_up)
    _, pull_norm2 = jax.vjp(rms_norm, resid, norm2_gain)
    grad_resid_norm, grad_norm2 = pull_norm2(grad_normed2)
    grad_resid = cot_low.astype(jnp.float32) + grad_resid_norm
    resid_low = grad_resid.astype(jnp.bfloat16)
    low = jnp.bfloat16
    ff, rest = backward_all(
        [g.astype(low) for g in (grad_down, grad_gate, grad_up)],
        (full_out, full_rate, full_input, full_branch, full_rec),
        (
            states.reshape(row_count, tok_count, rec_width),
            branch_pre,
            rate_pre,
            input_pre,
            conv_out,
            padded,
        ),
        (resid_low, marks, flat_tokens, grad_resid, normed, conv_low, mixed_in, carried),
        (conv_weight, rate_bias[None], input_bias[None], decay_scale, norm1_gain[None]),
    )
    rec_grads, (token_grad, sums, grad_norm1) = rest[:5], rest[5:]
    small = jnp.concatenate(
        [
            sums.reshape(-1, model_width),
            grad_norm1,
            grad_norm2[None],
            jnp.zeros((2, model_width), jnp.float32),
        ]
    )
    rec, small = reduce_all(rec_grads, small, 2)
    sums = small[:12].reshape(8, rec_width)
    return (
        mixed,
        token_grad.reshape(tokens.shape),
        small[12],
        rec[3],
        rec[4],
        sums[:4],
        sums[4],
        rec[1],
        sums[6],
        rec[2],
        sums[7],
        -8.0 * jax.nn.sigmoid(decay_param) * sums[5],
        rec[0],
        small[13],
        ff[1],
        ff[2],
        ff[0],
    )


def solution(mesh):
    in_specs = (
        P("rows", "seq", None),
        P("rows", None),
        P(),
        P("seq", None),
        P("seq", None),
        P(),
        P(),
        P("seq", None),
        P(),
        P("seq", None),
        P(),
        P(),
        P("seq", None),
        P(),
        P("seq", None),
        P("seq", None),
        P("seq", None),
        P("rows", "seq", None),
    )
    out_specs = (
        P("rows", "seq", None),
        P("rows", "seq", None),
        P(),
        P("seq", None),
        P("seq", None),
        P(),
        P(),
        P("seq", None),
        P(),
        P("seq", None),
        P(),
        P(),
        P("seq", None),
        P(),
        P("seq", None),
        P("seq", None),
        P("seq", None),
    )
    return jax.shard_map(
        body, mesh=mesh, in_specs=in_specs, out_specs=out_specs, check_vma=False)
```

```python
import functools

import jax
import jax.numpy as jnp
from jax import lax
from jax.experimental import pallas as pl
from jax.experimental.pallas import tpu as pltpu
from jax.sharding import PartitionSpec as P

epsilon = 1e-06
MESH = pl.DeviceIdType.MESH
ANY = pl.BlockSpec(memory_space=pl.ANY)
VMEM = pl.BlockSpec(memory_space=pltpu.VMEM)


def place():
    r = lax.axis_index("rows")
    s = lax.axis_index("seq")
    return r, s, lax.div(s, 2), lax.rem(s, 2)


def greet(peers):
    barrier = pltpu.get_barrier_semaphore()
    for peer in peers:
        pl.semaphore_signal(barrier, inc=1, device_id=peer, device_id_type=MESH)
    pl.semaphore_wait(barrier, len(peers))


def peers_of(r, s, z, c):
    mate = (r, s + 1 - 2 * c)
    along_x = (r + 1 - 2 * lax.rem(r, 2), s)
    along_y = (lax.rem(r + 2, 4), s)
    along_z = [(r, lax.rem(z + k, 4) * 2 + c) for k in (1, 2, 3)]
    return mate, along_x, along_y, along_z


def gelu_parts(v):
    inner = 0.7978845608028654 * (v + 0.044715 * v * v * v)
    t = jnp.tanh(inner)
    slope = 0.7978845608028654 * (1.0 + 0.134145 * v * v)
    return 0.5 * v * (1.0 + t), 0.5 * (1.0 + t) + 0.5 * v * (1.0 - t * t) * slope


def gelu_of(v):
    return 0.5 * v * (1.0 + jnp.tanh(0.7978845608028654 * (v + 0.044715 * v * v * v)))


def minus_expm1(v, power):
    total = 1.0 / 40320.0
    for term in (5040.0, 720.0, 120.0, 24.0, 6.0, 2.0, 1.0):
        total = total * v + 1.0 / term
    return jnp.where(v > -0.5, -v * total, 1.0 - power)


def tile_scan(a, b, reverse):
    spot = lax.broadcasted_iota(jnp.int32, a.shape, 0)
    for distance in (1, 2, 4):
        if reverse:
            inside = spot < 8 - distance
            back_a, back_b = pltpu.roll(a, 8 - distance, 0), pltpu.roll(b, 8 - distance, 0)
        else:
            inside = spot >= distance
            back_a, back_b = pltpu.roll(a, distance, 0), pltpu.roll(b, distance, 0)
        b = b + a * jnp.where(inside, back_b, 0.0)
        a = a * jnp.where(inside, back_a, 1.0)
    return a, b


def loop(count, body):
    def one(i, carry):
        body(i)
        return carry

    lax.fori_loop(0, count, one, 0)


def at(i, size):
    return pl.ds(pl.multiple_of(i * size, size), size)


def forward_kernel(*refs):
    refs = list(refs)

    def take(n):
        taken, refs[:n] = refs[:n], []
        return taken

    shards = take(8)
    cotangent, tokens, marks, gain1, conv_w, conv_b, rate_b, input_b, decay_scale, gain2 = take(10)
    fulls = take(8)
    outs = take(11)
    pair_normed2, pair_cotangent = take(2)
    (w_rec, w_rate, w_input, w_branch, w_out) = weights = take(5)
    normed, padded, conv_out, conv_low, rate_pre, input_pre = take(6)
    products, states, branch_pre, mixed_in, resid, normed2 = take(6)
    rim, ends, got, carry_in = take(4)
    send, recv, local, near_send, near_recv, load_sem, save_sem = refs
    count = 8
    r, s, z, c = place()
    mate, along_x, along_y, along_z = peers_of(r, s, z, c)
    across_x, across_y = along_x[0], along_y[0]
    parity = lax.rem(z, 2)
    twin = (r, s + 2 - 4 * parity)
    others = [(r, lax.rem(s + k, 8)) for k in range(1, 8)]
    greet(others + [along_x, along_y])
    live, pending = [], []

    def start(copy):
        copy.start()
        live.append(copy)
        return copy

    def remote(m, slot, src, dst, device):
        return start(
            pltpu.make_async_remote_copy(
                src_ref=src,
                dst_ref=dst,
                send_sem=send.at[m, slot],
                recv_sem=recv.at[m, slot],
                device_id=device,
                device_id_type=MESH,
            )
        )

    def near(slot, src, dst, device):
        return start(
            pltpu.make_async_remote_copy(
                src_ref=src,
                dst_ref=dst,
                send_sem=near_send.at[slot],
                recv_sem=near_recv.at[slot],
                device_id=device,
                device_id_type=MESH,
            )
        )

    def save(slot, src, dst):
        copy = pltpu.make_async_copy(src, dst, save_sem.at[slot])
        copy.start()
        pending.append(copy)

    def rows_of(m, source, core, begin, length):
        depth = shards[m].shape[0]
        block = lax.div(source, 2) * 2 + core if m == 7 else source * 2 + core
        return pl.ds(pl.multiple_of(block * depth + begin, 16), length)

    def region(m, source, quarter, begin, length):
        part = fulls[m].shape[1] // 4
        column = pl.multiple_of(quarter * part, 128)
        return fulls[m].at[rows_of(m, source, c, begin, length), pl.ds(column, part)]

    def turns(m):
        return (2,) if m == 7 else (1, 2, 3)

    stage_own, stage_z, stage_x, stage_y, stage_d, stage_c = {}, {}, {}, {}, {}, {}

    def begin(m):
        depth, width = shards[m].shape
        part = fulls[m].shape[1] // 4
        rows = rows_of(m, z, c, 0, depth)
        stage_z[m] = []
        for k in turns(m):
            column = r * part
            if m in (5, 6):
                half = lax.rem(parity + k, 2)
                column = (half + 2 * lax.div(r, 2)) * (2 * part) + lax.rem(r, 2) * part
            stage_z[m].append(
                remote(
                    m,
                    k,
                    shards[m].at[:, pl.ds(pl.multiple_of(column, 128), part)],
                    region(m, z, r, 0, depth),
                    along_z[k - 1],
                )
            )
        pieces = [(shards[m], fulls[m].at[rows])]
        if m in (5, 6):
            strip = 2 * part
            pieces = [
                (
                    shards[m].at[:, pl.ds(pl.multiple_of((parity + 2 * i) * strip, 128), strip)],
                    fulls[m].at[rows, pl.ds(i * strip, strip)],
                )
                for i in range(2)
            ]
        stage_own[m] = []
        for i, (src, dst) in enumerate(pieces):
            own = pltpu.make_async_copy(src, dst, local.at[m, i])
            own.start()
            stage_own[m].append((own, remote(m, 19 * i, src, dst, mate)))

    def sources(k):
        return lax.rem(z + 4 - k, 4)

    def tick(now):
        m = now
        if m < count:
            depth = shards[m].shape[0]
            stage_x[m], stage_y[m] = [], []
            for i, k in enumerate(turns(m)):
                stage_z[m][i].wait_recv()
                piece = region(m, sources(k), r, 0, depth)
                stage_x[m].append(remote(m, 3 + k, piece, piece, along_x))
                stage_y[m].append(remote(m, 6 + k, piece, piece, along_y))
        if now + 2 < count:
            begin(now + 2)
        m = now - 1
        if 0 <= m < count:
            depth = shards[m].shape[0]
            half = depth // 2
            stage_d[m] = []
            for i, k in enumerate(turns(m)):
                stage_x[m][i].wait_recv()
                piece = region(m, sources(k), across_x, 0, half)
                stage_d[m].append(remote(m, 9 + k, piece, piece, along_y))
                stage_y[m][i].wait_recv()
                piece = region(m, sources(k), across_y, half, half)
                stage_d[m].append(remote(m, 12 + k, piece, piece, along_x))
        m = now - 2
        if 0 <= m < count:
            depth = shards[m].shape[0]
            stage_c[m] = []
            for i, k in enumerate(turns(m)):
                stage_d[m][2 * i].wait_recv()
                stage_d[m][2 * i + 1].wait_recv()
                piece = fulls[m].at[rows_of(m, sources(k), c, 0, depth)]
                stage_c[m].append(remote(m, 15 + k, piece, piece, mate))

    loads = {}

    def arrive(m):
        for own, swapped in stage_own[m]:
            own.wait()
            swapped.wait_recv()
        for copy in stage_c[m]:
            copy.wait_recv()
        if m < 5:
            loads[m] = pltpu.make_async_copy(fulls[m], weights[m], load_sem.at[m])
            loads[m].start()

    def product(left, right, store):
        width = right.shape[1]

        def one(j):
            columns = at(j, 512)
            store(
                columns,
                jnp.dot(left[...], right[:, columns], preferred_element_type=jnp.float32),
            )

        loop(width // 512, one)

    def first_norm():
        def one(i):
            rows = at(i, 32)
            values = tokens[rows, :].astype(jnp.float32)
            scale = lax.rsqrt(jnp.mean(values * values, axis=-1, keepdims=True) + epsilon)
            normed[rows, :] = (values * scale * gain1[...]).astype(jnp.bfloat16)

        loop(12, one)
        save(0, normed, outs[0])

    def rec_product():
        loads[0].wait()

        def store(columns, values):
            for row in range(3):
                padded[row, 8:136, columns] = values[row * 128 : (row + 1) * 128]

        product(normed, w_rec, store)
        return near(0, padded.at[:, pl.ds(128, 8), :], rim, others[0])

    def convolution(copy):
        copy.wait_recv()
        for row in range(3):
            padded[row, 0:8, :] = jnp.where(s > 0, rim[row], 0.0)
        save(1, padded, outs[1])

        def one(i):
            row, rest = lax.div(i, 12), lax.rem(i, 12)
            block, column = lax.div(rest, 3), lax.rem(rest, 3)
            columns = at(column, 512)
            window = padded[row, pl.ds(pl.multiple_of(block * 32, 8), 40), columns]
            rows = pl.ds(pl.multiple_of(row * 128 + block * 32, 32), 32)
            spot = pl.ds(pl.multiple_of(block * 32, 32), 32)
            total = conv_b[:, columns] + conv_w[0:1, columns] * window[8:]
            for k in (1, 2, 3):
                shifted = pltpu.roll(window, k, 0)[8:]
                total = total + conv_w[k : k + 1, columns] * (marks[row, spot, k : k + 1] * shifted)
            conv_out[rows, columns] = total
            conv_low[rows, columns] = total.astype(jnp.bfloat16)

        loop(36, one)
        save(2, conv_out, outs[2])
        save(3, conv_low, outs[3])

    def gate_product(which):
        target, weight = ((rate_pre, w_rate), (input_pre, w_input))[which]
        loads[1 + which].wait()

        def store(columns, values):
            target[:, columns] = values

        product(conv_low, weight, store)
        save(4 + which, target, outs[4 + which])

    def branch_product():
        loads[3].wait()

        def store(columns, values):
            branch_pre[:, columns] = values

        product(normed, w_branch, store)
        save(7, branch_pre, outs[7])

    def local_scan():
        def one(column):
            columns = at(column, 512)

            def tile(t, carry):
                results = []
                for row in range(3):
                    rows = pl.ds(pl.multiple_of(row * 128 + t * 8, 8), 8)
                    reset = marks[row, pl.ds(pl.multiple_of(t * 8, 8), 8), 0:1]
                    rate_gate = jax.nn.sigmoid(rate_pre[rows, columns] + rate_b[:, columns])
                    input_gate = jax.nn.sigmoid(input_pre[rows, columns] + input_b[:, columns])
                    log_rate = decay_scale[:, columns] * rate_gate
                    keep = 1.0 - reset
                    pace = jnp.exp(log_rate)
                    left = minus_expm1(2.0 * log_rate, pace * pace)
                    scale = reset + keep * jnp.sqrt(left)
                    a, b = tile_scan(
                        pace * keep, scale * input_gate * conv_out[rows, columns], False
                    )
                    b = b + a * carry[2 * row + 1]
                    a = a * carry[2 * row]
                    products[rows, columns] = a
                    states[rows, columns] = b
                    results += [a[7:8], b[7:8]]
                return tuple(results)

            ones, zeros = jnp.ones((1, 512), jnp.float32), jnp.zeros((1, 512), jnp.float32)
            last = lax.fori_loop(0, 16, tile, (ones, zeros) * 3)
            for row in range(3):
                ends[row : row + 1, columns] = last[2 * row]
                ends[3 + row : 4 + row, columns] = last[2 * row + 1]

        loop(3, one)
        return [near(k, ends, got.at[k], others[k - 1]) for k in range(1, 8)]

    def carry_states(copies):
        for copy in copies:
            copy.wait_recv()

        def one(column):
            columns = at(column, 512)
            state = jnp.zeros((3, 512), jnp.float32)
            for k in range(7, 0, -1):
                after = got[k, 3:6, columns] + got[k, 0:3, columns] * state
                state = jnp.where(k <= s, after, state)
            carry_in[0:3, columns] = state

        loop(3, one)
        save(10, carry_in, outs[10])

    def mix():
        def one(i):
            row, rest = lax.div(i, 12), lax.rem(i, 12)
            block, column = lax.div(rest, 3), lax.rem(rest, 3)
            columns = at(column, 512)
            rows = pl.ds(pl.multiple_of(row * 128 + block * 32, 32), 32)
            carried = carry_in[pl.ds(row, 1), columns]
            state = states[rows, columns] + products[rows, columns] * carried
            states[rows, columns] = state
            mixed_in[rows, columns] = (state * gelu_of(branch_pre[rows, columns])).astype(
                jnp.bfloat16
            )

        loop(36, one)
        save(6, states, outs[6])
        save(8, mixed_in, outs[8])

    def out_product():
        loads[4].wait()

        def store(columns, values):
            resid[:, columns] = tokens[:, columns].astype(jnp.float32) + values

        product(mixed_in, w_out, store)
        save(9, resid, outs[9])

        def one(i):
            rows = at(i, 32)
            values = resid[rows, :]
            scale = lax.rsqrt(jnp.mean(values * values, axis=-1, keepdims=True) + epsilon)
            normed2[rows, :] = (values * scale * gain2[...]).astype(jnp.bfloat16)

        loop(12, one)
        save(11, normed2, pair_normed2.at[pl.ds(0, tok)])
        return near(8, normed2, pair_normed2.at[pl.ds(tok, tok)], twin)

    tok = tokens.shape[0]
    cotangent_copy = near(9, cotangent, pair_cotangent.at[pl.ds(tok, tok)], twin)
    save(12, cotangent, pair_cotangent.at[pl.ds(0, tok)])
    carry_in[...] = jnp.zeros_like(carry_in)
    ends[...] = jnp.zeros_like(ends)
    begin(0)
    begin(1)
    first_norm()
    tick(0)
    tick(1)
    tick(2)
    arrive(0)
    rim_copy = rec_product()
    tick(3)
    arrive(1)
    convolution(rim_copy)
    gate_product(0)
    tick(4)
    arrive(2)
    gate_product(1)
    tick(5)
    ends_copies = local_scan()
    arrive(3)
    branch_product()
    tick(6)
    carry_states(ends_copies)
    mix()
    arrive(4)
    tick(7)
    normed2_copy = out_product()
    tick(8)
    tick(9)
    for m in (5, 6, 7):
        arrive(m)
    cotangent_copy.wait_recv()
    normed2_copy.wait_recv()
    for copy in live:
        copy.wait_send()
    for copy in pending:
        copy.wait()


def forward_all(shards, cotangent, tokens, marks, vectors):
    low, full = jnp.bfloat16, jnp.float32
    tok, model = tokens.shape
    rec = shards[0].shape[1]
    shape = jax.ShapeDtypeStruct
    saved = (
        shape((tok, model), low),
        shape((3, 136, rec), full),
        shape((tok, rec), full),
        shape((tok, rec), low),
        shape((tok, rec), full),
        shape((tok, rec), full),
        shape((tok, rec), full),
        shape((tok, rec), full),
        shape((tok, rec), low),
        shape((tok, model), full),
        shape((8, rec), full),
        shape((2 * tok, model), low),
        shape((2 * tok, model), low),
    )
    fulls = [shape((a.shape[0] * 8, a.shape[1]), low) for a in shards]
    for m in (5, 6):
        fulls[m] = shape((fulls[m].shape[0], fulls[m].shape[1] // 2), low)
    fulls[7] = shape((fulls[7].shape[0] // 2, fulls[7].shape[1]), low)
    fulls = tuple(fulls)
    results = pl.pallas_call(
        forward_kernel,
        out_shape=fulls + saved,
        in_specs=[ANY] * 9 + [VMEM] * 9,
        out_specs=(ANY,) * 21,
        scratch_shapes=[pltpu.VMEM(a.shape, low) for a in fulls[:5]]
        + [
            pltpu.VMEM((tok, model), low),
            pltpu.VMEM((3, 136, rec), full),
            pltpu.VMEM((tok, rec), full),
            pltpu.VMEM((tok, rec), low),
            pltpu.VMEM((tok, rec), full),
            pltpu.VMEM((tok, rec), full),
            pltpu.VMEM((tok, rec), full),
            pltpu.VMEM((tok, rec), full),
            pltpu.VMEM((tok, rec), full),
            pltpu.VMEM((tok, rec), low),
            pltpu.VMEM((tok, model), full),
            pltpu.VMEM((tok, model), low),
            pltpu.VMEM((3, 8, rec), full),
            pltpu.VMEM((8, rec), full),
            pltpu.VMEM((8, 8, rec), full),
            pltpu.VMEM((8, rec), full),
            pltpu.SemaphoreType.DMA((8, 20)),
            pltpu.SemaphoreType.DMA((8, 20)),
            pltpu.SemaphoreType.DMA((8, 2)),
            pltpu.SemaphoreType.DMA((10,)),
            pltpu.SemaphoreType.DMA((10,)),
            pltpu.SemaphoreType.DMA((5,)),
            pltpu.SemaphoreType.DMA((13,)),
        ],
        compiler_params=pltpu.CompilerParams(
            collective_id=0, has_side_effects=True, vmem_limit_bytes=60 * 1024 * 1024
        ),
        name="recurrent_forward",
    )(*shards, cotangent, tokens, marks, *vectors)
    return results[:8], results[8:]

class Reduction:
    def __init__(self, kinds, grads, outs, scratch, sems):
        self.kinds = kinds
        self.grads, self.outs = grads, outs
        self.count = len(grads)
        self.held, self.own, self.first, self.second, self.third, self.final = scratch
        self.send, self.recv, self.local = sems
        self.live = []
        self.at_c, self.at_one, self.at_two, self.at_z, self.at_end, self.at_out = (
            {} for _ in range(6)
        )
        r, s, z, c = place()
        self.r, self.z, self.c = r, z, c
        self.mate, self.along_x, self.along_y, self.along_z = peers_of(r, s, z, c)
        self.diagonal = (3 - r, s)
        self.rx, self.ry = lax.rem(r, 2), lax.div(r, 2)

    def peers(self):
        return [self.mate, self.along_x, self.along_y, self.diagonal] + self.along_z

    def remote(self, m, slot, src, dst, device):
        copy = pltpu.make_async_remote_copy(
            src_ref=src,
            dst_ref=dst,
            send_sem=self.send.at[m, slot],
            recv_sem=self.recv.at[m, slot],
            device_id=device,
            device_id_type=MESH,
        )
        copy.start()
        self.live.append(copy)
        return copy

    def load(self, m, q):
        part = self.held[m].shape[3]
        near = pltpu.make_async_copy(
            self.grads[m].at[:, self.c, :, pl.ds(q * part, part)],
            self.own[m].at[q % 2],
            self.local.at[m, q],
        )
        near.start()
        return near

    def begin(self, m):
        part = self.held[m].shape[3]
        far = [
            self.remote(
                m,
                q,
                self.grads[m].at[:, 1 - self.c, :, pl.ds(q * part, part)],
                self.held[m].at[q],
                self.mate,
            )
            for q in range(4)
        ]
        self.at_c[m] = (far, [self.load(m, 0), self.load(m, 1)])

    def stage_core(self, m):
        held, own = self.held[m], self.own[m]
        half = held.shape[2] // 2
        far, near = self.at_c[m]
        for q in range(4):
            far[q].wait_recv()
            near[q].wait()

            def add(b):
                held[q, b] = held[q, b] + own[q % 2, b]

            loop(held.shape[1], add)
            if q < 2:
                near.append(self.load(m, q + 2))
        self.at_one[m] = []
        for other in range(2):
            quarter = other * 2 + (1 - self.rx)
            self.at_one[m].append(
                self.remote(
                    m,
                    4 + other,
                    held.at[quarter, :, pl.ds(0, half)],
                    self.first[m].at[0, other],
                    self.along_x,
                )
            )
            quarter = (1 - self.ry) * 2 + other
            self.at_one[m].append(
                self.remote(
                    m,
                    6 + other,
                    held.at[quarter, :, pl.ds(half, half)],
                    self.first[m].at[1, other],
                    self.along_y,
                )
            )

    def stage_one(self, m):
        held, first = self.held[m], self.first[m]
        count, half = held.shape[1], held.shape[2] // 2
        for copy in self.at_one[m]:
            copy.wait_recv()

        def add(i):
            other, b = lax.div(i, count), lax.rem(i, count)
            qx = other * 2 + self.rx
            held[qx, b, :half] = held[qx, b, :half] + first[0, other, b]
            qy = self.ry * 2 + other
            held[qy, b, half:] = held[qy, b, half:] + first[1, other, b]

        loop(2 * count, add)
        self.at_two[m] = [
            self.remote(
                m,
                8,
                held.at[(1 - self.ry) * 2 + self.rx, :, pl.ds(0, half)],
                self.second[m].at[0],
                self.along_y,
            ),
            self.remote(
                m,
                9,
                held.at[self.ry * 2 + (1 - self.rx), :, pl.ds(half, half)],
                self.second[m].at[1],
                self.along_x,
            ),
        ]

    def stage_two(self, m):
        held, second, r = self.held[m], self.second[m], self.r
        half = held.shape[2] // 2
        for copy in self.at_two[m]:
            copy.wait_recv()

        def add(b):
            held[r, b, :half] = held[r, b, :half] + second[0, b]
            held[r, b, half:] = held[r, b, half:] + second[1, b]

        loop(held.shape[1], add)
        rows = self.kinds[m] == "rows"
        self.at_z[m] = []
        for k in (2,) if rows else (1, 2, 3):
            target = 1 - lax.div(self.z, 2) if rows else lax.rem(self.z + k, 4)
            self.at_z[m].append(
                self.remote(
                    m,
                    9 + k,
                    held.at[r, target],
                    self.third[m].at[0 if rows else k - 1],
                    self.along_z[k - 1],
                )
            )

    def stage_z(self, m):
        held, third, final, r = self.held[m], self.third[m], self.final[m], self.r
        for copy in self.at_z[m]:
            copy.wait_recv()
        kind, parity = self.kinds[m], lax.rem(self.z, 2)
        own = lax.div(self.z, 2) if kind == "rows" else self.z

        def add(i):
            rows = at(i, 32)

            def total(first, *terms):
                values = first.astype(jnp.float32)
                for k in terms:
                    values = values + third[k, rows, :].astype(jnp.float32)
                return values.astype(jnp.bfloat16)

            mine = held[r, own, rows, :]
            if kind == "columns":
                final[r, parity, rows, :] = total(mine, 1)
                final[r, 1 - parity, rows, :] = total(third[0, rows, :], 2)
            else:
                final[r, rows, :] = total(mine, *((0,) if kind == "rows" else (0, 1, 2)))

        loop(held.shape[2] // 32, add)
        self.at_end[m] = [
            self.remote(m, 13 + i, final.at[r], final.at[r], device)
            for i, device in enumerate((self.along_x, self.along_y, self.diagonal))
        ]

    def stage_end(self, m):
        for copy in self.at_end[m]:
            copy.wait_recv()
        out = pltpu.make_async_copy(self.final[m], self.outs[m], self.local.at[m, 4])
        out.start()
        self.at_out[m] = out

    def tick(self, now):
        stages = (self.stage_core, self.stage_one, self.stage_two, self.stage_z, self.stage_end)
        for late, stage in enumerate(stages):
            if 0 <= now - late < self.count:
                stage(now - late)
            if late == 0 and now + 2 < self.count:
                self.begin(now + 2)

    def ticks(self):
        return self.count + 4

    def close(self):
        for m in range(self.count):
            self.at_out[m].wait()
        for copy in self.live:
            copy.wait_send()


REDUCTION_SEMS = 16


def reduction_memory(kinds, grads):
    low = jnp.bfloat16
    count = len(grads)
    shapes = [(2 if kind == "rows" else 4,) + quarter_shape(kind, g) for kind, g in zip(kinds, grads)]
    scratch = [pltpu.VMEM((4, zs, k, n), low) for zs, k, n in shapes]
    scratch += [pltpu.VMEM((2, zs, k, n), low) for zs, k, n in shapes]
    scratch += [pltpu.VMEM((2, 2, zs, k // 2, n), low) for zs, k, n in shapes]
    scratch += [pltpu.VMEM((2, zs, k // 2, n), low) for zs, k, n in shapes]
    scratch += [pltpu.VMEM((zs - 1, k, n), low) for zs, k, n in shapes]
    scratch += [pltpu.VMEM(a.shape, low) for a in reduced_shapes(kinds, grads)]
    return scratch + [
        pltpu.SemaphoreType.DMA((count, REDUCTION_SEMS)),
        pltpu.SemaphoreType.DMA((count, REDUCTION_SEMS)),
        pltpu.SemaphoreType.DMA((count, 5)),
    ]


def reduced_shapes(kinds, grads):
    shapes = [(kind, quarter_shape(kind, g)) for kind, g in zip(kinds, grads)]
    return tuple(
        jax.ShapeDtypeStruct((4, 2, k, n) if kind == "columns" else (4, k, n), jnp.bfloat16)
        for kind, (k, n) in shapes
    )


def take_reduction(take, count):
    scratch = [take(count) for _ in range(6)]
    return scratch, take(3)


def taker(refs):
    refs = list(refs)

    def take(n):
        taken, refs[:n] = refs[:n], []
        return taken

    return take


def split_rows(kind, grad):
    zs = 2 if kind == "rows" else 4
    return grad.reshape(zs, 2, grad.shape[0] // (2 * zs), grad.shape[1])


def quarter_shape(kind, grad):
    return grad.shape[0] // (4 if kind == "rows" else 8), grad.shape[1] // 4


def finish_kernel(count, *refs):
    for block, whole in zip(refs[:count], refs[count:]):
        part = block.shape[-1]
        for q in range(4):
            if len(block.shape) == 4:
                for half in range(2):
                    column = ((half + 2 * (q // 2)) * 2 + q % 2) * part
                    whole[:, column : column + part] = block[q, half].astype(jnp.float32)
            else:
                whole[:, q * part : (q + 1) * part] = block[q].astype(jnp.float32)


def finish(blocks):
    shapes = [(b.shape[-2], b.size // b.shape[-2]) for b in blocks]
    return pl.pallas_call(
        functools.partial(finish_kernel, len(blocks)),
        out_shape=tuple(jax.ShapeDtypeStruct(a, jnp.float32) for a in shapes),
        in_specs=[VMEM] * len(blocks),
        out_specs=(VMEM,) * len(blocks),
        compiler_params=pltpu.CompilerParams(vmem_limit_bytes=40 * 1024 * 1024),
        name="widen_gradients",
    )(*blocks)


def reduce_kernel(count, *refs):
    take = taker(refs)
    grads = take(count)
    (small_in,) = take(1)
    outs = take(count)
    (small_out,) = take(1)
    reduction = Reduction(("all",) * count, grads, outs, *take_reduction(take, count))
    small_held, small_got, small_send, small_recv = take(4)
    z = reduction.z
    greet(reduction.peers())
    small_copies = []

    def swap_small(slot, source, device):
        copy = pltpu.make_async_remote_copy(
            src_ref=small_held.at[source],
            dst_ref=small_got.at[slot],
            send_sem=small_send.at[slot],
            recv_sem=small_recv.at[slot],
            device_id=device,
            device_id_type=MESH,
        )
        copy.start()
        small_copies.append(copy)
        return copy

    small_held[0] = small_in[...]
    swap = swap_small(0, 0, reduction.mate)
    reduction.begin(0)
    if count > 1:
        reduction.begin(1)
    for now in range(reduction.ticks()):
        reduction.tick(now)
        if now < 2:
            swap.wait_recv()
            small_held[now + 1] = small_held[now] + small_got[now]
            swap = swap_small(now + 1, now + 1, (reduction.along_x, reduction.along_y)[now])
        if now == 2:
            swap.wait_recv()
            small_held[3] = small_held[2] + small_got[2]
            spread = [swap_small(2 + k, 3, reduction.along_z[k - 1]) for k in (1, 2, 3)]
    for copy in spread:
        copy.wait_recv()
    small_got[6] = small_held[3]
    total = None
    for source in range(4):
        k = lax.rem(z + 4 - source, 4)
        slot = jnp.where(k == 0, 6, 2 + k)
        term = small_got[slot]
        total = term if total is None else total + term
    small_out[...] = total
    for copy in small_copies:
        copy.wait_send()
    reduction.close()


def reduce_all(grads, small, tag):
    count = len(grads)
    kinds = ("all",) * count
    results = pl.pallas_call(
        functools.partial(reduce_kernel, count),
        out_shape=reduced_shapes(kinds, grads)
        + (jax.ShapeDtypeStruct(small.shape, small.dtype),),
        in_specs=[ANY] * count + [VMEM],
        out_specs=(ANY,) * count + (VMEM,),
        scratch_shapes=reduction_memory(kinds, grads)
        + [
            pltpu.VMEM((4,) + small.shape, small.dtype),
            pltpu.VMEM((7,) + small.shape, small.dtype),
            pltpu.SemaphoreType.DMA((6,)),
            pltpu.SemaphoreType.DMA((6,)),
        ],
        compiler_params=pltpu.CompilerParams(
            collective_id=tag, has_side_effects=True, vmem_limit_bytes=60 * 1024 * 1024
        ),
        name="reduce_grads",
    )(*[split_rows("all", g) for g in grads], small)
    return results[:count], results[count]


def backward_kernel(kinds, *refs):
    take = taker(refs)
    count = len(kinds)
    grads = take(count)
    part_mixed, part_normed2 = take(2)
    full_out, full_rate, full_input, full_branch, full_rec = take(5)
    saved_states, saved_branch, saved_rate, saved_input, saved_conv, saved_rec = take(6)
    marks, tokens, cotangent, resid, normed, conv_low, mixed_in, carried = take(8)
    conv_w, rate_b, input_b, decay_scale, gain1, gain2 = take(6)
    outs = take(count)
    d_out, d_rate, d_input, d_branch, d_rec, token_grad, mixed = take(7)
    small, small_norm, small_norm2 = take(3)
    reduction = Reduction(kinds, grads, outs, *take_reduction(take, count))
    ring, past, branch_pre, rate_pre, input_pre, conv_out = take(6)
    flow, grads_conv, branch_low, rate_low, input_low, stage = take(6)
    rim, ends, got, carry = take(4)
    own_parts, twin_parts, grad_resid, resid_low = take(4)
    near_send, near_recv, load_sem, ring_sem, stage_sem = take(5)
    r, s, z, c = place()
    others = [(r, lax.rem(s + k, 8)) for k in range(1, 8)]
    parity = lax.rem(z, 2)
    twin = (r, s + 2 - 4 * parity)
    greet(others + [reduction.along_x, reduction.along_y, reduction.diagonal])
    live = []

    def near(slot, src, dst, device):
        copy = pltpu.make_async_remote_copy(
            src_ref=src,
            dst_ref=dst,
            send_sem=near_send.at[slot],
            recv_sem=near_recv.at[slot],
            device_id=device,
            device_id_type=MESH,
        )
        copy.start()
        live.append(copy)
        return copy

    def bring(slot, src, dst):
        copy = pltpu.make_async_copy(src, dst, load_sem.at[slot])
        copy.start()
        return copy

    tiles = []
    for weight in (full_out, full_rate, full_input, full_branch, full_rec):
        tiles.append([(weight, j) for j in range(weight.shape[0] // 512)])
    out_tiles, rate_tiles, input_tiles, branch_tiles, rec_tiles = tiles
    order = list(out_tiles)
    for pair in zip(rate_tiles, input_tiles):
        order += pair
    for pair in zip(branch_tiles, rec_tiles):
        order += pair
    fetches = {}

    def fetch(i):
        if i < len(order):
            weight, j = order[i]
            copy = pltpu.make_async_copy(
                weight.at[pl.ds(j * 512, 512)],
                ring.at[i % 3, :, pl.ds(0, weight.shape[1])],
                ring_sem.at[i % 3],
            )
            copy.start()
            fetches[i] = copy

    def back_tile(i, left, depth):
        fetches[i].wait()
        return lax.dot_general(
            left[...],
            ring[i % 3, :, pl.ds(0, depth)],
            (((1,), (1,)), ((), ())),
            preferred_element_type=jnp.float32,
        )

    staged = [None, None]
    turn = [0]

    def outer_product(left, right, target):
        for strip in range(left.shape[1] // 512):
            slot = turn[0] % 2
            turn[0] += 1
            if staged[slot] is not None:
                staged[slot].wait()
            rows = pl.ds(strip * 512, 512)
            width = right.shape[1]

            def one(j):
                columns = at(j, 512)
                stage[slot, :, columns] = lax.dot_general(
                    left[:, rows],
                    right[:, columns],
                    (((0,), (0,)), ((), ())),
                    preferred_element_type=jnp.float32,
                ).astype(jnp.bfloat16)

            loop(width // 512, one)
            copy = pltpu.make_async_copy(
                stage.at[slot, :, pl.ds(0, width)], target.at[rows], stage_sem.at[slot]
            )
            copy.start()
            staged[slot] = copy

    def block_of(i):
        row, block = lax.div(i, 4), lax.rem(i, 4)
        return row, block, pl.ds(pl.multiple_of(row * 128 + block * 32, 32), 32)

    def folded(values):
        return values[0:8] + values[8:16] + values[16:24] + values[24:32]

    def gates(rows, columns, mark_rows):
        rate_gate = jax.nn.sigmoid(rate_pre[rows, columns] + rate_b[:, columns])
        log_rate = decay_scale[:, columns] * rate_gate
        return rate_gate, log_rate, jnp.exp(log_rate)

    def branch_back():
        def one(i):
            column, rest = lax.div(i, 12), lax.rem(i, 12)
            row, block, rows = block_of(rest)
            columns = at(column, 512)
            act, slope = gelu_parts(branch_pre[rows, columns])
            grad = flow[rows, columns]
            state = past[row, pl.ds(pl.multiple_of(block * 32 + 8, 8), 32), columns]
            flow[rows, columns] = grad * act
            branch_low[rows, columns] = (grad * state * slope).astype(jnp.bfloat16)

        loop(36, one)

    def scan_back():
        def one(column):
            columns = at(column, 512)
            spot = lax.broadcasted_iota(jnp.int32, (8, 512), 0)

            def tile(i, state):
                t = 15 - i
                results = []
                for row in range(3):
                    rows = pl.ds(pl.multiple_of(row * 128 + t * 8, 8), 8)
                    keep = 1.0 - marks[row, pl.ds(pl.multiple_of(t * 8, 8), 8), 0:1]
                    _, _, pace = gates(rows, columns, None)
                    decay = pace * keep
                    follow, carry_a, carry_b = state[3 * row : 3 * row + 3]
                    later = jnp.where(spot == 7, follow, pltpu.roll(decay, 7, 0))
                    a, b = tile_scan(later, flow[rows, columns], True)
                    b = b + a * carry_b
                    a = a * carry_a
                    branch_pre[rows, columns] = a
                    flow[rows, columns] = b
                    results += [decay[0:1], a[0:1], b[0:1]]
                return tuple(results)

            ones, zeros = jnp.ones((1, 512), jnp.float32), jnp.zeros((1, 512), jnp.float32)
            last = lax.fori_loop(0, 16, tile, (ones, ones, zeros) * 3)
            for row in range(3):
                decay, a, b = last[3 * row : 3 * row + 3]
                ends[row : row + 1, columns] = decay * a
                ends[3 + row : 4 + row, columns] = decay * b

        loop(3, one)
        return [near(k, ends, got.at[k], others[k - 1]) for k in range(1, 8)]

    def carry_back(copies):
        for copy in copies:
            copy.wait_recv()

        def one(column):
            columns = at(column, 512)
            state = jnp.zeros((3, 512), jnp.float32)
            for ahead in range(7, 0, -1):
                k = 8 - ahead
                after = got[k, 3:6, columns] + got[k, 0:3, columns] * state
                state = jnp.where(s + ahead <= 7, after, state)
            carry[0:3, columns] = state

        loop(3, one)

    def gates_back():
        def one(column):
            columns = at(column, 512)

            def block_step(i, sums):
                row, block, rows = block_of(i)
                mark = pl.ds(pl.multiple_of(block * 32, 32), 32)
                reset = marks[row, mark, 0:1]
                keep = 1.0 - reset
                rate_gate, log_rate, pace = gates(rows, columns, mark)
                input_gate = jax.nn.sigmoid(input_pre[rows, columns] + input_b[:, columns])
                power = pace * pace
                root = jnp.sqrt(minus_expm1(2.0 * log_rate, power))
                scale = reset + keep * root
                conv = conv_out[rows, columns]
                grad = flow[rows, columns] + branch_pre[rows, columns] * carry[
                    pl.ds(row, 1), columns
                ]
                window = past[row, pl.ds(pl.multiple_of(block * 32, 8), 40), columns]
                before = pltpu.roll(window, 1, 0)[8:]
                grad_log = keep * grad * (before * pace - input_gate * conv * power / root)
                decay_sum = rate_gate * grad_log
                rate_grad = decay_scale[:, columns] * decay_sum * (1.0 - rate_gate)
                direct = grad * scale * input_gate
                input_grad = direct * conv * (1.0 - input_gate)
                rate_low[rows, columns] = rate_grad.astype(jnp.bfloat16)
                input_low[rows, columns] = input_grad.astype(jnp.bfloat16)
                rate_pre[rows, columns] = direct
                return (
                    sums[0] + folded(decay_sum),
                    sums[1] + folded(rate_grad),
                    sums[2] + folded(input_grad),
                )

            zeros = jnp.zeros((8, 512), jnp.float32)
            sums = lax.fori_loop(0, 12, block_step, (zeros,) * 3)
            for spot, values in enumerate(sums):
                small[5 + spot : 6 + spot, columns] = jnp.sum(values, axis=0, keepdims=True)

        loop(3, one)

    def conv_back(copy):
        copy.wait_recv()
        for row in range(3):
            grads_conv[row, 128:136, :] = jnp.where(s < 7, rim[row], 0.0)

        def one(column):
            columns = at(column, 512)

            def block_step(i, sums):
                row, block, rows = block_of(i)
                span = pl.ds(pl.multiple_of(block * 32, 8), 40)
                ahead = grads_conv[row, span, columns]
                behind = past[row, span, columns]
                grad = ahead[:32]
                total = conv_w[0:1, columns] * grad
                new = [sums[0] + folded(grad * behind[8:])]
                for k in (1, 2, 3):
                    kept = ahead * marks[row, span, k : k + 1]
                    total = total + conv_w[k : k + 1, columns] * pltpu.roll(kept, 40 - k, 0)[:32]
                    new.append(
                        sums[k] + folded(kept[:32] * pltpu.roll(behind, k, 0)[8:])
                    )
                new.append(sums[4] + folded(grad))
                rate_low[rows, columns] = total.astype(jnp.bfloat16)
                return tuple(new)

            zeros = jnp.zeros((8, 512), jnp.float32)
            sums = lax.fori_loop(0, 12, block_step, (zeros,) * 5)
            for spot, values in enumerate(sums):
                small[spot : spot + 1, columns] = jnp.sum(values, axis=0, keepdims=True)

        loop(3, one)

    def second_norm_back():
        def one(i, total):
            rows = at(i, 16)
            grad = own_parts[1, rows, :].astype(jnp.float32) + twin_parts[1, rows, :].astype(
                jnp.float32
            )
            values = resid[rows, :]
            scale = lax.rsqrt(jnp.mean(values * values, axis=-1, keepdims=True) + epsilon)
            back = grad * gain2[...]
            mean = jnp.mean(values * back, axis=-1, keepdims=True)
            result = cotangent[rows, :].astype(jnp.float32) + scale * back
            result = result - values * (scale * scale * scale * mean)
            grad_resid[rows, :] = result
            resid_low[rows, :] = result.astype(jnp.bfloat16)
            part = grad * values * scale
            return total + part[0:8] + part[8:16]

        total = lax.fori_loop(0, 24, one, jnp.zeros((8, 1024), jnp.float32))
        small_norm2[...] = jnp.sum(total, axis=0, keepdims=True)

    def mix_back():
        def one(i):
            rows = at(i, 16)
            total = own_parts[0, rows, :].astype(jnp.float32)
            total = total + twin_parts[0, rows, :].astype(jnp.float32)
            own_parts[0, rows, :] = (resid[rows, :] + total).astype(jnp.bfloat16)

        loop(24, one)
        return bring(8, own_parts.at[0], mixed)

    def norm_back():
        def one(i, total):
            rows = at(i, 16)
            values = tokens[rows, :].astype(jnp.float32)
            scale = lax.rsqrt(jnp.mean(values * values, axis=-1, keepdims=True) + epsilon)
            grad = input_pre[rows, pl.ds(0, 1024)]
            back = grad * gain1[...]
            mean = jnp.mean(values * back, axis=-1, keepdims=True)
            result = grad_resid[rows, :] + scale * back - values * (scale * scale * scale * mean)
            stage[0, rows, pl.ds(0, 1024)] = result.astype(jnp.bfloat16)
            part = grad * values * scale
            return total + part[0:8] + part[8:16]

        if staged[0] is not None:
            staged[0].wait()
        total = lax.fori_loop(0, 24, one, jnp.zeros((8, 1024), jnp.float32))
        small_norm[...] = jnp.sum(total, axis=0, keepdims=True)
        copy = pltpu.make_async_copy(
            stage.at[0, pl.ds(0, 384), pl.ds(0, 1024)], token_grad, stage_sem.at[0]
        )
        copy.start()
        staged[0] = copy

    tok = tokens.shape[0]
    normed2_copy = near(8, part_normed2.at[pl.ds(tok, tok)], twin_parts.at[1], twin)
    reduction.begin(0)
    reduction.begin(1)
    mixed_copy = near(9, part_mixed.at[pl.ds(tok, tok)], twin_parts.at[0], twin)
    part_loads = [
        bring(6, part_normed2.at[pl.ds(0, tok)], own_parts.at[1]),
        bring(7, part_mixed.at[pl.ds(0, tok)], own_parts.at[0]),
    ]
    loads = [
        bring(0, saved_branch, branch_pre),
        bring(1, saved_states, past.at[:, pl.ds(8, 128), :]),
        bring(2, saved_rate, rate_pre),
        bring(3, saved_input, input_pre),
        bring(4, saved_conv, conv_out),
    ]
    for i in range(3):
        fetch(i)
    ends[...] = jnp.zeros_like(ends)
    for row in range(3):
        past[row, 0:8, :] = jnp.broadcast_to(carried[row : row + 1, :], (8, past.shape[2]))
    reduction.tick(0)
    part_loads[0].wait()
    normed2_copy.wait_recv()
    second_norm_back()
    for i in range(3):
        flow[:, pl.ds(i * 512, 512)] = back_tile(i, resid_low, 1024)
        fetch(i + 3)
    loads[0].wait()
    loads[1].wait()
    branch_back()
    loads[2].wait()
    copies = scan_back()
    outer_product(mixed_in, resid_low, d_out)
    reduction.tick(1)
    carry_back(copies)
    loads[3].wait()
    loads[4].wait()
    gates_back()
    loads.append(bring(5, saved_rec, past))
    at_tile = 3
    for j in range(3):
        columns = pl.ds(j * 512, 512)
        total = rate_pre[:, columns]
        total = total + back_tile(at_tile, rate_low, 1536)
        fetch(at_tile + 3)
        total = total + back_tile(at_tile + 1, input_low, 1536)
        fetch(at_tile + 4)
        at_tile += 2
        for row in range(3):
            grads_conv[row, 0:128, columns] = total[row * 128 : (row + 1) * 128]
    rim_copy = near(0, grads_conv.at[:, pl.ds(0, 8), :], rim, others[6])
    reduction.tick(2)
    outer_product(conv_low, rate_low, d_rate)
    loads[5].wait()
    conv_back(rim_copy)
    for j in range(2):
        columns = pl.ds(j * 512, 512)
        total = back_tile(at_tile, branch_low, 1536)
        fetch(at_tile + 3)
        total = total + back_tile(at_tile + 1, rate_low, 1536)
        fetch(at_tile + 4)
        at_tile += 2
        input_pre[:, columns] = total
    reduction.tick(3)
    outer_product(normed, rate_low, d_rec)
    outer_product(conv_low, input_low, d_input)
    reduction.tick(4)
    outer_product(normed, branch_low, d_branch)
    norm_back()
    part_loads[1].wait()
    mixed_copy.wait_recv()
    mixed_save = mix_back()
    for now in range(5, reduction.ticks()):
        reduction.tick(now)
    mixed_save.wait()
    for copy in staged:
        copy.wait()
    for copy in live:
        copy.wait_send()
    reduction.close()


def backward_all(grads, parts, fulls, saved, local, vectors):
    low, full = jnp.bfloat16, jnp.float32
    shape, memory = jax.ShapeDtypeStruct, pltpu.VMEM
    kinds = ("rows", "columns", "columns")
    count = len(grads)
    tok, model = local[1].shape
    rec = fulls[0].shape[0]
    out_shape = reduced_shapes(kinds, grads) + (
        shape((rec, model), low),
        shape((rec, rec), low),
        shape((rec, rec), low),
        shape((model, rec), low),
        shape((model, rec), low),
        shape((tok, model), low),
        shape((tok, model), low),
        shape((8, rec), full),
        shape((1, model), full),
        shape((1, model), full),
    )
    results = pl.pallas_call(
        functools.partial(backward_kernel, kinds),
        out_shape=out_shape,
        in_specs=[ANY] * (count + 13) + [VMEM] * 14,
        out_specs=(ANY,) * (count + 7) + (VMEM,) * 3,
        scratch_shapes=reduction_memory(kinds, grads)
        + [
            memory((3, 512, rec), low),
            memory((3, 136, rec), full),
            memory((tok, rec), full),
            memory((tok, rec), full),
            memory((tok, rec), full),
            memory((tok, rec), full),
            memory((tok, rec), full),
            memory((3, 136, rec), full),
            memory((tok, rec), low),
            memory((tok, rec), low),
            memory((tok, rec), low),
            memory((2, 512, rec), low),
            memory((3, 8, rec), full),
            memory((8, rec), full),
            memory((8, 8, rec), full),
            memory((8, rec), full),
            memory((2, tok, model), low),
            memory((2, tok, model), low),
            memory((tok, model), full),
            memory((tok, model), low),
            pltpu.SemaphoreType.DMA((10,)),
            pltpu.SemaphoreType.DMA((10,)),
            pltpu.SemaphoreType.DMA((9,)),
            pltpu.SemaphoreType.DMA((3,)),
            pltpu.SemaphoreType.DMA((2,)),
        ],
        compiler_params=pltpu.CompilerParams(
            collective_id=1, has_side_effects=True, vmem_limit_bytes=62 * 1024 * 1024
        ),
        name="recurrent_backward",
    )(*[split_rows(k, g) for k, g in zip(kinds, grads)], *parts, *fulls, *saved, *local, *vectors)
    return results[:count], results[count:]


def from_behind(block, axis, distance):
    devices = range(lax.axis_size(axis))
    route = [(i - distance, i) for i in devices if i - distance in devices]
    return lax.ppermute(block, axis, route)


def prefix(part, axis, combine, identity, reverse):
    count = lax.axis_size(axis)
    place = lax.axis_index(axis)
    ahead = count - 1 - place if reverse else place
    gathered = jax.tree.map(lambda a: lax.all_gather(a, axis), part)
    state = jax.tree.map(lambda a, e: jnp.zeros_like(a) + jnp.asarray(e, a.dtype), part, identity)

    def one(turn, state):
        source = count - 1 - turn if reverse else turn
        return combine(
            state, jax.tree.map(lambda a: lax.dynamic_index_in_dim(a, source, 0, False), gathered)
        )

    return lax.fori_loop(0, ahead, one, state)


def rms_norm(values, gain):
    return values * lax.rsqrt(jnp.mean(values * values, axis=-1, keepdims=True) + epsilon) * gain


def combine(earlier, latter):
    return (earlier[0] * latter[0], latter[0] * earlier[1] + latter[1])


def conv_masks(padded_resets):
    keep_mask = 1.0 - padded_resets
    first = keep_mask[..., 3:]
    second = first * keep_mask[..., 2:-1]
    third = second * keep_mask[..., 1:-2]
    return (first, second, third)


def convolve(padded, masks, conv_weight, conv_bias):
    result = conv_bias + conv_weight[0] * padded[..., 3:, :]
    result = result + conv_weight[1] * masks[0][..., None] * padded[..., 2:-1, :]
    result = result + conv_weight[2] * masks[1][..., None] * padded[..., 1:-2, :]
    return result + conv_weight[3] * masks[2][..., None] * padded[..., :-3, :]


def gate_terms(rate_pre, input_pre, conv_out, decay_param, rate_bias, input_bias, resets):
    rate_gate = jax.nn.sigmoid(rate_pre + rate_bias)
    input_gate = jax.nn.sigmoid(input_pre + input_bias)
    log_rate = -8.0 * jax.nn.softplus(decay_param) * rate_gate
    keep_mask = 1.0 - resets[..., None]
    decays = jnp.exp(log_rate) * keep_mask
    scales = resets[..., None] + keep_mask * jnp.sqrt(-jnp.expm1(2.0 * log_rate))
    return (decays, scales * input_gate * conv_out)


def forward_product(values, weight):
    return jnp.dot(values, weight, preferred_element_type=jnp.float32)


def outer(left, right):
    return lax.dot_general(
        left, right, (((0,), (0,)), ((), ())), preferred_element_type=jnp.float32
    )


def back_product(grads, weight):
    return lax.dot_general(
        grads, weight, (((1,), (1,)), ((), ())), preferred_element_type=jnp.float32
    )


def plain_body(
    tokens,
    bounds,
    norm1_gain,
    w_branch,
    w_rec,
    conv_weight,
    conv_bias,
    w_rate,
    rate_bias,
    w_input,
    input_bias,
    decay_param,
    w_out,
    norm2_gain,
    w_gate,
    w_up,
    w_down,
    cotangent,
):
    gathered = (
        lax.all_gather(w_branch, "seq", axis=0, tiled=True),
        lax.all_gather(w_rec, "seq", axis=0, tiled=True),
        lax.all_gather(w_rate, "seq", axis=0, tiled=True),
        lax.all_gather(w_input, "seq", axis=0, tiled=True),
        lax.all_gather(w_out, "seq", axis=0, tiled=True),
        lax.all_gather(w_gate, "seq", axis=0, tiled=True),
        lax.all_gather(w_up, "seq", axis=0, tiled=True),
        lax.all_gather(w_down, "seq", axis=0, tiled=True),
    )
    full_branch, full_rec, full_rate, full_input, full_out, full_gate, full_up, full_down = gathered
    row_count, tok_count, model_width = tokens.shape
    rec_width = full_rec.shape[1]
    offset = lax.axis_index("seq") * tok_count
    positions = offset - 3 + jnp.arange(tok_count + 3, dtype=jnp.int32)
    marked = (
        jnp.any(positions[None, :, None] == bounds[:, None, :], axis=2) | (positions == 0)[None, :]
    )
    padded_resets = marked.astype(jnp.float32)
    resets = padded_resets[:, 3:]
    masks = conv_masks(padded_resets)
    inputs = tokens.astype(jnp.float32).reshape(-1, model_width)
    normed = rms_norm(inputs, norm1_gain).astype(jnp.bfloat16)
    branch_pre = forward_product(normed, full_branch)
    rec_in = forward_product(normed, full_rec).reshape(row_count, tok_count, rec_width)
    rim = from_behind(rec_in[:, tok_count - 3 :, :], "seq", 1)
    padded = jnp.concatenate([rim, rec_in], axis=1)
    conv_out = convolve(padded, masks, conv_weight, conv_bias)
    conv_low = conv_out.astype(jnp.bfloat16).reshape(-1, rec_width)
    rate_pre = forward_product(conv_low, full_rate).reshape(conv_out.shape)
    input_pre = forward_product(conv_low, full_input).reshape(conv_out.shape)

    def gates_of(rate_arg, input_arg, conv_arg, decay_arg, rate_arg_bias, input_arg_bias):
        return gate_terms(
            rate_arg, input_arg, conv_arg, decay_arg, rate_arg_bias, input_arg_bias, resets
        )

    decays, drives = gates_of(rate_pre, input_pre, conv_out, decay_param, rate_bias, input_bias)
    prefix_decay, local_states = lax.associative_scan(combine, (decays, drives), axis=1)
    ones_pair = jnp.ones((row_count, rec_width), jnp.float32)
    zeros_pair = jnp.zeros((row_count, rec_width), jnp.float32)
    carry_in = prefix(
        (prefix_decay[:, -1], local_states[:, -1]), "seq", combine, (ones_pair, zeros_pair), False
    )[1]
    states = local_states + prefix_decay * carry_in[:, None, :]
    earlier_states = jnp.concatenate([carry_in[:, None, :], states[:, :-1, :]], axis=1)
    branch_act = jax.nn.gelu(branch_pre, approximate=True).reshape(states.shape)
    mixed_in = (states * branch_act).astype(jnp.bfloat16).reshape(-1, rec_width)
    resid = inputs + forward_product(mixed_in, full_out)
    normed2 = rms_norm(resid, norm2_gain).astype(jnp.bfloat16)
    gate_pre = forward_product(normed2, full_gate)
    up_pre = forward_product(normed2, full_up)
    hidden = (jax.nn.gelu(gate_pre, approximate=True) * up_pre).astype(jnp.bfloat16)
    mixed = (resid + forward_product(hidden, full_down)).astype(jnp.bfloat16).reshape(tokens.shape)
    cot_low = cotangent.reshape(-1, model_width)
    grad_down = outer(hidden, cot_low)
    grad_hidden = back_product(cot_low, full_down)
    _, pull_mlp = jax.vjp(
        lambda gate_arg, up_arg: jax.nn.gelu(gate_arg, approximate=True) * up_arg, gate_pre, up_pre
    )
    grad_gate_pre, grad_up_pre = pull_mlp(grad_hidden)
    gate_low = grad_gate_pre.astype(jnp.bfloat16)
    up_low = grad_up_pre.astype(jnp.bfloat16)
    grad_gate = outer(normed2, gate_low)
    grad_up = outer(normed2, up_low)
    grad_normed2 = back_product(gate_low, full_gate) + back_product(up_low, full_up)
    _, pull_norm2 = jax.vjp(rms_norm, resid, norm2_gain)
    grad_resid_norm, grad_norm2 = pull_norm2(grad_normed2)
    grad_resid = cot_low.astype(jnp.float32) + grad_resid_norm
    resid_low = grad_resid.astype(jnp.bfloat16)
    grad_out = outer(mixed_in, resid_low)
    grad_mixed = back_product(resid_low, full_out).reshape(states.shape)
    grad_states = grad_mixed * branch_act
    _, pull_branch = jax.vjp(lambda pre_arg: jax.nn.gelu(pre_arg, approximate=True), branch_pre)
    branch_low = pull_branch((grad_mixed * states).reshape(-1, rec_width))[0].astype(jnp.bfloat16)
    next_decays = jnp.concatenate([decays[:, 1:, :], ones_pair[:, None, :]], axis=1)
    suffix_decay, local_grads = lax.associative_scan(
        combine, (next_decays, grad_states), axis=1, reverse=True
    )
    element = (prefix_decay[:, -1], decays[:, 0] * local_grads[:, 0])
    carry_back = prefix(element, "seq", combine, (ones_pair, zeros_pair), True)[1]
    state_grads = local_grads + suffix_decay * carry_back[:, None, :]
    _, pull_gates = jax.vjp(
        gates_of, rate_pre, input_pre, conv_out, decay_param, rate_bias, input_bias
    )
    grad_rate_pre, grad_input_pre, grad_conv_direct, grad_decay, grad_rate_bias, grad_input_bias = (
        pull_gates((state_grads * earlier_states, state_grads))
    )
    rate_low = grad_rate_pre.astype(jnp.bfloat16).reshape(-1, rec_width)
    input_low = grad_input_pre.astype(jnp.bfloat16).reshape(-1, rec_width)
    grad_rate = outer(conv_low, rate_low)
    grad_input = outer(conv_low, input_low)
    grad_conv = grad_conv_direct + (
        back_product(rate_low, full_rate) + back_product(input_low, full_input)
    ).reshape(conv_out.shape)
    _, pull_conv = jax.vjp(
        lambda pad_arg, weight_arg, bias_arg: convolve(pad_arg, masks, weight_arg, bias_arg),
        padded,
        conv_weight,
        conv_bias,
    )
    grad_padded, grad_conv_weight, grad_conv_bias = pull_conv(grad_conv)
    rim_back = from_behind(grad_padded[:, :3, :], "seq", -1)
    grad_rec = grad_padded[:, 3:, :] + jnp.concatenate(
        [jnp.zeros((row_count, tok_count - 3, rec_width), jnp.float32), rim_back], axis=1
    )
    rec_low = grad_rec.astype(jnp.bfloat16).reshape(-1, rec_width)
    grad_rec_w = outer(normed, rec_low)
    grad_branch_w = outer(normed, branch_low)
    grad_normed = back_product(branch_low, full_branch) + back_product(rec_low, full_rec)
    _, pull_norm1 = jax.vjp(rms_norm, inputs, norm1_gain)
    grad_inputs, grad_norm1 = pull_norm1(grad_normed)
    token_grad = (grad_resid + grad_inputs).astype(jnp.bfloat16).reshape(tokens.shape)
    grad_mats = (
        grad_branch_w,
        grad_rec_w,
        grad_rate,
        grad_input,
        grad_out,
        grad_gate,
        grad_up,
        grad_down,
    )
    blocks = (
        lax.psum_scatter(grad_mats[0], "seq", scatter_dimension=0, tiled=True),
        lax.psum_scatter(grad_mats[1], "seq", scatter_dimension=0, tiled=True),
        lax.psum_scatter(grad_mats[2], "seq", scatter_dimension=0, tiled=True),
        lax.psum_scatter(grad_mats[3], "seq", scatter_dimension=0, tiled=True),
        lax.psum_scatter(grad_mats[4], "seq", scatter_dimension=0, tiled=True),
        lax.psum_scatter(grad_mats[5], "seq", scatter_dimension=0, tiled=True),
        lax.psum_scatter(grad_mats[6], "seq", scatter_dimension=0, tiled=True),
        lax.psum_scatter(grad_mats[7], "seq", scatter_dimension=0, tiled=True),
    )
    summed = lax.psum(
        (blocks[0], blocks[1], blocks[2], blocks[3], blocks[4], blocks[5], blocks[6], blocks[7]),
        "rows",
    )
    small = lax.psum(
        (
            grad_norm1,
            grad_conv_weight,
            grad_conv_bias,
            grad_rate_bias,
            grad_input_bias,
            grad_decay,
            grad_norm2,
        ),
        ("rows", "seq"),
    )
    return (
        mixed,
        token_grad,
        small[0],
        summed[0],
        summed[1],
        small[1],
        small[2],
        summed[2],
        small[3],
        summed[3],
        small[4],
        small[5],
        summed[4],
        small[6],
        summed[5],
        summed[6],
        summed[7],
    )


def body(*args):
    if lax.axis_size("rows") == 4 and lax.axis_size("seq") == 8:
        return staged_body(*args)
    return plain_body(*args)


def staged_body(
    tokens,
    bounds,
    norm1_gain,
    w_branch,
    w_rec,
    conv_weight,
    conv_bias,
    w_rate,
    rate_bias,
    w_input,
    input_bias,
    decay_param,
    w_out,
    norm2_gain,
    w_gate,
    w_up,
    w_down,
    cotangent,
):
    row_count, tok_count, model_width = tokens.shape
    rec_width = w_rec.shape[1]
    offset = lax.axis_index("seq") * tok_count
    positions = offset - 3 + jnp.arange(tok_count + 11, dtype=jnp.int32)
    marked = (
        jnp.any(positions[None, :, None] == bounds[:, None, :], axis=2) | (positions == 0)[None, :]
    )
    padded_resets = marked.astype(jnp.float32)
    resets = padded_resets[:, 3:]
    masks = conv_masks(padded_resets)
    marks = jnp.stack((resets,) + masks + (resets,) * 4, axis=2)
    flat_tokens = tokens.reshape(-1, model_width)
    decay_scale = (-8.0 * jax.nn.softplus(decay_param))[None]
    fulls, saved = forward_all(
        (w_rec, w_rate, w_input, w_branch, w_out, w_gate, w_up, w_down),
        cotangent.reshape(-1, model_width),
        flat_tokens,
        marks,
        (
            norm1_gain[None],
            conv_weight,
            conv_bias[None],
            rate_bias[None],
            input_bias[None],
            decay_scale,
            norm2_gain[None],
        ),
    )
    full_rec, full_rate, full_input, full_branch, full_out, half_gate, half_up, half_down = fulls
    normed, padded, conv_out, conv_low, rate_pre, input_pre = saved[:6]
    states, branch_pre, mixed_in, resid, carried, pair_normed2, pair_cotangent = saved[6:]
    gate_pre = forward_product(pair_normed2, half_gate)
    up_pre = forward_product(pair_normed2, half_up)
    hidden = (jax.nn.gelu(gate_pre, approximate=True) * up_pre).astype(jnp.bfloat16)
    part_mixed = forward_product(hidden, half_down).astype(jnp.bfloat16)
    grad_down = outer(hidden, pair_cotangent)
    grad_hidden = back_product(pair_cotangent, half_down)
    _, pull_mlp = jax.vjp(
        lambda gate_arg, up_arg: jax.nn.gelu(gate_arg, approximate=True) * up_arg, gate_pre, up_pre
    )
    grad_gate_pre, grad_up_pre = pull_mlp(grad_hidden)
    gate_low = grad_gate_pre.astype(jnp.bfloat16)
    up_low = grad_up_pre.astype(jnp.bfloat16)
    grad_gate = outer(pair_normed2, gate_low)
    grad_up = outer(pair_normed2, up_low)
    part_normed2 = (back_product(gate_low, half_gate) + back_product(up_low, half_up)).astype(
        jnp.bfloat16
    )
    low = jnp.bfloat16
    ff, rest = backward_all(
        [g.astype(low) for g in (grad_down, grad_gate, grad_up)],
        (part_mixed, part_normed2),
        (full_out, full_rate, full_input, full_branch, full_rec),
        (
            states.reshape(row_count, tok_count, rec_width),
            branch_pre,
            rate_pre,
            input_pre,
            conv_out,
            padded,
        ),
        (
            marks,
            flat_tokens,
            cotangent.reshape(-1, model_width),
            resid,
            normed,
            conv_low,
            mixed_in,
            carried,
        ),
        (conv_weight, rate_bias[None], input_bias[None], decay_scale, norm1_gain[None], norm2_gain[None]),
    )
    rec_grads, (token_grad, mixed, sums, grad_norm1, grad_norm2) = rest[:5], rest[5:]
    small = jnp.concatenate(
        [
            sums.reshape(-1, model_width),
            grad_norm1,
            grad_norm2,
            jnp.zeros((2, model_width), jnp.float32),
        ]
    )
    rec, small = reduce_all(rec_grads, small, 2)
    blocks = finish(tuple(rec) + tuple(ff))
    rec, ff = blocks[:5], blocks[5:]
    sums = small[:12].reshape(8, rec_width)
    return (
        mixed.reshape(tokens.shape),
        token_grad.reshape(tokens.shape),
        small[12],
        rec[3],
        rec[4],
        sums[:4],
        sums[4],
        rec[1],
        sums[6],
        rec[2],
        sums[7],
        -8.0 * jax.nn.sigmoid(decay_param) * sums[5],
        rec[0],
        small[13],
        ff[1],
        ff[2],
        ff[0],
    )


def solution(mesh):
    in_specs = (
        P("rows", "seq", None),
        P("rows", None),
        P(),
        P("seq", None),
        P("seq", None),
        P(),
        P(),
        P("seq", None),
        P(),
        P("seq", None),
        P(),
        P(),
        P("seq", None),
        P(),
        P("seq", None),
        P("seq", None),
        P("seq", None),
        P("rows", "seq", None),
    )
    out_specs = (
        P("rows", "seq", None),
        P("rows", "seq", None),
        P(),
        P("seq", None),
        P("seq", None),
        P(),
        P(),
        P("seq", None),
        P(),
        P("seq", None),
        P(),
        P(),
        P("seq", None),
        P(),
        P("seq", None),
        P("seq", None),
        P("seq", None),
    )
    return jax.shard_map(
        body, mesh=mesh, in_specs=in_specs, out_specs=out_specs, check_vma=False)
```

```python
import functools

import jax
import jax.numpy as jnp
from jax import lax
from jax.experimental import pallas as pl
from jax.experimental.pallas import tpu as pltpu
from jax.sharding import PartitionSpec as P

epsilon = 1e-06
MESH = pl.DeviceIdType.MESH
ANY = pl.BlockSpec(memory_space=pl.ANY)
VMEM = pl.BlockSpec(memory_space=pltpu.VMEM)


def place():
    r = lax.axis_index("rows")
    s = lax.axis_index("seq")
    return r, s, lax.div(s, 2), lax.rem(s, 2)


def greet(peers):
    barrier = pltpu.get_barrier_semaphore()
    for peer in peers:
        pl.semaphore_signal(barrier, inc=1, device_id=peer, device_id_type=MESH)
    pl.semaphore_wait(barrier, len(peers))


def peers_of(r, s, z, c):
    mate = (r, s + 1 - 2 * c)
    along_x = (r + 1 - 2 * lax.rem(r, 2), s)
    along_y = (lax.rem(r + 2, 4), s)
    along_z = [(r, lax.rem(z + k, 4) * 2 + c) for k in (1, 2, 3)]
    return mate, along_x, along_y, along_z


def gelu_parts(v):
    inner = 0.7978845608028654 * (v + 0.044715 * v * v * v)
    t = jnp.tanh(inner)
    slope = 0.7978845608028654 * (1.0 + 0.134145 * v * v)
    return 0.5 * v * (1.0 + t), 0.5 * (1.0 + t) + 0.5 * v * (1.0 - t * t) * slope


def gelu_of(v):
    return 0.5 * v * (1.0 + jnp.tanh(0.7978845608028654 * (v + 0.044715 * v * v * v)))


def minus_expm1(v, power):
    total = 1.0 / 40320.0
    for term in (5040.0, 720.0, 120.0, 24.0, 6.0, 2.0, 1.0):
        total = total * v + 1.0 / term
    return jnp.where(v > -0.5, -v * total, 1.0 - power)


def tile_scan(a, b, reverse):
    spot = lax.broadcasted_iota(jnp.int32, a.shape, 0)
    for distance in (1, 2, 4):
        if reverse:
            inside = spot < 8 - distance
            back_a, back_b = pltpu.roll(a, 8 - distance, 0), pltpu.roll(b, 8 - distance, 0)
        else:
            inside = spot >= distance
            back_a, back_b = pltpu.roll(a, distance, 0), pltpu.roll(b, distance, 0)
        b = b + a * jnp.where(inside, back_b, 0.0)
        a = a * jnp.where(inside, back_a, 1.0)
    return a, b


def loop(count, body):
    def one(i, carry):
        body(i)
        return carry

    lax.fori_loop(0, count, one, 0)


def at(i, size):
    return pl.ds(pl.multiple_of(i * size, size), size)


def split_vectors(ref):
    return ref.at[0:4], ref.at[4:5], ref.at[5:6], ref.at[6:7], ref.at[7:8]


def forward_kernel(*refs):
    refs = list(refs)

    def take(n):
        taken, refs[:n] = refs[:n], []
        return taken

    shards = take(8)
    cotangent, tokens, bounds, gains, vectors = take(5)
    gain1, gain2 = gains.at[0:1], gains.at[1:2]
    conv_w, conv_b, rate_b, input_b, decay_scale = split_vectors(vectors)
    fulls = take(8)
    outs = take(11)
    pair_normed2, pair_cotangent, saved_marks = take(3)
    (w_rec, w_rate, w_input, w_branch, w_out) = weights = take(5)
    normed, padded, conv_out, conv_low, rate_pre, input_pre = take(6)
    products, states, branch_pre, mixed_in, resid, normed2 = take(6)
    rim, ends, got, carry_in, marks = take(5)
    send, recv, local, near_send, near_recv, load_sem, save_sem = refs
    count = 8
    r, s, z, c = place()
    mate, along_x, along_y, along_z = peers_of(r, s, z, c)
    across_x, across_y = along_x[0], along_y[0]
    parity = lax.rem(z, 2)
    twin = (r, s + 2 - 4 * parity)
    others = [(r, lax.rem(s + k, 8)) for k in range(1, 8)]
    greet(others + [along_x, along_y])
    live, pending = [], []

    def start(copy):
        copy.start()
        live.append(copy)
        return copy

    def remote(m, slot, src, dst, device):
        return start(
            pltpu.make_async_remote_copy(
                src_ref=src,
                dst_ref=dst,
                send_sem=send.at[m, slot],
                recv_sem=recv.at[m, slot],
                device_id=device,
                device_id_type=MESH,
            )
        )

    def near(slot, src, dst, device):
        return start(
            pltpu.make_async_remote_copy(
                src_ref=src,
                dst_ref=dst,
                send_sem=near_send.at[slot],
                recv_sem=near_recv.at[slot],
                device_id=device,
                device_id_type=MESH,
            )
        )

    def save(slot, src, dst):
        copy = pltpu.make_async_copy(src, dst, save_sem.at[slot])
        copy.start()
        pending.append(copy)

    def rows_of(m, source, core, begin, length):
        depth = shards[m].shape[0]
        block = lax.div(source, 2) * 2 + core if m == 7 else source * 2 + core
        return pl.ds(pl.multiple_of(block * depth + begin, 16), length)

    def region(m, source, quarter, begin, length):
        part = fulls[m].shape[1] // 4
        column = pl.multiple_of(quarter * part, 128)
        return fulls[m].at[rows_of(m, source, c, begin, length), pl.ds(column, part)]

    def turns(m):
        return (2,) if m == 7 else (1, 2, 3)

    stage_own, stage_z, stage_x, stage_y, stage_d, stage_c = {}, {}, {}, {}, {}, {}

    def begin(m):
        depth, width = shards[m].shape
        part = fulls[m].shape[1] // 4
        rows = rows_of(m, z, c, 0, depth)
        stage_z[m] = []
        for k in turns(m):
            column = r * part
            if m in (5, 6):
                half = lax.rem(parity + k, 2)
                column = (half + 2 * lax.div(r, 2)) * (2 * part) + lax.rem(r, 2) * part
            stage_z[m].append(
                remote(
                    m,
                    k,
                    shards[m].at[:, pl.ds(pl.multiple_of(column, 128), part)],
                    region(m, z, r, 0, depth),
                    along_z[k - 1],
                )
            )
        pieces = [(shards[m], fulls[m].at[rows])]
        if m in (5, 6):
            strip = 2 * part
            pieces = [
                (
                    shards[m].at[:, pl.ds(pl.multiple_of((parity + 2 * i) * strip, 128), strip)],
                    fulls[m].at[rows, pl.ds(i * strip, strip)],
                )
                for i in range(2)
            ]
        stage_own[m] = []
        for i, (src, dst) in enumerate(pieces):
            own = pltpu.make_async_copy(src, dst, local.at[m, i])
            own.start()
            stage_own[m].append((own, remote(m, 19 * i, src, dst, mate)))

    def sources(k):
        return lax.rem(z + 4 - k, 4)

    def tick(now):
        m = now
        if m < count:
            depth = shards[m].shape[0]
            stage_x[m], stage_y[m] = [], []
            for i, k in enumerate(turns(m)):
                stage_z[m][i].wait_recv()
                piece = region(m, sources(k), r, 0, depth)
                stage_x[m].append(remote(m, 3 + k, piece, piece, along_x))
                stage_y[m].append(remote(m, 6 + k, piece, piece, along_y))
        if now + 2 < count:
            begin(now + 2)
        m = now - 1
        if 0 <= m < count:
            depth = shards[m].shape[0]
            half = depth // 2
            stage_d[m] = []
            for i, k in enumerate(turns(m)):
                stage_x[m][i].wait_recv()
                piece = region(m, sources(k), across_x, 0, half)
                stage_d[m].append(remote(m, 9 + k, piece, piece, along_y))
                stage_y[m][i].wait_recv()
                piece = region(m, sources(k), across_y, half, half)
                stage_d[m].append(remote(m, 12 + k, piece, piece, along_x))
        m = now - 2
        if 0 <= m < count:
            depth = shards[m].shape[0]
            stage_c[m] = []
            for i, k in enumerate(turns(m)):
                stage_d[m][2 * i].wait_recv()
                stage_d[m][2 * i + 1].wait_recv()
                piece = fulls[m].at[rows_of(m, sources(k), c, 0, depth)]
                stage_c[m].append(remote(m, 15 + k, piece, piece, mate))

    loads = {}

    def arrive(m):
        for own, swapped in stage_own[m]:
            own.wait()
            swapped.wait_recv()
        for copy in stage_c[m]:
            copy.wait_recv()
        if m < 5:
            loads[m] = pltpu.make_async_copy(fulls[m], weights[m], load_sem.at[m])
            loads[m].start()

    def product(left, right, store):
        width = right.shape[1]

        def one(j):
            columns = at(j, 512)
            store(
                columns,
                jnp.dot(left[...], right[:, columns], preferred_element_type=jnp.float32),
            )

        loop(width // 512, one)

    def first_norm():
        def one(i):
            rows = at(i, 32)
            values = tokens[rows, :].astype(jnp.float32)
            scale = lax.rsqrt(jnp.mean(values * values, axis=-1, keepdims=True) + epsilon)
            normed[rows, :] = (values * scale * gain1[...]).astype(jnp.bfloat16)

        loop(12, one)
        save(0, normed, outs[0])

    def mark():
        place_of = lax.broadcasted_iota(jnp.int32, (144, 8), 0) + (s * 128 - 8)
        column = lax.broadcasted_iota(jnp.int32, (136, 8), 1)
        for row in range(3):
            met = (place_of == bounds[row : row + 1, :]).astype(jnp.float32)
            reset = jnp.max(met, axis=1, keepdims=True) + (place_of == 0).astype(jnp.float32)
            keep = 1.0 - reset
            second = keep * pltpu.roll(keep, 1, 0)
            third = second * pltpu.roll(keep, 2, 0)
            first, second, third = keep[8:], second[8:], third[8:]
            values = jnp.where(column == 1, first, reset[8:])
            values = jnp.where(column == 2, second, values)
            marks[row] = jnp.where(column == 3, third, values)
        save(11, marks, saved_marks)

    def rec_product():
        loads[0].wait()

        def store(columns, values):
            for row in range(3):
                padded[row, 8:136, columns] = values[row * 128 : (row + 1) * 128]

        product(normed, w_rec, store)
        return near(0, padded.at[:, pl.ds(128, 8), :], rim, others[0])

    def convolution(copy):
        copy.wait_recv()
        for row in range(3):
            padded[row, 0:8, :] = jnp.where(s > 0, rim[row], 0.0)
        save(1, padded, outs[1])

        def one(i):
            row, rest = lax.div(i, 12), lax.rem(i, 12)
            block, column = lax.div(rest, 3), lax.rem(rest, 3)
            columns = at(column, 512)
            window = padded[row, pl.ds(pl.multiple_of(block * 32, 8), 40), columns]
            rows = pl.ds(pl.multiple_of(row * 128 + block * 32, 32), 32)
            spot = pl.ds(pl.multiple_of(block * 32, 32), 32)
            total = conv_b[:, columns] + conv_w[0:1, columns] * window[8:]
            for k in (1, 2, 3):
                shifted = pltpu.roll(window, k, 0)[8:]
                total = total + conv_w[k : k + 1, columns] * (marks[row, spot, k : k + 1] * shifted)
            conv_out[rows, columns] = total
            conv_low[rows, columns] = total.astype(jnp.bfloat16)

        loop(36, one)
        save(2, conv_out, outs[2])
        save(3, conv_low, outs[3])

    def gate_product(which):
        target, weight = ((rate_pre, w_rate), (input_pre, w_input))[which]
        loads[1 + which].wait()

        def store(columns, values):
            target[:, columns] = values

        product(conv_low, weight, store)
        save(4 + which, target, outs[4 + which])

    def branch_product():
        loads[3].wait()

        def store(columns, values):
            branch_pre[:, columns] = values

        product(normed, w_branch, store)
        save(7, branch_pre, outs[7])

    def local_scan():
        def one(column):
            columns = at(column, 512)

            def tile(t, carry):
                results = []
                for row in range(3):
                    rows = pl.ds(pl.multiple_of(row * 128 + t * 8, 8), 8)
                    reset = marks[row, pl.ds(pl.multiple_of(t * 8, 8), 8), 0:1]
                    rate_gate = jax.nn.sigmoid(rate_pre[rows, columns] + rate_b[:, columns])
                    input_gate = jax.nn.sigmoid(input_pre[rows, columns] + input_b[:, columns])
                    log_rate = decay_scale[:, columns] * rate_gate
                    keep = 1.0 - reset
                    pace = jnp.exp(log_rate)
                    left = minus_expm1(2.0 * log_rate, pace * pace)
                    scale = reset + keep * jnp.sqrt(left)
                    a, b = tile_scan(
                        pace * keep, scale * input_gate * conv_out[rows, columns], False
                    )
                    b = b + a * carry[2 * row + 1]
                    a = a * carry[2 * row]
                    products[rows, columns] = a
                    states[rows, columns] = b
                    results += [a[7:8], b[7:8]]
                return tuple(results)

            ones, zeros = jnp.ones((1, 512), jnp.float32), jnp.zeros((1, 512), jnp.float32)
            last = lax.fori_loop(0, 16, tile, (ones, zeros) * 3)
            for row in range(3):
                ends[row : row + 1, columns] = last[2 * row]
                ends[3 + row : 4 + row, columns] = last[2 * row + 1]

        loop(3, one)
        return [near(k, ends, got.at[k], others[k - 1]) for k in range(1, 8)]

    def carry_states(copies):
        for copy in copies:
            copy.wait_recv()

        def one(column):
            columns = at(column, 512)
            state = jnp.zeros((3, 512), jnp.float32)
            for k in range(7, 0, -1):
                after = got[k, 3:6, columns] + got[k, 0:3, columns] * state
                state = jnp.where(k <= s, after, state)
            carry_in[0:3, columns] = state

        loop(3, one)
        save(10, carry_in, outs[10])

    def mix():
        def one(i):
            row, rest = lax.div(i, 12), lax.rem(i, 12)
            block, column = lax.div(rest, 3), lax.rem(rest, 3)
            columns = at(column, 512)
            rows = pl.ds(pl.multiple_of(row * 128 + block * 32, 32), 32)
            carried = carry_in[pl.ds(row, 1), columns]
            state = states[rows, columns] + products[rows, columns] * carried
            states[rows, columns] = state
            mixed_in[rows, columns] = (state * gelu_of(branch_pre[rows, columns])).astype(
                jnp.bfloat16
            )

        loop(36, one)
        save(6, states, outs[6])
        save(8, mixed_in, outs[8])

    def out_product():
        loads[4].wait()

        def store(columns, values):
            resid[:, columns] = tokens[:, columns].astype(jnp.float32) + values

        product(mixed_in, w_out, store)
        save(9, resid, outs[9])

        def one(i):
            rows = at(i, 32)
            values = resid[rows, :]
            scale = lax.rsqrt(jnp.mean(values * values, axis=-1, keepdims=True) + epsilon)
            normed2[rows, :] = (values * scale * gain2[...]).astype(jnp.bfloat16)

        loop(12, one)
        save(13, normed2, pair_normed2.at[pl.ds(0, tok)])
        return near(8, normed2, pair_normed2.at[pl.ds(tok, tok)], twin)

    tok = tokens.shape[0]
    cotangent_copy = near(9, cotangent, pair_cotangent.at[pl.ds(tok, tok)], twin)
    save(12, cotangent, pair_cotangent.at[pl.ds(0, tok)])
    carry_in[...] = jnp.zeros_like(carry_in)
    ends[...] = jnp.zeros_like(ends)
    begin(0)
    begin(1)
    mark()
    first_norm()
    tick(0)
    tick(1)
    tick(2)
    arrive(0)
    rim_copy = rec_product()
    tick(3)
    arrive(1)
    convolution(rim_copy)
    gate_product(0)
    tick(4)
    arrive(2)
    gate_product(1)
    tick(5)
    ends_copies = local_scan()
    arrive(3)
    branch_product()
    tick(6)
    carry_states(ends_copies)
    mix()
    arrive(4)
    tick(7)
    normed2_copy = out_product()
    tick(8)
    tick(9)
    for m in (5, 6, 7):
        arrive(m)
    cotangent_copy.wait_recv()
    normed2_copy.wait_recv()
    for copy in live:
        copy.wait_send()
    for copy in pending:
        copy.wait()


def forward_all(shards, cotangent, tokens, bounds, gains, vectors):
    low, full = jnp.bfloat16, jnp.float32
    tok, model = tokens.shape
    rec = shards[0].shape[1]
    shape = jax.ShapeDtypeStruct
    saved = (
        shape((tok, model), low),
        shape((3, 136, rec), full),
        shape((tok, rec), full),
        shape((tok, rec), low),
        shape((tok, rec), full),
        shape((tok, rec), full),
        shape((tok, rec), full),
        shape((tok, rec), full),
        shape((tok, rec), low),
        shape((tok, model), full),
        shape((8, rec), full),
        shape((2 * tok, model), low),
        shape((2 * tok, model), low),
        shape((3, 136, 8), full),
    )
    fulls = [shape((a.shape[0] * 8, a.shape[1]), low) for a in shards]
    for m in (5, 6):
        fulls[m] = shape((fulls[m].shape[0], fulls[m].shape[1] // 2), low)
    fulls[7] = shape((fulls[7].shape[0] // 2, fulls[7].shape[1]), low)
    fulls = tuple(fulls)
    results = pl.pallas_call(
        forward_kernel,
        out_shape=fulls + saved,
        in_specs=[VMEM] * 13,
        out_specs=(ANY,) * 22,
        scratch_shapes=[pltpu.VMEM(a.shape, low) for a in fulls[:5]]
        + [
            pltpu.VMEM((tok, model), low),
            pltpu.VMEM((3, 136, rec), full),
            pltpu.VMEM((tok, rec), full),
            pltpu.VMEM((tok, rec), low),
            pltpu.VMEM((tok, rec), full),
            pltpu.VMEM((tok, rec), full),
            pltpu.VMEM((tok, rec), full),
            pltpu.VMEM((tok, rec), full),
            pltpu.VMEM((tok, rec), full),
            pltpu.VMEM((tok, rec), low),
            pltpu.VMEM((tok, model), full),
            pltpu.VMEM((tok, model), low),
            pltpu.VMEM((3, 8, rec), full),
            pltpu.VMEM((8, rec), full),
            pltpu.VMEM((8, 8, rec), full),
            pltpu.VMEM((8, rec), full),
            pltpu.VMEM((3, 136, 8), full),
            pltpu.SemaphoreType.DMA((8, 20)),
            pltpu.SemaphoreType.DMA((8, 20)),
            pltpu.SemaphoreType.DMA((8, 2)),
            pltpu.SemaphoreType.DMA((10,)),
            pltpu.SemaphoreType.DMA((10,)),
            pltpu.SemaphoreType.DMA((5,)),
            pltpu.SemaphoreType.DMA((14,)),
        ],
        compiler_params=pltpu.CompilerParams(
            collective_id=0, has_side_effects=True, vmem_limit_bytes=60 * 1024 * 1024
        ),
        name="recurrent_forward",
    )(*shards, cotangent, tokens, bounds, gains, vectors)
    return results[:8], results[8:]

class Reduction:
    def __init__(self, kinds, grads, outs, scratch, sems):
        self.kinds = kinds
        self.grads, self.outs = grads, outs
        self.count = len(grads)
        self.held, self.own, self.first, self.second, self.third, self.final = scratch
        self.send, self.recv, self.local = sems
        self.live = []
        self.at_c, self.at_one, self.at_two, self.at_z, self.at_end, self.at_out = (
            {} for _ in range(6)
        )
        r, s, z, c = place()
        self.r, self.z, self.c = r, z, c
        self.mate, self.along_x, self.along_y, self.along_z = peers_of(r, s, z, c)
        self.diagonal = (3 - r, s)
        self.rx, self.ry = lax.rem(r, 2), lax.div(r, 2)

    def peers(self):
        return [self.mate, self.along_x, self.along_y, self.diagonal] + self.along_z

    def remote(self, m, slot, src, dst, device):
        copy = pltpu.make_async_remote_copy(
            src_ref=src,
            dst_ref=dst,
            send_sem=self.send.at[m, slot],
            recv_sem=self.recv.at[m, slot],
            device_id=device,
            device_id_type=MESH,
        )
        copy.start()
        self.live.append(copy)
        return copy

    def load(self, m, q):
        part = self.held[m].shape[3]
        near = pltpu.make_async_copy(
            self.grads[m].at[:, self.c, :, pl.ds(q * part, part)],
            self.own[m].at[q % 2],
            self.local.at[m, q],
        )
        near.start()
        return near

    def begin(self, m):
        part = self.held[m].shape[3]
        far = [
            self.remote(
                m,
                q,
                self.grads[m].at[:, 1 - self.c, :, pl.ds(q * part, part)],
                self.held[m].at[q],
                self.mate,
            )
            for q in range(4)
        ]
        self.at_c[m] = (far, [self.load(m, 0), self.load(m, 1)])

    def stage_core(self, m):
        held, own = self.held[m], self.own[m]
        half = held.shape[2] // 2
        far, near = self.at_c[m]
        for q in range(4):
            far[q].wait_recv()
            near[q].wait()

            def add(b):
                held[q, b] = held[q, b] + own[q % 2, b]

            loop(held.shape[1], add)
            if q < 2:
                near.append(self.load(m, q + 2))
        self.at_one[m] = []
        for other in range(2):
            quarter = other * 2 + (1 - self.rx)
            self.at_one[m].append(
                self.remote(
                    m,
                    4 + other,
                    held.at[quarter, :, pl.ds(0, half)],
                    self.first[m].at[0, other],
                    self.along_x,
                )
            )
            quarter = (1 - self.ry) * 2 + other
            self.at_one[m].append(
                self.remote(
                    m,
                    6 + other,
                    held.at[quarter, :, pl.ds(half, half)],
                    self.first[m].at[1, other],
                    self.along_y,
                )
            )

    def stage_one(self, m):
        held, first = self.held[m], self.first[m]
        count, half = held.shape[1], held.shape[2] // 2
        for copy in self.at_one[m]:
            copy.wait_recv()

        def add(i):
            other, b = lax.div(i, count), lax.rem(i, count)
            qx = other * 2 + self.rx
            held[qx, b, :half] = held[qx, b, :half] + first[0, other, b]
            qy = self.ry * 2 + other
            held[qy, b, half:] = held[qy, b, half:] + first[1, other, b]

        loop(2 * count, add)
        self.at_two[m] = [
            self.remote(
                m,
                8,
                held.at[(1 - self.ry) * 2 + self.rx, :, pl.ds(0, half)],
                self.second[m].at[0],
                self.along_y,
            ),
            self.remote(
                m,
                9,
                held.at[self.ry * 2 + (1 - self.rx), :, pl.ds(half, half)],
                self.second[m].at[1],
                self.along_x,
            ),
        ]

    def stage_two(self, m):
        held, second, r = self.held[m], self.second[m], self.r
        half = held.shape[2] // 2
        for copy in self.at_two[m]:
            copy.wait_recv()

        def add(b):
            held[r, b, :half] = held[r, b, :half] + second[0, b]
            held[r, b, half:] = held[r, b, half:] + second[1, b]

        loop(held.shape[1], add)
        rows = self.kinds[m] == "rows"
        self.at_z[m] = []
        for k in (2,) if rows else (1, 2, 3):
            target = 1 - lax.div(self.z, 2) if rows else lax.rem(self.z + k, 4)
            self.at_z[m].append(
                self.remote(
                    m,
                    9 + k,
                    held.at[r, target],
                    self.third[m].at[0 if rows else k - 1],
                    self.along_z[k - 1],
                )
            )

    def stage_z(self, m):
        held, third, final, r = self.held[m], self.third[m], self.final[m], self.r
        for copy in self.at_z[m]:
            copy.wait_recv()
        kind, parity = self.kinds[m], lax.rem(self.z, 2)
        own = lax.div(self.z, 2) if kind == "rows" else self.z

        def add(i):
            rows = at(i, 32)

            def total(first, *terms):
                values = first.astype(jnp.float32)
                for k in terms:
                    values = values + third[k, rows, :].astype(jnp.float32)
                return values.astype(jnp.bfloat16)

            mine = held[r, own, rows, :]
            if kind == "columns":
                final[r, parity, rows, :] = total(mine, 1)
                final[r, 1 - parity, rows, :] = total(third[0, rows, :], 2)
            else:
                final[r, rows, :] = total(mine, *((0,) if kind == "rows" else (0, 1, 2)))

        loop(held.shape[2] // 32, add)
        self.at_end[m] = [
            self.remote(m, 13 + i, final.at[r], final.at[r], device)
            for i, device in enumerate((self.along_x, self.along_y, self.diagonal))
        ]

    def stage_end(self, m):
        for copy in self.at_end[m]:
            copy.wait_recv()
        out = pltpu.make_async_copy(self.final[m], self.outs[m], self.local.at[m, 4])
        out.start()
        self.at_out[m] = out

    def tick(self, now):
        stages = (self.stage_core, self.stage_one, self.stage_two, self.stage_z, self.stage_end)
        for late, stage in enumerate(stages):
            if 0 <= now - late < self.count:
                stage(now - late)
            if late == 0 and now + 2 < self.count:
                self.begin(now + 2)

    def ticks(self):
        return self.count + 4

    def close(self):
        for m in range(self.count):
            self.at_out[m].wait()
        for copy in self.live:
            copy.wait_send()


REDUCTION_SEMS = 16


def reduction_memory(kinds, grads):
    low = jnp.bfloat16
    count = len(grads)
    shapes = [(2 if kind == "rows" else 4,) + quarter_shape(kind, g) for kind, g in zip(kinds, grads)]
    scratch = [pltpu.VMEM((4, zs, k, n), low) for zs, k, n in shapes]
    scratch += [pltpu.VMEM((2, zs, k, n), low) for zs, k, n in shapes]
    scratch += [pltpu.VMEM((2, 2, zs, k // 2, n), low) for zs, k, n in shapes]
    scratch += [pltpu.VMEM((2, zs, k // 2, n), low) for zs, k, n in shapes]
    scratch += [pltpu.VMEM((zs - 1, k, n), low) for zs, k, n in shapes]
    scratch += [pltpu.VMEM(a.shape, low) for a in reduced_shapes(kinds, grads)]
    return scratch + [
        pltpu.SemaphoreType.DMA((count, REDUCTION_SEMS)),
        pltpu.SemaphoreType.DMA((count, REDUCTION_SEMS)),
        pltpu.SemaphoreType.DMA((count, 5)),
    ]


def reduced_shapes(kinds, grads):
    shapes = [(kind, quarter_shape(kind, g)) for kind, g in zip(kinds, grads)]
    return tuple(
        jax.ShapeDtypeStruct((4, 2, k, n) if kind == "columns" else (4, k, n), jnp.bfloat16)
        for kind, (k, n) in shapes
    )


def take_reduction(take, count):
    scratch = [take(count) for _ in range(6)]
    return scratch, take(3)


def taker(refs):
    refs = list(refs)

    def take(n):
        taken, refs[:n] = refs[:n], []
        return taken

    return take


def split_rows(kind, grad):
    zs = 2 if kind == "rows" else 4
    return grad.reshape(zs, 2, grad.shape[0] // (2 * zs), grad.shape[1])


def quarter_shape(kind, grad):
    return grad.shape[0] // (4 if kind == "rows" else 8), grad.shape[1] // 4


def finish_kernel(count, plain, *refs):
    take = taker(refs)
    blocks, same = take(count), take(plain)
    wholes, same_out = take(count), take(plain)
    brought, wide, passed = take(count), take(count), take(plain)
    sem_in, sem_out = take(2)
    entries = [(a, b, i) for i, (a, b) in enumerate(zip(blocks + same, brought + passed))]
    fetched = [pltpu.make_async_copy(a, b, sem_in.at[i]) for a, b, i in entries]
    for copy in fetched:
        copy.start()
    written = []
    for i in range(count + plain):
        fetched[i].wait()
        if i < count:
            block, whole = brought[i], wide[i]
            part = block.shape[-1]
            for q in range(4):
                for half in range(2 if len(block.shape) == 4 else 1):
                    if len(block.shape) == 4:
                        column = ((half + 2 * (q // 2)) * 2 + q % 2) * part
                        values = block[q, half]
                    else:
                        column, values = q * part, block[q]
                    whole[:, column : column + part] = values.astype(jnp.float32)
            copy = pltpu.make_async_copy(whole, wholes[i], sem_out.at[i])
        else:
            copy = pltpu.make_async_copy(passed[i - count], same_out[i - count], sem_out.at[i])
        copy.start()
        written.append(copy)
    for copy in written:
        copy.wait()


def finish(blocks, same):
    shape = jax.ShapeDtypeStruct
    whole = [(b.shape[-2], b.size // b.shape[-2]) for b in blocks]
    count, plain = len(blocks), len(same)
    results = pl.pallas_call(
        functools.partial(finish_kernel, count, plain),
        out_shape=tuple(shape(a, jnp.float32) for a in whole)
        + tuple(shape(a.shape, a.dtype) for a in same),
        in_specs=[ANY] * (count + plain),
        out_specs=(ANY,) * (count + plain),
        scratch_shapes=[pltpu.VMEM(b.shape, b.dtype) for b in blocks]
        + [pltpu.VMEM(a, jnp.float32) for a in whole]
        + [pltpu.VMEM(a.shape, a.dtype) for a in same]
        + [pltpu.SemaphoreType.DMA((count + plain,))] * 2,
        compiler_params=pltpu.CompilerParams(vmem_limit_bytes=62 * 1024 * 1024),
        name="widen_gradients",
    )(*blocks, *same)
    return results[:count], results[count:]


def reduce_kernel(count, *refs):
    take = taker(refs)
    grads = take(count)
    (small_in,) = take(1)
    outs = take(count)
    (small_out,) = take(1)
    reduction = Reduction(("all",) * count, grads, outs, *take_reduction(take, count))
    small_held, small_got, small_send, small_recv = take(4)
    z = reduction.z
    greet(reduction.peers())
    small_copies = []

    def swap_small(slot, source, device):
        copy = pltpu.make_async_remote_copy(
            src_ref=small_held.at[source],
            dst_ref=small_got.at[slot],
            send_sem=small_send.at[slot],
            recv_sem=small_recv.at[slot],
            device_id=device,
            device_id_type=MESH,
        )
        copy.start()
        small_copies.append(copy)
        return copy

    small_held[0] = small_in[...]
    swap = swap_small(0, 0, reduction.mate)
    reduction.begin(0)
    if count > 1:
        reduction.begin(1)
    for now in range(reduction.ticks()):
        reduction.tick(now)
        if now < 2:
            swap.wait_recv()
            small_held[now + 1] = small_held[now] + small_got[now]
            swap = swap_small(now + 1, now + 1, (reduction.along_x, reduction.along_y)[now])
        if now == 2:
            swap.wait_recv()
            small_held[3] = small_held[2] + small_got[2]
            spread = [swap_small(2 + k, 3, reduction.along_z[k - 1]) for k in (1, 2, 3)]
    for copy in spread:
        copy.wait_recv()
    small_got[6] = small_held[3]
    total = None
    for source in range(4):
        k = lax.rem(z + 4 - source, 4)
        slot = jnp.where(k == 0, 6, 2 + k)
        term = small_got[slot]
        total = term if total is None else total + term
    small_out[...] = total
    for copy in small_copies:
        copy.wait_send()
    reduction.close()


def reduce_all(grads, small, tag):
    count = len(grads)
    kinds = ("all",) * count
    results = pl.pallas_call(
        functools.partial(reduce_kernel, count),
        out_shape=reduced_shapes(kinds, grads)
        + (jax.ShapeDtypeStruct(small.shape, small.dtype),),
        in_specs=[ANY] * count + [VMEM],
        out_specs=(ANY,) * count + (VMEM,),
        scratch_shapes=reduction_memory(kinds, grads)
        + [
            pltpu.VMEM((4,) + small.shape, small.dtype),
            pltpu.VMEM((7,) + small.shape, small.dtype),
            pltpu.SemaphoreType.DMA((6,)),
            pltpu.SemaphoreType.DMA((6,)),
        ],
        compiler_params=pltpu.CompilerParams(
            collective_id=tag, has_side_effects=True, vmem_limit_bytes=60 * 1024 * 1024
        ),
        name="reduce_grads",
    )(*[split_rows("all", g) for g in grads], small)
    return results[:count], results[count]


def backward_kernel(kinds, *refs):
    take = taker(refs)
    count = len(kinds)
    grads = take(count - 1)
    part_mixed, part_normed2, twin_normed2 = take(3)
    full_out, full_rate, full_input, full_branch, full_rec = take(5)
    saved_states, saved_branch, saved_rate, saved_input, saved_conv, saved_rec = take(6)
    marks, tokens, cotangent, resid, normed, conv_low, mixed_in, carried = take(8)
    gains, vectors = take(2)
    gain1, gain2 = gains.at[0:1], gains.at[1:2]
    conv_w, _, rate_b, input_b, decay_scale = split_vectors(vectors)
    outs = take(count)
    d_rate, d_input, d_branch, d_rec, token_grad, mixed = take(6)
    (small,) = take(1)
    parts = take_reduction(take, count)
    (d_out,) = take(1)
    reduction = Reduction(kinds, grads + [d_out], outs, *parts)
    ring, past, branch_pre, rate_pre, input_pre, conv_out = take(6)
    flow, grads_conv, branch_low, rate_low, input_low, stage = take(6)
    rim, ends, got, carry = take(4)
    own_parts, twin_parts, grad_resid, resid_low = take(4)
    near_send, near_recv, load_sem, ring_sem, stage_sem = take(5)
    r, s, z, c = place()
    others = [(r, lax.rem(s + k, 8)) for k in range(1, 8)]
    greet(others + [reduction.along_x, reduction.along_y, reduction.diagonal])
    live = []

    def near(slot, src, dst, device):
        copy = pltpu.make_async_remote_copy(
            src_ref=src,
            dst_ref=dst,
            send_sem=near_send.at[slot],
            recv_sem=near_recv.at[slot],
            device_id=device,
            device_id_type=MESH,
        )
        copy.start()
        live.append(copy)
        return copy

    def bring(slot, src, dst):
        copy = pltpu.make_async_copy(src, dst, load_sem.at[slot])
        copy.start()
        return copy

    tiles = []
    for weight in (full_out, full_rate, full_input, full_branch, full_rec):
        tiles.append([(weight, j) for j in range(weight.shape[0] // 512)])
    out_tiles, rate_tiles, input_tiles, branch_tiles, rec_tiles = tiles
    order = list(out_tiles)
    for pair in zip(rate_tiles, input_tiles):
        order += pair
    for pair in zip(branch_tiles, rec_tiles):
        order += pair
    fetches = {}

    def fetch(i):
        if i < len(order):
            weight, j = order[i]
            copy = pltpu.make_async_copy(
                weight.at[pl.ds(j * 512, 512)],
                ring.at[i % 3, :, pl.ds(0, weight.shape[1])],
                ring_sem.at[i % 3],
            )
            copy.start()
            fetches[i] = copy

    def back_tile(i, left, depth):
        fetches[i].wait()
        return lax.dot_general(
            left[...],
            ring[i % 3, :, pl.ds(0, depth)],
            (((1,), (1,)), ((), ())),
            preferred_element_type=jnp.float32,
        )

    staged = [None, None]
    turn = [0]

    def outer_product(left, right, target):
        for strip in range(left.shape[1] // 256):
            slot = turn[0] % 2
            turn[0] += 1
            if staged[slot] is not None:
                staged[slot].wait()
            rows = pl.ds(strip * 256, 256)
            width = right.shape[1]

            def one(j):
                columns = at(j, 512)
                stage[slot, :, columns] = lax.dot_general(
                    left[:, rows],
                    right[:, columns],
                    (((0,), (0,)), ((), ())),
                    preferred_element_type=jnp.float32,
                ).astype(jnp.bfloat16)

            loop(width // 512, one)
            copy = pltpu.make_async_copy(
                stage.at[slot, :, pl.ds(0, width)], target.at[rows], stage_sem.at[slot]
            )
            copy.start()
            staged[slot] = copy

    def out_weight():
        depth = d_out.shape[2]

        def one(i):
            source, column = lax.div(i, 2), lax.rem(i, 2)
            columns = at(column, 512)
            values = lax.dot_general(
                mixed_in[:, at(source, 2 * depth)],
                resid_low[:, columns],
                (((0,), (0,)), ((), ())),
                preferred_element_type=jnp.float32,
            ).astype(jnp.bfloat16)
            d_out[source, 0, :, columns] = values[:depth]
            d_out[source, 1, :, columns] = values[depth:]

        loop(8, one)

    def block_of(i):
        row, block = lax.div(i, 4), lax.rem(i, 4)
        return row, block, pl.ds(pl.multiple_of(row * 128 + block * 32, 32), 32)

    def folded(values):
        return values[0:8] + values[8:16] + values[16:24] + values[24:32]

    def gates(rows, columns, mark_rows):
        rate_gate = jax.nn.sigmoid(rate_pre[rows, columns] + rate_b[:, columns])
        log_rate = decay_scale[:, columns] * rate_gate
        return rate_gate, log_rate, jnp.exp(log_rate)

    def branch_back():
        def one(i):
            column, rest = lax.div(i, 12), lax.rem(i, 12)
            row, block, rows = block_of(rest)
            columns = at(column, 512)
            act, slope = gelu_parts(branch_pre[rows, columns])
            grad = flow[rows, columns]
            state = past[row, pl.ds(pl.multiple_of(block * 32 + 8, 8), 32), columns]
            flow[rows, columns] = grad * act
            branch_low[rows, columns] = (grad * state * slope).astype(jnp.bfloat16)

        loop(36, one)

    def scan_back():
        def one(column):
            columns = at(column, 512)
            spot = lax.broadcasted_iota(jnp.int32, (8, 512), 0)

            def tile(i, state):
                t = 15 - i
                results = []
                for row in range(3):
                    rows = pl.ds(pl.multiple_of(row * 128 + t * 8, 8), 8)
                    keep = 1.0 - marks[row, pl.ds(pl.multiple_of(t * 8, 8), 8), 0:1]
                    _, _, pace = gates(rows, columns, None)
                    decay = pace * keep
                    follow, carry_a, carry_b = state[3 * row : 3 * row + 3]
                    later = jnp.where(spot == 7, follow, pltpu.roll(decay, 7, 0))
                    a, b = tile_scan(later, flow[rows, columns], True)
                    b = b + a * carry_b
                    a = a * carry_a
                    branch_pre[rows, columns] = a
                    flow[rows, columns] = b
                    results += [decay[0:1], a[0:1], b[0:1]]
                return tuple(results)

            ones, zeros = jnp.ones((1, 512), jnp.float32), jnp.zeros((1, 512), jnp.float32)
            last = lax.fori_loop(0, 16, tile, (ones, ones, zeros) * 3)
            for row in range(3):
                decay, a, b = last[3 * row : 3 * row + 3]
                ends[row : row + 1, columns] = decay * a
                ends[3 + row : 4 + row, columns] = decay * b

        loop(3, one)
        return [near(k, ends, got.at[k], others[k - 1]) for k in range(1, 8)]

    def carry_back(copies):
        for copy in copies:
            copy.wait_recv()

        def one(column):
            columns = at(column, 512)
            state = jnp.zeros((3, 512), jnp.float32)
            for ahead in range(7, 0, -1):
                k = 8 - ahead
                after = got[k, 3:6, columns] + got[k, 0:3, columns] * state
                state = jnp.where(s + ahead <= 7, after, state)
            carry[0:3, columns] = state

        loop(3, one)

    def gates_back():
        def one(column):
            columns = at(column, 512)

            def block_step(i, sums):
                row, block, rows = block_of(i)
                mark = pl.ds(pl.multiple_of(block * 32, 32), 32)
                reset = marks[row, mark, 0:1]
                keep = 1.0 - reset
                rate_gate, log_rate, pace = gates(rows, columns, mark)
                input_gate = jax.nn.sigmoid(input_pre[rows, columns] + input_b[:, columns])
                power = pace * pace
                root = jnp.sqrt(minus_expm1(2.0 * log_rate, power))
                scale = reset + keep * root
                conv = conv_out[rows, columns]
                grad = flow[rows, columns] + branch_pre[rows, columns] * carry[
                    pl.ds(row, 1), columns
                ]
                window = past[row, pl.ds(pl.multiple_of(block * 32, 8), 40), columns]
                before = pltpu.roll(window, 1, 0)[8:]
                grad_log = keep * grad * (before * pace - input_gate * conv * power / root)
                decay_sum = rate_gate * grad_log
                rate_grad = decay_scale[:, columns] * decay_sum * (1.0 - rate_gate)
                direct = grad * scale * input_gate
                input_grad = direct * conv * (1.0 - input_gate)
                rate_low[rows, columns] = rate_grad.astype(jnp.bfloat16)
                input_low[rows, columns] = input_grad.astype(jnp.bfloat16)
                rate_pre[rows, columns] = direct
                return (
                    sums[0] + folded(decay_sum),
                    sums[1] + folded(rate_grad),
                    sums[2] + folded(input_grad),
                )

            zeros = jnp.zeros((8, 512), jnp.float32)
            sums = lax.fori_loop(0, 12, block_step, (zeros,) * 3)
            for spot, values in enumerate(sums):
                small[5 + spot : 6 + spot, columns] = jnp.sum(values, axis=0, keepdims=True)

        loop(3, one)

    def conv_back(copy):
        copy.wait_recv()
        for row in range(3):
            grads_conv[row, 128:136, :] = jnp.where(s < 7, rim[row], 0.0)

        def one(column):
            columns = at(column, 512)

            def block_step(i, sums):
                row, block, rows = block_of(i)
                span = pl.ds(pl.multiple_of(block * 32, 8), 40)
                ahead = grads_conv[row, span, columns]
                behind = past[row, span, columns]
                grad = ahead[:32]
                total = conv_w[0:1, columns] * grad
                new = [sums[0] + folded(grad * behind[8:])]
                for k in (1, 2, 3):
                    kept = ahead * marks[row, span, k : k + 1]
                    total = total + conv_w[k : k + 1, columns] * pltpu.roll(kept, 40 - k, 0)[:32]
                    new.append(
                        sums[k] + folded(kept[:32] * pltpu.roll(behind, k, 0)[8:])
                    )
                new.append(sums[4] + folded(grad))
                rate_low[rows, columns] = total.astype(jnp.bfloat16)
                return tuple(new)

            zeros = jnp.zeros((8, 512), jnp.float32)
            sums = lax.fori_loop(0, 12, block_step, (zeros,) * 5)
            for spot, values in enumerate(sums):
                small[spot : spot + 1, columns] = jnp.sum(values, axis=0, keepdims=True)

        loop(3, one)

    def second_norm_back():
        def one(i, total):
            rows = at(i, 16)
            grad = own_parts[1, rows, :].astype(jnp.float32) + twin_parts[1, rows, :].astype(
                jnp.float32
            )
            values = resid[rows, :]
            scale = lax.rsqrt(jnp.mean(values * values, axis=-1, keepdims=True) + epsilon)
            back = grad * gain2[...]
            mean = jnp.mean(values * back, axis=-1, keepdims=True)
            result = cotangent[rows, :].astype(jnp.float32) + scale * back
            result = result - values * (scale * scale * scale * mean)
            grad_resid[rows, :] = result
            resid_low[rows, :] = result.astype(jnp.bfloat16)
            part = grad * values * scale
            return total + part[0:8] + part[8:16]

        total = lax.fori_loop(0, 24, one, jnp.zeros((8, 1024), jnp.float32))
        small[9:10, 0:1024] = jnp.sum(total, axis=0, keepdims=True)

    def mix_back():
        def one(i):
            rows = at(i, 16)
            total = own_parts[0, rows, :].astype(jnp.float32)
            total = total + twin_parts[0, rows, :].astype(jnp.float32)
            own_parts[0, rows, :] = (resid[rows, :] + total).astype(jnp.bfloat16)

        loop(24, one)
        return bring(8, own_parts.at[0], mixed)

    def norm_back():
        def one(i, total):
            rows = at(i, 16)
            values = tokens[rows, :].astype(jnp.float32)
            scale = lax.rsqrt(jnp.mean(values * values, axis=-1, keepdims=True) + epsilon)
            grad = input_pre[rows, pl.ds(0, 1024)]
            back = grad * gain1[...]
            mean = jnp.mean(values * back, axis=-1, keepdims=True)
            result = grad_resid[rows, :] + scale * back - values * (scale * scale * scale * mean)
            own_parts[1, rows, :] = result.astype(jnp.bfloat16)
            part = grad * values * scale
            return total + part[0:8] + part[8:16]

        total = lax.fori_loop(0, 24, one, jnp.zeros((8, 1024), jnp.float32))
        small[8:9, 0:1024] = jnp.sum(total, axis=0, keepdims=True)
        return bring(10, own_parts.at[1], token_grad)

    tok = tokens.shape[0]
    twin = (r, s + 2 - 4 * lax.rem(z, 2))
    reduction.begin(0)
    reduction.begin(1)
    mixed_copy = near(8, part_mixed.at[pl.ds(tok, tok)], twin_parts.at[0], twin)
    part_loads = [
        bring(6, part_normed2.at[pl.ds(0, tok)], own_parts.at[1]),
        bring(9, twin_normed2, twin_parts.at[1]),
        bring(7, part_mixed.at[pl.ds(0, tok)], own_parts.at[0]),
    ]
    loads = [
        bring(0, saved_branch, branch_pre),
        bring(1, saved_states, past.at[:, pl.ds(8, 128), :]),
        bring(2, saved_rate, rate_pre),
        bring(3, saved_input, input_pre),
        bring(4, saved_conv, conv_out),
    ]
    for i in range(3):
        fetch(i)
    small[...] = jnp.zeros_like(small)
    ends[...] = jnp.zeros_like(ends)
    for row in range(3):
        past[row, 0:8, :] = jnp.broadcast_to(carried[row : row + 1, :], (8, past.shape[2]))
    part_loads[0].wait()
    part_loads[1].wait()
    second_norm_back()
    for i in range(3):
        flow[:, pl.ds(i * 512, 512)] = back_tile(i, resid_low, 1024)
        fetch(i + 3)
    reduction.tick(0)
    out_weight()
    loads[0].wait()
    loads[1].wait()
    branch_back()
    reduction.tick(1)
    loads[2].wait()
    copies = scan_back()
    reduction.tick(2)
    carry_back(copies)
    loads[3].wait()
    loads[4].wait()
    gates_back()
    loads.append(bring(5, saved_rec, past))
    reduction.tick(3)
    at_tile = 3
    for j in range(3):
        columns = pl.ds(j * 512, 512)
        total = rate_pre[:, columns]
        total = total + back_tile(at_tile, rate_low, 1536)
        fetch(at_tile + 3)
        total = total + back_tile(at_tile + 1, input_low, 1536)
        fetch(at_tile + 4)
        at_tile += 2
        for row in range(3):
            grads_conv[row, 0:128, columns] = total[row * 128 : (row + 1) * 128]
    rim_copy = near(0, grads_conv.at[:, pl.ds(0, 8), :], rim, others[6])
    reduction.tick(4)
    outer_product(conv_low, rate_low, d_rate)
    loads[5].wait()
    conv_back(rim_copy)
    reduction.tick(5)
    for j in range(2):
        columns = pl.ds(j * 512, 512)
        total = back_tile(at_tile, branch_low, 1536)
        fetch(at_tile + 3)
        total = total + back_tile(at_tile + 1, rate_low, 1536)
        fetch(at_tile + 4)
        at_tile += 2
        input_pre[:, columns] = total
    outer_product(normed, rate_low, d_rec)
    reduction.tick(6)
    outer_product(conv_low, input_low, d_input)
    outer_product(normed, branch_low, d_branch)
    token_save = norm_back()
    part_loads[2].wait()
    mixed_copy.wait_recv()
    mixed_save = mix_back()
    for now in range(7, reduction.ticks()):
        reduction.tick(now)
    mixed_save.wait()
    token_save.wait()
    for copy in staged:
        copy.wait()
    for copy in live:
        copy.wait_send()
    reduction.close()


def backward_all(grads, parts, fulls, saved, local, vectors):
    low, full = jnp.bfloat16, jnp.float32
    shape, memory = jax.ShapeDtypeStruct, pltpu.VMEM
    kinds = ("rows", "columns", "columns", "all")
    count = len(kinds)
    tok, model = local[1].shape
    rec = fulls[0].shape[0]
    all_grads = tuple(grads) + (shape((rec, model), low),)
    out_shape = reduced_shapes(kinds, all_grads) + (
        shape((rec, rec), low),
        shape((rec, rec), low),
        shape((model, rec), low),
        shape((model, rec), low),
        shape((tok, model), low),
        shape((tok, model), low),
        shape((16, rec), full),
    )
    results = pl.pallas_call(
        functools.partial(backward_kernel, kinds),
        out_shape=out_shape,
        in_specs=[ANY] * (count + 13) + [VMEM] * 10,
        out_specs=(ANY,) * (count + 6) + (VMEM,),
        scratch_shapes=reduction_memory(kinds, all_grads)
        + [
            memory((4, 2, rec // 8, model), low),
            memory((3, 512, rec), low),
            memory((3, 136, rec), full),
            memory((tok, rec), full),
            memory((tok, rec), full),
            memory((tok, rec), full),
            memory((tok, rec), full),
            memory((tok, rec), full),
            memory((3, 136, rec), full),
            memory((tok, rec), low),
            memory((tok, rec), low),
            memory((tok, rec), low),
            memory((2, 256, rec), low),
            memory((3, 8, rec), full),
            memory((8, rec), full),
            memory((8, 8, rec), full),
            memory((8, rec), full),
            memory((2, tok, model), low),
            memory((2, tok, model), low),
            memory((tok, model), full),
            memory((tok, model), low),
            pltpu.SemaphoreType.DMA((9,)),
            pltpu.SemaphoreType.DMA((9,)),
            pltpu.SemaphoreType.DMA((11,)),
            pltpu.SemaphoreType.DMA((3,)),
            pltpu.SemaphoreType.DMA((2,)),
        ],
        compiler_params=pltpu.CompilerParams(
            collective_id=1, has_side_effects=True, vmem_limit_bytes=62 * 1024 * 1024
        ),
        name="recurrent_backward",
    )(*[split_rows(k, g) for k, g in zip(kinds, grads)], *parts, *fulls, *saved, *local, *vectors)
    return results[:count], results[count:]


def from_behind(block, axis, distance):
    devices = range(lax.axis_size(axis))
    route = [(i - distance, i) for i in devices if i - distance in devices]
    return lax.ppermute(block, axis, route)


def prefix(part, axis, combine, identity, reverse):
    count = lax.axis_size(axis)
    place = lax.axis_index(axis)
    ahead = count - 1 - place if reverse else place
    gathered = jax.tree.map(lambda a: lax.all_gather(a, axis), part)
    state = jax.tree.map(lambda a, e: jnp.zeros_like(a) + jnp.asarray(e, a.dtype), part, identity)

    def one(turn, state):
        source = count - 1 - turn if reverse else turn
        return combine(
            state, jax.tree.map(lambda a: lax.dynamic_index_in_dim(a, source, 0, False), gathered)
        )

    return lax.fori_loop(0, ahead, one, state)


def rms_norm(values, gain):
    return values * lax.rsqrt(jnp.mean(values * values, axis=-1, keepdims=True) + epsilon) * gain


def combine(earlier, latter):
    return (earlier[0] * latter[0], latter[0] * earlier[1] + latter[1])


def conv_masks(padded_resets):
    keep_mask = 1.0 - padded_resets
    first = keep_mask[..., 3:]
    second = first * keep_mask[..., 2:-1]
    third = second * keep_mask[..., 1:-2]
    return (first, second, third)


def convolve(padded, masks, conv_weight, conv_bias):
    result = conv_bias + conv_weight[0] * padded[..., 3:, :]
    result = result + conv_weight[1] * masks[0][..., None] * padded[..., 2:-1, :]
    result = result + conv_weight[2] * masks[1][..., None] * padded[..., 1:-2, :]
    return result + conv_weight[3] * masks[2][..., None] * padded[..., :-3, :]


def gate_terms(rate_pre, input_pre, conv_out, decay_param, rate_bias, input_bias, resets):
    rate_gate = jax.nn.sigmoid(rate_pre + rate_bias)
    input_gate = jax.nn.sigmoid(input_pre + input_bias)
    log_rate = -8.0 * jax.nn.softplus(decay_param) * rate_gate
    keep_mask = 1.0 - resets[..., None]
    decays = jnp.exp(log_rate) * keep_mask
    scales = resets[..., None] + keep_mask * jnp.sqrt(-jnp.expm1(2.0 * log_rate))
    return (decays, scales * input_gate * conv_out)


def forward_product(values, weight):
    return jnp.dot(values, weight, preferred_element_type=jnp.float32)


def outer(left, right):
    return lax.dot_general(
        left, right, (((0,), (0,)), ((), ())), preferred_element_type=jnp.float32
    )


def back_product(grads, weight):
    return lax.dot_general(
        grads, weight, (((1,), (1,)), ((), ())), preferred_element_type=jnp.float32
    )


def plain_body(
    tokens,
    bounds,
    norm1_gain,
    w_branch,
    w_rec,
    conv_weight,
    conv_bias,
    w_rate,
    rate_bias,
    w_input,
    input_bias,
    decay_param,
    w_out,
    norm2_gain,
    w_gate,
    w_up,
    w_down,
    cotangent,
):
    gathered = (
        lax.all_gather(w_branch, "seq", axis=0, tiled=True),
        lax.all_gather(w_rec, "seq", axis=0, tiled=True),
        lax.all_gather(w_rate, "seq", axis=0, tiled=True),
        lax.all_gather(w_input, "seq", axis=0, tiled=True),
        lax.all_gather(w_out, "seq", axis=0, tiled=True),
        lax.all_gather(w_gate, "seq", axis=0, tiled=True),
        lax.all_gather(w_up, "seq", axis=0, tiled=True),
        lax.all_gather(w_down, "seq", axis=0, tiled=True),
    )
    full_branch, full_rec, full_rate, full_input, full_out, full_gate, full_up, full_down = gathered
    row_count, tok_count, model_width = tokens.shape
    rec_width = full_rec.shape[1]
    offset = lax.axis_index("seq") * tok_count
    positions = offset - 3 + jnp.arange(tok_count + 3, dtype=jnp.int32)
    marked = (
        jnp.any(positions[None, :, None] == bounds[:, None, :], axis=2) | (positions == 0)[None, :]
    )
    padded_resets = marked.astype(jnp.float32)
    resets = padded_resets[:, 3:]
    masks = conv_masks(padded_resets)
    inputs = tokens.astype(jnp.float32).reshape(-1, model_width)
    normed = rms_norm(inputs, norm1_gain).astype(jnp.bfloat16)
    branch_pre = forward_product(normed, full_branch)
    rec_in = forward_product(normed, full_rec).reshape(row_count, tok_count, rec_width)
    rim = from_behind(rec_in[:, tok_count - 3 :, :], "seq", 1)
    padded = jnp.concatenate([rim, rec_in], axis=1)
    conv_out = convolve(padded, masks, conv_weight, conv_bias)
    conv_low = conv_out.astype(jnp.bfloat16).reshape(-1, rec_width)
    rate_pre = forward_product(conv_low, full_rate).reshape(conv_out.shape)
    input_pre = forward_product(conv_low, full_input).reshape(conv_out.shape)

    def gates_of(rate_arg, input_arg, conv_arg, decay_arg, rate_arg_bias, input_arg_bias):
        return gate_terms(
            rate_arg, input_arg, conv_arg, decay_arg, rate_arg_bias, input_arg_bias, resets
        )

    decays, drives = gates_of(rate_pre, input_pre, conv_out, decay_param, rate_bias, input_bias)
    prefix_decay, local_states = lax.associative_scan(combine, (decays, drives), axis=1)
    ones_pair = jnp.ones((row_count, rec_width), jnp.float32)
    zeros_pair = jnp.zeros((row_count, rec_width), jnp.float32)
    carry_in = prefix(
        (prefix_decay[:, -1], local_states[:, -1]), "seq", combine, (ones_pair, zeros_pair), False
    )[1]
    states = local_states + prefix_decay * carry_in[:, None, :]
    earlier_states = jnp.concatenate([carry_in[:, None, :], states[:, :-1, :]], axis=1)
    branch_act = jax.nn.gelu(branch_pre, approximate=True).reshape(states.shape)
    mixed_in = (states * branch_act).astype(jnp.bfloat16).reshape(-1, rec_width)
    resid = inputs + forward_product(mixed_in, full_out)
    normed2 = rms_norm(resid, norm2_gain).astype(jnp.bfloat16)
    gate_pre = forward_product(normed2, full_gate)
    up_pre = forward_product(normed2, full_up)
    hidden = (jax.nn.gelu(gate_pre, approximate=True) * up_pre).astype(jnp.bfloat16)
    mixed = (resid + forward_product(hidden, full_down)).astype(jnp.bfloat16).reshape(tokens.shape)
    cot_low = cotangent.reshape(-1, model_width)
    grad_down = outer(hidden, cot_low)
    grad_hidden = back_product(cot_low, full_down)
    _, pull_mlp = jax.vjp(
        lambda gate_arg, up_arg: jax.nn.gelu(gate_arg, approximate=True) * up_arg, gate_pre, up_pre
    )
    grad_gate_pre, grad_up_pre = pull_mlp(grad_hidden)
    gate_low = grad_gate_pre.astype(jnp.bfloat16)
    up_low = grad_up_pre.astype(jnp.bfloat16)
    grad_gate = outer(normed2, gate_low)
    grad_up = outer(normed2, up_low)
    grad_normed2 = back_product(gate_low, full_gate) + back_product(up_low, full_up)
    _, pull_norm2 = jax.vjp(rms_norm, resid, norm2_gain)
    grad_resid_norm, grad_norm2 = pull_norm2(grad_normed2)
    grad_resid = cot_low.astype(jnp.float32) + grad_resid_norm
    resid_low = grad_resid.astype(jnp.bfloat16)
    grad_out = outer(mixed_in, resid_low)
    grad_mixed = back_product(resid_low, full_out).reshape(states.shape)
    grad_states = grad_mixed * branch_act
    _, pull_branch = jax.vjp(lambda pre_arg: jax.nn.gelu(pre_arg, approximate=True), branch_pre)
    branch_low = pull_branch((grad_mixed * states).reshape(-1, rec_width))[0].astype(jnp.bfloat16)
    next_decays = jnp.concatenate([decays[:, 1:, :], ones_pair[:, None, :]], axis=1)
    suffix_decay, local_grads = lax.associative_scan(
        combine, (next_decays, grad_states), axis=1, reverse=True
    )
    element = (prefix_decay[:, -1], decays[:, 0] * local_grads[:, 0])
    carry_back = prefix(element, "seq", combine, (ones_pair, zeros_pair), True)[1]
    state_grads = local_grads + suffix_decay * carry_back[:, None, :]
    _, pull_gates = jax.vjp(
        gates_of, rate_pre, input_pre, conv_out, decay_param, rate_bias, input_bias
    )
    grad_rate_pre, grad_input_pre, grad_conv_direct, grad_decay, grad_rate_bias, grad_input_bias = (
        pull_gates((state_grads * earlier_states, state_grads))
    )
    rate_low = grad_rate_pre.astype(jnp.bfloat16).reshape(-1, rec_width)
    input_low = grad_input_pre.astype(jnp.bfloat16).reshape(-1, rec_width)
    grad_rate = outer(conv_low, rate_low)
    grad_input = outer(conv_low, input_low)
    grad_conv = grad_conv_direct + (
        back_product(rate_low, full_rate) + back_product(input_low, full_input)
    ).reshape(conv_out.shape)
    _, pull_conv = jax.vjp(
        lambda pad_arg, weight_arg, bias_arg: convolve(pad_arg, masks, weight_arg, bias_arg),
        padded,
        conv_weight,
        conv_bias,
    )
    grad_padded, grad_conv_weight, grad_conv_bias = pull_conv(grad_conv)
    rim_back = from_behind(grad_padded[:, :3, :], "seq", -1)
    grad_rec = grad_padded[:, 3:, :] + jnp.concatenate(
        [jnp.zeros((row_count, tok_count - 3, rec_width), jnp.float32), rim_back], axis=1
    )
    rec_low = grad_rec.astype(jnp.bfloat16).reshape(-1, rec_width)
    grad_rec_w = outer(normed, rec_low)
    grad_branch_w = outer(normed, branch_low)
    grad_normed = back_product(branch_low, full_branch) + back_product(rec_low, full_rec)
    _, pull_norm1 = jax.vjp(rms_norm, inputs, norm1_gain)
    grad_inputs, grad_norm1 = pull_norm1(grad_normed)
    token_grad = (grad_resid + grad_inputs).astype(jnp.bfloat16).reshape(tokens.shape)
    grad_mats = (
        grad_branch_w,
        grad_rec_w,
        grad_rate,
        grad_input,
        grad_out,
        grad_gate,
        grad_up,
        grad_down,
    )
    blocks = (
        lax.psum_scatter(grad_mats[0], "seq", scatter_dimension=0, tiled=True),
        lax.psum_scatter(grad_mats[1], "seq", scatter_dimension=0, tiled=True),
        lax.psum_scatter(grad_mats[2], "seq", scatter_dimension=0, tiled=True),
        lax.psum_scatter(grad_mats[3], "seq", scatter_dimension=0, tiled=True),
        lax.psum_scatter(grad_mats[4], "seq", scatter_dimension=0, tiled=True),
        lax.psum_scatter(grad_mats[5], "seq", scatter_dimension=0, tiled=True),
        lax.psum_scatter(grad_mats[6], "seq", scatter_dimension=0, tiled=True),
        lax.psum_scatter(grad_mats[7], "seq", scatter_dimension=0, tiled=True),
    )
    summed = lax.psum(
        (blocks[0], blocks[1], blocks[2], blocks[3], blocks[4], blocks[5], blocks[6], blocks[7]),
        "rows",
    )
    small = lax.psum(
        (
            grad_norm1,
            grad_conv_weight,
            grad_conv_bias,
            grad_rate_bias,
            grad_input_bias,
            grad_decay,
            grad_norm2,
        ),
        ("rows", "seq"),
    )
    return (
        mixed,
        token_grad,
        small[0],
        summed[0],
        summed[1],
        small[1],
        small[2],
        summed[2],
        small[3],
        summed[3],
        small[4],
        small[5],
        summed[4],
        small[6],
        summed[5],
        summed[6],
        summed[7],
    )


def body(*args):
    if lax.axis_size("rows") == 4 and lax.axis_size("seq") == 8:
        return staged_body(*args)
    return plain_body(*args)


def staged_body(
    tokens,
    bounds,
    norm1_gain,
    w_branch,
    w_rec,
    conv_weight,
    conv_bias,
    w_rate,
    rate_bias,
    w_input,
    input_bias,
    decay_param,
    w_out,
    norm2_gain,
    w_gate,
    w_up,
    w_down,
    cotangent,
):
    row_count, tok_count, model_width = tokens.shape
    rec_width = w_rec.shape[1]
    flat_tokens = tokens.reshape(-1, model_width)
    gains = jnp.stack([norm1_gain, norm2_gain])
    vectors = jnp.concatenate(
        [
            conv_weight,
            jnp.stack([conv_bias, rate_bias, input_bias, -8.0 * jax.nn.softplus(decay_param)]),
        ]
    )
    fulls, saved = forward_all(
        (w_rec, w_rate, w_input, w_branch, w_out, w_gate, w_up, w_down),
        cotangent.reshape(-1, model_width),
        flat_tokens,
        bounds,
        gains,
        vectors,
    )
    full_rec, full_rate, full_input, full_branch, full_out, half_gate, half_up, half_down = fulls
    normed, padded, conv_out, conv_low, rate_pre, input_pre = saved[:6]
    states, branch_pre, mixed_in, resid, carried, pair_normed2, pair_cotangent, marks = saved[6:]
    gate_pre = forward_product(pair_normed2, half_gate)
    up_pre = forward_product(pair_normed2, half_up)
    hidden = (jax.nn.gelu(gate_pre, approximate=True) * up_pre).astype(jnp.bfloat16)
    part_mixed = forward_product(hidden, half_down).astype(jnp.bfloat16)
    grad_down = outer(hidden, pair_cotangent)
    grad_hidden = back_product(pair_cotangent, half_down)
    _, pull_mlp = jax.vjp(
        lambda gate_arg, up_arg: jax.nn.gelu(gate_arg, approximate=True) * up_arg, gate_pre, up_pre
    )
    grad_gate_pre, grad_up_pre = pull_mlp(grad_hidden)
    gate_low = grad_gate_pre.astype(jnp.bfloat16)
    up_low = grad_up_pre.astype(jnp.bfloat16)
    part_normed2 = (back_product(gate_low, half_gate) + back_product(up_low, half_up)).astype(
        jnp.bfloat16
    )
    half = part_mixed.shape[0] // 2
    twins = [(s, s + 2 - 4 * (s // 2 % 2)) for s in range(lax.axis_size("seq"))]
    twin_normed2 = lax.ppermute(part_normed2[half:], "seq", twins)
    grad_gate = outer(pair_normed2, gate_low)
    grad_up = outer(pair_normed2, up_low)
    low = jnp.bfloat16
    ff, rest = backward_all(
        [g.astype(low) for g in (grad_down, grad_gate, grad_up)],
        (part_mixed, part_normed2, twin_normed2),
        (full_out, full_rate, full_input, full_branch, full_rec),
        (
            states.reshape(row_count, tok_count, rec_width),
            branch_pre,
            rate_pre,
            input_pre,
            conv_out,
            padded,
        ),
        (
            marks,
            flat_tokens,
            cotangent.reshape(-1, model_width),
            resid,
            normed,
            conv_low,
            mixed_in,
            carried,
        ),
        (gains, vectors),
    )
    reduced, (token_grad, mixed, sums) = tuple(ff), rest[4:]
    rec, sums = reduce_all(rest[:4], sums, 2)
    (down, gate, up, out, rate, into, branch, recur), (mixed, token_grad) = finish(
        reduced + tuple(rec), (mixed, token_grad)
    )
    return (
        mixed.reshape(tokens.shape),
        token_grad.reshape(tokens.shape),
        sums[8, :model_width],
        branch,
        recur,
        sums[:4],
        sums[4],
        rate,
        sums[6],
        into,
        sums[7],
        -8.0 * jax.nn.sigmoid(decay_param) * sums[5],
        out,
        sums[9, :model_width],
        gate,
        up,
        down,
    )


def solution(mesh):
    in_specs = (
        P("rows", "seq", None),
        P("rows", None),
        P(),
        P("seq", None),
        P("seq", None),
        P(),
        P(),
        P("seq", None),
        P(),
        P("seq", None),
        P(),
        P(),
        P("seq", None),
        P(),
        P("seq", None),
        P("seq", None),
        P("seq", None),
        P("rows", "seq", None),
    )
    out_specs = (
        P("rows", "seq", None),
        P("rows", "seq", None),
        P(),
        P("seq", None),
        P("seq", None),
        P(),
        P(),
        P("seq", None),
        P(),
        P("seq", None),
        P(),
        P(),
        P("seq", None),
        P(),
        P("seq", None),
        P("seq", None),
        P("seq", None),
    )
    return jax.shard_map(
        body, mesh=mesh, in_specs=in_specs, out_specs=out_specs, check_vma=False)
```

```python
import functools

import jax
import jax.numpy as jnp
from jax import lax
from jax.experimental import pallas as pl
from jax.experimental.pallas import tpu as pltpu
from jax.sharding import PartitionSpec as P

epsilon = 1e-06
MESH = pl.DeviceIdType.MESH
ANY = pl.BlockSpec(memory_space=pl.ANY)
VMEM = pl.BlockSpec(memory_space=pltpu.VMEM)


def place():
    r = lax.axis_index("rows")
    s = lax.axis_index("seq")
    return r, s, lax.div(s, 2), lax.rem(s, 2)


def greet(peers):
    barrier = pltpu.get_barrier_semaphore()
    for peer in peers:
        pl.semaphore_signal(barrier, inc=1, device_id=peer, device_id_type=MESH)
    pl.semaphore_wait(barrier, len(peers))


def peers_of(r, s, z, c):
    mate = (r, s + 1 - 2 * c)
    along_x = (r + 1 - 2 * lax.rem(r, 2), s)
    along_y = (lax.rem(r + 2, 4), s)
    along_z = [(r, lax.rem(z + k, 4) * 2 + c) for k in (1, 2, 3)]
    return mate, along_x, along_y, along_z


def gelu_parts(v):
    inner = 0.7978845608028654 * (v + 0.044715 * v * v * v)
    t = jnp.tanh(inner)
    slope = 0.7978845608028654 * (1.0 + 0.134145 * v * v)
    return 0.5 * v * (1.0 + t), 0.5 * (1.0 + t) + 0.5 * v * (1.0 - t * t) * slope


def gelu_of(v):
    return 0.5 * v * (1.0 + jnp.tanh(0.7978845608028654 * (v + 0.044715 * v * v * v)))


def minus_expm1(v, power):
    total = 1.0 / 40320.0
    for term in (5040.0, 720.0, 120.0, 24.0, 6.0, 2.0, 1.0):
        total = total * v + 1.0 / term
    return jnp.where(v > -0.5, -v * total, 1.0 - power)


def tile_scan(a, b, reverse):
    spot = lax.broadcasted_iota(jnp.int32, a.shape, 0)
    for distance in (1, 2, 4):
        if reverse:
            inside = spot < 8 - distance
            back_a, back_b = pltpu.roll(a, 8 - distance, 0), pltpu.roll(b, 8 - distance, 0)
        else:
            inside = spot >= distance
            back_a, back_b = pltpu.roll(a, distance, 0), pltpu.roll(b, distance, 0)
        b = b + a * jnp.where(inside, back_b, 0.0)
        a = a * jnp.where(inside, back_a, 1.0)
    return a, b


def loop(count, body):
    def one(i, carry):
        body(i)
        return carry

    lax.fori_loop(0, count, one, 0)


def at(i, size):
    return pl.ds(pl.multiple_of(i * size, size), size)


def split_vectors(ref):
    return ref.at[0:4], ref.at[4:5], ref.at[5:6], ref.at[6:7], ref.at[7:8]


def forward_kernel(*refs):
    refs = list(refs)

    def take(n):
        taken, refs[:n] = refs[:n], []
        return taken

    shards = take(8)
    cotangent, tokens, bounds, gains, vectors = take(5)
    gain1, gain2 = gains.at[0:1], gains.at[1:2]
    conv_w, conv_b, rate_b, input_b, decay_scale = split_vectors(vectors)
    fulls = take(8)
    outs = take(11)
    pair_normed2, pair_cotangent, saved_marks = take(3)
    (w_rec, w_rate, w_input, w_branch, w_out) = weights = take(5)
    normed, padded, conv_out, conv_low, rate_pre, input_pre = take(6)
    products, states, branch_pre, mixed_in, resid, normed2 = take(6)
    rim, ends, got, carry_in, marks = take(5)
    send, recv, local, near_send, near_recv, load_sem, save_sem = refs
    count = 8
    r, s, z, c = place()
    mate, along_x, along_y, along_z = peers_of(r, s, z, c)
    across_x, across_y = along_x[0], along_y[0]
    parity = lax.rem(z, 2)
    twin = (r, s + 2 - 4 * parity)
    others = [(r, lax.rem(s + k, 8)) for k in range(1, 8)]
    greet(others + [along_x, along_y])
    live, pending = [], []

    def start(copy):
        copy.start()
        live.append(copy)
        return copy

    def remote(m, slot, src, dst, device):
        return start(
            pltpu.make_async_remote_copy(
                src_ref=src,
                dst_ref=dst,
                send_sem=send.at[m, slot],
                recv_sem=recv.at[m, slot],
                device_id=device,
                device_id_type=MESH,
            )
        )

    def near(slot, src, dst, device):
        return start(
            pltpu.make_async_remote_copy(
                src_ref=src,
                dst_ref=dst,
                send_sem=near_send.at[slot],
                recv_sem=near_recv.at[slot],
                device_id=device,
                device_id_type=MESH,
            )
        )

    def save(slot, src, dst):
        copy = pltpu.make_async_copy(src, dst, save_sem.at[slot])
        copy.start()
        pending.append(copy)

    def rows_of(m, source, core, begin, length):
        depth = shards[m].shape[0]
        block = lax.div(source, 2) * 2 + core if m == 7 else source * 2 + core
        return pl.ds(pl.multiple_of(block * depth + begin, 16), length)

    def region(m, source, quarter, begin, length):
        part = fulls[m].shape[1] // 4
        column = pl.multiple_of(quarter * part, 128)
        return fulls[m].at[rows_of(m, source, c, begin, length), pl.ds(column, part)]

    def turns(m):
        return (2,) if m == 7 else (1, 2, 3)

    stage_own, stage_z, stage_x, stage_y, stage_d, stage_c = {}, {}, {}, {}, {}, {}

    def begin(m):
        depth, width = shards[m].shape
        part = fulls[m].shape[1] // 4
        rows = rows_of(m, z, c, 0, depth)
        stage_z[m] = []
        for k in turns(m):
            column = r * part
            if m in (5, 6):
                half = lax.rem(parity + k, 2)
                column = (half + 2 * lax.div(r, 2)) * (2 * part) + lax.rem(r, 2) * part
            stage_z[m].append(
                remote(
                    m,
                    k,
                    shards[m].at[:, pl.ds(pl.multiple_of(column, 128), part)],
                    region(m, z, r, 0, depth),
                    along_z[k - 1],
                )
            )
        pieces = [(shards[m], fulls[m].at[rows])]
        if m in (5, 6):
            strip = 2 * part
            pieces = [
                (
                    shards[m].at[:, pl.ds(pl.multiple_of((parity + 2 * i) * strip, 128), strip)],
                    fulls[m].at[rows, pl.ds(i * strip, strip)],
                )
                for i in range(2)
            ]
        stage_own[m] = []
        for i, (src, dst) in enumerate(pieces):
            own = pltpu.make_async_copy(src, dst, local.at[m, i])
            own.start()
            stage_own[m].append((own, remote(m, 19 * i, src, dst, mate)))

    def sources(k):
        return lax.rem(z + 4 - k, 4)

    def tick(now):
        m = now
        if m < count:
            depth = shards[m].shape[0]
            stage_x[m], stage_y[m] = [], []
            for i, k in enumerate(turns(m)):
                stage_z[m][i].wait_recv()
                piece = region(m, sources(k), r, 0, depth)
                stage_x[m].append(remote(m, 3 + k, piece, piece, along_x))
                stage_y[m].append(remote(m, 6 + k, piece, piece, along_y))
        if now + 2 < count:
            begin(now + 2)
        m = now - 1
        if 0 <= m < count:
            depth = shards[m].shape[0]
            half = depth // 2
            stage_d[m] = []
            for i, k in enumerate(turns(m)):
                stage_x[m][i].wait_recv()
                piece = region(m, sources(k), across_x, 0, half)
                stage_d[m].append(remote(m, 9 + k, piece, piece, along_y))
                stage_y[m][i].wait_recv()
                piece = region(m, sources(k), across_y, half, half)
                stage_d[m].append(remote(m, 12 + k, piece, piece, along_x))
        m = now - 2
        if 0 <= m < count:
            depth = shards[m].shape[0]
            stage_c[m] = []
            for i, k in enumerate(turns(m)):
                stage_d[m][2 * i].wait_recv()
                stage_d[m][2 * i + 1].wait_recv()
                piece = fulls[m].at[rows_of(m, sources(k), c, 0, depth)]
                stage_c[m].append(remote(m, 15 + k, piece, piece, mate))

    loads = {}

    def arrive(m):
        for own, swapped in stage_own[m]:
            own.wait()
            swapped.wait_recv()
        for copy in stage_c[m]:
            copy.wait_recv()
        if m < 5:
            loads[m] = pltpu.make_async_copy(fulls[m], weights[m], load_sem.at[m])
            loads[m].start()

    def product(left, right, store):
        width = right.shape[1]

        def one(j):
            columns = at(j, 512)
            store(
                columns,
                jnp.dot(left[...], right[:, columns], preferred_element_type=jnp.float32),
            )

        loop(width // 512, one)

    def first_norm():
        def one(i):
            rows = at(i, 32)
            values = tokens[rows, :].astype(jnp.float32)
            scale = lax.rsqrt(jnp.mean(values * values, axis=-1, keepdims=True) + epsilon)
            normed[rows, :] = (values * scale * gain1[...]).astype(jnp.bfloat16)

        loop(12, one)
        save(0, normed, outs[0])

    def mark():
        place_of = lax.broadcasted_iota(jnp.int32, (144, 8), 0) + (s * 128 - 8)
        column = lax.broadcasted_iota(jnp.int32, (136, 8), 1)
        for row in range(3):
            met = (place_of == bounds[row : row + 1, :]).astype(jnp.float32)
            reset = jnp.max(met, axis=1, keepdims=True) + (place_of == 0).astype(jnp.float32)
            keep = 1.0 - reset
            second = keep * pltpu.roll(keep, 1, 0)
            third = second * pltpu.roll(keep, 2, 0)
            first, second, third = keep[8:], second[8:], third[8:]
            values = jnp.where(column == 1, first, reset[8:])
            values = jnp.where(column == 2, second, values)
            marks[row] = jnp.where(column == 3, third, values)
        save(11, marks, saved_marks)

    def rec_product():
        loads[0].wait()

        def store(columns, values):
            for row in range(3):
                padded[row, 8:136, columns] = values[row * 128 : (row + 1) * 128]

        product(normed, w_rec, store)
        return near(0, padded.at[:, pl.ds(128, 8), :], rim, others[0])

    def convolution(copy):
        copy.wait_recv()
        for row in range(3):
            padded[row, 0:8, :] = jnp.where(s > 0, rim[row], 0.0)
        save(1, padded, outs[1])

        def one(i):
            row, rest = lax.div(i, 12), lax.rem(i, 12)
            block, column = lax.div(rest, 3), lax.rem(rest, 3)
            columns = at(column, 512)
            window = padded[row, pl.ds(pl.multiple_of(block * 32, 8), 40), columns]
            rows = pl.ds(pl.multiple_of(row * 128 + block * 32, 32), 32)
            spot = pl.ds(pl.multiple_of(block * 32, 32), 32)
            total = conv_b[:, columns] + conv_w[0:1, columns] * window[8:]
            for k in (1, 2, 3):
                shifted = pltpu.roll(window, k, 0)[8:]
                total = total + conv_w[k : k + 1, columns] * (marks[row, spot, k : k + 1] * shifted)
            conv_out[rows, columns] = total
            conv_low[rows, columns] = total.astype(jnp.bfloat16)

        loop(36, one)
        save(2, conv_out, outs[2])
        save(3, conv_low, outs[3])

    def gate_product(which):
        target, weight = ((rate_pre, w_rate), (input_pre, w_input))[which]
        loads[1 + which].wait()

        def store(columns, values):
            target[:, columns] = values

        product(conv_low, weight, store)
        save(4 + which, target, outs[4 + which])

    def branch_product():
        loads[3].wait()

        def store(columns, values):
            branch_pre[:, columns] = values

        product(normed, w_branch, store)
        save(7, branch_pre, outs[7])

    def local_scan():
        def one(column):
            columns = at(column, 512)

            def tile(t, carry):
                results = []
                for row in range(3):
                    rows = pl.ds(pl.multiple_of(row * 128 + t * 8, 8), 8)
                    reset = marks[row, pl.ds(pl.multiple_of(t * 8, 8), 8), 0:1]
                    rate_gate = jax.nn.sigmoid(rate_pre[rows, columns] + rate_b[:, columns])
                    input_gate = jax.nn.sigmoid(input_pre[rows, columns] + input_b[:, columns])
                    log_rate = decay_scale[:, columns] * rate_gate
                    keep = 1.0 - reset
                    pace = jnp.exp(log_rate)
                    left = minus_expm1(2.0 * log_rate, pace * pace)
                    scale = reset + keep * jnp.sqrt(left)
                    a, b = tile_scan(
                        pace * keep, scale * input_gate * conv_out[rows, columns], False
                    )
                    b = b + a * carry[2 * row + 1]
                    a = a * carry[2 * row]
                    products[rows, columns] = a
                    states[rows, columns] = b
                    results += [a[7:8], b[7:8]]
                return tuple(results)

            ones, zeros = jnp.ones((1, 512), jnp.float32), jnp.zeros((1, 512), jnp.float32)
            last = lax.fori_loop(0, 16, tile, (ones, zeros) * 3)
            for row in range(3):
                ends[row : row + 1, columns] = last[2 * row]
                ends[3 + row : 4 + row, columns] = last[2 * row + 1]

        loop(3, one)
        return [near(k, ends, got.at[k], others[k - 1]) for k in range(1, 8)]

    def carry_states(copies):
        for copy in copies:
            copy.wait_recv()

        def one(column):
            columns = at(column, 512)
            state = jnp.zeros((3, 512), jnp.float32)
            for k in range(7, 0, -1):
                after = got[k, 3:6, columns] + got[k, 0:3, columns] * state
                state = jnp.where(k <= s, after, state)
            carry_in[0:3, columns] = state

        loop(3, one)
        save(10, carry_in, outs[10])

    def mix():
        def one(i):
            row, rest = lax.div(i, 12), lax.rem(i, 12)
            block, column = lax.div(rest, 3), lax.rem(rest, 3)
            columns = at(column, 512)
            rows = pl.ds(pl.multiple_of(row * 128 + block * 32, 32), 32)
            carried = carry_in[pl.ds(row, 1), columns]
            state = states[rows, columns] + products[rows, columns] * carried
            states[rows, columns] = state
            mixed_in[rows, columns] = (state * gelu_of(branch_pre[rows, columns])).astype(
                jnp.bfloat16
            )

        loop(36, one)
        save(6, states, outs[6])
        save(8, mixed_in, outs[8])

    def out_product():
        loads[4].wait()

        def store(columns, values):
            resid[:, columns] = tokens[:, columns].astype(jnp.float32) + values

        product(mixed_in, w_out, store)
        save(9, resid, outs[9])

        def one(i):
            rows = at(i, 32)
            values = resid[rows, :]
            scale = lax.rsqrt(jnp.mean(values * values, axis=-1, keepdims=True) + epsilon)
            normed2[rows, :] = (values * scale * gain2[...]).astype(jnp.bfloat16)

        loop(12, one)
        save(13, normed2, pair_normed2.at[pl.ds(0, tok)])
        return near(8, normed2, pair_normed2.at[pl.ds(tok, tok)], twin)

    tok = tokens.shape[0]
    cotangent_copy = near(9, cotangent, pair_cotangent.at[pl.ds(tok, tok)], twin)
    save(12, cotangent, pair_cotangent.at[pl.ds(0, tok)])
    carry_in[...] = jnp.zeros_like(carry_in)
    ends[...] = jnp.zeros_like(ends)
    begin(0)
    begin(1)
    mark()
    first_norm()
    tick(0)
    tick(1)
    tick(2)
    arrive(0)
    rim_copy = rec_product()
    tick(3)
    arrive(1)
    convolution(rim_copy)
    gate_product(0)
    tick(4)
    arrive(2)
    gate_product(1)
    tick(5)
    ends_copies = local_scan()
    arrive(3)
    branch_product()
    tick(6)
    carry_states(ends_copies)
    mix()
    arrive(4)
    tick(7)
    normed2_copy = out_product()
    tick(8)
    tick(9)
    for m in (5, 6, 7):
        arrive(m)
    cotangent_copy.wait_recv()
    normed2_copy.wait_recv()
    for copy in live:
        copy.wait_send()
    for copy in pending:
        copy.wait()


def forward_all(shards, cotangent, tokens, bounds, gains, vectors):
    low, full = jnp.bfloat16, jnp.float32
    tok, model = tokens.shape
    rec = shards[0].shape[1]
    shape = jax.ShapeDtypeStruct
    saved = (
        shape((tok, model), low),
        shape((3, 136, rec), full),
        shape((tok, rec), full),
        shape((tok, rec), low),
        shape((tok, rec), full),
        shape((tok, rec), full),
        shape((tok, rec), full),
        shape((tok, rec), full),
        shape((tok, rec), low),
        shape((tok, model), full),
        shape((8, rec), full),
        shape((2 * tok, model), low),
        shape((2 * tok, model), low),
        shape((3, 136, 8), full),
    )
    fulls = [shape((a.shape[0] * 8, a.shape[1]), low) for a in shards]
    for m in (5, 6):
        fulls[m] = shape((fulls[m].shape[0], fulls[m].shape[1] // 2), low)
    fulls[7] = shape((fulls[7].shape[0] // 2, fulls[7].shape[1]), low)
    fulls = tuple(fulls)
    results = pl.pallas_call(
        forward_kernel,
        out_shape=fulls + saved,
        in_specs=[VMEM] * 13,
        out_specs=(ANY,) * 22,
        scratch_shapes=[pltpu.VMEM(a.shape, low) for a in fulls[:5]]
        + [
            pltpu.VMEM((tok, model), low),
            pltpu.VMEM((3, 136, rec), full),
            pltpu.VMEM((tok, rec), full),
            pltpu.VMEM((tok, rec), low),
            pltpu.VMEM((tok, rec), full),
            pltpu.VMEM((tok, rec), full),
            pltpu.VMEM((tok, rec), full),
            pltpu.VMEM((tok, rec), full),
            pltpu.VMEM((tok, rec), full),
            pltpu.VMEM((tok, rec), low),
            pltpu.VMEM((tok, model), full),
            pltpu.VMEM((tok, model), low),
            pltpu.VMEM((3, 8, rec), full),
            pltpu.VMEM((8, rec), full),
            pltpu.VMEM((8, 8, rec), full),
            pltpu.VMEM((8, rec), full),
            pltpu.VMEM((3, 136, 8), full),
            pltpu.SemaphoreType.DMA((8, 20)),
            pltpu.SemaphoreType.DMA((8, 20)),
            pltpu.SemaphoreType.DMA((8, 2)),
            pltpu.SemaphoreType.DMA((10,)),
            pltpu.SemaphoreType.DMA((10,)),
            pltpu.SemaphoreType.DMA((5,)),
            pltpu.SemaphoreType.DMA((14,)),
        ],
        compiler_params=pltpu.CompilerParams(
            collective_id=0, has_side_effects=True, vmem_limit_bytes=60 * 1024 * 1024
        ),
        name="recurrent_forward",
    )(*shards, cotangent, tokens, bounds, gains, vectors)
    return results[:8], results[8:]

class Reduction:
    def __init__(self, kinds, grads, outs, scratch, sems, swapped=()):
        self.kinds, self.swapped = kinds, swapped
        self.grads, self.outs = grads, outs
        self.count = len(grads)
        self.held, self.own, self.first, self.second, self.third, self.final = scratch
        self.send, self.recv, self.local = sems
        self.live = []
        self.at_c, self.at_one, self.at_two, self.at_z, self.at_end, self.at_out = (
            {} for _ in range(6)
        )
        r, s, z, c = place()
        self.r, self.z, self.c = r, z, c
        self.mate, self.along_x, self.along_y, self.along_z = peers_of(r, s, z, c)
        self.diagonal = (3 - r, s)
        self.rx, self.ry = lax.rem(r, 2), lax.div(r, 2)

    def peers(self):
        return [self.mate, self.along_x, self.along_y, self.diagonal] + self.along_z

    def remote(self, m, slot, src, dst, device):
        copy = pltpu.make_async_remote_copy(
            src_ref=src,
            dst_ref=dst,
            send_sem=self.send.at[m, slot],
            recv_sem=self.recv.at[m, slot],
            device_id=device,
            device_id_type=MESH,
        )
        copy.start()
        self.live.append(copy)
        return copy

    def load(self, m, q):
        part = self.held[m].shape[3]
        near = pltpu.make_async_copy(
            self.grads[m].at[:, self.c, :, pl.ds(q * part, part)],
            self.own[m].at[q % 2],
            self.local.at[m, q],
        )
        near.start()
        return near

    def begin(self, m):
        part = self.held[m].shape[3]
        if m < len(self.swapped):
            far = [
                pltpu.make_async_copy(
                    self.swapped[m].at[:, :, pl.ds(q * part, part)],
                    self.held[m].at[q],
                    self.local.at[m, 5 + q],
                )
                for q in range(4)
            ]
            for copy in far:
                copy.start()
            self.at_c[m] = (far, [self.load(m, 0), self.load(m, 1)])
            return
        far = [
            self.remote(
                m,
                q,
                self.grads[m].at[:, 1 - self.c, :, pl.ds(q * part, part)],
                self.held[m].at[q],
                self.mate,
            )
            for q in range(4)
        ]
        self.at_c[m] = (far, [self.load(m, 0), self.load(m, 1)])

    def stage_core(self, m):
        held, own = self.held[m], self.own[m]
        half = held.shape[2] // 2
        far, near = self.at_c[m]
        for q in range(4):
            if m < len(self.swapped):
                far[q].wait()
            else:
                far[q].wait_recv()
            near[q].wait()

            def add(b):
                held[q, b] = held[q, b] + own[q % 2, b]

            loop(held.shape[1], add)
            if q < 2:
                near.append(self.load(m, q + 2))
        if self.kinds[m] == "early":
            self.at_z[m] = [
                self.remote(
                    m,
                    9 + k,
                    held.at[:, lax.rem(self.z + k, 4)],
                    self.third[m].at[k - 1],
                    self.along_z[k - 1],
                )
                for k in (1, 2, 3)
            ]
        else:
            self.send_one(m)

    def sources(self, m):
        return pl.ds(self.z, 1) if self.kinds[m] == "early" else pl.ds(0, self.held[m].shape[1])

    def stage_early(self, m):
        held, third, z = self.held[m], self.third[m], self.z
        blocks = held.shape[2] // 32
        for copy in self.at_z[m]:
            copy.wait_recv()

        def add(i):
            q, rows = lax.div(i, blocks), at(lax.rem(i, blocks), 32)
            values = held[q, z, rows, :].astype(jnp.float32)
            for k in range(3):
                values = values + third[k, q, rows, :].astype(jnp.float32)
            held[q, z, rows, :] = values.astype(jnp.bfloat16)

        loop(4 * blocks, add)
        self.send_one(m)

    def send_one(self, m):
        held, half, sources = self.held[m], self.held[m].shape[2] // 2, self.sources(m)
        self.at_one[m] = []
        for other in range(2):
            quarter = other * 2 + (1 - self.rx)
            self.at_one[m].append(
                self.remote(
                    m,
                    4 + other,
                    held.at[quarter, sources, pl.ds(0, half)],
                    self.first[m].at[0, other],
                    self.along_x,
                )
            )
            quarter = (1 - self.ry) * 2 + other
            self.at_one[m].append(
                self.remote(
                    m,
                    6 + other,
                    held.at[quarter, sources, pl.ds(half, half)],
                    self.first[m].at[1, other],
                    self.along_y,
                )
            )

    def stage_one(self, m):
        held, first, sources = self.held[m], self.first[m], self.sources(m)
        count, half = first.shape[2], held.shape[2] // 2
        base = self.z if self.kinds[m] == "early" else 0
        for copy in self.at_one[m]:
            copy.wait_recv()

        def add(i):
            other, b = lax.div(i, count), lax.rem(i, count)
            at_b = base + b
            qx = other * 2 + self.rx
            held[qx, at_b, :half] = held[qx, at_b, :half] + first[0, other, b]
            qy = self.ry * 2 + other
            held[qy, at_b, half:] = held[qy, at_b, half:] + first[1, other, b]

        loop(2 * count, add)
        self.at_two[m] = [
            self.remote(
                m,
                8,
                held.at[(1 - self.ry) * 2 + self.rx, sources, pl.ds(0, half)],
                self.second[m].at[0],
                self.along_y,
            ),
            self.remote(
                m,
                9,
                held.at[self.ry * 2 + (1 - self.rx), sources, pl.ds(half, half)],
                self.second[m].at[1],
                self.along_x,
            ),
        ]

    def stage_two(self, m):
        held, second, r = self.held[m], self.second[m], self.r
        count, half = second.shape[1], held.shape[2] // 2
        early = self.kinds[m] == "early"
        base = self.z if early else 0
        for copy in self.at_two[m]:
            copy.wait_recv()

        def add(b):
            held[r, base + b, :half] = held[r, base + b, :half] + second[0, b]
            held[r, base + b, half:] = held[r, base + b, half:] + second[1, b]

        loop(count, add)
        if early:
            self.final[m][r] = held[r, self.z]
            self.send_final(m)
            return
        rows = self.kinds[m] == "rows"
        self.at_z[m] = []
        for k in (2,) if rows else (1, 2, 3):
            target = 1 - lax.div(self.z, 2) if rows else lax.rem(self.z + k, 4)
            self.at_z[m].append(
                self.remote(
                    m,
                    9 + k,
                    held.at[r, target],
                    self.third[m].at[0 if rows else k - 1],
                    self.along_z[k - 1],
                )
            )

    def stage_z(self, m):
        held, third, final, r = self.held[m], self.third[m], self.final[m], self.r
        for copy in self.at_z[m]:
            copy.wait_recv()
        kind, parity = self.kinds[m], lax.rem(self.z, 2)
        own = lax.div(self.z, 2) if kind == "rows" else self.z

        def add(i):
            rows = at(i, 32)

            def total(first, *terms):
                values = first.astype(jnp.float32)
                for k in terms:
                    values = values + third[k, rows, :].astype(jnp.float32)
                return values.astype(jnp.bfloat16)

            mine = held[r, own, rows, :]
            if kind == "columns":
                final[r, parity, rows, :] = total(mine, 1)
                final[r, 1 - parity, rows, :] = total(third[0, rows, :], 2)
            else:
                final[r, rows, :] = total(mine, *((0,) if kind == "rows" else (0, 1, 2)))

        loop(held.shape[2] // 32, add)
        self.send_final(m)

    def send_final(self, m):
        final, r = self.final[m], self.r
        self.at_end[m] = [
            self.remote(m, 13 + i, final.at[r], final.at[r], device)
            for i, device in enumerate((self.along_x, self.along_y, self.diagonal))
        ]

    def stage_end(self, m):
        for copy in self.at_end[m]:
            copy.wait_recv()
        out = pltpu.make_async_copy(self.final[m], self.outs[m], self.local.at[m, 4])
        out.start()
        self.at_out[m] = out

    def tick(self, now):
        stages = (self.stage_core, self.stage_one, self.stage_two, self.stage_z, self.stage_end)
        for late, stage in enumerate(stages):
            if 0 <= now - late < self.count:
                stage(now - late)
            if late == 0 and now + 2 < self.count:
                self.begin(now + 2)

    def ticks(self):
        return self.count + 4

    def close(self):
        for m in range(self.count):
            self.at_out[m].wait()
        for copy in self.live:
            copy.wait_send()


REDUCTION_SEMS = 16


def reduction_memory(kinds, grads):
    low = jnp.bfloat16
    count = len(grads)
    shapes = [(2 if kind == "rows" else 4,) + quarter_shape(kind, g) for kind, g in zip(kinds, grads)]
    scratch = [pltpu.VMEM((4, zs, k, n), low) for zs, k, n in shapes]
    scratch += [pltpu.VMEM((2, zs, k, n), low) for zs, k, n in shapes]
    summed = [1 if kind == "early" else zs for kind, (zs, _, _) in zip(kinds, shapes)]
    scratch += [pltpu.VMEM((2, 2, zs, k // 2, n), low) for zs, (_, k, n) in zip(summed, shapes)]
    scratch += [pltpu.VMEM((2, zs, k // 2, n), low) for zs, (_, k, n) in zip(summed, shapes)]
    scratch += [
        pltpu.VMEM((3, 4, k, n) if kind == "early" else (zs - 1, k, n), low)
        for kind, (zs, k, n) in zip(kinds, shapes)
    ]
    scratch += [pltpu.VMEM(a.shape, low) for a in reduced_shapes(kinds, grads)]
    return scratch + [
        pltpu.SemaphoreType.DMA((count, REDUCTION_SEMS)),
        pltpu.SemaphoreType.DMA((count, REDUCTION_SEMS)),
        pltpu.SemaphoreType.DMA((count, 9)),
    ]


def reduced_shapes(kinds, grads):
    shapes = [(kind, quarter_shape(kind, g)) for kind, g in zip(kinds, grads)]
    return tuple(
        jax.ShapeDtypeStruct((4, 2, k, n) if kind == "columns" else (4, k, n), jnp.bfloat16)
        for kind, (k, n) in shapes
    )


def take_reduction(take, count):
    scratch = [take(count) for _ in range(6)]
    return scratch, take(3)


def taker(refs):
    refs = list(refs)

    def take(n):
        taken, refs[:n] = refs[:n], []
        return taken

    return take


def split_rows(kind, grad):
    zs = 2 if kind == "rows" else 4
    return grad.reshape(zs, 2, grad.shape[0] // (2 * zs), grad.shape[1])


def quarter_shape(kind, grad):
    return grad.shape[0] // (4 if kind == "rows" else 8), grad.shape[1] // 4


def finish_kernel(count, plain, *refs):
    take = taker(refs)
    blocks, same = take(count), take(plain)
    wholes, same_out = take(count), take(plain)
    brought, wide, passed = take(count), take(count), take(plain)
    sem_in, sem_out = take(2)
    entries = [(a, b, i) for i, (a, b) in enumerate(zip(blocks + same, brought + passed))]
    fetched = [pltpu.make_async_copy(a, b, sem_in.at[i]) for a, b, i in entries]
    for copy in fetched:
        copy.start()
    written = []
    for i in range(count + plain):
        fetched[i].wait()
        if i < count:
            block, whole = brought[i], wide[i]
            part = block.shape[-1]
            for q in range(4):
                for half in range(2 if len(block.shape) == 4 else 1):
                    if len(block.shape) == 4:
                        column = ((half + 2 * (q // 2)) * 2 + q % 2) * part
                        values = block[q, half]
                    else:
                        column, values = q * part, block[q]
                    whole[:, column : column + part] = values.astype(jnp.float32)
            copy = pltpu.make_async_copy(whole, wholes[i], sem_out.at[i])
        else:
            copy = pltpu.make_async_copy(passed[i - count], same_out[i - count], sem_out.at[i])
        copy.start()
        written.append(copy)
    for copy in written:
        copy.wait()


def finish(blocks, same):
    shape = jax.ShapeDtypeStruct
    whole = [(b.shape[-2], b.size // b.shape[-2]) for b in blocks]
    count, plain = len(blocks), len(same)
    results = pl.pallas_call(
        functools.partial(finish_kernel, count, plain),
        out_shape=tuple(shape(a, jnp.float32) for a in whole)
        + tuple(shape(a.shape, a.dtype) for a in same),
        in_specs=[ANY] * (count + plain),
        out_specs=(ANY,) * (count + plain),
        scratch_shapes=[pltpu.VMEM(b.shape, b.dtype) for b in blocks]
        + [pltpu.VMEM(a, jnp.float32) for a in whole]
        + [pltpu.VMEM(a.shape, a.dtype) for a in same]
        + [pltpu.SemaphoreType.DMA((count + plain,))] * 2,
        compiler_params=pltpu.CompilerParams(vmem_limit_bytes=62 * 1024 * 1024),
        name="widen_gradients",
    )(*blocks, *same)
    return results[:count], results[count:]


REC_KINDS = ("early", "all", "all", "all")


def reduce_kernel(count, swaps, *refs):
    take = taker(refs)
    grads = take(count)
    swapped = take(swaps)
    (small_in,) = take(1)
    outs = take(count)
    (small_out,) = take(1)
    reduction = Reduction(REC_KINDS, grads, outs, *take_reduction(take, count), swapped)
    small_held, small_got, small_send, small_recv = take(4)
    z = reduction.z
    greet(reduction.peers())
    small_copies = []

    def swap_small(slot, source, device):
        copy = pltpu.make_async_remote_copy(
            src_ref=small_held.at[source],
            dst_ref=small_got.at[slot],
            send_sem=small_send.at[slot],
            recv_sem=small_recv.at[slot],
            device_id=device,
            device_id_type=MESH,
        )
        copy.start()
        small_copies.append(copy)
        return copy

    small_held[0] = small_in[...]
    swap = swap_small(0, 0, reduction.mate)
    begin, core, early = reduction.begin, reduction.stage_core, reduction.stage_early
    one, two, over_z, end = (
        reduction.stage_one,
        reduction.stage_two,
        reduction.stage_z,
        reduction.stage_end,
    )
    begin(0)
    begin(1)
    core(0)
    begin(2)
    core(1)
    begin(3)
    core(2)
    one(1)
    swap.wait_recv()
    small_held[1] = small_held[0] + small_got[0]
    swap = swap_small(1, 1, reduction.along_x)
    core(3)
    one(2)
    two(1)
    swap.wait_recv()
    small_held[2] = small_held[1] + small_got[1]
    swap = swap_small(2, 2, reduction.along_y)
    one(3)
    early(0)
    two(2)
    swap.wait_recv()
    small_held[3] = small_held[2] + small_got[2]
    spread = [swap_small(2 + k, 3, reduction.along_z[k - 1]) for k in (1, 2, 3)]
    over_z(1)
    one(0)
    two(3)
    two(0)
    over_z(2)
    end(1)
    over_z(3)
    end(0)
    end(2)
    end(3)
    for copy in spread:
        copy.wait_recv()
    small_got[6] = small_held[3]
    total = None
    for source in range(4):
        k = lax.rem(z + 4 - source, 4)
        slot = jnp.where(k == 0, 6, 2 + k)
        term = small_got[slot]
        total = term if total is None else total + term
    small_out[...] = total
    for copy in small_copies:
        copy.wait_send()
    reduction.close()


def reduce_all(grads, swapped, small, tag):
    count = len(grads)
    kinds = REC_KINDS
    results = pl.pallas_call(
        functools.partial(reduce_kernel, count, len(swapped)),
        out_shape=reduced_shapes(kinds, grads)
        + (jax.ShapeDtypeStruct(small.shape, small.dtype),),
        in_specs=[ANY] * (count + len(swapped)) + [VMEM],
        out_specs=(ANY,) * count + (VMEM,),
        scratch_shapes=reduction_memory(kinds, grads)
        + [
            pltpu.VMEM((4,) + small.shape, small.dtype),
            pltpu.VMEM((7,) + small.shape, small.dtype),
            pltpu.SemaphoreType.DMA((6,)),
            pltpu.SemaphoreType.DMA((6,)),
        ],
        compiler_params=pltpu.CompilerParams(
            collective_id=tag, has_side_effects=True, vmem_limit_bytes=60 * 1024 * 1024
        ),
        name="reduce_grads",
    )(*[split_rows("all", g) for g in grads], *swapped, small)
    return results[:count], results[count]


def backward_kernel(kinds, *refs):
    take = taker(refs)
    count = len(kinds)
    grads = take(count - 1)
    part_mixed, part_normed2, twin_normed2 = take(3)
    full_out, full_rate, full_input, full_branch, full_rec = take(5)
    saved_states, saved_branch, saved_rate, saved_input, saved_conv, saved_rec = take(6)
    marks, tokens, cotangent, resid, normed, conv_low, mixed_in, carried = take(8)
    gains, vectors = take(2)
    gain1, gain2 = gains.at[0:1], gains.at[1:2]
    conv_w, _, rate_b, input_b, decay_scale = split_vectors(vectors)
    outs = take(count)
    d_rate, d_input, d_branch, d_rec, token_grad, mixed, swap_rec, swap_rate = take(8)
    (small,) = take(1)
    parts = take_reduction(take, count)
    (d_out,) = take(1)
    reduction = Reduction(kinds, grads + [d_out], outs, *parts)
    ring, past, branch_pre, rate_pre, input_pre, conv_out = take(6)
    flow, grads_conv, branch_low, rate_low, input_low, stage = take(6)
    rim, ends, got, carry = take(4)
    own_parts, twin_parts, grad_resid, resid_low = take(4)
    near_send, near_recv, load_sem, ring_sem, stage_sem = take(5)
    r, s, z, c = place()
    others = [(r, lax.rem(s + k, 8)) for k in range(1, 8)]
    greet(others + [reduction.along_x, reduction.along_y, reduction.diagonal])
    live = []

    def near(slot, src, dst, device):
        copy = pltpu.make_async_remote_copy(
            src_ref=src,
            dst_ref=dst,
            send_sem=near_send.at[slot],
            recv_sem=near_recv.at[slot],
            device_id=device,
            device_id_type=MESH,
        )
        copy.start()
        live.append(copy)
        return copy

    def bring(slot, src, dst):
        copy = pltpu.make_async_copy(src, dst, load_sem.at[slot])
        copy.start()
        return copy

    tiles = []
    for weight in (full_out, full_rate, full_input, full_branch, full_rec):
        tiles.append([(weight, j) for j in range(weight.shape[0] // 512)])
    out_tiles, rate_tiles, input_tiles, branch_tiles, rec_tiles = tiles
    order = list(out_tiles)
    for pair in zip(rate_tiles, input_tiles):
        order += pair
    for pair in zip(branch_tiles, rec_tiles):
        order += pair
    fetches = {}

    def fetch(i):
        if i < len(order):
            weight, j = order[i]
            copy = pltpu.make_async_copy(
                weight.at[pl.ds(j * 512, 512)],
                ring.at[i % 3, :, pl.ds(0, weight.shape[1])],
                ring_sem.at[i % 3],
            )
            copy.start()
            fetches[i] = copy

    def back_tile(i, left, depth):
        fetches[i].wait()
        return lax.dot_general(
            left[...],
            ring[i % 3, :, pl.ds(0, depth)],
            (((1,), (1,)), ((), ())),
            preferred_element_type=jnp.float32,
        )

    staged = [None, None]
    turn = [0]

    def outer_product(left, right, target):
        for strip in range(left.shape[1] // 256):
            slot = turn[0] % 2
            turn[0] += 1
            if staged[slot] is not None:
                staged[slot].wait()
            rows = pl.ds(strip * 256, 256)
            width = right.shape[1]

            def one(j):
                columns = at(j, 512)
                stage[slot, :, columns] = lax.dot_general(
                    left[:, rows],
                    right[:, columns],
                    (((0,), (0,)), ((), ())),
                    preferred_element_type=jnp.float32,
                ).astype(jnp.bfloat16)

            loop(width // 512, one)
            copy = pltpu.make_async_copy(
                stage.at[slot, :, pl.ds(0, width)], target.at[rows], stage_sem.at[slot]
            )
            copy.start()
            staged[slot] = copy

    def out_weight():
        depth = d_out.shape[2]

        def one(i):
            source, column = lax.div(i, 2), lax.rem(i, 2)
            columns = at(column, 512)
            values = lax.dot_general(
                mixed_in[:, at(source, 2 * depth)],
                resid_low[:, columns],
                (((0,), (0,)), ((), ())),
                preferred_element_type=jnp.float32,
            ).astype(jnp.bfloat16)
            d_out[source, 0, :, columns] = values[:depth]
            d_out[source, 1, :, columns] = values[depth:]

        loop(8, one)

    swaps = []

    def swap_halves(first, source, target):
        for slot in range(2):
            if staged[slot] is not None:
                staged[slot].wait()
                staged[slot] = None
        depth = target.shape[1]
        for block in range(4):
            row = pl.multiple_of((block * 2 + 1 - c) * depth, 16)
            swaps.append(
                near(
                    first + block,
                    source.at[pl.ds(row, depth)],
                    target.at[block],
                    reduction.mate,
                )
            )

    def block_of(i):
        row, block = lax.div(i, 4), lax.rem(i, 4)
        return row, block, pl.ds(pl.multiple_of(row * 128 + block * 32, 32), 32)

    def folded(values):
        return values[0:8] + values[8:16] + values[16:24] + values[24:32]

    def gates(rows, columns, mark_rows):
        rate_gate = jax.nn.sigmoid(rate_pre[rows, columns] + rate_b[:, columns])
        log_rate = decay_scale[:, columns] * rate_gate
        return rate_gate, log_rate, jnp.exp(log_rate)

    def branch_back():
        def one(i):
            column, rest = lax.div(i, 12), lax.rem(i, 12)
            row, block, rows = block_of(rest)
            columns = at(column, 512)
            act, slope = gelu_parts(branch_pre[rows, columns])
            grad = flow[rows, columns]
            state = past[row, pl.ds(pl.multiple_of(block * 32 + 8, 8), 32), columns]
            flow[rows, columns] = grad * act
            branch_low[rows, columns] = (grad * state * slope).astype(jnp.bfloat16)

        loop(36, one)

    def scan_back():
        def one(column):
            columns = at(column, 512)
            spot = lax.broadcasted_iota(jnp.int32, (8, 512), 0)

            def tile(i, state):
                t = 15 - i
                results = []
                for row in range(3):
                    rows = pl.ds(pl.multiple_of(row * 128 + t * 8, 8), 8)
                    keep = 1.0 - marks[row, pl.ds(pl.multiple_of(t * 8, 8), 8), 0:1]
                    _, _, pace = gates(rows, columns, None)
                    decay = pace * keep
                    follow, carry_a, carry_b = state[3 * row : 3 * row + 3]
                    later = jnp.where(spot == 7, follow, pltpu.roll(decay, 7, 0))
                    a, b = tile_scan(later, flow[rows, columns], True)
                    b = b + a * carry_b
                    a = a * carry_a
                    branch_pre[rows, columns] = a
                    flow[rows, columns] = b
                    results += [decay[0:1], a[0:1], b[0:1]]
                return tuple(results)

            ones, zeros = jnp.ones((1, 512), jnp.float32), jnp.zeros((1, 512), jnp.float32)
            last = lax.fori_loop(0, 16, tile, (ones, ones, zeros) * 3)
            for row in range(3):
                decay, a, b = last[3 * row : 3 * row + 3]
                ends[row : row + 1, columns] = decay * a
                ends[3 + row : 4 + row, columns] = decay * b

        loop(3, one)
        return [near(k, ends, got.at[k], others[k - 1]) for k in range(1, 8)]

    def carry_back(copies):
        for copy in copies:
            copy.wait_recv()

        def one(column):
            columns = at(column, 512)
            state = jnp.zeros((3, 512), jnp.float32)
            for ahead in range(7, 0, -1):
                k = 8 - ahead
                after = got[k, 3:6, columns] + got[k, 0:3, columns] * state
                state = jnp.where(s + ahead <= 7, after, state)
            carry[0:3, columns] = state

        loop(3, one)

    def gates_back():
        def one(column):
            columns = at(column, 512)

            def block_step(i, sums):
                row, block, rows = block_of(i)
                mark = pl.ds(pl.multiple_of(block * 32, 32), 32)
                reset = marks[row, mark, 0:1]
                keep = 1.0 - reset
                rate_gate, log_rate, pace = gates(rows, columns, mark)
                input_gate = jax.nn.sigmoid(input_pre[rows, columns] + input_b[:, columns])
                power = pace * pace
                root = jnp.sqrt(minus_expm1(2.0 * log_rate, power))
                scale = reset + keep * root
                conv = conv_out[rows, columns]
                grad = flow[rows, columns] + branch_pre[rows, columns] * carry[
                    pl.ds(row, 1), columns
                ]
                window = past[row, pl.ds(pl.multiple_of(block * 32, 8), 40), columns]
                before = pltpu.roll(window, 1, 0)[8:]
                grad_log = keep * grad * (before * pace - input_gate * conv * power / root)
                decay_sum = rate_gate * grad_log
                rate_grad = decay_scale[:, columns] * decay_sum * (1.0 - rate_gate)
                direct = grad * scale * input_gate
                input_grad = direct * conv * (1.0 - input_gate)
                rate_low[rows, columns] = rate_grad.astype(jnp.bfloat16)
                input_low[rows, columns] = input_grad.astype(jnp.bfloat16)
                rate_pre[rows, columns] = direct
                return (
                    sums[0] + folded(decay_sum),
                    sums[1] + folded(rate_grad),
                    sums[2] + folded(input_grad),
                )

            zeros = jnp.zeros((8, 512), jnp.float32)
            sums = lax.fori_loop(0, 12, block_step, (zeros,) * 3)
            for spot, values in enumerate(sums):
                small[5 + spot : 6 + spot, columns] = jnp.sum(values, axis=0, keepdims=True)

        loop(3, one)

    def conv_back(copy):
        copy.wait_recv()
        for row in range(3):
            grads_conv[row, 128:136, :] = jnp.where(s < 7, rim[row], 0.0)

        def one(column):
            columns = at(column, 512)

            def block_step(i, sums):
                row, block, rows = block_of(i)
                span = pl.ds(pl.multiple_of(block * 32, 8), 40)
                ahead = grads_conv[row, span, columns]
                behind = past[row, span, columns]
                grad = ahead[:32]
                total = conv_w[0:1, columns] * grad
                new = [sums[0] + folded(grad * behind[8:])]
                for k in (1, 2, 3):
                    kept = ahead * marks[row, span, k : k + 1]
                    total = total + conv_w[k : k + 1, columns] * pltpu.roll(kept, 40 - k, 0)[:32]
                    new.append(
                        sums[k] + folded(kept[:32] * pltpu.roll(behind, k, 0)[8:])
                    )
                new.append(sums[4] + folded(grad))
                rate_low[rows, columns] = total.astype(jnp.bfloat16)
                return tuple(new)

            zeros = jnp.zeros((8, 512), jnp.float32)
            sums = lax.fori_loop(0, 12, block_step, (zeros,) * 5)
            for spot, values in enumerate(sums):
                small[spot : spot + 1, columns] = jnp.sum(values, axis=0, keepdims=True)

        loop(3, one)

    def second_norm_back():
        def one(i, total):
            rows = at(i, 16)
            grad = own_parts[1, rows, :].astype(jnp.float32) + twin_parts[1, rows, :].astype(
                jnp.float32
            )
            values = resid[rows, :]
            scale = lax.rsqrt(jnp.mean(values * values, axis=-1, keepdims=True) + epsilon)
            back = grad * gain2[...]
            mean = jnp.mean(values * back, axis=-1, keepdims=True)
            result = cotangent[rows, :].astype(jnp.float32) + scale * back
            result = result - values * (scale * scale * scale * mean)
            grad_resid[rows, :] = result
            resid_low[rows, :] = result.astype(jnp.bfloat16)
            part = grad * values * scale
            return total + part[0:8] + part[8:16]

        total = lax.fori_loop(0, 24, one, jnp.zeros((8, 1024), jnp.float32))
        small[9:10, 0:1024] = jnp.sum(total, axis=0, keepdims=True)

    def mix_back():
        def one(i):
            rows = at(i, 16)
            total = own_parts[0, rows, :].astype(jnp.float32)
            total = total + twin_parts[0, rows, :].astype(jnp.float32)
            own_parts[0, rows, :] = (resid[rows, :] + total).astype(jnp.bfloat16)

        loop(24, one)
        return bring(8, own_parts.at[0], mixed)

    def norm_back():
        def one(i, total):
            rows = at(i, 16)
            values = tokens[rows, :].astype(jnp.float32)
            scale = lax.rsqrt(jnp.mean(values * values, axis=-1, keepdims=True) + epsilon)
            grad = input_pre[rows, pl.ds(0, 1024)]
            back = grad * gain1[...]
            mean = jnp.mean(values * back, axis=-1, keepdims=True)
            result = grad_resid[rows, :] + scale * back - values * (scale * scale * scale * mean)
            own_parts[1, rows, :] = result.astype(jnp.bfloat16)
            part = grad * values * scale
            return total + part[0:8] + part[8:16]

        total = lax.fori_loop(0, 24, one, jnp.zeros((8, 1024), jnp.float32))
        small[8:9, 0:1024] = jnp.sum(total, axis=0, keepdims=True)
        return bring(10, own_parts.at[1], token_grad)

    tok = tokens.shape[0]
    twin = (r, s + 2 - 4 * lax.rem(z, 2))
    reduction.begin(0)
    reduction.begin(1)
    mixed_copy = near(8, part_mixed.at[pl.ds(tok, tok)], twin_parts.at[0], twin)
    part_loads = [
        bring(6, part_normed2.at[pl.ds(0, tok)], own_parts.at[1]),
        bring(9, twin_normed2, twin_parts.at[1]),
        bring(7, part_mixed.at[pl.ds(0, tok)], own_parts.at[0]),
    ]
    loads = [
        bring(0, saved_branch, branch_pre),
        bring(1, saved_states, past.at[:, pl.ds(8, 128), :]),
        bring(2, saved_rate, rate_pre),
        bring(3, saved_input, input_pre),
        bring(4, saved_conv, conv_out),
    ]
    for i in range(3):
        fetch(i)
    small[...] = jnp.zeros_like(small)
    ends[...] = jnp.zeros_like(ends)
    for row in range(3):
        past[row, 0:8, :] = jnp.broadcast_to(carried[row : row + 1, :], (8, past.shape[2]))
    part_loads[0].wait()
    part_loads[1].wait()
    second_norm_back()
    for i in range(3):
        flow[:, pl.ds(i * 512, 512)] = back_tile(i, resid_low, 1024)
        fetch(i + 3)
    reduction.tick(0)
    out_weight()
    loads[0].wait()
    loads[1].wait()
    branch_back()
    reduction.tick(1)
    loads[2].wait()
    copies = scan_back()
    reduction.tick(2)
    part_loads[2].wait()
    mixed_copy.wait_recv()
    mixed_save = mix_back()
    carry_back(copies)
    loads[3].wait()
    loads[4].wait()
    gates_back()
    loads.append(bring(5, saved_rec, past))
    reduction.tick(3)
    at_tile = 3
    for j in range(3):
        columns = pl.ds(j * 512, 512)
        total = rate_pre[:, columns]
        total = total + back_tile(at_tile, rate_low, 1536)
        fetch(at_tile + 3)
        total = total + back_tile(at_tile + 1, input_low, 1536)
        fetch(at_tile + 4)
        at_tile += 2
        for row in range(3):
            grads_conv[row, 0:128, columns] = total[row * 128 : (row + 1) * 128]
    rim_copy = near(0, grads_conv.at[:, pl.ds(0, 8), :], rim, others[6])
    reduction.tick(4)
    outer_product(conv_low, rate_low, d_rate)
    loads[5].wait()
    conv_back(rim_copy)
    swap_halves(9, d_rate, swap_rate)
    reduction.tick(5)
    for j in range(2):
        columns = pl.ds(j * 512, 512)
        total = back_tile(at_tile, branch_low, 1536)
        fetch(at_tile + 3)
        total = total + back_tile(at_tile + 1, rate_low, 1536)
        fetch(at_tile + 4)
        at_tile += 2
        input_pre[:, columns] = total
    outer_product(normed, rate_low, d_rec)
    reduction.tick(6)
    swap_halves(13, d_rec, swap_rec)
    outer_product(conv_low, input_low, d_input)
    outer_product(normed, branch_low, d_branch)
    token_save = norm_back()
    for now in range(7, reduction.ticks()):
        reduction.tick(now)
    for copy in swaps:
        copy.wait_recv()
    mixed_save.wait()
    token_save.wait()
    for copy in staged:
        if copy is not None:
            copy.wait()
    for copy in live:
        copy.wait_send()
    reduction.close()


def backward_all(grads, parts, fulls, saved, local, vectors):
    low, full = jnp.bfloat16, jnp.float32
    shape, memory = jax.ShapeDtypeStruct, pltpu.VMEM
    kinds = ("rows", "columns", "columns", "all")
    count = len(kinds)
    tok, model = local[1].shape
    rec = fulls[0].shape[0]
    all_grads = tuple(grads) + (shape((rec, model), low),)
    out_shape = reduced_shapes(kinds, all_grads) + (
        shape((rec, rec), low),
        shape((rec, rec), low),
        shape((model, rec), low),
        shape((model, rec), low),
        shape((tok, model), low),
        shape((tok, model), low),
        shape((4, model // 8, rec), low),
        shape((4, rec // 8, rec), low),
        shape((16, rec), full),
    )
    results = pl.pallas_call(
        functools.partial(backward_kernel, kinds),
        out_shape=out_shape,
        in_specs=[ANY] * (count + 13) + [VMEM] * 10,
        out_specs=(ANY,) * (count + 8) + (VMEM,),
        scratch_shapes=reduction_memory(kinds, all_grads)
        + [
            memory((4, 2, rec // 8, model), low),
            memory((3, 512, rec), low),
            memory((3, 136, rec), full),
            memory((tok, rec), full),
            memory((tok, rec), full),
            memory((tok, rec), full),
            memory((tok, rec), full),
            memory((tok, rec), full),
            memory((3, 136, rec), full),
            memory((tok, rec), low),
            memory((tok, rec), low),
            memory((tok, rec), low),
            memory((2, 256, rec), low),
            memory((3, 8, rec), full),
            memory((8, rec), full),
            memory((8, 8, rec), full),
            memory((8, rec), full),
            memory((2, tok, model), low),
            memory((2, tok, model), low),
            memory((tok, model), full),
            memory((tok, model), low),
            pltpu.SemaphoreType.DMA((17,)),
            pltpu.SemaphoreType.DMA((17,)),
            pltpu.SemaphoreType.DMA((11,)),
            pltpu.SemaphoreType.DMA((3,)),
            pltpu.SemaphoreType.DMA((2,)),
        ],
        compiler_params=pltpu.CompilerParams(
            collective_id=1, has_side_effects=True, vmem_limit_bytes=62 * 1024 * 1024
        ),
        name="recurrent_backward",
    )(*[split_rows(k, g) for k, g in zip(kinds, grads)], *parts, *fulls, *saved, *local, *vectors)
    return results[:count], results[count:]


def from_behind(block, axis, distance):
    devices = range(lax.axis_size(axis))
    route = [(i - distance, i) for i in devices if i - distance in devices]
    return lax.ppermute(block, axis, route)


def prefix(part, axis, combine, identity, reverse):
    count = lax.axis_size(axis)
    place = lax.axis_index(axis)
    ahead = count - 1 - place if reverse else place
    gathered = jax.tree.map(lambda a: lax.all_gather(a, axis), part)
    state = jax.tree.map(lambda a, e: jnp.zeros_like(a) + jnp.asarray(e, a.dtype), part, identity)

    def one(turn, state):
        source = count - 1 - turn if reverse else turn
        return combine(
            state, jax.tree.map(lambda a: lax.dynamic_index_in_dim(a, source, 0, False), gathered)
        )

    return lax.fori_loop(0, ahead, one, state)


def rms_norm(values, gain):
    return values * lax.rsqrt(jnp.mean(values * values, axis=-1, keepdims=True) + epsilon) * gain


def combine(earlier, latter):
    return (earlier[0] * latter[0], latter[0] * earlier[1] + latter[1])


def conv_masks(padded_resets):
    keep_mask = 1.0 - padded_resets
    first = keep_mask[..., 3:]
    second = first * keep_mask[..., 2:-1]
    third = second * keep_mask[..., 1:-2]
    return (first, second, third)


def convolve(padded, masks, conv_weight, conv_bias):
    result = conv_bias + conv_weight[0] * padded[..., 3:, :]
    result = result + conv_weight[1] * masks[0][..., None] * padded[..., 2:-1, :]
    result = result + conv_weight[2] * masks[1][..., None] * padded[..., 1:-2, :]
    return result + conv_weight[3] * masks[2][..., None] * padded[..., :-3, :]


def gate_terms(rate_pre, input_pre, conv_out, decay_param, rate_bias, input_bias, resets):
    rate_gate = jax.nn.sigmoid(rate_pre + rate_bias)
    input_gate = jax.nn.sigmoid(input_pre + input_bias)
    log_rate = -8.0 * jax.nn.softplus(decay_param) * rate_gate
    keep_mask = 1.0 - resets[..., None]
    decays = jnp.exp(log_rate) * keep_mask
    scales = resets[..., None] + keep_mask * jnp.sqrt(-jnp.expm1(2.0 * log_rate))
    return (decays, scales * input_gate * conv_out)


def forward_product(values, weight):
    return jnp.dot(values, weight, preferred_element_type=jnp.float32)


def outer(left, right):
    return lax.dot_general(
        left, right, (((0,), (0,)), ((), ())), preferred_element_type=jnp.float32
    )


def back_product(grads, weight):
    return lax.dot_general(
        grads, weight, (((1,), (1,)), ((), ())), preferred_element_type=jnp.float32
    )


def plain_body(
    tokens,
    bounds,
    norm1_gain,
    w_branch,
    w_rec,
    conv_weight,
    conv_bias,
    w_rate,
    rate_bias,
    w_input,
    input_bias,
    decay_param,
    w_out,
    norm2_gain,
    w_gate,
    w_up,
    w_down,
    cotangent,
):
    gathered = (
        lax.all_gather(w_branch, "seq", axis=0, tiled=True),
        lax.all_gather(w_rec, "seq", axis=0, tiled=True),
        lax.all_gather(w_rate, "seq", axis=0, tiled=True),
        lax.all_gather(w_input, "seq", axis=0, tiled=True),
        lax.all_gather(w_out, "seq", axis=0, tiled=True),
        lax.all_gather(w_gate, "seq", axis=0, tiled=True),
        lax.all_gather(w_up, "seq", axis=0, tiled=True),
        lax.all_gather(w_down, "seq", axis=0, tiled=True),
    )
    full_branch, full_rec, full_rate, full_input, full_out, full_gate, full_up, full_down = gathered
    row_count, tok_count, model_width = tokens.shape
    rec_width = full_rec.shape[1]
    offset = lax.axis_index("seq") * tok_count
    positions = offset - 3 + jnp.arange(tok_count + 3, dtype=jnp.int32)
    marked = (
        jnp.any(positions[None, :, None] == bounds[:, None, :], axis=2) | (positions == 0)[None, :]
    )
    padded_resets = marked.astype(jnp.float32)
    resets = padded_resets[:, 3:]
    masks = conv_masks(padded_resets)
    inputs = tokens.astype(jnp.float32).reshape(-1, model_width)
    normed = rms_norm(inputs, norm1_gain).astype(jnp.bfloat16)
    branch_pre = forward_product(normed, full_branch)
    rec_in = forward_product(normed, full_rec).reshape(row_count, tok_count, rec_width)
    rim = from_behind(rec_in[:, tok_count - 3 :, :], "seq", 1)
    padded = jnp.concatenate([rim, rec_in], axis=1)
    conv_out = convolve(padded, masks, conv_weight, conv_bias)
    conv_low = conv_out.astype(jnp.bfloat16).reshape(-1, rec_width)
    rate_pre = forward_product(conv_low, full_rate).reshape(conv_out.shape)
    input_pre = forward_product(conv_low, full_input).reshape(conv_out.shape)

    def gates_of(rate_arg, input_arg, conv_arg, decay_arg, rate_arg_bias, input_arg_bias):
        return gate_terms(
            rate_arg, input_arg, conv_arg, decay_arg, rate_arg_bias, input_arg_bias, resets
        )

    decays, drives = gates_of(rate_pre, input_pre, conv_out, decay_param, rate_bias, input_bias)
    prefix_decay, local_states = lax.associative_scan(combine, (decays, drives), axis=1)
    ones_pair = jnp.ones((row_count, rec_width), jnp.float32)
    zeros_pair = jnp.zeros((row_count, rec_width), jnp.float32)
    carry_in = prefix(
        (prefix_decay[:, -1], local_states[:, -1]), "seq", combine, (ones_pair, zeros_pair), False
    )[1]
    states = local_states + prefix_decay * carry_in[:, None, :]
    earlier_states = jnp.concatenate([carry_in[:, None, :], states[:, :-1, :]], axis=1)
    branch_act = jax.nn.gelu(branch_pre, approximate=True).reshape(states.shape)
    mixed_in = (states * branch_act).astype(jnp.bfloat16).reshape(-1, rec_width)
    resid = inputs + forward_product(mixed_in, full_out)
    normed2 = rms_norm(resid, norm2_gain).astype(jnp.bfloat16)
    gate_pre = forward_product(normed2, full_gate)
    up_pre = forward_product(normed2, full_up)
    hidden = (jax.nn.gelu(gate_pre, approximate=True) * up_pre).astype(jnp.bfloat16)
    mixed = (resid + forward_product(hidden, full_down)).astype(jnp.bfloat16).reshape(tokens.shape)
    cot_low = cotangent.reshape(-1, model_width)
    grad_down = outer(hidden, cot_low)
    grad_hidden = back_product(cot_low, full_down)
    _, pull_mlp = jax.vjp(
        lambda gate_arg, up_arg: jax.nn.gelu(gate_arg, approximate=True) * up_arg, gate_pre, up_pre
    )
    grad_gate_pre, grad_up_pre = pull_mlp(grad_hidden)
    gate_low = grad_gate_pre.astype(jnp.bfloat16)
    up_low = grad_up_pre.astype(jnp.bfloat16)
    grad_gate = outer(normed2, gate_low)
    grad_up = outer(normed2, up_low)
    grad_normed2 = back_product(gate_low, full_gate) + back_product(up_low, full_up)
    _, pull_norm2 = jax.vjp(rms_norm, resid, norm2_gain)
    grad_resid_norm, grad_norm2 = pull_norm2(grad_normed2)
    grad_resid = cot_low.astype(jnp.float32) + grad_resid_norm
    resid_low = grad_resid.astype(jnp.bfloat16)
    grad_out = outer(mixed_in, resid_low)
    grad_mixed = back_product(resid_low, full_out).reshape(states.shape)
    grad_states = grad_mixed * branch_act
    _, pull_branch = jax.vjp(lambda pre_arg: jax.nn.gelu(pre_arg, approximate=True), branch_pre)
    branch_low = pull_branch((grad_mixed * states).reshape(-1, rec_width))[0].astype(jnp.bfloat16)
    next_decays = jnp.concatenate([decays[:, 1:, :], ones_pair[:, None, :]], axis=1)
    suffix_decay, local_grads = lax.associative_scan(
        combine, (next_decays, grad_states), axis=1, reverse=True
    )
    element = (prefix_decay[:, -1], decays[:, 0] * local_grads[:, 0])
    carry_back = prefix(element, "seq", combine, (ones_pair, zeros_pair), True)[1]
    state_grads = local_grads + suffix_decay * carry_back[:, None, :]
    _, pull_gates = jax.vjp(
        gates_of, rate_pre, input_pre, conv_out, decay_param, rate_bias, input_bias
    )
    grad_rate_pre, grad_input_pre, grad_conv_direct, grad_decay, grad_rate_bias, grad_input_bias = (
        pull_gates((state_grads * earlier_states, state_grads))
    )
    rate_low = grad_rate_pre.astype(jnp.bfloat16).reshape(-1, rec_width)
    input_low = grad_input_pre.astype(jnp.bfloat16).reshape(-1, rec_width)
    grad_rate = outer(conv_low, rate_low)
    grad_input = outer(conv_low, input_low)
    grad_conv = grad_conv_direct + (
        back_product(rate_low, full_rate) + back_product(input_low, full_input)
    ).reshape(conv_out.shape)
    _, pull_conv = jax.vjp(
        lambda pad_arg, weight_arg, bias_arg: convolve(pad_arg, masks, weight_arg, bias_arg),
        padded,
        conv_weight,
        conv_bias,
    )
    grad_padded, grad_conv_weight, grad_conv_bias = pull_conv(grad_conv)
    rim_back = from_behind(grad_padded[:, :3, :], "seq", -1)
    grad_rec = grad_padded[:, 3:, :] + jnp.concatenate(
        [jnp.zeros((row_count, tok_count - 3, rec_width), jnp.float32), rim_back], axis=1
    )
    rec_low = grad_rec.astype(jnp.bfloat16).reshape(-1, rec_width)
    grad_rec_w = outer(normed, rec_low)
    grad_branch_w = outer(normed, branch_low)
    grad_normed = back_product(branch_low, full_branch) + back_product(rec_low, full_rec)
    _, pull_norm1 = jax.vjp(rms_norm, inputs, norm1_gain)
    grad_inputs, grad_norm1 = pull_norm1(grad_normed)
    token_grad = (grad_resid + grad_inputs).astype(jnp.bfloat16).reshape(tokens.shape)
    grad_mats = (
        grad_branch_w,
        grad_rec_w,
        grad_rate,
        grad_input,
        grad_out,
        grad_gate,
        grad_up,
        grad_down,
    )
    blocks = (
        lax.psum_scatter(grad_mats[0], "seq", scatter_dimension=0, tiled=True),
        lax.psum_scatter(grad_mats[1], "seq", scatter_dimension=0, tiled=True),
        lax.psum_scatter(grad_mats[2], "seq", scatter_dimension=0, tiled=True),
        lax.psum_scatter(grad_mats[3], "seq", scatter_dimension=0, tiled=True),
        lax.psum_scatter(grad_mats[4], "seq", scatter_dimension=0, tiled=True),
        lax.psum_scatter(grad_mats[5], "seq", scatter_dimension=0, tiled=True),
        lax.psum_scatter(grad_mats[6], "seq", scatter_dimension=0, tiled=True),
        lax.psum_scatter(grad_mats[7], "seq", scatter_dimension=0, tiled=True),
    )
    summed = lax.psum(
        (blocks[0], blocks[1], blocks[2], blocks[3], blocks[4], blocks[5], blocks[6], blocks[7]),
        "rows",
    )
    small = lax.psum(
        (
            grad_norm1,
            grad_conv_weight,
            grad_conv_bias,
            grad_rate_bias,
            grad_input_bias,
            grad_decay,
            grad_norm2,
        ),
        ("rows", "seq"),
    )
    return (
        mixed,
        token_grad,
        small[0],
        summed[0],
        summed[1],
        small[1],
        small[2],
        summed[2],
        small[3],
        summed[3],
        small[4],
        small[5],
        summed[4],
        small[6],
        summed[5],
        summed[6],
        summed[7],
    )


def body(*args):
    if lax.axis_size("rows") == 4 and lax.axis_size("seq") == 8:
        return staged_body(*args)
    return plain_body(*args)


def staged_body(
    tokens,
    bounds,
    norm1_gain,
    w_branch,
    w_rec,
    conv_weight,
    conv_bias,
    w_rate,
    rate_bias,
    w_input,
    input_bias,
    decay_param,
    w_out,
    norm2_gain,
    w_gate,
    w_up,
    w_down,
    cotangent,
):
    row_count, tok_count, model_width = tokens.shape
    rec_width = w_rec.shape[1]
    flat_tokens = tokens.reshape(-1, model_width)
    gains = jnp.stack([norm1_gain, norm2_gain])
    vectors = jnp.concatenate(
        [
            conv_weight,
            jnp.stack([conv_bias, rate_bias, input_bias, -8.0 * jax.nn.softplus(decay_param)]),
        ]
    )
    fulls, saved = forward_all(
        (w_rec, w_rate, w_input, w_branch, w_out, w_gate, w_up, w_down),
        cotangent.reshape(-1, model_width),
        flat_tokens,
        bounds,
        gains,
        vectors,
    )
    full_rec, full_rate, full_input, full_branch, full_out, half_gate, half_up, half_down = fulls
    normed, padded, conv_out, conv_low, rate_pre, input_pre = saved[:6]
    states, branch_pre, mixed_in, resid, carried, pair_normed2, pair_cotangent, marks = saved[6:]
    gate_pre = forward_product(pair_normed2, half_gate)
    up_pre = forward_product(pair_normed2, half_up)
    hidden = (jax.nn.gelu(gate_pre, approximate=True) * up_pre).astype(jnp.bfloat16)
    part_mixed = forward_product(hidden, half_down).astype(jnp.bfloat16)
    grad_down = outer(hidden, pair_cotangent)
    grad_hidden = back_product(pair_cotangent, half_down)
    _, pull_mlp = jax.vjp(
        lambda gate_arg, up_arg: jax.nn.gelu(gate_arg, approximate=True) * up_arg, gate_pre, up_pre
    )
    grad_gate_pre, grad_up_pre = pull_mlp(grad_hidden)
    gate_low = grad_gate_pre.astype(jnp.bfloat16)
    up_low = grad_up_pre.astype(jnp.bfloat16)
    part_normed2 = (back_product(gate_low, half_gate) + back_product(up_low, half_up)).astype(
        jnp.bfloat16
    )
    half = part_mixed.shape[0] // 2
    twins = [(s, s + 2 - 4 * (s // 2 % 2)) for s in range(lax.axis_size("seq"))]
    twin_normed2 = lax.ppermute(part_normed2[half:], "seq", twins)
    grad_gate = outer(pair_normed2, gate_low)
    grad_up = outer(pair_normed2, up_low)
    low = jnp.bfloat16
    ff, rest = backward_all(
        [g.astype(low) for g in (grad_down, grad_gate, grad_up)],
        (part_mixed, part_normed2, twin_normed2),
        (full_out, full_rate, full_input, full_branch, full_rec),
        (
            states.reshape(row_count, tok_count, rec_width),
            branch_pre,
            rate_pre,
            input_pre,
            conv_out,
            padded,
        ),
        (
            marks,
            flat_tokens,
            cotangent.reshape(-1, model_width),
            resid,
            normed,
            conv_low,
            mixed_in,
            carried,
        ),
        (gains, vectors),
    )
    reduced, (token_grad, mixed, swap_rec, swap_rate, sums) = tuple(ff), rest[4:]
    rate, into, branch, recur = rest[:4]
    rec, sums = reduce_all((recur, rate, into, branch), (swap_rec, swap_rate), sums, 2)
    (down, gate, up, out, recur, rate, into, branch), (mixed, token_grad) = finish(
        reduced + tuple(rec), (mixed, token_grad)
    )
    return (
        mixed.reshape(tokens.shape),
        token_grad.reshape(tokens.shape),
        sums[8, :model_width],
        branch,
        recur,
        sums[:4],
        sums[4],
        rate,
        sums[6],
        into,
        sums[7],
        -8.0 * jax.nn.sigmoid(decay_param) * sums[5],
        out,
        sums[9, :model_width],
        gate,
        up,
        down,
    )


def solution(mesh):
    in_specs = (
        P("rows", "seq", None),
        P("rows", None),
        P(),
        P("seq", None),
        P("seq", None),
        P(),
        P(),
        P("seq", None),
        P(),
        P("seq", None),
        P(),
        P(),
        P("seq", None),
        P(),
        P("seq", None),
        P("seq", None),
        P("seq", None),
        P("rows", "seq", None),
    )
    out_specs = (
        P("rows", "seq", None),
        P("rows", "seq", None),
        P(),
        P("seq", None),
        P("seq", None),
        P(),
        P(),
        P("seq", None),
        P(),
        P("seq", None),
        P(),
        P(),
        P("seq", None),
        P(),
        P("seq", None),
        P("seq", None),
        P("seq", None),
    )
    return jax.shard_map(
        body, mesh=mesh, in_specs=in_specs, out_specs=out_specs, check_vma=False)
```

```python
import functools

import jax
import jax.numpy as jnp
from jax import lax
from jax.experimental import pallas as pl
from jax.experimental.pallas import tpu as pltpu
from jax.sharding import PartitionSpec as P

epsilon = 1e-06
MESH = pl.DeviceIdType.MESH
ANY = pl.BlockSpec(memory_space=pl.ANY)
VMEM = pl.BlockSpec(memory_space=pltpu.VMEM)


def place():
    r = lax.axis_index("rows")
    s = lax.axis_index("seq")
    return r, s, lax.div(s, 2), lax.rem(s, 2)


def greet(peers):
    barrier = pltpu.get_barrier_semaphore()
    for peer in peers:
        pl.semaphore_signal(barrier, inc=1, device_id=peer, device_id_type=MESH)
    pl.semaphore_wait(barrier, len(peers))


def peers_of(r, s, z, c):
    mate = (r, s + 1 - 2 * c)
    along_x = (r + 1 - 2 * lax.rem(r, 2), s)
    along_y = (lax.rem(r + 2, 4), s)
    along_z = [(r, lax.rem(z + k, 4) * 2 + c) for k in (1, 2, 3)]
    return mate, along_x, along_y, along_z


def gelu_parts(v):
    inner = 0.7978845608028654 * (v + 0.044715 * v * v * v)
    t = jnp.tanh(inner)
    slope = 0.7978845608028654 * (1.0 + 0.134145 * v * v)
    return 0.5 * v * (1.0 + t), 0.5 * (1.0 + t) + 0.5 * v * (1.0 - t * t) * slope


def gelu_of(v):
    return 0.5 * v * (1.0 + jnp.tanh(0.7978845608028654 * (v + 0.044715 * v * v * v)))


def minus_expm1(v, power):
    total = 1.0 / 40320.0
    for term in (5040.0, 720.0, 120.0, 24.0, 6.0, 2.0, 1.0):
        total = total * v + 1.0 / term
    return jnp.where(v > -0.5, -v * total, 1.0 - power)


def tile_scan(a, b, reverse):
    spot = lax.broadcasted_iota(jnp.int32, a.shape, 0)
    for distance in (1, 2, 4):
        if reverse:
            inside = spot < 8 - distance
            back_a, back_b = pltpu.roll(a, 8 - distance, 0), pltpu.roll(b, 8 - distance, 0)
        else:
            inside = spot >= distance
            back_a, back_b = pltpu.roll(a, distance, 0), pltpu.roll(b, distance, 0)
        b = b + a * jnp.where(inside, back_b, 0.0)
        a = a * jnp.where(inside, back_a, 1.0)
    return a, b


def loop(count, body):
    def one(i, carry):
        body(i)
        return carry

    lax.fori_loop(0, count, one, 0)


def at(i, size):
    return pl.ds(pl.multiple_of(i * size, size), size)


def split_vectors(ref):
    return ref.at[0:4], ref.at[4:5], ref.at[5:6], ref.at[6:7], ref.at[7:8]


def forward_kernel(*refs):
    refs = list(refs)

    def take(n):
        taken, refs[:n] = refs[:n], []
        return taken

    shards = take(8)
    cotangent, tokens, bounds, gains, vectors = take(5)
    gain1, gain2 = gains.at[0:1], gains.at[1:2]
    conv_w, conv_b, rate_b, input_b, decay_scale = split_vectors(vectors)
    fulls = take(8)
    outs = take(11)
    pair_normed2, pair_cotangent, saved_marks = take(3)
    (w_rec, w_rate, w_input, w_branch, w_out) = weights = take(5)
    normed, padded, conv_out, conv_low, rate_pre, input_pre = take(6)
    products, states, branch_pre, mixed_in, resid, normed2 = take(6)
    rim, ends, got, carry_in, marks = take(5)
    send, recv, local, near_send, near_recv, load_sem, save_sem = refs
    count = 8
    r, s, z, c = place()
    mate, along_x, along_y, along_z = peers_of(r, s, z, c)
    across_x, across_y = along_x[0], along_y[0]
    parity = lax.rem(z, 2)
    twin = (r, s + 2 - 4 * parity)
    others = [(r, lax.rem(s + k, 8)) for k in range(1, 8)]
    greet(others + [along_x, along_y])
    live, pending = [], []

    def start(copy):
        copy.start()
        live.append(copy)
        return copy

    def remote(m, slot, src, dst, device):
        return start(
            pltpu.make_async_remote_copy(
                src_ref=src,
                dst_ref=dst,
                send_sem=send.at[m, slot],
                recv_sem=recv.at[m, slot],
                device_id=device,
                device_id_type=MESH,
            )
        )

    def near(slot, src, dst, device):
        return start(
            pltpu.make_async_remote_copy(
                src_ref=src,
                dst_ref=dst,
                send_sem=near_send.at[slot],
                recv_sem=near_recv.at[slot],
                device_id=device,
                device_id_type=MESH,
            )
        )

    def save(slot, src, dst):
        copy = pltpu.make_async_copy(src, dst, save_sem.at[slot])
        copy.start()
        pending.append(copy)

    def rows_of(m, source, core, begin, length):
        depth = shards[m].shape[0]
        block = lax.div(source, 2) * 2 + core if m == 7 else source * 2 + core
        return pl.ds(pl.multiple_of(block * depth + begin, 16), length)

    def region(m, source, quarter, begin, length):
        part = fulls[m].shape[1] // 4
        column = pl.multiple_of(quarter * part, 128)
        return fulls[m].at[rows_of(m, source, c, begin, length), pl.ds(column, part)]

    def turns(m):
        return (2,) if m == 7 else (1, 2, 3)

    stage_own, stage_z, stage_x, stage_y, stage_d, stage_c = {}, {}, {}, {}, {}, {}

    def begin(m):
        depth, width = shards[m].shape
        part = fulls[m].shape[1] // 4
        rows = rows_of(m, z, c, 0, depth)
        stage_z[m] = []
        for k in turns(m):
            column = r * part
            if m in (5, 6):
                half = lax.rem(parity + k, 2)
                column = (half + 2 * lax.div(r, 2)) * (2 * part) + lax.rem(r, 2) * part
            stage_z[m].append(
                remote(
                    m,
                    k,
                    shards[m].at[:, pl.ds(pl.multiple_of(column, 128), part)],
                    region(m, z, r, 0, depth),
                    along_z[k - 1],
                )
            )
        pieces = [(shards[m], fulls[m].at[rows])]
        if m in (5, 6):
            strip = 2 * part
            pieces = [
                (
                    shards[m].at[:, pl.ds(pl.multiple_of((parity + 2 * i) * strip, 128), strip)],
                    fulls[m].at[rows, pl.ds(i * strip, strip)],
                )
                for i in range(2)
            ]
        stage_own[m] = []
        for i, (src, dst) in enumerate(pieces):
            own = pltpu.make_async_copy(src, dst, local.at[m, i])
            own.start()
            stage_own[m].append((own, remote(m, 19 * i, src, dst, mate)))

    def sources(k):
        return lax.rem(z + 4 - k, 4)

    def tick(now):
        m = now
        if m < count:
            depth = shards[m].shape[0]
            stage_x[m], stage_y[m] = [], []
            for i, k in enumerate(turns(m)):
                stage_z[m][i].wait_recv()
                piece = region(m, sources(k), r, 0, depth)
                stage_x[m].append(remote(m, 3 + k, piece, piece, along_x))
                stage_y[m].append(remote(m, 6 + k, piece, piece, along_y))
        if now + 2 < count:
            begin(now + 2)
        m = now - 1
        if 0 <= m < count:
            depth = shards[m].shape[0]
            half = depth // 2
            stage_d[m] = []
            for i, k in enumerate(turns(m)):
                stage_x[m][i].wait_recv()
                piece = region(m, sources(k), across_x, 0, half)
                stage_d[m].append(remote(m, 9 + k, piece, piece, along_y))
                stage_y[m][i].wait_recv()
                piece = region(m, sources(k), across_y, half, half)
                stage_d[m].append(remote(m, 12 + k, piece, piece, along_x))
        m = now - 2
        if 0 <= m < count:
            depth = shards[m].shape[0]
            stage_c[m] = []
            for i, k in enumerate(turns(m)):
                stage_d[m][2 * i].wait_recv()
                stage_d[m][2 * i + 1].wait_recv()
                piece = fulls[m].at[rows_of(m, sources(k), c, 0, depth)]
                stage_c[m].append(remote(m, 15 + k, piece, piece, mate))

    loads = {}

    def arrive(m):
        for own, swapped in stage_own[m]:
            own.wait()
            swapped.wait_recv()
        for copy in stage_c[m]:
            copy.wait_recv()
        if m < 5:
            loads[m] = pltpu.make_async_copy(fulls[m], weights[m], load_sem.at[m])
            loads[m].start()

    def product(left, right, store):
        width = right.shape[1]

        def one(j):
            columns = at(j, 512)
            store(
                columns,
                jnp.dot(left[...], right[:, columns], preferred_element_type=jnp.float32),
            )

        loop(width // 512, one)

    def first_norm():
        def one(i):
            rows = at(i, 32)
            values = tokens[rows, :].astype(jnp.float32)
            scale = lax.rsqrt(jnp.mean(values * values, axis=-1, keepdims=True) + epsilon)
            normed[rows, :] = (values * scale * gain1[...]).astype(jnp.bfloat16)

        loop(12, one)
        save(0, normed, outs[0])

    def mark():
        place_of = lax.broadcasted_iota(jnp.int32, (144, 8), 0) + (s * 128 - 8)
        column = lax.broadcasted_iota(jnp.int32, (136, 8), 1)
        for row in range(3):
            met = (place_of == bounds[row : row + 1, :]).astype(jnp.float32)
            reset = jnp.max(met, axis=1, keepdims=True) + (place_of == 0).astype(jnp.float32)
            keep = 1.0 - reset
            second = keep * pltpu.roll(keep, 1, 0)
            third = second * pltpu.roll(keep, 2, 0)
            first, second, third = keep[8:], second[8:], third[8:]
            values = jnp.where(column == 1, first, reset[8:])
            values = jnp.where(column == 2, second, values)
            marks[row] = jnp.where(column == 3, third, values)
        save(11, marks, saved_marks)

    def rec_product():
        loads[0].wait()

        def store(columns, values):
            for row in range(3):
                padded[row, 8:136, columns] = values[row * 128 : (row + 1) * 128]

        product(normed, w_rec, store)
        return near(0, padded.at[:, pl.ds(128, 8), :], rim, others[0])

    def convolution(copy):
        copy.wait_recv()
        for row in range(3):
            padded[row, 0:8, :] = jnp.where(s > 0, rim[row], 0.0)
        save(1, padded, outs[1])

        def one(i):
            row, rest = lax.div(i, 12), lax.rem(i, 12)
            block, column = lax.div(rest, 3), lax.rem(rest, 3)
            columns = at(column, 512)
            window = padded[row, pl.ds(pl.multiple_of(block * 32, 8), 40), columns]
            rows = pl.ds(pl.multiple_of(row * 128 + block * 32, 32), 32)
            spot = pl.ds(pl.multiple_of(block * 32, 32), 32)
            total = conv_b[:, columns] + conv_w[0:1, columns] * window[8:]
            for k in (1, 2, 3):
                shifted = pltpu.roll(window, k, 0)[8:]
                total = total + conv_w[k : k + 1, columns] * (marks[row, spot, k : k + 1] * shifted)
            conv_out[rows, columns] = total
            conv_low[rows, columns] = total.astype(jnp.bfloat16)

        loop(36, one)
        save(2, conv_out, outs[2])
        save(3, conv_low, outs[3])

    def gate_product(which):
        target, weight = ((rate_pre, w_rate), (input_pre, w_input))[which]
        loads[1 + which].wait()

        def store(columns, values):
            target[:, columns] = values

        product(conv_low, weight, store)
        save(4 + which, target, outs[4 + which])

    def branch_product():
        loads[3].wait()

        def store(columns, values):
            branch_pre[:, columns] = values

        product(normed, w_branch, store)
        save(7, branch_pre, outs[7])

    def local_scan():
        def one(column):
            columns = at(column, 512)

            def tile(t, carry):
                results = []
                for row in range(3):
                    rows = pl.ds(pl.multiple_of(row * 128 + t * 8, 8), 8)
                    reset = marks[row, pl.ds(pl.multiple_of(t * 8, 8), 8), 0:1]
                    rate_gate = jax.nn.sigmoid(rate_pre[rows, columns] + rate_b[:, columns])
                    input_gate = jax.nn.sigmoid(input_pre[rows, columns] + input_b[:, columns])
                    log_rate = decay_scale[:, columns] * rate_gate
                    keep = 1.0 - reset
                    pace = jnp.exp(log_rate)
                    left = minus_expm1(2.0 * log_rate, pace * pace)
                    scale = reset + keep * jnp.sqrt(left)
                    a, b = tile_scan(
                        pace * keep, scale * input_gate * conv_out[rows, columns], False
                    )
                    b = b + a * carry[2 * row + 1]
                    a = a * carry[2 * row]
                    products[rows, columns] = a
                    states[rows, columns] = b
                    results += [a[7:8], b[7:8]]
                return tuple(results)

            ones, zeros = jnp.ones((1, 512), jnp.float32), jnp.zeros((1, 512), jnp.float32)
            last = lax.fori_loop(0, 16, tile, (ones, zeros) * 3)
            for row in range(3):
                ends[row : row + 1, columns] = last[2 * row]
                ends[3 + row : 4 + row, columns] = last[2 * row + 1]

        loop(3, one)
        return [near(k, ends, got.at[k], others[k - 1]) for k in range(1, 8)]

    def carry_states(copies):
        for copy in copies:
            copy.wait_recv()

        def one(column):
            columns = at(column, 512)
            state = jnp.zeros((3, 512), jnp.float32)
            for k in range(7, 0, -1):
                after = got[k, 3:6, columns] + got[k, 0:3, columns] * state
                state = jnp.where(k <= s, after, state)
            carry_in[0:3, columns] = state

        loop(3, one)
        save(10, carry_in, outs[10])

    def mix():
        def one(i):
            row, rest = lax.div(i, 12), lax.rem(i, 12)
            block, column = lax.div(rest, 3), lax.rem(rest, 3)
            columns = at(column, 512)
            rows = pl.ds(pl.multiple_of(row * 128 + block * 32, 32), 32)
            carried = carry_in[pl.ds(row, 1), columns]
            state = states[rows, columns] + products[rows, columns] * carried
            states[rows, columns] = state
            mixed_in[rows, columns] = (state * gelu_of(branch_pre[rows, columns])).astype(
                jnp.bfloat16
            )

        loop(36, one)
        save(6, states, outs[6])
        save(8, mixed_in, outs[8])

    def out_product():
        loads[4].wait()

        def store(columns, values):
            resid[:, columns] = tokens[:, columns].astype(jnp.float32) + values

        product(mixed_in, w_out, store)
        save(9, resid, outs[9])

        def one(i):
            rows = at(i, 32)
            values = resid[rows, :]
            scale = lax.rsqrt(jnp.mean(values * values, axis=-1, keepdims=True) + epsilon)
            normed2[rows, :] = (values * scale * gain2[...]).astype(jnp.bfloat16)

        loop(12, one)
        save(13, normed2, pair_normed2.at[pl.ds(0, tok)])
        return near(8, normed2, pair_normed2.at[pl.ds(tok, tok)], twin)

    tok = tokens.shape[0]
    cotangent_copy = near(9, cotangent, pair_cotangent.at[pl.ds(tok, tok)], twin)
    save(12, cotangent, pair_cotangent.at[pl.ds(0, tok)])
    carry_in[...] = jnp.zeros_like(carry_in)
    ends[...] = jnp.zeros_like(ends)
    begin(0)
    begin(1)
    mark()
    first_norm()
    tick(0)
    tick(1)
    tick(2)
    arrive(0)
    rim_copy = rec_product()
    tick(3)
    arrive(1)
    convolution(rim_copy)
    gate_product(0)
    tick(4)
    arrive(2)
    gate_product(1)
    tick(5)
    ends_copies = local_scan()
    arrive(3)
    branch_product()
    tick(6)
    carry_states(ends_copies)
    mix()
    arrive(4)
    tick(7)
    normed2_copy = out_product()
    tick(8)
    tick(9)
    for m in (5, 6, 7):
        arrive(m)
    cotangent_copy.wait_recv()
    normed2_copy.wait_recv()
    for copy in live:
        copy.wait_send()
    for copy in pending:
        copy.wait()


def forward_all(shards, cotangent, tokens, bounds, gains, vectors):
    low, full = jnp.bfloat16, jnp.float32
    tok, model = tokens.shape
    rec = shards[0].shape[1]
    shape = jax.ShapeDtypeStruct
    saved = (
        shape((tok, model), low),
        shape((3, 136, rec), full),
        shape((tok, rec), full),
        shape((tok, rec), low),
        shape((tok, rec), full),
        shape((tok, rec), full),
        shape((tok, rec), full),
        shape((tok, rec), full),
        shape((tok, rec), low),
        shape((tok, model), full),
        shape((8, rec), full),
        shape((2 * tok, model), low),
        shape((2 * tok, model), low),
        shape((3, 136, 8), full),
    )
    fulls = [shape((a.shape[0] * 8, a.shape[1]), low) for a in shards]
    for m in (5, 6):
        fulls[m] = shape((fulls[m].shape[0], fulls[m].shape[1] // 2), low)
    fulls[7] = shape((fulls[7].shape[0] // 2, fulls[7].shape[1]), low)
    fulls = tuple(fulls)
    results = pl.pallas_call(
        forward_kernel,
        out_shape=fulls + saved,
        in_specs=[VMEM] * 13,
        out_specs=(ANY,) * 22,
        scratch_shapes=[pltpu.VMEM(a.shape, low) for a in fulls[:5]]
        + [
            pltpu.VMEM((tok, model), low),
            pltpu.VMEM((3, 136, rec), full),
            pltpu.VMEM((tok, rec), full),
            pltpu.VMEM((tok, rec), low),
            pltpu.VMEM((tok, rec), full),
            pltpu.VMEM((tok, rec), full),
            pltpu.VMEM((tok, rec), full),
            pltpu.VMEM((tok, rec), full),
            pltpu.VMEM((tok, rec), full),
            pltpu.VMEM((tok, rec), low),
            pltpu.VMEM((tok, model), full),
            pltpu.VMEM((tok, model), low),
            pltpu.VMEM((3, 8, rec), full),
            pltpu.VMEM((8, rec), full),
            pltpu.VMEM((8, 8, rec), full),
            pltpu.VMEM((8, rec), full),
            pltpu.VMEM((3, 136, 8), full),
            pltpu.SemaphoreType.DMA((8, 20)),
            pltpu.SemaphoreType.DMA((8, 20)),
            pltpu.SemaphoreType.DMA((8, 2)),
            pltpu.SemaphoreType.DMA((10,)),
            pltpu.SemaphoreType.DMA((10,)),
            pltpu.SemaphoreType.DMA((5,)),
            pltpu.SemaphoreType.DMA((14,)),
        ],
        compiler_params=pltpu.CompilerParams(
            collective_id=0, has_side_effects=True, vmem_limit_bytes=60 * 1024 * 1024
        ),
        name="recurrent_forward",
    )(*shards, cotangent, tokens, bounds, gains, vectors)
    return results[:8], results[8:]

class Reduction:
    def __init__(self, kinds, grads, outs, scratch, sems, swapped=()):
        self.kinds, self.swapped = kinds, swapped
        self.grads, self.outs = grads, outs
        self.count = len(grads)
        self.held, self.own, self.first, self.second, self.third, self.final = scratch
        self.send, self.recv, self.local = sems
        self.live = []
        self.at_c, self.at_one, self.at_two, self.at_z = {}, {}, {}, {}
        self.at_end, self.at_last, self.at_out = {}, {}, {}
        r, s, z, c = place()
        self.r, self.z, self.c = r, z, c
        self.mate, self.along_x, self.along_y, self.along_z = peers_of(r, s, z, c)
        self.diagonal = (3 - r, s)
        self.rx, self.ry = lax.rem(r, 2), lax.div(r, 2)

    def peers(self):
        return [self.mate, self.along_x, self.along_y, self.diagonal] + self.along_z

    def remote(self, m, slot, src, dst, device):
        copy = pltpu.make_async_remote_copy(
            src_ref=src,
            dst_ref=dst,
            send_sem=self.send.at[m, slot],
            recv_sem=self.recv.at[m, slot],
            device_id=device,
            device_id_type=MESH,
        )
        copy.start()
        self.live.append(copy)
        return copy

    def load(self, m, q):
        part = self.held[m].shape[3]
        near = pltpu.make_async_copy(
            self.grads[m].at[:, self.c, :, pl.ds(q * part, part)],
            self.own[m].at[q % 2],
            self.local.at[m, q],
        )
        near.start()
        return near

    def begin(self, m):
        part = self.held[m].shape[3]
        if m < len(self.swapped):
            far = [
                pltpu.make_async_copy(
                    self.swapped[m].at[:, :, pl.ds(q * part, part)],
                    self.held[m].at[q],
                    self.local.at[m, 5 + q],
                )
                for q in range(4)
            ]
            for copy in far:
                copy.start()
            self.at_c[m] = (far, [self.load(m, 0), self.load(m, 1)])
            return
        far = [
            self.remote(
                m,
                q,
                self.grads[m].at[:, 1 - self.c, :, pl.ds(q * part, part)],
                self.held[m].at[q],
                self.mate,
            )
            for q in range(4)
        ]
        self.at_c[m] = (far, [self.load(m, 0), self.load(m, 1)])

    def stage_core(self, m):
        held, own = self.held[m], self.own[m]
        half = held.shape[2] // 2
        far, near = self.at_c[m]
        for q in range(4):
            if m < len(self.swapped):
                far[q].wait()
            else:
                far[q].wait_recv()
            near[q].wait()

            def add(b):
                held[q, b] = held[q, b] + own[q % 2, b]

            loop(held.shape[1], add)
            if q < 2:
                near.append(self.load(m, q + 2))
        if self.kinds[m] == "early":
            self.at_z[m] = [
                self.remote(
                    m,
                    9 + k,
                    held.at[:, lax.rem(self.z + k, 4)],
                    self.third[m].at[k - 1],
                    self.along_z[k - 1],
                )
                for k in (1, 2, 3)
            ]
        else:
            self.send_one(m)

    def sources(self, m):
        return pl.ds(self.z, 1) if self.kinds[m] == "early" else pl.ds(0, self.held[m].shape[1])

    def stage_early(self, m):
        held, third, z = self.held[m], self.third[m], self.z
        blocks = held.shape[2] // 32
        for copy in self.at_z[m]:
            copy.wait_recv()

        def add(i):
            q, rows = lax.div(i, blocks), at(lax.rem(i, blocks), 32)
            values = held[q, z, rows, :].astype(jnp.float32)
            for k in range(3):
                values = values + third[k, q, rows, :].astype(jnp.float32)
            held[q, z, rows, :] = values.astype(jnp.bfloat16)

        loop(4 * blocks, add)
        self.send_one(m)

    def send_one(self, m):
        held, half, sources = self.held[m], self.held[m].shape[2] // 2, self.sources(m)
        self.at_one[m] = []
        for other in range(2):
            quarter = other * 2 + (1 - self.rx)
            self.at_one[m].append(
                self.remote(
                    m,
                    4 + other,
                    held.at[quarter, sources, pl.ds(0, half)],
                    self.first[m].at[0, other],
                    self.along_x,
                )
            )
            quarter = (1 - self.ry) * 2 + other
            self.at_one[m].append(
                self.remote(
                    m,
                    6 + other,
                    held.at[quarter, sources, pl.ds(half, half)],
                    self.first[m].at[1, other],
                    self.along_y,
                )
            )

    def stage_one(self, m):
        held, first, sources = self.held[m], self.first[m], self.sources(m)
        count, half = first.shape[2], held.shape[2] // 2
        base = self.z if self.kinds[m] == "early" else 0
        for copy in self.at_one[m]:
            copy.wait_recv()

        def add(i):
            other, b = lax.div(i, count), lax.rem(i, count)
            at_b = base + b
            qx = other * 2 + self.rx
            held[qx, at_b, :half] = held[qx, at_b, :half] + first[0, other, b]
            qy = self.ry * 2 + other
            held[qy, at_b, half:] = held[qy, at_b, half:] + first[1, other, b]

        loop(2 * count, add)
        self.at_two[m] = [
            self.remote(
                m,
                8,
                held.at[(1 - self.ry) * 2 + self.rx, sources, pl.ds(0, half)],
                self.second[m].at[0],
                self.along_y,
            ),
            self.remote(
                m,
                9,
                held.at[self.ry * 2 + (1 - self.rx), sources, pl.ds(half, half)],
                self.second[m].at[1],
                self.along_x,
            ),
        ]

    def stage_two(self, m):
        held, second, r = self.held[m], self.second[m], self.r
        count, half = second.shape[1], held.shape[2] // 2
        early = self.kinds[m] == "early"
        base = self.z if early else 0
        for copy in self.at_two[m]:
            copy.wait_recv()

        def add(b):
            held[r, base + b, :half] = held[r, base + b, :half] + second[0, b]
            held[r, base + b, half:] = held[r, base + b, half:] + second[1, b]

        loop(count, add)
        if early:
            self.final[m][r] = held[r, self.z]
            self.send_final(m)
            return
        rows = self.kinds[m] == "rows"
        self.at_z[m] = []
        for k in (2,) if rows else (1, 2, 3):
            target = 1 - lax.div(self.z, 2) if rows else lax.rem(self.z + k, 4)
            self.at_z[m].append(
                self.remote(
                    m,
                    9 + k,
                    held.at[r, target],
                    self.third[m].at[0 if rows else k - 1],
                    self.along_z[k - 1],
                )
            )

    def stage_z(self, m):
        held, third, final, r = self.held[m], self.third[m], self.final[m], self.r
        for copy in self.at_z[m]:
            copy.wait_recv()
        kind, parity = self.kinds[m], lax.rem(self.z, 2)
        own = lax.div(self.z, 2) if kind == "rows" else self.z

        def add(i):
            rows = at(i, 32)

            def total(first, *terms):
                values = first.astype(jnp.float32)
                for k in terms:
                    values = values + third[k, rows, :].astype(jnp.float32)
                return values.astype(jnp.bfloat16)

            mine = held[r, own, rows, :]
            if kind == "columns":
                final[r, parity, rows, :] = total(mine, 1)
                final[r, 1 - parity, rows, :] = total(third[0, rows, :], 2)
            else:
                final[r, rows, :] = total(mine, *((0,) if kind == "rows" else (0, 1, 2)))

        loop(held.shape[2] // 32, add)
        self.send_final(m)

    def send_final(self, m):
        final, r = self.final[m], self.r
        targets = [self.along_x, self.along_y]
        if m == self.count - 1:
            targets.append(self.diagonal)
        self.at_end[m] = [
            self.remote(m, 13 + i, final.at[r], final.at[r], device)
            for i, device in enumerate(targets)
        ]

    def stage_end(self, m):
        for copy in self.at_end[m]:
            copy.wait_recv()
        if m == self.count - 1:
            self.write(m)
            return
        final = self.final[m]

        def part(quarter, which):
            if self.kinds[m] == "columns":
                return final.at[quarter, which]
            half = final.shape[1] // 2
            return final.at[quarter, pl.ds(which * half, half)]

        from_x, from_y = part(self.along_x[0], 0), part(self.along_y[0], 1)
        self.at_last[m] = [
            self.remote(m, 15, from_x, from_x, self.along_y),
            self.remote(m, 16, from_y, from_y, self.along_x),
        ]

    def stage_last(self, m):
        for copy in self.at_last[m]:
            copy.wait_recv()
        self.write(m)

    def write(self, m):
        out = pltpu.make_async_copy(self.final[m], self.outs[m], self.local.at[m, 4])
        out.start()
        self.at_out[m] = out

    def tick(self, now):
        stages = (self.stage_core, self.stage_one, self.stage_two, self.stage_z, self.stage_end)
        for late, stage in enumerate(stages):
            if 0 <= now - late < self.count:
                stage(now - late)
            if late == 0 and now + 2 < self.count:
                self.begin(now + 2)
        if 0 <= now - 5 < self.count - 1:
            self.stage_last(now - 5)

    def ticks(self):
        return self.count + 4

    def close(self):
        for m in range(self.count):
            self.at_out[m].wait()
        for copy in self.live:
            copy.wait_send()


REDUCTION_SEMS = 17


def reduction_memory(kinds, grads):
    low = jnp.bfloat16
    count = len(grads)
    shapes = [(2 if kind == "rows" else 4,) + quarter_shape(kind, g) for kind, g in zip(kinds, grads)]
    scratch = [pltpu.VMEM((4, zs, k, n), low) for zs, k, n in shapes]
    scratch += [pltpu.VMEM((2, zs, k, n), low) for zs, k, n in shapes]
    summed = [1 if kind == "early" else zs for kind, (zs, _, _) in zip(kinds, shapes)]
    scratch += [pltpu.VMEM((2, 2, zs, k // 2, n), low) for zs, (_, k, n) in zip(summed, shapes)]
    scratch += [pltpu.VMEM((2, zs, k // 2, n), low) for zs, (_, k, n) in zip(summed, shapes)]
    scratch += [
        pltpu.VMEM((3, 4, k, n) if kind == "early" else (zs - 1, k, n), low)
        for kind, (zs, k, n) in zip(kinds, shapes)
    ]
    scratch += [pltpu.VMEM(a.shape, low) for a in reduced_shapes(kinds, grads)]
    return scratch + [
        pltpu.SemaphoreType.DMA((count, REDUCTION_SEMS)),
        pltpu.SemaphoreType.DMA((count, REDUCTION_SEMS)),
        pltpu.SemaphoreType.DMA((count, 9)),
    ]


def reduced_shapes(kinds, grads):
    shapes = [(kind, quarter_shape(kind, g)) for kind, g in zip(kinds, grads)]
    return tuple(
        jax.ShapeDtypeStruct((4, 2, k, n) if kind == "columns" else (4, k, n), jnp.bfloat16)
        for kind, (k, n) in shapes
    )


def take_reduction(take, count):
    scratch = [take(count) for _ in range(6)]
    return scratch, take(3)


def taker(refs):
    refs = list(refs)

    def take(n):
        taken, refs[:n] = refs[:n], []
        return taken

    return take


def split_rows(kind, grad):
    zs = 2 if kind == "rows" else 4
    return grad.reshape(zs, 2, grad.shape[0] // (2 * zs), grad.shape[1])


def quarter_shape(kind, grad):
    return grad.shape[0] // (4 if kind == "rows" else 8), grad.shape[1] // 4


def finish_kernel(count, plain, *refs):
    take = taker(refs)
    blocks, same = take(count), take(plain)
    wholes, same_out = take(count), take(plain)
    brought, wide, passed = take(count), take(count), take(plain)
    sem_in, sem_out = take(2)
    entries = [(a, b, i) for i, (a, b) in enumerate(zip(blocks + same, brought + passed))]
    fetched = [pltpu.make_async_copy(a, b, sem_in.at[i]) for a, b, i in entries]
    for copy in fetched:
        copy.start()
    written = []
    for i in range(count + plain):
        fetched[i].wait()
        if i < count:
            block, whole = brought[i], wide[i]
            part = block.shape[-1]
            for q in range(4):
                for half in range(2 if len(block.shape) == 4 else 1):
                    if len(block.shape) == 4:
                        column = ((half + 2 * (q // 2)) * 2 + q % 2) * part
                        values = block[q, half]
                    else:
                        column, values = q * part, block[q]
                    whole[:, column : column + part] = values.astype(jnp.float32)
            copy = pltpu.make_async_copy(whole, wholes[i], sem_out.at[i])
        else:
            copy = pltpu.make_async_copy(passed[i - count], same_out[i - count], sem_out.at[i])
        copy.start()
        written.append(copy)
    for copy in written:
        copy.wait()


def finish(blocks, same):
    shape = jax.ShapeDtypeStruct
    whole = [(b.shape[-2], b.size // b.shape[-2]) for b in blocks]
    count, plain = len(blocks), len(same)
    results = pl.pallas_call(
        functools.partial(finish_kernel, count, plain),
        out_shape=tuple(shape(a, jnp.float32) for a in whole)
        + tuple(shape(a.shape, a.dtype) for a in same),
        in_specs=[ANY] * (count + plain),
        out_specs=(ANY,) * (count + plain),
        scratch_shapes=[pltpu.VMEM(b.shape, b.dtype) for b in blocks]
        + [pltpu.VMEM(a, jnp.float32) for a in whole]
        + [pltpu.VMEM(a.shape, a.dtype) for a in same]
        + [pltpu.SemaphoreType.DMA((count + plain,))] * 2,
        compiler_params=pltpu.CompilerParams(vmem_limit_bytes=62 * 1024 * 1024),
        name="widen_gradients",
    )(*blocks, *same)
    return results[:count], results[count:]


REC_KINDS = ("early", "all", "all", "all")


def reduce_kernel(count, swaps, *refs):
    take = taker(refs)
    grads = take(count)
    swapped = take(swaps)
    (small_in,) = take(1)
    outs = take(count)
    (small_out,) = take(1)
    reduction = Reduction(REC_KINDS, grads, outs, *take_reduction(take, count), swapped)
    small_held, small_got, small_send, small_recv = take(4)
    z = reduction.z
    greet(reduction.peers())
    small_copies = []

    def swap_small(slot, source, device):
        copy = pltpu.make_async_remote_copy(
            src_ref=small_held.at[source],
            dst_ref=small_got.at[slot],
            send_sem=small_send.at[slot],
            recv_sem=small_recv.at[slot],
            device_id=device,
            device_id_type=MESH,
        )
        copy.start()
        small_copies.append(copy)
        return copy

    small_held[0] = small_in[...]
    swap = swap_small(0, 0, reduction.mate)
    begin, core, early = reduction.begin, reduction.stage_core, reduction.stage_early
    one, two, over_z = reduction.stage_one, reduction.stage_two, reduction.stage_z
    end, last = reduction.stage_end, reduction.stage_last
    begin(0)
    begin(1)
    core(0)
    begin(2)
    core(1)
    begin(3)
    core(2)
    one(1)
    swap.wait_recv()
    small_held[1] = small_held[0] + small_got[0]
    swap = swap_small(1, 1, reduction.along_x)
    core(3)
    one(2)
    two(1)
    swap.wait_recv()
    small_held[2] = small_held[1] + small_got[1]
    swap = swap_small(2, 2, reduction.along_y)
    one(3)
    early(0)
    two(2)
    swap.wait_recv()
    small_held[3] = small_held[2] + small_got[2]
    spread = [swap_small(2 + k, 3, reduction.along_z[k - 1]) for k in (1, 2, 3)]
    over_z(1)
    one(0)
    two(3)
    two(0)
    over_z(2)
    end(1)
    over_z(3)
    end(0)
    last(1)
    end(2)
    last(0)
    end(3)
    last(2)
    for copy in spread:
        copy.wait_recv()
    small_got[6] = small_held[3]
    total = None
    for source in range(4):
        k = lax.rem(z + 4 - source, 4)
        slot = jnp.where(k == 0, 6, 2 + k)
        term = small_got[slot]
        total = term if total is None else total + term
    small_out[...] = total
    for copy in small_copies:
        copy.wait_send()
    reduction.close()


def reduce_all(grads, swapped, small, tag):
    count = len(grads)
    kinds = REC_KINDS
    results = pl.pallas_call(
        functools.partial(reduce_kernel, count, len(swapped)),
        out_shape=reduced_shapes(kinds, grads)
        + (jax.ShapeDtypeStruct(small.shape, small.dtype),),
        in_specs=[ANY] * (count + len(swapped)) + [VMEM],
        out_specs=(ANY,) * count + (VMEM,),
        scratch_shapes=reduction_memory(kinds, grads)
        + [
            pltpu.VMEM((4,) + small.shape, small.dtype),
            pltpu.VMEM((7,) + small.shape, small.dtype),
            pltpu.SemaphoreType.DMA((6,)),
            pltpu.SemaphoreType.DMA((6,)),
        ],
        compiler_params=pltpu.CompilerParams(
            collective_id=tag, has_side_effects=True, vmem_limit_bytes=60 * 1024 * 1024
        ),
        name="reduce_grads",
    )(*[split_rows("all", g) for g in grads], *swapped, small)
    return results[:count], results[count]


def backward_kernel(kinds, *refs):
    take = taker(refs)
    count = len(kinds)
    grads = take(count - 1)
    part_mixed, part_normed2, twin_normed2 = take(3)
    full_out, full_rate, full_input, full_branch, full_rec = take(5)
    saved_states, saved_branch, saved_rate, saved_input, saved_conv, saved_rec = take(6)
    marks, tokens, cotangent, resid, normed, conv_low, mixed_in, carried = take(8)
    gains, vectors = take(2)
    gain1, gain2 = gains.at[0:1], gains.at[1:2]
    conv_w, _, rate_b, input_b, decay_scale = split_vectors(vectors)
    outs = take(count)
    d_rate, d_input, d_branch, d_rec, token_grad, mixed, swap_rec, swap_rate = take(8)
    (small,) = take(1)
    parts = take_reduction(take, count)
    (d_out,) = take(1)
    reduction = Reduction(kinds, grads + [d_out], outs, *parts)
    ring, past, branch_pre, rate_pre, input_pre, conv_out = take(6)
    flow, grads_conv, branch_low, rate_low, input_low, stage = take(6)
    rim, ends, got, carry = take(4)
    own_parts, twin_parts, grad_resid, resid_low = take(4)
    near_send, near_recv, load_sem, ring_sem, stage_sem = take(5)
    r, s, z, c = place()
    others = [(r, lax.rem(s + k, 8)) for k in range(1, 8)]
    greet(others + [reduction.along_x, reduction.along_y, reduction.diagonal])
    live = []

    def near(slot, src, dst, device):
        copy = pltpu.make_async_remote_copy(
            src_ref=src,
            dst_ref=dst,
            send_sem=near_send.at[slot],
            recv_sem=near_recv.at[slot],
            device_id=device,
            device_id_type=MESH,
        )
        copy.start()
        live.append(copy)
        return copy

    def bring(slot, src, dst):
        copy = pltpu.make_async_copy(src, dst, load_sem.at[slot])
        copy.start()
        return copy

    tiles = []
    for weight in (full_out, full_rate, full_input, full_branch, full_rec):
        tiles.append([(weight, j) for j in range(weight.shape[0] // 512)])
    out_tiles, rate_tiles, input_tiles, branch_tiles, rec_tiles = tiles
    order = list(out_tiles)
    for pair in zip(rate_tiles, input_tiles):
        order += pair
    for pair in zip(branch_tiles, rec_tiles):
        order += pair
    fetches = {}

    def fetch(i):
        if i < len(order):
            weight, j = order[i]
            copy = pltpu.make_async_copy(
                weight.at[pl.ds(j * 512, 512)],
                ring.at[i % 3, :, pl.ds(0, weight.shape[1])],
                ring_sem.at[i % 3],
            )
            copy.start()
            fetches[i] = copy

    def back_tile(i, left, depth):
        fetches[i].wait()
        return lax.dot_general(
            left[...],
            ring[i % 3, :, pl.ds(0, depth)],
            (((1,), (1,)), ((), ())),
            preferred_element_type=jnp.float32,
        )

    staged = [None, None]
    turn = [0]

    def outer_product(left, right, target):
        for strip in range(left.shape[1] // 256):
            slot = turn[0] % 2
            turn[0] += 1
            if staged[slot] is not None:
                staged[slot].wait()
            rows = pl.ds(strip * 256, 256)
            width = right.shape[1]

            def one(j):
                columns = at(j, 512)
                stage[slot, :, columns] = lax.dot_general(
                    left[:, rows],
                    right[:, columns],
                    (((0,), (0,)), ((), ())),
                    preferred_element_type=jnp.float32,
                ).astype(jnp.bfloat16)

            loop(width // 512, one)
            copy = pltpu.make_async_copy(
                stage.at[slot, :, pl.ds(0, width)], target.at[rows], stage_sem.at[slot]
            )
            copy.start()
            staged[slot] = copy

    def out_weight():
        depth = d_out.shape[2]

        def one(i):
            source, column = lax.div(i, 2), lax.rem(i, 2)
            columns = at(column, 512)
            values = lax.dot_general(
                mixed_in[:, at(source, 2 * depth)],
                resid_low[:, columns],
                (((0,), (0,)), ((), ())),
                preferred_element_type=jnp.float32,
            ).astype(jnp.bfloat16)
            d_out[source, 0, :, columns] = values[:depth]
            d_out[source, 1, :, columns] = values[depth:]

        loop(8, one)

    swaps = []

    def swap_halves(first, source, target):
        for slot in range(2):
            if staged[slot] is not None:
                staged[slot].wait()
                staged[slot] = None
        depth = target.shape[1]
        for block in range(4):
            row = pl.multiple_of((block * 2 + 1 - c) * depth, 16)
            swaps.append(
                near(
                    first + block,
                    source.at[pl.ds(row, depth)],
                    target.at[block],
                    reduction.mate,
                )
            )

    def block_of(i):
        row, block = lax.div(i, 4), lax.rem(i, 4)
        return row, block, pl.ds(pl.multiple_of(row * 128 + block * 32, 32), 32)

    def folded(values):
        return values[0:8] + values[8:16] + values[16:24] + values[24:32]

    def gates(rows, columns, mark_rows):
        rate_gate = jax.nn.sigmoid(rate_pre[rows, columns] + rate_b[:, columns])
        log_rate = decay_scale[:, columns] * rate_gate
        return rate_gate, log_rate, jnp.exp(log_rate)

    def branch_back():
        def one(i):
            column, rest = lax.div(i, 12), lax.rem(i, 12)
            row, block, rows = block_of(rest)
            columns = at(column, 512)
            act, slope = gelu_parts(branch_pre[rows, columns])
            grad = flow[rows, columns]
            state = past[row, pl.ds(pl.multiple_of(block * 32 + 8, 8), 32), columns]
            flow[rows, columns] = grad * act
            branch_low[rows, columns] = (grad * state * slope).astype(jnp.bfloat16)

        loop(36, one)

    def scan_back():
        def one(column):
            columns = at(column, 512)
            spot = lax.broadcasted_iota(jnp.int32, (8, 512), 0)

            def tile(i, state):
                t = 15 - i
                results = []
                for row in range(3):
                    rows = pl.ds(pl.multiple_of(row * 128 + t * 8, 8), 8)
                    keep = 1.0 - marks[row, pl.ds(pl.multiple_of(t * 8, 8), 8), 0:1]
                    _, _, pace = gates(rows, columns, None)
                    decay = pace * keep
                    follow, carry_a, carry_b = state[3 * row : 3 * row + 3]
                    later = jnp.where(spot == 7, follow, pltpu.roll(decay, 7, 0))
                    a, b = tile_scan(later, flow[rows, columns], True)
                    b = b + a * carry_b
                    a = a * carry_a
                    branch_pre[rows, columns] = a
                    flow[rows, columns] = b
                    results += [decay[0:1], a[0:1], b[0:1]]
                return tuple(results)

            ones, zeros = jnp.ones((1, 512), jnp.float32), jnp.zeros((1, 512), jnp.float32)
            last = lax.fori_loop(0, 16, tile, (ones, ones, zeros) * 3)
            for row in range(3):
                decay, a, b = last[3 * row : 3 * row + 3]
                ends[row : row + 1, columns] = decay * a
                ends[3 + row : 4 + row, columns] = decay * b

        loop(3, one)
        return [near(k, ends, got.at[k], others[k - 1]) for k in range(1, 8)]

    def carry_back(copies):
        for copy in copies:
            copy.wait_recv()

        def one(column):
            columns = at(column, 512)
            state = jnp.zeros((3, 512), jnp.float32)
            for ahead in range(7, 0, -1):
                k = 8 - ahead
                after = got[k, 3:6, columns] + got[k, 0:3, columns] * state
                state = jnp.where(s + ahead <= 7, after, state)
            carry[0:3, columns] = state

        loop(3, one)

    def gates_back():
        def one(column):
            columns = at(column, 512)

            def block_step(i, sums):
                row, block, rows = block_of(i)
                mark = pl.ds(pl.multiple_of(block * 32, 32), 32)
                reset = marks[row, mark, 0:1]
                keep = 1.0 - reset
                rate_gate, log_rate, pace = gates(rows, columns, mark)
                input_gate = jax.nn.sigmoid(input_pre[rows, columns] + input_b[:, columns])
                power = pace * pace
                root = jnp.sqrt(minus_expm1(2.0 * log_rate, power))
                scale = reset + keep * root
                conv = conv_out[rows, columns]
                grad = flow[rows, columns] + branch_pre[rows, columns] * carry[
                    pl.ds(row, 1), columns
                ]
                window = past[row, pl.ds(pl.multiple_of(block * 32, 8), 40), columns]
                before = pltpu.roll(window, 1, 0)[8:]
                grad_log = keep * grad * (before * pace - input_gate * conv * power / root)
                decay_sum = rate_gate * grad_log
                rate_grad = decay_scale[:, columns] * decay_sum * (1.0 - rate_gate)
                direct = grad * scale * input_gate
                input_grad = direct * conv * (1.0 - input_gate)
                rate_low[rows, columns] = rate_grad.astype(jnp.bfloat16)
                input_low[rows, columns] = input_grad.astype(jnp.bfloat16)
                rate_pre[rows, columns] = direct
                return (
                    sums[0] + folded(decay_sum),
                    sums[1] + folded(rate_grad),
                    sums[2] + folded(input_grad),
                )

            zeros = jnp.zeros((8, 512), jnp.float32)
            sums = lax.fori_loop(0, 12, block_step, (zeros,) * 3)
            for spot, values in enumerate(sums):
                small[5 + spot : 6 + spot, columns] = jnp.sum(values, axis=0, keepdims=True)

        loop(3, one)

    def conv_back(copy):
        copy.wait_recv()
        for row in range(3):
            grads_conv[row, 128:136, :] = jnp.where(s < 7, rim[row], 0.0)

        def one(column):
            columns = at(column, 512)

            def block_step(i, sums):
                row, block, rows = block_of(i)
                span = pl.ds(pl.multiple_of(block * 32, 8), 40)
                ahead = grads_conv[row, span, columns]
                behind = past[row, span, columns]
                grad = ahead[:32]
                total = conv_w[0:1, columns] * grad
                new = [sums[0] + folded(grad * behind[8:])]
                for k in (1, 2, 3):
                    kept = ahead * marks[row, span, k : k + 1]
                    total = total + conv_w[k : k + 1, columns] * pltpu.roll(kept, 40 - k, 0)[:32]
                    new.append(
                        sums[k] + folded(kept[:32] * pltpu.roll(behind, k, 0)[8:])
                    )
                new.append(sums[4] + folded(grad))
                rate_low[rows, columns] = total.astype(jnp.bfloat16)
                return tuple(new)

            zeros = jnp.zeros((8, 512), jnp.float32)
            sums = lax.fori_loop(0, 12, block_step, (zeros,) * 5)
            for spot, values in enumerate(sums):
                small[spot : spot + 1, columns] = jnp.sum(values, axis=0, keepdims=True)

        loop(3, one)

    def second_norm_back():
        def one(i, total):
            rows = at(i, 16)
            grad = own_parts[1, rows, :].astype(jnp.float32) + twin_parts[1, rows, :].astype(
                jnp.float32
            )
            values = resid[rows, :]
            scale = lax.rsqrt(jnp.mean(values * values, axis=-1, keepdims=True) + epsilon)
            back = grad * gain2[...]
            mean = jnp.mean(values * back, axis=-1, keepdims=True)
            result = cotangent[rows, :].astype(jnp.float32) + scale * back
            result = result - values * (scale * scale * scale * mean)
            grad_resid[rows, :] = result
            resid_low[rows, :] = result.astype(jnp.bfloat16)
            part = grad * values * scale
            return total + part[0:8] + part[8:16]

        total = lax.fori_loop(0, 24, one, jnp.zeros((8, 1024), jnp.float32))
        small[9:10, 0:1024] = jnp.sum(total, axis=0, keepdims=True)

    def mix_back():
        def one(i):
            rows = at(i, 16)
            total = own_parts[0, rows, :].astype(jnp.float32)
            total = total + twin_parts[0, rows, :].astype(jnp.float32)
            own_parts[0, rows, :] = (resid[rows, :] + total).astype(jnp.bfloat16)

        loop(24, one)
        return bring(8, own_parts.at[0], mixed)

    def norm_back():
        def one(i, total):
            rows = at(i, 16)
            values = tokens[rows, :].astype(jnp.float32)
            scale = lax.rsqrt(jnp.mean(values * values, axis=-1, keepdims=True) + epsilon)
            grad = input_pre[rows, pl.ds(0, 1024)]
            back = grad * gain1[...]
            mean = jnp.mean(values * back, axis=-1, keepdims=True)
            result = grad_resid[rows, :] + scale * back - values * (scale * scale * scale * mean)
            own_parts[1, rows, :] = result.astype(jnp.bfloat16)
            part = grad * values * scale
            return total + part[0:8] + part[8:16]

        total = lax.fori_loop(0, 24, one, jnp.zeros((8, 1024), jnp.float32))
        small[8:9, 0:1024] = jnp.sum(total, axis=0, keepdims=True)
        return bring(10, own_parts.at[1], token_grad)

    tok = tokens.shape[0]
    twin = (r, s + 2 - 4 * lax.rem(z, 2))
    reduction.begin(0)
    reduction.begin(1)
    mixed_copy = near(8, part_mixed.at[pl.ds(tok, tok)], twin_parts.at[0], twin)
    part_loads = [
        bring(6, part_normed2.at[pl.ds(0, tok)], own_parts.at[1]),
        bring(9, twin_normed2, twin_parts.at[1]),
        bring(7, part_mixed.at[pl.ds(0, tok)], own_parts.at[0]),
    ]
    loads = [
        bring(0, saved_branch, branch_pre),
        bring(1, saved_states, past.at[:, pl.ds(8, 128), :]),
        bring(2, saved_rate, rate_pre),
        bring(3, saved_input, input_pre),
        bring(4, saved_conv, conv_out),
    ]
    for i in range(3):
        fetch(i)
    small[...] = jnp.zeros_like(small)
    ends[...] = jnp.zeros_like(ends)
    for row in range(3):
        past[row, 0:8, :] = jnp.broadcast_to(carried[row : row + 1, :], (8, past.shape[2]))
    part_loads[0].wait()
    part_loads[1].wait()
    second_norm_back()
    for i in range(3):
        flow[:, pl.ds(i * 512, 512)] = back_tile(i, resid_low, 1024)
        fetch(i + 3)
    reduction.tick(0)
    loads[0].wait()
    loads[1].wait()
    branch_back()
    loads[2].wait()
    copies = scan_back()
    out_weight()
    reduction.tick(1)
    part_loads[2].wait()
    mixed_copy.wait_recv()
    mixed_save = mix_back()
    reduction.tick(2)
    carry_back(copies)
    loads[3].wait()
    loads[4].wait()
    gates_back()
    loads.append(bring(5, saved_rec, past))
    reduction.tick(3)
    at_tile = 3
    for j in range(3):
        columns = pl.ds(j * 512, 512)
        total = rate_pre[:, columns]
        total = total + back_tile(at_tile, rate_low, 1536)
        fetch(at_tile + 3)
        total = total + back_tile(at_tile + 1, input_low, 1536)
        fetch(at_tile + 4)
        at_tile += 2
        for row in range(3):
            grads_conv[row, 0:128, columns] = total[row * 128 : (row + 1) * 128]
    rim_copy = near(0, grads_conv.at[:, pl.ds(0, 8), :], rim, others[6])
    reduction.tick(4)
    outer_product(conv_low, rate_low, d_rate)
    loads[5].wait()
    conv_back(rim_copy)
    swap_halves(9, d_rate, swap_rate)
    reduction.tick(5)
    for j in range(2):
        columns = pl.ds(j * 512, 512)
        total = back_tile(at_tile, branch_low, 1536)
        fetch(at_tile + 3)
        total = total + back_tile(at_tile + 1, rate_low, 1536)
        fetch(at_tile + 4)
        at_tile += 2
        input_pre[:, columns] = total
    outer_product(normed, rate_low, d_rec)
    reduction.tick(6)
    swap_halves(13, d_rec, swap_rec)
    outer_product(conv_low, input_low, d_input)
    outer_product(normed, branch_low, d_branch)
    token_save = norm_back()
    for now in range(7, reduction.ticks()):
        reduction.tick(now)
    for copy in swaps:
        copy.wait_recv()
    mixed_save.wait()
    token_save.wait()
    for copy in staged:
        if copy is not None:
            copy.wait()
    for copy in live:
        copy.wait_send()
    reduction.close()


def backward_all(grads, parts, fulls, saved, local, vectors):
    low, full = jnp.bfloat16, jnp.float32
    shape, memory = jax.ShapeDtypeStruct, pltpu.VMEM
    kinds = ("rows", "columns", "columns", "all")
    count = len(kinds)
    tok, model = local[1].shape
    rec = fulls[0].shape[0]
    all_grads = tuple(grads) + (shape((rec, model), low),)
    out_shape = reduced_shapes(kinds, all_grads) + (
        shape((rec, rec), low),
        shape((rec, rec), low),
        shape((model, rec), low),
        shape((model, rec), low),
        shape((tok, model), low),
        shape((tok, model), low),
        shape((4, model // 8, rec), low),
        shape((4, rec // 8, rec), low),
        shape((16, rec), full),
    )
    results = pl.pallas_call(
        functools.partial(backward_kernel, kinds),
        out_shape=out_shape,
        in_specs=[ANY] * (count + 13) + [VMEM] * 10,
        out_specs=(ANY,) * (count + 8) + (VMEM,),
        scratch_shapes=reduction_memory(kinds, all_grads)
        + [
            memory((4, 2, rec // 8, model), low),
            memory((3, 512, rec), low),
            memory((3, 136, rec), full),
            memory((tok, rec), full),
            memory((tok, rec), full),
            memory((tok, rec), full),
            memory((tok, rec), full),
            memory((tok, rec), full),
            memory((3, 136, rec), full),
            memory((tok, rec), low),
            memory((tok, rec), low),
            memory((tok, rec), low),
            memory((2, 256, rec), low),
            memory((3, 8, rec), full),
            memory((8, rec), full),
            memory((8, 8, rec), full),
            memory((8, rec), full),
            memory((2, tok, model), low),
            memory((2, tok, model), low),
            memory((tok, model), full),
            memory((tok, model), low),
            pltpu.SemaphoreType.DMA((17,)),
            pltpu.SemaphoreType.DMA((17,)),
            pltpu.SemaphoreType.DMA((11,)),
            pltpu.SemaphoreType.DMA((3,)),
            pltpu.SemaphoreType.DMA((2,)),
        ],
        compiler_params=pltpu.CompilerParams(
            collective_id=1, has_side_effects=True, vmem_limit_bytes=62 * 1024 * 1024
        ),
        name="recurrent_backward",
    )(*[split_rows(k, g) for k, g in zip(kinds, grads)], *parts, *fulls, *saved, *local, *vectors)
    return results[:count], results[count:]


def from_behind(block, axis, distance):
    devices = range(lax.axis_size(axis))
    route = [(i - distance, i) for i in devices if i - distance in devices]
    return lax.ppermute(block, axis, route)


def prefix(part, axis, combine, identity, reverse):
    count = lax.axis_size(axis)
    place = lax.axis_index(axis)
    ahead = count - 1 - place if reverse else place
    gathered = jax.tree.map(lambda a: lax.all_gather(a, axis), part)
    state = jax.tree.map(lambda a, e: jnp.zeros_like(a) + jnp.asarray(e, a.dtype), part, identity)

    def one(turn, state):
        source = count - 1 - turn if reverse else turn
        return combine(
            state, jax.tree.map(lambda a: lax.dynamic_index_in_dim(a, source, 0, False), gathered)
        )

    return lax.fori_loop(0, ahead, one, state)


def rms_norm(values, gain):
    return values * lax.rsqrt(jnp.mean(values * values, axis=-1, keepdims=True) + epsilon) * gain


def combine(earlier, latter):
    return (earlier[0] * latter[0], latter[0] * earlier[1] + latter[1])


def conv_masks(padded_resets):
    keep_mask = 1.0 - padded_resets
    first = keep_mask[..., 3:]
    second = first * keep_mask[..., 2:-1]
    third = second * keep_mask[..., 1:-2]
    return (first, second, third)


def convolve(padded, masks, conv_weight, conv_bias):
    result = conv_bias + conv_weight[0] * padded[..., 3:, :]
    result = result + conv_weight[1] * masks[0][..., None] * padded[..., 2:-1, :]
    result = result + conv_weight[2] * masks[1][..., None] * padded[..., 1:-2, :]
    return result + conv_weight[3] * masks[2][..., None] * padded[..., :-3, :]


def gate_terms(rate_pre, input_pre, conv_out, decay_param, rate_bias, input_bias, resets):
    rate_gate = jax.nn.sigmoid(rate_pre + rate_bias)
    input_gate = jax.nn.sigmoid(input_pre + input_bias)
    log_rate = -8.0 * jax.nn.softplus(decay_param) * rate_gate
    keep_mask = 1.0 - resets[..., None]
    decays = jnp.exp(log_rate) * keep_mask
    scales = resets[..., None] + keep_mask * jnp.sqrt(-jnp.expm1(2.0 * log_rate))
    return (decays, scales * input_gate * conv_out)


def forward_product(values, weight):
    return jnp.dot(values, weight, preferred_element_type=jnp.float32)


def outer(left, right):
    return lax.dot_general(
        left, right, (((0,), (0,)), ((), ())), preferred_element_type=jnp.float32
    )


def back_product(grads, weight):
    return lax.dot_general(
        grads, weight, (((1,), (1,)), ((), ())), preferred_element_type=jnp.float32
    )


def plain_body(
    tokens,
    bounds,
    norm1_gain,
    w_branch,
    w_rec,
    conv_weight,
    conv_bias,
    w_rate,
    rate_bias,
    w_input,
    input_bias,
    decay_param,
    w_out,
    norm2_gain,
    w_gate,
    w_up,
    w_down,
    cotangent,
):
    gathered = (
        lax.all_gather(w_branch, "seq", axis=0, tiled=True),
        lax.all_gather(w_rec, "seq", axis=0, tiled=True),
        lax.all_gather(w_rate, "seq", axis=0, tiled=True),
        lax.all_gather(w_input, "seq", axis=0, tiled=True),
        lax.all_gather(w_out, "seq", axis=0, tiled=True),
        lax.all_gather(w_gate, "seq", axis=0, tiled=True),
        lax.all_gather(w_up, "seq", axis=0, tiled=True),
        lax.all_gather(w_down, "seq", axis=0, tiled=True),
    )
    full_branch, full_rec, full_rate, full_input, full_out, full_gate, full_up, full_down = gathered
    row_count, tok_count, model_width = tokens.shape
    rec_width = full_rec.shape[1]
    offset = lax.axis_index("seq") * tok_count
    positions = offset - 3 + jnp.arange(tok_count + 3, dtype=jnp.int32)
    marked = (
        jnp.any(positions[None, :, None] == bounds[:, None, :], axis=2) | (positions == 0)[None, :]
    )
    padded_resets = marked.astype(jnp.float32)
    resets = padded_resets[:, 3:]
    masks = conv_masks(padded_resets)
    inputs = tokens.astype(jnp.float32).reshape(-1, model_width)
    normed = rms_norm(inputs, norm1_gain).astype(jnp.bfloat16)
    branch_pre = forward_product(normed, full_branch)
    rec_in = forward_product(normed, full_rec).reshape(row_count, tok_count, rec_width)
    rim = from_behind(rec_in[:, tok_count - 3 :, :], "seq", 1)
    padded = jnp.concatenate([rim, rec_in], axis=1)
    conv_out = convolve(padded, masks, conv_weight, conv_bias)
    conv_low = conv_out.astype(jnp.bfloat16).reshape(-1, rec_width)
    rate_pre = forward_product(conv_low, full_rate).reshape(conv_out.shape)
    input_pre = forward_product(conv_low, full_input).reshape(conv_out.shape)

    def gates_of(rate_arg, input_arg, conv_arg, decay_arg, rate_arg_bias, input_arg_bias):
        return gate_terms(
            rate_arg, input_arg, conv_arg, decay_arg, rate_arg_bias, input_arg_bias, resets
        )

    decays, drives = gates_of(rate_pre, input_pre, conv_out, decay_param, rate_bias, input_bias)
    prefix_decay, local_states = lax.associative_scan(combine, (decays, drives), axis=1)
    ones_pair = jnp.ones((row_count, rec_width), jnp.float32)
    zeros_pair = jnp.zeros((row_count, rec_width), jnp.float32)
    carry_in = prefix(
        (prefix_decay[:, -1], local_states[:, -1]), "seq", combine, (ones_pair, zeros_pair), False
    )[1]
    states = local_states + prefix_decay * carry_in[:, None, :]
    earlier_states = jnp.concatenate([carry_in[:, None, :], states[:, :-1, :]], axis=1)
    branch_act = jax.nn.gelu(branch_pre, approximate=True).reshape(states.shape)
    mixed_in = (states * branch_act).astype(jnp.bfloat16).reshape(-1, rec_width)
    resid = inputs + forward_product(mixed_in, full_out)
    normed2 = rms_norm(resid, norm2_gain).astype(jnp.bfloat16)
    gate_pre = forward_product(normed2, full_gate)
    up_pre = forward_product(normed2, full_up)
    hidden = (jax.nn.gelu(gate_pre, approximate=True) * up_pre).astype(jnp.bfloat16)
    mixed = (resid + forward_product(hidden, full_down)).astype(jnp.bfloat16).reshape(tokens.shape)
    cot_low = cotangent.reshape(-1, model_width)
    grad_down = outer(hidden, cot_low)
    grad_hidden = back_product(cot_low, full_down)
    _, pull_mlp = jax.vjp(
        lambda gate_arg, up_arg: jax.nn.gelu(gate_arg, approximate=True) * up_arg, gate_pre, up_pre
    )
    grad_gate_pre, grad_up_pre = pull_mlp(grad_hidden)
    gate_low = grad_gate_pre.astype(jnp.bfloat16)
    up_low = grad_up_pre.astype(jnp.bfloat16)
    grad_gate = outer(normed2, gate_low)
    grad_up = outer(normed2, up_low)
    grad_normed2 = back_product(gate_low, full_gate) + back_product(up_low, full_up)
    _, pull_norm2 = jax.vjp(rms_norm, resid, norm2_gain)
    grad_resid_norm, grad_norm2 = pull_norm2(grad_normed2)
    grad_resid = cot_low.astype(jnp.float32) + grad_resid_norm
    resid_low = grad_resid.astype(jnp.bfloat16)
    grad_out = outer(mixed_in, resid_low)
    grad_mixed = back_product(resid_low, full_out).reshape(states.shape)
    grad_states = grad_mixed * branch_act
    _, pull_branch = jax.vjp(lambda pre_arg: jax.nn.gelu(pre_arg, approximate=True), branch_pre)
    branch_low = pull_branch((grad_mixed * states).reshape(-1, rec_width))[0].astype(jnp.bfloat16)
    next_decays = jnp.concatenate([decays[:, 1:, :], ones_pair[:, None, :]], axis=1)
    suffix_decay, local_grads = lax.associative_scan(
        combine, (next_decays, grad_states), axis=1, reverse=True
    )
    element = (prefix_decay[:, -1], decays[:, 0] * local_grads[:, 0])
    carry_back = prefix(element, "seq", combine, (ones_pair, zeros_pair), True)[1]
    state_grads = local_grads + suffix_decay * carry_back[:, None, :]
    _, pull_gates = jax.vjp(
        gates_of, rate_pre, input_pre, conv_out, decay_param, rate_bias, input_bias
    )
    grad_rate_pre, grad_input_pre, grad_conv_direct, grad_decay, grad_rate_bias, grad_input_bias = (
        pull_gates((state_grads * earlier_states, state_grads))
    )
    rate_low = grad_rate_pre.astype(jnp.bfloat16).reshape(-1, rec_width)
    input_low = grad_input_pre.astype(jnp.bfloat16).reshape(-1, rec_width)
    grad_rate = outer(conv_low, rate_low)
    grad_input = outer(conv_low, input_low)
    grad_conv = grad_conv_direct + (
        back_product(rate_low, full_rate) + back_product(input_low, full_input)
    ).reshape(conv_out.shape)
    _, pull_conv = jax.vjp(
        lambda pad_arg, weight_arg, bias_arg: convolve(pad_arg, masks, weight_arg, bias_arg),
        padded,
        conv_weight,
        conv_bias,
    )
    grad_padded, grad_conv_weight, grad_conv_bias = pull_conv(grad_conv)
    rim_back = from_behind(grad_padded[:, :3, :], "seq", -1)
    grad_rec = grad_padded[:, 3:, :] + jnp.concatenate(
        [jnp.zeros((row_count, tok_count - 3, rec_width), jnp.float32), rim_back], axis=1
    )
    rec_low = grad_rec.astype(jnp.bfloat16).reshape(-1, rec_width)
    grad_rec_w = outer(normed, rec_low)
    grad_branch_w = outer(normed, branch_low)
    grad_normed = back_product(branch_low, full_branch) + back_product(rec_low, full_rec)
    _, pull_norm1 = jax.vjp(rms_norm, inputs, norm1_gain)
    grad_inputs, grad_norm1 = pull_norm1(grad_normed)
    token_grad = (grad_resid + grad_inputs).astype(jnp.bfloat16).reshape(tokens.shape)
    grad_mats = (
        grad_branch_w,
        grad_rec_w,
        grad_rate,
        grad_input,
        grad_out,
        grad_gate,
        grad_up,
        grad_down,
    )
    blocks = (
        lax.psum_scatter(grad_mats[0], "seq", scatter_dimension=0, tiled=True),
        lax.psum_scatter(grad_mats[1], "seq", scatter_dimension=0, tiled=True),
        lax.psum_scatter(grad_mats[2], "seq", scatter_dimension=0, tiled=True),
        lax.psum_scatter(grad_mats[3], "seq", scatter_dimension=0, tiled=True),
        lax.psum_scatter(grad_mats[4], "seq", scatter_dimension=0, tiled=True),
        lax.psum_scatter(grad_mats[5], "seq", scatter_dimension=0, tiled=True),
        lax.psum_scatter(grad_mats[6], "seq", scatter_dimension=0, tiled=True),
        lax.psum_scatter(grad_mats[7], "seq", scatter_dimension=0, tiled=True),
    )
    summed = lax.psum(
        (blocks[0], blocks[1], blocks[2], blocks[3], blocks[4], blocks[5], blocks[6], blocks[7]),
        "rows",
    )
    small = lax.psum(
        (
            grad_norm1,
            grad_conv_weight,
            grad_conv_bias,
            grad_rate_bias,
            grad_input_bias,
            grad_decay,
            grad_norm2,
        ),
        ("rows", "seq"),
    )
    return (
        mixed,
        token_grad,
        small[0],
        summed[0],
        summed[1],
        small[1],
        small[2],
        summed[2],
        small[3],
        summed[3],
        small[4],
        small[5],
        summed[4],
        small[6],
        summed[5],
        summed[6],
        summed[7],
    )


def body(*args):
    if lax.axis_size("rows") == 4 and lax.axis_size("seq") == 8:
        return staged_body(*args)
    return plain_body(*args)


def staged_body(
    tokens,
    bounds,
    norm1_gain,
    w_branch,
    w_rec,
    conv_weight,
    conv_bias,
    w_rate,
    rate_bias,
    w_input,
    input_bias,
    decay_param,
    w_out,
    norm2_gain,
    w_gate,
    w_up,
    w_down,
    cotangent,
):
    row_count, tok_count, model_width = tokens.shape
    rec_width = w_rec.shape[1]
    flat_tokens = tokens.reshape(-1, model_width)
    gains = jnp.stack([norm1_gain, norm2_gain])
    vectors = jnp.concatenate(
        [
            conv_weight,
            jnp.stack([conv_bias, rate_bias, input_bias, -8.0 * jax.nn.softplus(decay_param)]),
        ]
    )
    fulls, saved = forward_all(
        (w_rec, w_rate, w_input, w_branch, w_out, w_gate, w_up, w_down),
        cotangent.reshape(-1, model_width),
        flat_tokens,
        bounds,
        gains,
        vectors,
    )
    full_rec, full_rate, full_input, full_branch, full_out, half_gate, half_up, half_down = fulls
    normed, padded, conv_out, conv_low, rate_pre, input_pre = saved[:6]
    states, branch_pre, mixed_in, resid, carried, pair_normed2, pair_cotangent, marks = saved[6:]
    gate_pre = forward_product(pair_normed2, half_gate)
    up_pre = forward_product(pair_normed2, half_up)
    hidden = (jax.nn.gelu(gate_pre, approximate=True) * up_pre).astype(jnp.bfloat16)
    part_mixed = forward_product(hidden, half_down).astype(jnp.bfloat16)
    grad_down = outer(hidden, pair_cotangent)
    grad_hidden = back_product(pair_cotangent, half_down)
    _, pull_mlp = jax.vjp(
        lambda gate_arg, up_arg: jax.nn.gelu(gate_arg, approximate=True) * up_arg, gate_pre, up_pre
    )
    grad_gate_pre, grad_up_pre = pull_mlp(grad_hidden)
    gate_low = grad_gate_pre.astype(jnp.bfloat16)
    up_low = grad_up_pre.astype(jnp.bfloat16)
    part_normed2 = (back_product(gate_low, half_gate) + back_product(up_low, half_up)).astype(
        jnp.bfloat16
    )
    half = part_mixed.shape[0] // 2
    twins = [(s, s + 2 - 4 * (s // 2 % 2)) for s in range(lax.axis_size("seq"))]
    twin_normed2 = lax.ppermute(part_normed2[half:], "seq", twins)
    grad_gate = outer(pair_normed2, gate_low)
    grad_up = outer(pair_normed2, up_low)
    low = jnp.bfloat16
    ff, rest = backward_all(
        [g.astype(low) for g in (grad_down, grad_gate, grad_up)],
        (part_mixed, part_normed2, twin_normed2),
        (full_out, full_rate, full_input, full_branch, full_rec),
        (
            states.reshape(row_count, tok_count, rec_width),
            branch_pre,
            rate_pre,
            input_pre,
            conv_out,
            padded,
        ),
        (
            marks,
            flat_tokens,
            cotangent.reshape(-1, model_width),
            resid,
            normed,
            conv_low,
            mixed_in,
            carried,
        ),
        (gains, vectors),
    )
    reduced, (token_grad, mixed, swap_rec, swap_rate, sums) = tuple(ff), rest[4:]
    rate, into, branch, recur = rest[:4]
    rec, sums = reduce_all((recur, rate, into, branch), (swap_rec, swap_rate), sums, 2)
    (down, gate, up, out, recur, rate, into, branch), (mixed, token_grad) = finish(
        reduced + tuple(rec), (mixed, token_grad)
    )
    return (
        mixed.reshape(tokens.shape),
        token_grad.reshape(tokens.shape),
        sums[8, :model_width],
        branch,
        recur,
        sums[:4],
        sums[4],
        rate,
        sums[6],
        into,
        sums[7],
        -8.0 * jax.nn.sigmoid(decay_param) * sums[5],
        out,
        sums[9, :model_width],
        gate,
        up,
        down,
    )


def solution(mesh):
    in_specs = (
        P("rows", "seq", None),
        P("rows", None),
        P(),
        P("seq", None),
        P("seq", None),
        P(),
        P(),
        P("seq", None),
        P(),
        P("seq", None),
        P(),
        P(),
        P("seq", None),
        P(),
        P("seq", None),
        P("seq", None),
        P("seq", None),
        P("rows", "seq", None),
    )
    out_specs = (
        P("rows", "seq", None),
        P("rows", "seq", None),
        P(),
        P("seq", None),
        P("seq", None),
        P(),
        P(),
        P("seq", None),
        P(),
        P("seq", None),
        P(),
        P(),
        P("seq", None),
        P(),
        P("seq", None),
        P("seq", None),
        P("seq", None),
    )
    return jax.shard_map(
        body, mesh=mesh, in_specs=in_specs, out_specs=out_specs, check_vma=False)
```

```python
import functools

import jax
import jax.numpy as jnp
from jax import lax
from jax.experimental import pallas as pl
from jax.experimental.pallas import tpu as pltpu
from jax.sharding import PartitionSpec as P

epsilon = 1e-06
MESH = pl.DeviceIdType.MESH
ANY = pl.BlockSpec(memory_space=pl.ANY)
VMEM = pl.BlockSpec(memory_space=pltpu.VMEM)


def place():
    r = lax.axis_index("rows")
    s = lax.axis_index("seq")
    return r, s, lax.div(s, 2), lax.rem(s, 2)


def greet(peers):
    barrier = pltpu.get_barrier_semaphore()
    for peer in peers:
        pl.semaphore_signal(barrier, inc=1, device_id=peer, device_id_type=MESH)
    pl.semaphore_wait(barrier, len(peers))


def peers_of(r, s, z, c):
    mate = (r, s + 1 - 2 * c)
    along_x = (r + 1 - 2 * lax.rem(r, 2), s)
    along_y = (lax.rem(r + 2, 4), s)
    along_z = [(r, lax.rem(z + k, 4) * 2 + c) for k in (1, 2, 3)]
    return mate, along_x, along_y, along_z


def gelu_parts(v):
    inner = 0.7978845608028654 * (v + 0.044715 * v * v * v)
    t = jnp.tanh(inner)
    slope = 0.7978845608028654 * (1.0 + 0.134145 * v * v)
    return 0.5 * v * (1.0 + t), 0.5 * (1.0 + t) + 0.5 * v * (1.0 - t * t) * slope


def gelu_of(v):
    return 0.5 * v * (1.0 + jnp.tanh(0.7978845608028654 * (v + 0.044715 * v * v * v)))


def minus_expm1(v, power):
    total = 1.0 / 40320.0
    for term in (5040.0, 720.0, 120.0, 24.0, 6.0, 2.0, 1.0):
        total = total * v + 1.0 / term
    return jnp.where(v > -0.5, -v * total, 1.0 - power)


def tile_scan(a, b, reverse):
    spot = lax.broadcasted_iota(jnp.int32, a.shape, 0)
    for distance in (1, 2, 4):
        if reverse:
            inside = spot < 8 - distance
            back_a, back_b = pltpu.roll(a, 8 - distance, 0), pltpu.roll(b, 8 - distance, 0)
        else:
            inside = spot >= distance
            back_a, back_b = pltpu.roll(a, distance, 0), pltpu.roll(b, distance, 0)
        b = b + a * jnp.where(inside, back_b, 0.0)
        a = a * jnp.where(inside, back_a, 1.0)
    return a, b


def loop(count, body):
    def one(i, carry):
        body(i)
        return carry

    lax.fori_loop(0, count, one, 0)


def at(i, size):
    return pl.ds(pl.multiple_of(i * size, size), size)


def split_vectors(ref):
    return ref.at[0:4], ref.at[4:5], ref.at[5:6], ref.at[6:7], ref.at[7:8]


def forward_kernel(*refs):
    refs = list(refs)

    def take(n):
        taken, refs[:n] = refs[:n], []
        return taken

    shards = take(8)
    cotangent, tokens, bounds, gains, vectors = take(5)
    gain1, gain2 = gains.at[0:1], gains.at[1:2]
    conv_w, conv_b, rate_b, input_b, decay_scale = split_vectors(vectors)
    fulls = take(8)
    outs = take(11)
    pair_normed2, pair_cotangent, saved_marks = take(3)
    (w_rec, w_rate, w_input, w_branch, w_out) = weights = take(5)
    normed, padded, conv_out, conv_low, rate_pre, input_pre = take(6)
    products, states, branch_pre, mixed_in, resid, normed2 = take(6)
    rim, ends, got, carry_in, marks = take(5)
    send, recv, local, near_send, near_recv, load_sem, save_sem = refs
    count = 8
    r, s, z, c = place()
    mate, along_x, along_y, along_z = peers_of(r, s, z, c)
    across_x, across_y = along_x[0], along_y[0]
    parity = lax.rem(z, 2)
    twin = (r, s + 2 - 4 * parity)
    others = [(r, lax.rem(s + k, 8)) for k in range(1, 8)]
    greet(others + [along_x, along_y])
    live, pending = [], []

    def start(copy):
        copy.start()
        live.append(copy)
        return copy

    def remote(m, slot, src, dst, device):
        return start(
            pltpu.make_async_remote_copy(
                src_ref=src,
                dst_ref=dst,
                send_sem=send.at[m, slot],
                recv_sem=recv.at[m, slot],
                device_id=device,
                device_id_type=MESH,
            )
        )

    def near(slot, src, dst, device):
        return start(
            pltpu.make_async_remote_copy(
                src_ref=src,
                dst_ref=dst,
                send_sem=near_send.at[slot],
                recv_sem=near_recv.at[slot],
                device_id=device,
                device_id_type=MESH,
            )
        )

    def save(slot, src, dst):
        copy = pltpu.make_async_copy(src, dst, save_sem.at[slot])
        copy.start()
        pending.append(copy)

    def rows_of(m, source, core, begin, length):
        depth = shards[m].shape[0]
        block = lax.div(source, 2) * 2 + core if m == 7 else source * 2 + core
        return pl.ds(pl.multiple_of(block * depth + begin, 16), length)

    def region(m, source, quarter, begin, length):
        part = fulls[m].shape[1] // 4
        column = pl.multiple_of(quarter * part, 128)
        return fulls[m].at[rows_of(m, source, c, begin, length), pl.ds(column, part)]

    def turns(m):
        return (2,) if m == 7 else (1, 2, 3)

    stage_own, stage_z, stage_x, stage_y, stage_d, stage_c = {}, {}, {}, {}, {}, {}

    def begin(m):
        depth, width = shards[m].shape
        part = fulls[m].shape[1] // 4
        rows = rows_of(m, z, c, 0, depth)
        stage_z[m] = []
        for k in turns(m):
            column = r * part
            if m in (5, 6):
                half = lax.rem(parity + k, 2)
                column = (half + 2 * lax.div(r, 2)) * (2 * part) + lax.rem(r, 2) * part
            stage_z[m].append(
                remote(
                    m,
                    k,
                    shards[m].at[:, pl.ds(pl.multiple_of(column, 128), part)],
                    region(m, z, r, 0, depth),
                    along_z[k - 1],
                )
            )
        pieces = [(shards[m], fulls[m].at[rows])]
        if m in (5, 6):
            strip = 2 * part
            pieces = [
                (
                    shards[m].at[:, pl.ds(pl.multiple_of((parity + 2 * i) * strip, 128), strip)],
                    fulls[m].at[rows, pl.ds(i * strip, strip)],
                )
                for i in range(2)
            ]
        stage_own[m] = []
        for i, (src, dst) in enumerate(pieces):
            own = pltpu.make_async_copy(src, dst, local.at[m, i])
            own.start()
            stage_own[m].append((own, remote(m, 19 * i, src, dst, mate)))

    def sources(k):
        return lax.rem(z + 4 - k, 4)

    def tick(now):
        m = now
        if m < count:
            depth = shards[m].shape[0]
            stage_x[m], stage_y[m] = [], []
            for i, k in enumerate(turns(m)):
                stage_z[m][i].wait_recv()
                piece = region(m, sources(k), r, 0, depth)
                stage_x[m].append(remote(m, 3 + k, piece, piece, along_x))
                stage_y[m].append(remote(m, 6 + k, piece, piece, along_y))
        if now + 2 < count:
            begin(now + 2)
        m = now - 1
        if 0 <= m < count:
            depth = shards[m].shape[0]
            half = depth // 2
            stage_d[m] = []
            for i, k in enumerate(turns(m)):
                stage_x[m][i].wait_recv()
                piece = region(m, sources(k), across_x, 0, half)
                stage_d[m].append(remote(m, 9 + k, piece, piece, along_y))
                stage_y[m][i].wait_recv()
                piece = region(m, sources(k), across_y, half, half)
                stage_d[m].append(remote(m, 12 + k, piece, piece, along_x))
        m = now - 2
        if 0 <= m < count:
            depth = shards[m].shape[0]
            stage_c[m] = []
            for i, k in enumerate(turns(m)):
                stage_d[m][2 * i].wait_recv()
                stage_d[m][2 * i + 1].wait_recv()
                piece = fulls[m].at[rows_of(m, sources(k), c, 0, depth)]
                stage_c[m].append(remote(m, 15 + k, piece, piece, mate))

    loads = {}

    def arrive(m):
        for own, swapped in stage_own[m]:
            own.wait()
            swapped.wait_recv()
        for copy in stage_c[m]:
            copy.wait_recv()
        if m < 5:
            loads[m] = pltpu.make_async_copy(fulls[m], weights[m], load_sem.at[m])
            loads[m].start()

    def product(left, right, store):
        width = right.shape[1]

        def one(j):
            columns = at(j, 512)
            store(
                columns,
                jnp.dot(left[...], right[:, columns], preferred_element_type=jnp.float32),
            )

        loop(width // 512, one)

    def first_norm():
        def one(i):
            rows = at(i, 32)
            values = tokens[rows, :].astype(jnp.float32)
            scale = lax.rsqrt(jnp.mean(values * values, axis=-1, keepdims=True) + epsilon)
            normed[rows, :] = (values * scale * gain1[...]).astype(jnp.bfloat16)

        loop(12, one)
        save(0, normed, outs[0])

    def mark():
        place_of = lax.broadcasted_iota(jnp.int32, (144, 8), 0) + (s * 128 - 8)
        column = lax.broadcasted_iota(jnp.int32, (136, 8), 1)
        for row in range(3):
            met = (place_of == bounds[row : row + 1, :]).astype(jnp.float32)
            reset = jnp.max(met, axis=1, keepdims=True) + (place_of == 0).astype(jnp.float32)
            keep = 1.0 - reset
            second = keep * pltpu.roll(keep, 1, 0)
            third = second * pltpu.roll(keep, 2, 0)
            first, second, third = keep[8:], second[8:], third[8:]
            values = jnp.where(column == 1, first, reset[8:])
            values = jnp.where(column == 2, second, values)
            marks[row] = jnp.where(column == 3, third, values)
        save(11, marks, saved_marks)

    def rec_product():
        loads[0].wait()

        def store(columns, values):
            for row in range(3):
                padded[row, 8:136, columns] = values[row * 128 : (row + 1) * 128]

        product(normed, w_rec, store)
        return near(0, padded.at[:, pl.ds(128, 8), :], rim, others[0])

    def convolution(copy):
        copy.wait_recv()
        for row in range(3):
            padded[row, 0:8, :] = jnp.where(s > 0, rim[row], 0.0)
        save(1, padded, outs[1])

        def one(i):
            row, rest = lax.div(i, 12), lax.rem(i, 12)
            block, column = lax.div(rest, 3), lax.rem(rest, 3)
            columns = at(column, 512)
            window = padded[row, pl.ds(pl.multiple_of(block * 32, 8), 40), columns]
            rows = pl.ds(pl.multiple_of(row * 128 + block * 32, 32), 32)
            spot = pl.ds(pl.multiple_of(block * 32, 32), 32)
            total = conv_b[:, columns] + conv_w[0:1, columns] * window[8:]
            for k in (1, 2, 3):
                shifted = pltpu.roll(window, k, 0)[8:]
                total = total + conv_w[k : k + 1, columns] * (marks[row, spot, k : k + 1] * shifted)
            conv_out[rows, columns] = total
            conv_low[rows, columns] = total.astype(jnp.bfloat16)

        loop(36, one)
        save(2, conv_out, outs[2])
        save(3, conv_low, outs[3])

    def gate_product(which):
        target, weight = ((rate_pre, w_rate), (input_pre, w_input))[which]
        loads[1 + which].wait()

        def store(columns, values):
            target[:, columns] = values

        product(conv_low, weight, store)
        save(4 + which, target, outs[4 + which])

    def branch_product():
        loads[3].wait()

        def store(columns, values):
            branch_pre[:, columns] = values

        product(normed, w_branch, store)
        save(7, branch_pre, outs[7])

    def local_scan():
        def one(column):
            columns = at(column, 512)

            def tile(t, carry):
                results = []
                for row in range(3):
                    rows = pl.ds(pl.multiple_of(row * 128 + t * 8, 8), 8)
                    reset = marks[row, pl.ds(pl.multiple_of(t * 8, 8), 8), 0:1]
                    rate_gate = jax.nn.sigmoid(rate_pre[rows, columns] + rate_b[:, columns])
                    input_gate = jax.nn.sigmoid(input_pre[rows, columns] + input_b[:, columns])
                    log_rate = decay_scale[:, columns] * rate_gate
                    keep = 1.0 - reset
                    pace = jnp.exp(log_rate)
                    left = minus_expm1(2.0 * log_rate, pace * pace)
                    scale = reset + keep * jnp.sqrt(left)
                    a, b = tile_scan(
                        pace * keep, scale * input_gate * conv_out[rows, columns], False
                    )
                    b = b + a * carry[2 * row + 1]
                    a = a * carry[2 * row]
                    products[rows, columns] = a
                    states[rows, columns] = b
                    results += [a[7:8], b[7:8]]
                return tuple(results)

            ones, zeros = jnp.ones((1, 512), jnp.float32), jnp.zeros((1, 512), jnp.float32)
            last = lax.fori_loop(0, 16, tile, (ones, zeros) * 3)
            for row in range(3):
                ends[row : row + 1, columns] = last[2 * row]
                ends[3 + row : 4 + row, columns] = last[2 * row + 1]

        loop(3, one)
        return [near(k, ends, got.at[k], others[k - 1]) for k in range(1, 8)]

    def carry_states(copies):
        for copy in copies:
            copy.wait_recv()

        def one(column):
            columns = at(column, 512)
            state = jnp.zeros((3, 512), jnp.float32)
            for k in range(7, 0, -1):
                after = got[k, 3:6, columns] + got[k, 0:3, columns] * state
                state = jnp.where(k <= s, after, state)
            carry_in[0:3, columns] = state

        loop(3, one)
        save(10, carry_in, outs[10])

    def mix():
        def one(i):
            row, rest = lax.div(i, 12), lax.rem(i, 12)
            block, column = lax.div(rest, 3), lax.rem(rest, 3)
            columns = at(column, 512)
            rows = pl.ds(pl.multiple_of(row * 128 + block * 32, 32), 32)
            carried = carry_in[pl.ds(row, 1), columns]
            state = states[rows, columns] + products[rows, columns] * carried
            states[rows, columns] = state
            mixed_in[rows, columns] = (state * gelu_of(branch_pre[rows, columns])).astype(
                jnp.bfloat16
            )

        loop(36, one)
        save(6, states, outs[6])
        save(8, mixed_in, outs[8])

    def out_product():
        loads[4].wait()

        def store(columns, values):
            resid[:, columns] = tokens[:, columns].astype(jnp.float32) + values

        product(mixed_in, w_out, store)
        save(9, resid, outs[9])

        def one(i):
            rows = at(i, 32)
            values = resid[rows, :]
            scale = lax.rsqrt(jnp.mean(values * values, axis=-1, keepdims=True) + epsilon)
            normed2[rows, :] = (values * scale * gain2[...]).astype(jnp.bfloat16)

        loop(12, one)
        save(13, normed2, pair_normed2.at[pl.ds(0, tok)])
        return near(8, normed2, pair_normed2.at[pl.ds(tok, tok)], twin)

    tok = tokens.shape[0]
    cotangent_copy = near(9, cotangent, pair_cotangent.at[pl.ds(tok, tok)], twin)
    save(12, cotangent, pair_cotangent.at[pl.ds(0, tok)])
    carry_in[...] = jnp.zeros_like(carry_in)
    ends[...] = jnp.zeros_like(ends)
    begin(0)
    begin(1)
    mark()
    first_norm()
    tick(0)
    tick(1)
    tick(2)
    arrive(0)
    rim_copy = rec_product()
    tick(3)
    arrive(1)
    convolution(rim_copy)
    gate_product(0)
    tick(4)
    arrive(2)
    gate_product(1)
    tick(5)
    ends_copies = local_scan()
    arrive(3)
    branch_product()
    tick(6)
    carry_states(ends_copies)
    mix()
    arrive(4)
    normed2_copy = out_product()
    tick(7)
    tick(8)
    tick(9)
    for m in (5, 6, 7):
        arrive(m)
    cotangent_copy.wait_recv()
    normed2_copy.wait_recv()
    for copy in live:
        copy.wait_send()
    for copy in pending:
        copy.wait()


def forward_all(shards, cotangent, tokens, bounds, gains, vectors):
    low, full = jnp.bfloat16, jnp.float32
    tok, model = tokens.shape
    rec = shards[0].shape[1]
    shape = jax.ShapeDtypeStruct
    saved = (
        shape((tok, model), low),
        shape((3, 136, rec), full),
        shape((tok, rec), full),
        shape((tok, rec), low),
        shape((tok, rec), full),
        shape((tok, rec), full),
        shape((tok, rec), full),
        shape((tok, rec), full),
        shape((tok, rec), low),
        shape((tok, model), full),
        shape((8, rec), full),
        shape((2 * tok, model), low),
        shape((2 * tok, model), low),
        shape((3, 136, 8), full),
    )
    fulls = [shape((a.shape[0] * 8, a.shape[1]), low) for a in shards]
    for m in (5, 6):
        fulls[m] = shape((fulls[m].shape[0], fulls[m].shape[1] // 2), low)
    fulls[7] = shape((fulls[7].shape[0] // 2, fulls[7].shape[1]), low)
    fulls = tuple(fulls)
    results = pl.pallas_call(
        forward_kernel,
        out_shape=fulls + saved,
        in_specs=[VMEM] * 13,
        out_specs=(ANY,) * 22,
        scratch_shapes=[pltpu.VMEM(a.shape, low) for a in fulls[:5]]
        + [
            pltpu.VMEM((tok, model), low),
            pltpu.VMEM((3, 136, rec), full),
            pltpu.VMEM((tok, rec), full),
            pltpu.VMEM((tok, rec), low),
            pltpu.VMEM((tok, rec), full),
            pltpu.VMEM((tok, rec), full),
            pltpu.VMEM((tok, rec), full),
            pltpu.VMEM((tok, rec), full),
            pltpu.VMEM((tok, rec), full),
            pltpu.VMEM((tok, rec), low),
            pltpu.VMEM((tok, model), full),
            pltpu.VMEM((tok, model), low),
            pltpu.VMEM((3, 8, rec), full),
            pltpu.VMEM((8, rec), full),
            pltpu.VMEM((8, 8, rec), full),
            pltpu.VMEM((8, rec), full),
            pltpu.VMEM((3, 136, 8), full),
            pltpu.SemaphoreType.DMA((8, 20)),
            pltpu.SemaphoreType.DMA((8, 20)),
            pltpu.SemaphoreType.DMA((8, 2)),
            pltpu.SemaphoreType.DMA((10,)),
            pltpu.SemaphoreType.DMA((10,)),
            pltpu.SemaphoreType.DMA((5,)),
            pltpu.SemaphoreType.DMA((14,)),
        ],
        compiler_params=pltpu.CompilerParams(
            collective_id=0, has_side_effects=True, vmem_limit_bytes=60 * 1024 * 1024
        ),
        name="recurrent_forward",
    )(*shards, cotangent, tokens, bounds, gains, vectors)
    return results[:8], results[8:]

class Reduction:
    def __init__(self, kinds, grads, outs, scratch, sems, swapped=()):
        self.kinds, self.swapped = kinds, swapped
        self.grads, self.outs = grads, outs
        self.count = len(grads)
        self.held, self.own, self.first, self.second, self.third, self.final = scratch
        self.send, self.recv, self.local = sems
        self.live = []
        self.at_c, self.at_one, self.at_two, self.at_z = {}, {}, {}, {}
        self.at_end, self.at_last, self.at_out = {}, {}, {}
        r, s, z, c = place()
        self.r, self.z, self.c = r, z, c
        self.mate, self.along_x, self.along_y, self.along_z = peers_of(r, s, z, c)
        self.diagonal = (3 - r, s)
        self.rx, self.ry = lax.rem(r, 2), lax.div(r, 2)

    def peers(self):
        return [self.mate, self.along_x, self.along_y, self.diagonal] + self.along_z

    def remote(self, m, slot, src, dst, device):
        copy = pltpu.make_async_remote_copy(
            src_ref=src,
            dst_ref=dst,
            send_sem=self.send.at[m, slot],
            recv_sem=self.recv.at[m, slot],
            device_id=device,
            device_id_type=MESH,
        )
        copy.start()
        self.live.append(copy)
        return copy

    def load(self, m, q):
        part = self.held[m].shape[3]
        near = pltpu.make_async_copy(
            self.grads[m].at[:, self.c, :, pl.ds(q * part, part)],
            self.own[m].at[q % 2],
            self.local.at[m, q],
        )
        near.start()
        return near

    def begin(self, m):
        part = self.held[m].shape[3]
        if m < len(self.swapped):
            far = [
                pltpu.make_async_copy(
                    self.swapped[m].at[:, :, pl.ds(q * part, part)],
                    self.held[m].at[q],
                    self.local.at[m, 5 + q],
                )
                for q in range(4)
            ]
            for copy in far:
                copy.start()
            self.at_c[m] = (far, [self.load(m, 0), self.load(m, 1)])
            return
        far = [
            self.remote(
                m,
                q,
                self.grads[m].at[:, 1 - self.c, :, pl.ds(q * part, part)],
                self.held[m].at[q],
                self.mate,
            )
            for q in range(4)
        ]
        self.at_c[m] = (far, [self.load(m, 0), self.load(m, 1)])

    def stage_core(self, m):
        held, own = self.held[m], self.own[m]
        half = held.shape[2] // 2
        far, near = self.at_c[m]
        for q in range(4):
            if m < len(self.swapped):
                far[q].wait()
            else:
                far[q].wait_recv()
            near[q].wait()

            def add(b):
                held[q, b] = held[q, b] + own[q % 2, b]

            loop(held.shape[1], add)
            if q < 2:
                near.append(self.load(m, q + 2))
        if self.kinds[m] == "early":
            self.at_z[m] = [
                self.remote(
                    m,
                    9 + k,
                    held.at[:, lax.rem(self.z + k, 4)],
                    self.third[m].at[k - 1],
                    self.along_z[k - 1],
                )
                for k in (1, 2, 3)
            ]
        else:
            self.send_one(m)

    def sources(self, m):
        return pl.ds(self.z, 1) if self.kinds[m] == "early" else pl.ds(0, self.held[m].shape[1])

    def stage_early(self, m):
        held, third, z = self.held[m], self.third[m], self.z
        blocks = held.shape[2] // 32
        for copy in self.at_z[m]:
            copy.wait_recv()

        def add(i):
            q, rows = lax.div(i, blocks), at(lax.rem(i, blocks), 32)
            values = held[q, z, rows, :].astype(jnp.float32)
            for k in range(3):
                values = values + third[k, q, rows, :].astype(jnp.float32)
            held[q, z, rows, :] = values.astype(jnp.bfloat16)

        loop(4 * blocks, add)
        self.send_one(m)

    def send_one(self, m):
        held, half, sources = self.held[m], self.held[m].shape[2] // 2, self.sources(m)
        self.at_one[m] = []
        for other in range(2):
            quarter = other * 2 + (1 - self.rx)
            self.at_one[m].append(
                self.remote(
                    m,
                    4 + other,
                    held.at[quarter, sources, pl.ds(0, half)],
                    self.first[m].at[0, other],
                    self.along_x,
                )
            )
            quarter = (1 - self.ry) * 2 + other
            self.at_one[m].append(
                self.remote(
                    m,
                    6 + other,
                    held.at[quarter, sources, pl.ds(half, half)],
                    self.first[m].at[1, other],
                    self.along_y,
                )
            )

    def stage_one(self, m):
        held, first, sources = self.held[m], self.first[m], self.sources(m)
        count, half = first.shape[2], held.shape[2] // 2
        base = self.z if self.kinds[m] == "early" else 0
        for copy in self.at_one[m]:
            copy.wait_recv()

        def add(i):
            other, b = lax.div(i, count), lax.rem(i, count)
            at_b = base + b
            qx = other * 2 + self.rx
            held[qx, at_b, :half] = held[qx, at_b, :half] + first[0, other, b]
            qy = self.ry * 2 + other
            held[qy, at_b, half:] = held[qy, at_b, half:] + first[1, other, b]

        loop(2 * count, add)
        self.at_two[m] = [
            self.remote(
                m,
                8,
                held.at[(1 - self.ry) * 2 + self.rx, sources, pl.ds(0, half)],
                self.second[m].at[0],
                self.along_y,
            ),
            self.remote(
                m,
                9,
                held.at[self.ry * 2 + (1 - self.rx), sources, pl.ds(half, half)],
                self.second[m].at[1],
                self.along_x,
            ),
        ]

    def stage_two(self, m):
        held, second, r = self.held[m], self.second[m], self.r
        count, half = second.shape[1], held.shape[2] // 2
        early = self.kinds[m] == "early"
        base = self.z if early else 0
        for copy in self.at_two[m]:
            copy.wait_recv()

        def add(b):
            held[r, base + b, :half] = held[r, base + b, :half] + second[0, b]
            held[r, base + b, half:] = held[r, base + b, half:] + second[1, b]

        loop(count, add)
        if early:
            self.final[m][r] = held[r, self.z]
            self.send_final(m)
            return
        rows = self.kinds[m] == "rows"
        self.at_z[m] = []
        for k in (2,) if rows else (1, 2, 3):
            target = 1 - lax.div(self.z, 2) if rows else lax.rem(self.z + k, 4)
            self.at_z[m].append(
                self.remote(
                    m,
                    9 + k,
                    held.at[r, target],
                    self.third[m].at[0 if rows else k - 1],
                    self.along_z[k - 1],
                )
            )

    def stage_z(self, m):
        held, third, final, r = self.held[m], self.third[m], self.final[m], self.r
        for copy in self.at_z[m]:
            copy.wait_recv()
        kind, parity = self.kinds[m], lax.rem(self.z, 2)
        own = lax.div(self.z, 2) if kind == "rows" else self.z

        def add(i):
            rows = at(i, 32)

            def total(first, *terms):
                values = first.astype(jnp.float32)
                for k in terms:
                    values = values + third[k, rows, :].astype(jnp.float32)
                return values.astype(jnp.bfloat16)

            mine = held[r, own, rows, :]
            if kind == "columns":
                final[r, parity, rows, :] = total(mine, 1)
                final[r, 1 - parity, rows, :] = total(third[0, rows, :], 2)
            else:
                final[r, rows, :] = total(mine, *((0,) if kind == "rows" else (0, 1, 2)))

        loop(held.shape[2] // 32, add)
        self.send_final(m)

    def send_final(self, m):
        final, r = self.final[m], self.r
        targets = [self.along_x, self.along_y]
        if m == self.count - 1:
            targets.append(self.diagonal)
        self.at_end[m] = [
            self.remote(m, 13 + i, final.at[r], final.at[r], device)
            for i, device in enumerate(targets)
        ]

    def stage_end(self, m):
        for copy in self.at_end[m]:
            copy.wait_recv()
        if m == self.count - 1:
            self.write(m)
            return
        final = self.final[m]

        def part(quarter, which):
            if self.kinds[m] == "columns":
                return final.at[quarter, which]
            half = final.shape[1] // 2
            return final.at[quarter, pl.ds(which * half, half)]

        from_x, from_y = part(self.along_x[0], 0), part(self.along_y[0], 1)
        self.at_last[m] = [
            self.remote(m, 15, from_x, from_x, self.along_y),
            self.remote(m, 16, from_y, from_y, self.along_x),
        ]

    def stage_last(self, m):
        for copy in self.at_last[m]:
            copy.wait_recv()
        self.write(m)

    def write(self, m):
        out = pltpu.make_async_copy(self.final[m], self.outs[m], self.local.at[m, 4])
        out.start()
        self.at_out[m] = out

    def tick(self, now):
        stages = (self.stage_core, self.stage_one, self.stage_two, self.stage_z, self.stage_end)
        for late, stage in enumerate(stages):
            if 0 <= now - late < self.count:
                stage(now - late)
            if late == 0 and now + 2 < self.count:
                self.begin(now + 2)
        if 0 <= now - 5 < self.count - 1:
            self.stage_last(now - 5)

    def ticks(self):
        return self.count + 4

    def close(self):
        for m in range(self.count):
            self.at_out[m].wait()
        for copy in self.live:
            copy.wait_send()


REDUCTION_SEMS = 17


def reduction_memory(kinds, grads):
    low = jnp.bfloat16
    count = len(grads)
    shapes = [(2 if kind == "rows" else 4,) + quarter_shape(kind, g) for kind, g in zip(kinds, grads)]
    scratch = [pltpu.VMEM((4, zs, k, n), low) for zs, k, n in shapes]
    scratch += [pltpu.VMEM((2, zs, k, n), low) for zs, k, n in shapes]
    summed = [1 if kind == "early" else zs for kind, (zs, _, _) in zip(kinds, shapes)]
    scratch += [pltpu.VMEM((2, 2, zs, k // 2, n), low) for zs, (_, k, n) in zip(summed, shapes)]
    scratch += [pltpu.VMEM((2, zs, k // 2, n), low) for zs, (_, k, n) in zip(summed, shapes)]
    scratch += [
        pltpu.VMEM((3, 4, k, n) if kind == "early" else (zs - 1, k, n), low)
        for kind, (zs, k, n) in zip(kinds, shapes)
    ]
    scratch += [pltpu.VMEM(a.shape, low) for a in reduced_shapes(kinds, grads)]
    return scratch + [
        pltpu.SemaphoreType.DMA((count, REDUCTION_SEMS)),
        pltpu.SemaphoreType.DMA((count, REDUCTION_SEMS)),
        pltpu.SemaphoreType.DMA((count, 9)),
    ]


def reduced_shapes(kinds, grads):
    shapes = [(kind, quarter_shape(kind, g)) for kind, g in zip(kinds, grads)]
    return tuple(
        jax.ShapeDtypeStruct((4, 2, k, n) if kind == "columns" else (4, k, n), jnp.bfloat16)
        for kind, (k, n) in shapes
    )


def take_reduction(take, count):
    scratch = [take(count) for _ in range(6)]
    return scratch, take(3)


def taker(refs):
    refs = list(refs)

    def take(n):
        taken, refs[:n] = refs[:n], []
        return taken

    return take


def split_rows(kind, grad):
    zs = 2 if kind == "rows" else 4
    return grad.reshape(zs, 2, grad.shape[0] // (2 * zs), grad.shape[1])


def quarter_shape(kind, grad):
    return grad.shape[0] // (4 if kind == "rows" else 8), grad.shape[1] // 4


def finish_kernel(count, plain, *refs):
    take = taker(refs)
    blocks, same = take(count), take(plain)
    wholes, same_out = take(count), take(plain)
    brought, wide, passed = take(count), take(count), take(plain)
    sem_in, sem_out = take(2)
    entries = [(a, b, i) for i, (a, b) in enumerate(zip(blocks + same, brought + passed))]
    fetched = [pltpu.make_async_copy(a, b, sem_in.at[i]) for a, b, i in entries]
    for copy in fetched:
        copy.start()
    written = []
    for i in range(count + plain):
        fetched[i].wait()
        if i < count:
            block, whole = brought[i], wide[i]
            part = block.shape[-1]
            for q in range(4):
                for half in range(2 if len(block.shape) == 4 else 1):
                    if len(block.shape) == 4:
                        column = ((half + 2 * (q // 2)) * 2 + q % 2) * part
                        values = block[q, half]
                    else:
                        column, values = q * part, block[q]
                    whole[:, column : column + part] = values.astype(jnp.float32)
            copy = pltpu.make_async_copy(whole, wholes[i], sem_out.at[i])
        else:
            copy = pltpu.make_async_copy(passed[i - count], same_out[i - count], sem_out.at[i])
        copy.start()
        written.append(copy)
    for copy in written:
        copy.wait()


def finish(blocks, same):
    shape = jax.ShapeDtypeStruct
    whole = [(b.shape[-2], b.size // b.shape[-2]) for b in blocks]
    count, plain = len(blocks), len(same)
    results = pl.pallas_call(
        functools.partial(finish_kernel, count, plain),
        out_shape=tuple(shape(a, jnp.float32) for a in whole)
        + tuple(shape(a.shape, a.dtype) for a in same),
        in_specs=[ANY] * (count + plain),
        out_specs=(ANY,) * (count + plain),
        scratch_shapes=[pltpu.VMEM(b.shape, b.dtype) for b in blocks]
        + [pltpu.VMEM(a, jnp.float32) for a in whole]
        + [pltpu.VMEM(a.shape, a.dtype) for a in same]
        + [pltpu.SemaphoreType.DMA((count + plain,))] * 2,
        compiler_params=pltpu.CompilerParams(vmem_limit_bytes=62 * 1024 * 1024),
        name="widen_gradients",
    )(*blocks, *same)
    return results[:count], results[count:]


REC_KINDS = ("early", "all", "all", "all")


def reduce_kernel(count, swaps, *refs):
    take = taker(refs)
    grads = take(count)
    swapped = take(swaps)
    (small_in,) = take(1)
    outs = take(count)
    (small_out,) = take(1)
    reduction = Reduction(REC_KINDS, grads, outs, *take_reduction(take, count), swapped)
    small_held, small_got, small_send, small_recv = take(4)
    z = reduction.z
    greet(reduction.peers())
    small_copies = []

    def swap_small(slot, source, device):
        copy = pltpu.make_async_remote_copy(
            src_ref=small_held.at[source],
            dst_ref=small_got.at[slot],
            send_sem=small_send.at[slot],
            recv_sem=small_recv.at[slot],
            device_id=device,
            device_id_type=MESH,
        )
        copy.start()
        small_copies.append(copy)
        return copy

    small_held[0] = small_in[...]
    swap = swap_small(0, 0, reduction.mate)
    begin, core, early = reduction.begin, reduction.stage_core, reduction.stage_early
    one, two, over_z = reduction.stage_one, reduction.stage_two, reduction.stage_z
    end, last = reduction.stage_end, reduction.stage_last
    begin(0)
    begin(1)
    core(0)
    begin(2)
    core(1)
    begin(3)
    core(2)
    one(1)
    swap.wait_recv()
    small_held[1] = small_held[0] + small_got[0]
    swap = swap_small(1, 1, reduction.along_x)
    core(3)
    one(2)
    two(1)
    swap.wait_recv()
    small_held[2] = small_held[1] + small_got[1]
    swap = swap_small(2, 2, reduction.along_y)
    one(3)
    early(0)
    two(2)
    swap.wait_recv()
    small_held[3] = small_held[2] + small_got[2]
    spread = [swap_small(2 + k, 3, reduction.along_z[k - 1]) for k in (1, 2, 3)]
    over_z(1)
    one(0)
    two(3)
    two(0)
    over_z(2)
    end(1)
    over_z(3)
    end(0)
    last(1)
    end(2)
    last(0)
    end(3)
    last(2)
    for copy in spread:
        copy.wait_recv()
    small_got[6] = small_held[3]
    total = None
    for source in range(4):
        k = lax.rem(z + 4 - source, 4)
        slot = jnp.where(k == 0, 6, 2 + k)
        term = small_got[slot]
        total = term if total is None else total + term
    small_out[...] = total
    for copy in small_copies:
        copy.wait_send()
    reduction.close()


def reduce_all(grads, swapped, small, tag):
    count = len(grads)
    kinds = REC_KINDS
    results = pl.pallas_call(
        functools.partial(reduce_kernel, count, len(swapped)),
        out_shape=reduced_shapes(kinds, grads)
        + (jax.ShapeDtypeStruct(small.shape, small.dtype),),
        in_specs=[ANY] * (count + len(swapped)) + [VMEM],
        out_specs=(ANY,) * count + (VMEM,),
        scratch_shapes=reduction_memory(kinds, grads)
        + [
            pltpu.VMEM((4,) + small.shape, small.dtype),
            pltpu.VMEM((7,) + small.shape, small.dtype),
            pltpu.SemaphoreType.DMA((6,)),
            pltpu.SemaphoreType.DMA((6,)),
        ],
        compiler_params=pltpu.CompilerParams(
            collective_id=tag, has_side_effects=True, vmem_limit_bytes=60 * 1024 * 1024
        ),
        name="reduce_grads",
    )(*[split_rows("all", g) for g in grads], *swapped, small)
    return results[:count], results[count]


def backward_kernel(kinds, *refs):
    take = taker(refs)
    count = len(kinds)
    grads = take(count - 1)
    part_mixed, part_normed2, twin_normed2 = take(3)
    full_out, full_rate, full_input, full_branch, full_rec = take(5)
    saved_states, saved_branch, saved_rate, saved_input, saved_conv, saved_rec = take(6)
    marks, tokens, cotangent, resid, normed, conv_low, mixed_in, carried = take(8)
    gains, vectors = take(2)
    gain1, gain2 = gains.at[0:1], gains.at[1:2]
    conv_w, _, rate_b, input_b, decay_scale = split_vectors(vectors)
    outs = take(count)
    d_rate, d_input, d_branch, d_rec, token_grad, mixed, swap_rec, swap_rate = take(8)
    (small,) = take(1)
    parts = take_reduction(take, count)
    (d_out,) = take(1)
    reduction = Reduction(kinds, grads + [d_out], outs, *parts)
    ring, past, branch_pre, rate_pre, input_pre, conv_out = take(6)
    flow, grads_conv, branch_low, rate_low, input_low, stage = take(6)
    rim, ends, got, carry = take(4)
    own_parts, twin_parts, grad_resid, resid_low = take(4)
    near_send, near_recv, load_sem, ring_sem, stage_sem = take(5)
    r, s, z, c = place()
    others = [(r, lax.rem(s + k, 8)) for k in range(1, 8)]
    greet(others + [reduction.along_x, reduction.along_y, reduction.diagonal])
    live = []

    def near(slot, src, dst, device):
        copy = pltpu.make_async_remote_copy(
            src_ref=src,
            dst_ref=dst,
            send_sem=near_send.at[slot],
            recv_sem=near_recv.at[slot],
            device_id=device,
            device_id_type=MESH,
        )
        copy.start()
        live.append(copy)
        return copy

    def bring(slot, src, dst):
        copy = pltpu.make_async_copy(src, dst, load_sem.at[slot])
        copy.start()
        return copy

    tiles = []
    for weight in (full_out, full_rate, full_input, full_branch, full_rec):
        tiles.append([(weight, j) for j in range(weight.shape[0] // 512)])
    out_tiles, rate_tiles, input_tiles, branch_tiles, rec_tiles = tiles
    order = list(out_tiles)
    for pair in zip(rate_tiles, input_tiles):
        order += pair
    for pair in zip(branch_tiles, rec_tiles):
        order += pair
    fetches = {}

    def fetch(i):
        if i < len(order):
            weight, j = order[i]
            copy = pltpu.make_async_copy(
                weight.at[pl.ds(j * 512, 512)],
                ring.at[i % 3, :, pl.ds(0, weight.shape[1])],
                ring_sem.at[i % 3],
            )
            copy.start()
            fetches[i] = copy

    def back_tile(i, left, depth):
        fetches[i].wait()
        return lax.dot_general(
            left[...],
            ring[i % 3, :, pl.ds(0, depth)],
            (((1,), (1,)), ((), ())),
            preferred_element_type=jnp.float32,
        )

    staged = [None, None]
    turn = [0]

    def outer_product(left, right, target):
        for strip in range(left.shape[1] // 256):
            slot = turn[0] % 2
            turn[0] += 1
            if staged[slot] is not None:
                staged[slot].wait()
            rows = pl.ds(strip * 256, 256)
            width = right.shape[1]

            def one(j):
                columns = at(j, 512)
                stage[slot, :, columns] = lax.dot_general(
                    left[:, rows],
                    right[:, columns],
                    (((0,), (0,)), ((), ())),
                    preferred_element_type=jnp.float32,
                ).astype(jnp.bfloat16)

            loop(width // 512, one)
            copy = pltpu.make_async_copy(
                stage.at[slot, :, pl.ds(0, width)], target.at[rows], stage_sem.at[slot]
            )
            copy.start()
            staged[slot] = copy

    def out_weight():
        depth = d_out.shape[2]

        def one(i):
            source, column = lax.div(i, 2), lax.rem(i, 2)
            columns = at(column, 512)
            values = lax.dot_general(
                mixed_in[:, at(source, 2 * depth)],
                resid_low[:, columns],
                (((0,), (0,)), ((), ())),
                preferred_element_type=jnp.float32,
            ).astype(jnp.bfloat16)
            d_out[source, 0, :, columns] = values[:depth]
            d_out[source, 1, :, columns] = values[depth:]

        loop(8, one)

    swaps = []

    def swap_halves(first, source, target):
        for slot in range(2):
            if staged[slot] is not None:
                staged[slot].wait()
                staged[slot] = None
        depth = target.shape[1]
        for block in range(4):
            row = pl.multiple_of((block * 2 + 1 - c) * depth, 16)
            swaps.append(
                near(
                    first + block,
                    source.at[pl.ds(row, depth)],
                    target.at[block],
                    reduction.mate,
                )
            )

    def block_of(i):
        row, block = lax.div(i, 4), lax.rem(i, 4)
        return row, block, pl.ds(pl.multiple_of(row * 128 + block * 32, 32), 32)

    def folded(values):
        return values[0:8] + values[8:16] + values[16:24] + values[24:32]

    def gates(rows, columns, mark_rows):
        rate_gate = jax.nn.sigmoid(rate_pre[rows, columns] + rate_b[:, columns])
        log_rate = decay_scale[:, columns] * rate_gate
        return rate_gate, log_rate, jnp.exp(log_rate)

    def branch_back():
        def one(i):
            column, rest = lax.div(i, 12), lax.rem(i, 12)
            row, block, rows = block_of(rest)
            columns = at(column, 512)
            act, slope = gelu_parts(branch_pre[rows, columns])
            grad = flow[rows, columns]
            state = past[row, pl.ds(pl.multiple_of(block * 32 + 8, 8), 32), columns]
            flow[rows, columns] = grad * act
            branch_low[rows, columns] = (grad * state * slope).astype(jnp.bfloat16)

        loop(36, one)

    def scan_back():
        def one(column):
            columns = at(column, 512)
            spot = lax.broadcasted_iota(jnp.int32, (8, 512), 0)

            def tile(i, state):
                t = 15 - i
                results = []
                for row in range(3):
                    rows = pl.ds(pl.multiple_of(row * 128 + t * 8, 8), 8)
                    keep = 1.0 - marks[row, pl.ds(pl.multiple_of(t * 8, 8), 8), 0:1]
                    _, _, pace = gates(rows, columns, None)
                    decay = pace * keep
                    follow, carry_a, carry_b = state[3 * row : 3 * row + 3]
                    later = jnp.where(spot == 7, follow, pltpu.roll(decay, 7, 0))
                    a, b = tile_scan(later, flow[rows, columns], True)
                    b = b + a * carry_b
                    a = a * carry_a
                    branch_pre[rows, columns] = a
                    flow[rows, columns] = b
                    results += [decay[0:1], a[0:1], b[0:1]]
                return tuple(results)

            ones, zeros = jnp.ones((1, 512), jnp.float32), jnp.zeros((1, 512), jnp.float32)
            last = lax.fori_loop(0, 16, tile, (ones, ones, zeros) * 3)
            for row in range(3):
                decay, a, b = last[3 * row : 3 * row + 3]
                ends[row : row + 1, columns] = decay * a
                ends[3 + row : 4 + row, columns] = decay * b

        loop(3, one)
        return [near(k, ends, got.at[k], others[k - 1]) for k in range(1, 8)]

    def carry_back(copies):
        for copy in copies:
            copy.wait_recv()

        def one(column):
            columns = at(column, 512)
            state = jnp.zeros((3, 512), jnp.float32)
            for ahead in range(7, 0, -1):
                k = 8 - ahead
                after = got[k, 3:6, columns] + got[k, 0:3, columns] * state
                state = jnp.where(s + ahead <= 7, after, state)
            carry[0:3, columns] = state

        loop(3, one)

    def gates_back():
        def one(column):
            columns = at(column, 512)

            def block_step(i, sums):
                row, block, rows = block_of(i)
                mark = pl.ds(pl.multiple_of(block * 32, 32), 32)
                reset = marks[row, mark, 0:1]
                keep = 1.0 - reset
                rate_gate, log_rate, pace = gates(rows, columns, mark)
                input_gate = jax.nn.sigmoid(input_pre[rows, columns] + input_b[:, columns])
                power = pace * pace
                root = jnp.sqrt(minus_expm1(2.0 * log_rate, power))
                scale = reset + keep * root
                conv = conv_out[rows, columns]
                grad = flow[rows, columns] + branch_pre[rows, columns] * carry[
                    pl.ds(row, 1), columns
                ]
                window = past[row, pl.ds(pl.multiple_of(block * 32, 8), 40), columns]
                before = pltpu.roll(window, 1, 0)[8:]
                grad_log = keep * grad * (before * pace - input_gate * conv * power / root)
                decay_sum = rate_gate * grad_log
                rate_grad = decay_scale[:, columns] * decay_sum * (1.0 - rate_gate)
                direct = grad * scale * input_gate
                input_grad = direct * conv * (1.0 - input_gate)
                rate_low[rows, columns] = rate_grad.astype(jnp.bfloat16)
                input_low[rows, columns] = input_grad.astype(jnp.bfloat16)
                rate_pre[rows, columns] = direct
                return (
                    sums[0] + folded(decay_sum),
                    sums[1] + folded(rate_grad),
                    sums[2] + folded(input_grad),
                )

            zeros = jnp.zeros((8, 512), jnp.float32)
            sums = lax.fori_loop(0, 12, block_step, (zeros,) * 3)
            for spot, values in enumerate(sums):
                small[5 + spot : 6 + spot, columns] = jnp.sum(values, axis=0, keepdims=True)

        loop(3, one)

    def conv_back(copy):
        copy.wait_recv()
        for row in range(3):
            grads_conv[row, 128:136, :] = jnp.where(s < 7, rim[row], 0.0)

        def one(column):
            columns = at(column, 512)

            def block_step(i, sums):
                row, block, rows = block_of(i)
                span = pl.ds(pl.multiple_of(block * 32, 8), 40)
                ahead = grads_conv[row, span, columns]
                behind = past[row, span, columns]
                grad = ahead[:32]
                total = conv_w[0:1, columns] * grad
                new = [sums[0] + folded(grad * behind[8:])]
                for k in (1, 2, 3):
                    kept = ahead * marks[row, span, k : k + 1]
                    total = total + conv_w[k : k + 1, columns] * pltpu.roll(kept, 40 - k, 0)[:32]
                    new.append(
                        sums[k] + folded(kept[:32] * pltpu.roll(behind, k, 0)[8:])
                    )
                new.append(sums[4] + folded(grad))
                rate_low[rows, columns] = total.astype(jnp.bfloat16)
                return tuple(new)

            zeros = jnp.zeros((8, 512), jnp.float32)
            sums = lax.fori_loop(0, 12, block_step, (zeros,) * 5)
            for spot, values in enumerate(sums):
                small[spot : spot + 1, columns] = jnp.sum(values, axis=0, keepdims=True)

        loop(3, one)

    def second_norm_back():
        def one(i, total):
            rows = at(i, 16)
            grad = own_parts[1, rows, :].astype(jnp.float32) + twin_parts[1, rows, :].astype(
                jnp.float32
            )
            values = resid[rows, :]
            scale = lax.rsqrt(jnp.mean(values * values, axis=-1, keepdims=True) + epsilon)
            back = grad * gain2[...]
            mean = jnp.mean(values * back, axis=-1, keepdims=True)
            result = cotangent[rows, :].astype(jnp.float32) + scale * back
            result = result - values * (scale * scale * scale * mean)
            grad_resid[rows, :] = result
            resid_low[rows, :] = result.astype(jnp.bfloat16)
            part = grad * values * scale
            return total + part[0:8] + part[8:16]

        total = lax.fori_loop(0, 24, one, jnp.zeros((8, 1024), jnp.float32))
        small[9:10, 0:1024] = jnp.sum(total, axis=0, keepdims=True)

    def mix_back():
        def one(i):
            rows = at(i, 16)
            total = own_parts[0, rows, :].astype(jnp.float32)
            total = total + twin_parts[0, rows, :].astype(jnp.float32)
            own_parts[0, rows, :] = (resid[rows, :] + total).astype(jnp.bfloat16)

        loop(24, one)
        return bring(8, own_parts.at[0], mixed)

    def norm_back():
        def one(i, total):
            rows = at(i, 16)
            values = tokens[rows, :].astype(jnp.float32)
            scale = lax.rsqrt(jnp.mean(values * values, axis=-1, keepdims=True) + epsilon)
            grad = input_pre[rows, pl.ds(0, 1024)]
            back = grad * gain1[...]
            mean = jnp.mean(values * back, axis=-1, keepdims=True)
            result = grad_resid[rows, :] + scale * back - values * (scale * scale * scale * mean)
            own_parts[1, rows, :] = result.astype(jnp.bfloat16)
            part = grad * values * scale
            return total + part[0:8] + part[8:16]

        total = lax.fori_loop(0, 24, one, jnp.zeros((8, 1024), jnp.float32))
        small[8:9, 0:1024] = jnp.sum(total, axis=0, keepdims=True)
        return bring(10, own_parts.at[1], token_grad)

    tok = tokens.shape[0]
    twin = (r, s + 2 - 4 * lax.rem(z, 2))
    reduction.begin(0)
    reduction.begin(1)
    mixed_copy = near(8, part_mixed.at[pl.ds(tok, tok)], twin_parts.at[0], twin)
    part_loads = [
        bring(6, part_normed2.at[pl.ds(0, tok)], own_parts.at[1]),
        bring(9, twin_normed2, twin_parts.at[1]),
        bring(7, part_mixed.at[pl.ds(0, tok)], own_parts.at[0]),
    ]
    loads = [
        bring(0, saved_branch, branch_pre),
        bring(1, saved_states, past.at[:, pl.ds(8, 128), :]),
        bring(2, saved_rate, rate_pre),
        bring(3, saved_input, input_pre),
        bring(4, saved_conv, conv_out),
    ]
    for i in range(3):
        fetch(i)
    small[...] = jnp.zeros_like(small)
    ends[...] = jnp.zeros_like(ends)
    for row in range(3):
        past[row, 0:8, :] = jnp.broadcast_to(carried[row : row + 1, :], (8, past.shape[2]))
    part_loads[0].wait()
    part_loads[1].wait()
    second_norm_back()
    for i in range(3):
        flow[:, pl.ds(i * 512, 512)] = back_tile(i, resid_low, 1024)
        fetch(i + 3)
    reduction.tick(0)
    loads[0].wait()
    loads[1].wait()
    branch_back()
    loads[2].wait()
    copies = scan_back()
    out_weight()
    reduction.tick(1)
    part_loads[2].wait()
    mixed_copy.wait_recv()
    mixed_save = mix_back()
    reduction.tick(2)
    carry_back(copies)
    loads[3].wait()
    loads[4].wait()
    gates_back()
    loads.append(bring(5, saved_rec, past))
    reduction.tick(3)
    at_tile = 3
    for j in range(3):
        columns = pl.ds(j * 512, 512)
        total = rate_pre[:, columns]
        total = total + back_tile(at_tile, rate_low, 1536)
        fetch(at_tile + 3)
        total = total + back_tile(at_tile + 1, input_low, 1536)
        fetch(at_tile + 4)
        at_tile += 2
        for row in range(3):
            grads_conv[row, 0:128, columns] = total[row * 128 : (row + 1) * 128]
    rim_copy = near(0, grads_conv.at[:, pl.ds(0, 8), :], rim, others[6])
    reduction.tick(4)
    outer_product(conv_low, rate_low, d_rate)
    loads[5].wait()
    conv_back(rim_copy)
    swap_halves(9, d_rate, swap_rate)
    reduction.tick(5)
    for j in range(2):
        columns = pl.ds(j * 512, 512)
        total = back_tile(at_tile, branch_low, 1536)
        fetch(at_tile + 3)
        total = total + back_tile(at_tile + 1, rate_low, 1536)
        fetch(at_tile + 4)
        at_tile += 2
        input_pre[:, columns] = total
    outer_product(normed, rate_low, d_rec)
    reduction.tick(6)
    swap_halves(13, d_rec, swap_rec)
    outer_product(conv_low, input_low, d_input)
    outer_product(normed, branch_low, d_branch)
    token_save = norm_back()
    for now in range(7, reduction.ticks()):
        reduction.tick(now)
    for copy in swaps:
        copy.wait_recv()
    mixed_save.wait()
    token_save.wait()
    for copy in staged:
        if copy is not None:
            copy.wait()
    for copy in live:
        copy.wait_send()
    reduction.close()


def backward_all(grads, parts, fulls, saved, local, vectors):
    low, full = jnp.bfloat16, jnp.float32
    shape, memory = jax.ShapeDtypeStruct, pltpu.VMEM
    kinds = ("rows", "columns", "columns", "all")
    count = len(kinds)
    tok, model = local[1].shape
    rec = fulls[0].shape[0]
    all_grads = tuple(grads) + (shape((rec, model), low),)
    out_shape = reduced_shapes(kinds, all_grads) + (
        shape((rec, rec), low),
        shape((rec, rec), low),
        shape((model, rec), low),
        shape((model, rec), low),
        shape((tok, model), low),
        shape((tok, model), low),
        shape((4, model // 8, rec), low),
        shape((4, rec // 8, rec), low),
        shape((16, rec), full),
    )
    results = pl.pallas_call(
        functools.partial(backward_kernel, kinds),
        out_shape=out_shape,
        in_specs=[ANY] * (count + 13) + [VMEM] * 10,
        out_specs=(ANY,) * (count + 8) + (VMEM,),
        scratch_shapes=reduction_memory(kinds, all_grads)
        + [
            memory((4, 2, rec // 8, model), low),
            memory((3, 512, rec), low),
            memory((3, 136, rec), full),
            memory((tok, rec), full),
            memory((tok, rec), full),
            memory((tok, rec), full),
            memory((tok, rec), full),
            memory((tok, rec), full),
            memory((3, 136, rec), full),
            memory((tok, rec), low),
            memory((tok, rec), low),
            memory((tok, rec), low),
            memory((2, 256, rec), low),
            memory((3, 8, rec), full),
            memory((8, rec), full),
            memory((8, 8, rec), full),
            memory((8, rec), full),
            memory((2, tok, model), low),
            memory((2, tok, model), low),
            memory((tok, model), full),
            memory((tok, model), low),
            pltpu.SemaphoreType.DMA((17,)),
            pltpu.SemaphoreType.DMA((17,)),
            pltpu.SemaphoreType.DMA((11,)),
            pltpu.SemaphoreType.DMA((3,)),
            pltpu.SemaphoreType.DMA((2,)),
        ],
        compiler_params=pltpu.CompilerParams(
            collective_id=1, has_side_effects=True, vmem_limit_bytes=62 * 1024 * 1024
        ),
        name="recurrent_backward",
    )(*[split_rows(k, g) for k, g in zip(kinds, grads)], *parts, *fulls, *saved, *local, *vectors)
    return results[:count], results[count:]


def from_behind(block, axis, distance):
    devices = range(lax.axis_size(axis))
    route = [(i - distance, i) for i in devices if i - distance in devices]
    return lax.ppermute(block, axis, route)


def prefix(part, axis, combine, identity, reverse):
    count = lax.axis_size(axis)
    place = lax.axis_index(axis)
    ahead = count - 1 - place if reverse else place
    gathered = jax.tree.map(lambda a: lax.all_gather(a, axis), part)
    state = jax.tree.map(lambda a, e: jnp.zeros_like(a) + jnp.asarray(e, a.dtype), part, identity)

    def one(turn, state):
        source = count - 1 - turn if reverse else turn
        return combine(
            state, jax.tree.map(lambda a: lax.dynamic_index_in_dim(a, source, 0, False), gathered)
        )

    return lax.fori_loop(0, ahead, one, state)


def rms_norm(values, gain):
    return values * lax.rsqrt(jnp.mean(values * values, axis=-1, keepdims=True) + epsilon) * gain


def combine(earlier, latter):
    return (earlier[0] * latter[0], latter[0] * earlier[1] + latter[1])


def conv_masks(padded_resets):
    keep_mask = 1.0 - padded_resets
    first = keep_mask[..., 3:]
    second = first * keep_mask[..., 2:-1]
    third = second * keep_mask[..., 1:-2]
    return (first, second, third)


def convolve(padded, masks, conv_weight, conv_bias):
    result = conv_bias + conv_weight[0] * padded[..., 3:, :]
    result = result + conv_weight[1] * masks[0][..., None] * padded[..., 2:-1, :]
    result = result + conv_weight[2] * masks[1][..., None] * padded[..., 1:-2, :]
    return result + conv_weight[3] * masks[2][..., None] * padded[..., :-3, :]


def gate_terms(rate_pre, input_pre, conv_out, decay_param, rate_bias, input_bias, resets):
    rate_gate = jax.nn.sigmoid(rate_pre + rate_bias)
    input_gate = jax.nn.sigmoid(input_pre + input_bias)
    log_rate = -8.0 * jax.nn.softplus(decay_param) * rate_gate
    keep_mask = 1.0 - resets[..., None]
    decays = jnp.exp(log_rate) * keep_mask
    scales = resets[..., None] + keep_mask * jnp.sqrt(-jnp.expm1(2.0 * log_rate))
    return (decays, scales * input_gate * conv_out)


def forward_product(values, weight):
    return jnp.dot(values, weight, preferred_element_type=jnp.float32)


def outer(left, right):
    return lax.dot_general(
        left, right, (((0,), (0,)), ((), ())), preferred_element_type=jnp.float32
    )


def back_product(grads, weight):
    return lax.dot_general(
        grads, weight, (((1,), (1,)), ((), ())), preferred_element_type=jnp.float32
    )


def plain_body(
    tokens,
    bounds,
    norm1_gain,
    w_branch,
    w_rec,
    conv_weight,
    conv_bias,
    w_rate,
    rate_bias,
    w_input,
    input_bias,
    decay_param,
    w_out,
    norm2_gain,
    w_gate,
    w_up,
    w_down,
    cotangent,
):
    gathered = (
        lax.all_gather(w_branch, "seq", axis=0, tiled=True),
        lax.all_gather(w_rec, "seq", axis=0, tiled=True),
        lax.all_gather(w_rate, "seq", axis=0, tiled=True),
        lax.all_gather(w_input, "seq", axis=0, tiled=True),
        lax.all_gather(w_out, "seq", axis=0, tiled=True),
        lax.all_gather(w_gate, "seq", axis=0, tiled=True),
        lax.all_gather(w_up, "seq", axis=0, tiled=True),
        lax.all_gather(w_down, "seq", axis=0, tiled=True),
    )
    full_branch, full_rec, full_rate, full_input, full_out, full_gate, full_up, full_down = gathered
    row_count, tok_count, model_width = tokens.shape
    rec_width = full_rec.shape[1]
    offset = lax.axis_index("seq") * tok_count
    positions = offset - 3 + jnp.arange(tok_count + 3, dtype=jnp.int32)
    marked = (
        jnp.any(positions[None, :, None] == bounds[:, None, :], axis=2) | (positions == 0)[None, :]
    )
    padded_resets = marked.astype(jnp.float32)
    resets = padded_resets[:, 3:]
    masks = conv_masks(padded_resets)
    inputs = tokens.astype(jnp.float32).reshape(-1, model_width)
    normed = rms_norm(inputs, norm1_gain).astype(jnp.bfloat16)
    branch_pre = forward_product(normed, full_branch)
    rec_in = forward_product(normed, full_rec).reshape(row_count, tok_count, rec_width)
    rim = from_behind(rec_in[:, tok_count - 3 :, :], "seq", 1)
    padded = jnp.concatenate([rim, rec_in], axis=1)
    conv_out = convolve(padded, masks, conv_weight, conv_bias)
    conv_low = conv_out.astype(jnp.bfloat16).reshape(-1, rec_width)
    rate_pre = forward_product(conv_low, full_rate).reshape(conv_out.shape)
    input_pre = forward_product(conv_low, full_input).reshape(conv_out.shape)

    def gates_of(rate_arg, input_arg, conv_arg, decay_arg, rate_arg_bias, input_arg_bias):
        return gate_terms(
            rate_arg, input_arg, conv_arg, decay_arg, rate_arg_bias, input_arg_bias, resets
        )

    decays, drives = gates_of(rate_pre, input_pre, conv_out, decay_param, rate_bias, input_bias)
    prefix_decay, local_states = lax.associative_scan(combine, (decays, drives), axis=1)
    ones_pair = jnp.ones((row_count, rec_width), jnp.float32)
    zeros_pair = jnp.zeros((row_count, rec_width), jnp.float32)
    carry_in = prefix(
        (prefix_decay[:, -1], local_states[:, -1]), "seq", combine, (ones_pair, zeros_pair), False
    )[1]
    states = local_states + prefix_decay * carry_in[:, None, :]
    earlier_states = jnp.concatenate([carry_in[:, None, :], states[:, :-1, :]], axis=1)
    branch_act = jax.nn.gelu(branch_pre, approximate=True).reshape(states.shape)
    mixed_in = (states * branch_act).astype(jnp.bfloat16).reshape(-1, rec_width)
    resid = inputs + forward_product(mixed_in, full_out)
    normed2 = rms_norm(resid, norm2_gain).astype(jnp.bfloat16)
    gate_pre = forward_product(normed2, full_gate)
    up_pre = forward_product(normed2, full_up)
    hidden = (jax.nn.gelu(gate_pre, approximate=True) * up_pre).astype(jnp.bfloat16)
    mixed = (resid + forward_product(hidden, full_down)).astype(jnp.bfloat16).reshape(tokens.shape)
    cot_low = cotangent.reshape(-1, model_width)
    grad_down = outer(hidden, cot_low)
    grad_hidden = back_product(cot_low, full_down)
    _, pull_mlp = jax.vjp(
        lambda gate_arg, up_arg: jax.nn.gelu(gate_arg, approximate=True) * up_arg, gate_pre, up_pre
    )
    grad_gate_pre, grad_up_pre = pull_mlp(grad_hidden)
    gate_low = grad_gate_pre.astype(jnp.bfloat16)
    up_low = grad_up_pre.astype(jnp.bfloat16)
    grad_gate = outer(normed2, gate_low)
    grad_up = outer(normed2, up_low)
    grad_normed2 = back_product(gate_low, full_gate) + back_product(up_low, full_up)
    _, pull_norm2 = jax.vjp(rms_norm, resid, norm2_gain)
    grad_resid_norm, grad_norm2 = pull_norm2(grad_normed2)
    grad_resid = cot_low.astype(jnp.float32) + grad_resid_norm
    resid_low = grad_resid.astype(jnp.bfloat16)
    grad_out = outer(mixed_in, resid_low)
    grad_mixed = back_product(resid_low, full_out).reshape(states.shape)
    grad_states = grad_mixed * branch_act
    _, pull_branch = jax.vjp(lambda pre_arg: jax.nn.gelu(pre_arg, approximate=True), branch_pre)
    branch_low = pull_branch((grad_mixed * states).reshape(-1, rec_width))[0].astype(jnp.bfloat16)
    next_decays = jnp.concatenate([decays[:, 1:, :], ones_pair[:, None, :]], axis=1)
    suffix_decay, local_grads = lax.associative_scan(
        combine, (next_decays, grad_states), axis=1, reverse=True
    )
    element = (prefix_decay[:, -1], decays[:, 0] * local_grads[:, 0])
    carry_back = prefix(element, "seq", combine, (ones_pair, zeros_pair), True)[1]
    state_grads = local_grads + suffix_decay * carry_back[:, None, :]
    _, pull_gates = jax.vjp(
        gates_of, rate_pre, input_pre, conv_out, decay_param, rate_bias, input_bias
    )
    grad_rate_pre, grad_input_pre, grad_conv_direct, grad_decay, grad_rate_bias, grad_input_bias = (
        pull_gates((state_grads * earlier_states, state_grads))
    )
    rate_low = grad_rate_pre.astype(jnp.bfloat16).reshape(-1, rec_width)
    input_low = grad_input_pre.astype(jnp.bfloat16).reshape(-1, rec_width)
    grad_rate = outer(conv_low, rate_low)
    grad_input = outer(conv_low, input_low)
    grad_conv = grad_conv_direct + (
        back_product(rate_low, full_rate) + back_product(input_low, full_input)
    ).reshape(conv_out.shape)
    _, pull_conv = jax.vjp(
        lambda pad_arg, weight_arg, bias_arg: convolve(pad_arg, masks, weight_arg, bias_arg),
        padded,
        conv_weight,
        conv_bias,
    )
    grad_padded, grad_conv_weight, grad_conv_bias = pull_conv(grad_conv)
    rim_back = from_behind(grad_padded[:, :3, :], "seq", -1)
    grad_rec = grad_padded[:, 3:, :] + jnp.concatenate(
        [jnp.zeros((row_count, tok_count - 3, rec_width), jnp.float32), rim_back], axis=1
    )
    rec_low = grad_rec.astype(jnp.bfloat16).reshape(-1, rec_width)
    grad_rec_w = outer(normed, rec_low)
    grad_branch_w = outer(normed, branch_low)
    grad_normed = back_product(branch_low, full_branch) + back_product(rec_low, full_rec)
    _, pull_norm1 = jax.vjp(rms_norm, inputs, norm1_gain)
    grad_inputs, grad_norm1 = pull_norm1(grad_normed)
    token_grad = (grad_resid + grad_inputs).astype(jnp.bfloat16).reshape(tokens.shape)
    grad_mats = (
        grad_branch_w,
        grad_rec_w,
        grad_rate,
        grad_input,
        grad_out,
        grad_gate,
        grad_up,
        grad_down,
    )
    blocks = (
        lax.psum_scatter(grad_mats[0], "seq", scatter_dimension=0, tiled=True),
        lax.psum_scatter(grad_mats[1], "seq", scatter_dimension=0, tiled=True),
        lax.psum_scatter(grad_mats[2], "seq", scatter_dimension=0, tiled=True),
        lax.psum_scatter(grad_mats[3], "seq", scatter_dimension=0, tiled=True),
        lax.psum_scatter(grad_mats[4], "seq", scatter_dimension=0, tiled=True),
        lax.psum_scatter(grad_mats[5], "seq", scatter_dimension=0, tiled=True),
        lax.psum_scatter(grad_mats[6], "seq", scatter_dimension=0, tiled=True),
        lax.psum_scatter(grad_mats[7], "seq", scatter_dimension=0, tiled=True),
    )
    summed = lax.psum(
        (blocks[0], blocks[1], blocks[2], blocks[3], blocks[4], blocks[5], blocks[6], blocks[7]),
        "rows",
    )
    small = lax.psum(
        (
            grad_norm1,
            grad_conv_weight,
            grad_conv_bias,
            grad_rate_bias,
            grad_input_bias,
            grad_decay,
            grad_norm2,
        ),
        ("rows", "seq"),
    )
    return (
        mixed,
        token_grad,
        small[0],
        summed[0],
        summed[1],
        small[1],
        small[2],
        summed[2],
        small[3],
        summed[3],
        small[4],
        small[5],
        summed[4],
        small[6],
        summed[5],
        summed[6],
        summed[7],
    )


def body(*args):
    if lax.axis_size("rows") == 4 and lax.axis_size("seq") == 8:
        return staged_body(*args)
    return plain_body(*args)


def staged_body(
    tokens,
    bounds,
    norm1_gain,
    w_branch,
    w_rec,
    conv_weight,
    conv_bias,
    w_rate,
    rate_bias,
    w_input,
    input_bias,
    decay_param,
    w_out,
    norm2_gain,
    w_gate,
    w_up,
    w_down,
    cotangent,
):
    row_count, tok_count, model_width = tokens.shape
    rec_width = w_rec.shape[1]
    flat_tokens = tokens.reshape(-1, model_width)
    gains = jnp.stack([norm1_gain, norm2_gain])
    decay_scale = -8.0 * jax.nn.softplus(decay_param)
    vectors = jnp.concatenate(
        [conv_weight.reshape(-1), conv_bias, rate_bias, input_bias, decay_scale]
    ).reshape(8, rec_width)
    fulls, saved = forward_all(
        (w_rec, w_rate, w_input, w_branch, w_out, w_gate, w_up, w_down),
        cotangent.reshape(-1, model_width),
        flat_tokens,
        bounds,
        gains,
        vectors,
    )
    full_rec, full_rate, full_input, full_branch, full_out, half_gate, half_up, half_down = fulls
    normed, padded, conv_out, conv_low, rate_pre, input_pre = saved[:6]
    states, branch_pre, mixed_in, resid, carried, pair_normed2, pair_cotangent, marks = saved[6:]
    gate_pre = forward_product(pair_normed2, half_gate)
    up_pre = forward_product(pair_normed2, half_up)
    hidden = (jax.nn.gelu(gate_pre, approximate=True) * up_pre).astype(jnp.bfloat16)
    part_mixed = forward_product(hidden, half_down).astype(jnp.bfloat16)
    grad_down = outer(hidden, pair_cotangent)
    grad_hidden = back_product(pair_cotangent, half_down)
    _, pull_mlp = jax.vjp(
        lambda gate_arg, up_arg: jax.nn.gelu(gate_arg, approximate=True) * up_arg, gate_pre, up_pre
    )
    grad_gate_pre, grad_up_pre = pull_mlp(grad_hidden)
    gate_low = grad_gate_pre.astype(jnp.bfloat16)
    up_low = grad_up_pre.astype(jnp.bfloat16)
    part_normed2 = (back_product(gate_low, half_gate) + back_product(up_low, half_up)).astype(
        jnp.bfloat16
    )
    half = part_mixed.shape[0] // 2
    twins = [(s, s + 2 - 4 * (s // 2 % 2)) for s in range(lax.axis_size("seq"))]
    twin_normed2 = lax.ppermute(part_normed2[half:], "seq", twins)
    grad_gate = outer(pair_normed2, gate_low)
    grad_up = outer(pair_normed2, up_low)
    low = jnp.bfloat16
    ff, rest = backward_all(
        [g.astype(low) for g in (grad_down, grad_gate, grad_up)],
        (part_mixed, part_normed2, twin_normed2),
        (full_out, full_rate, full_input, full_branch, full_rec),
        (
            states.reshape(row_count, tok_count, rec_width),
            branch_pre,
            rate_pre,
            input_pre,
            conv_out,
            padded,
        ),
        (
            marks,
            flat_tokens,
            cotangent.reshape(-1, model_width),
            resid,
            normed,
            conv_low,
            mixed_in,
            carried,
        ),
        (gains, vectors),
    )
    reduced, (token_grad, mixed, swap_rec, swap_rate, sums) = tuple(ff), rest[4:]
    rate, into, branch, recur = rest[:4]
    rec, sums = reduce_all((recur, rate, into, branch), (swap_rec, swap_rate), sums, 2)
    (down, gate, up, out, recur, rate, into, branch), (mixed, token_grad) = finish(
        reduced + tuple(rec), (mixed, token_grad)
    )
    return (
        mixed.reshape(tokens.shape),
        token_grad.reshape(tokens.shape),
        sums[8, :model_width],
        branch,
        recur,
        sums[:4],
        sums[4],
        rate,
        sums[6],
        into,
        sums[7],
        -8.0 * jax.nn.sigmoid(decay_param) * sums[5],
        out,
        sums[9, :model_width],
        gate,
        up,
        down,
    )


def solution(mesh):
    in_specs = (
        P("rows", "seq", None),
        P("rows", None),
        P(),
        P("seq", None),
        P("seq", None),
        P(),
        P(),
        P("seq", None),
        P(),
        P("seq", None),
        P(),
        P(),
        P("seq", None),
        P(),
        P("seq", None),
        P("seq", None),
        P("seq", None),
        P("rows", "seq", None),
    )
    out_specs = (
        P("rows", "seq", None),
        P("rows", "seq", None),
        P(),
        P("seq", None),
        P("seq", None),
        P(),
        P(),
        P("seq", None),
        P(),
        P("seq", None),
        P(),
        P(),
        P("seq", None),
        P(),
        P("seq", None),
        P("seq", None),
        P("seq", None),
    )
    return jax.shard_map(
        body, mesh=mesh, in_specs=in_specs, out_specs=out_specs, check_vma=False)
```
